32 devices in a mesh: seq: 2 (over x), rows: 16 (over z, y, core).
Axes of the slice: x: 2, y: 2, z: 4, core: 2. Of those that a mesh axis runs over, the one named last changes fastest.
Arguments:
- tokens: bfloat16 [64, 512, 768], P('rows', 'seq'), may hold values from -6 to 6
- doc_lengths: int32 [64], P('rows'), may hold values from 64 to 512, as said below
- rel_buckets: int32 [1023], replicated, may hold values from 0 to 31
- w_query: bfloat16 [768, 768], P(('seq', 'rows')), may hold values from -0.0546875 to 0.0546875
- w_key: bfloat16 [768, 768], P(('seq', 'rows')), may hold values from -0.21875 to 0.21875
- w_value: bfloat16 [768, 768], P(('seq', 'rows')), may hold values from -0.21875 to 0.21875
- w_output: bfloat16 [768, 768], P(('seq', 'rows')), may hold values from -0.875 to 0.875
- w_inner: bfloat16 [768, 3072], P(('seq', 'rows')), may hold values from -0.21875 to 0.21875
- w_outer: bfloat16 [3072, 768], P(('seq', 'rows')), may hold values from -0.109375 to 0.109375
- attn_gain: bfloat16 [768], P(('seq', 'rows')), may hold values from 0.5 to 1.5
- ffn_gain: bfloat16 [768], P(('seq', 'rows')), may hold values from 0.5 to 1.5
- bias_table: bfloat16 [32, 12], replicated, may hold values from -4 to 4
- out_grad: bfloat16 [64, 512, 768], P('rows', 'seq'), may hold values from -6 to 6
Outputs:
- activations: bfloat16 [64, 512, 768], P('rows', 'seq')
- tokens_grad: float32 [64, 512, 768], P('rows', 'seq')
- grad_query: float32 [768, 768], P(('seq', 'rows'))
- grad_key: float32 [768, 768], P(('seq', 'rows'))
- grad_value: float32 [768, 768], P(('seq', 'rows'))
- grad_output: float32 [768, 768], P(('seq', 'rows'))
- grad_inner: float32 [768, 3072], P(('seq', 'rows'))
- grad_outer: float32 [3072, 768], P(('seq', 'rows'))
- grad_attn_gain: float32 [768], P(('seq', 'rows'))
- grad_ffn_gain: float32 [768], P(('seq', 'rows'))
- grad_table: float32 [32, 12], replicated
The draws below stay inside these ranges and needn't reach their ends.
Inputs may be any that keep to these rules, and one draw needn't show every extreme that they name: Each row holds one document of doc_lengths tokens, then padding. Among the 4 rows of each index of rows, at least one has length 512.
All inputs are finite; a program needn't handle non-finite values.
Results may differ from the reference program's by a relative error of at most 0.012.
The reference program's roundings to bfloat16 on the way count: a program that leaves them out, or rounds other values in their place, can miss the bound.
Values may be sent and summed in bfloat16 or wider, within the bound.
A program may use at most 256 MiB of HBM per device.

```python
import jax
import jax.numpy as jnp
from jax import lax

D = 768
H = 12
HD = 64
FF = 3072
NB = 32
LEN = 512
ROWS_DEV = 4
ROWS = 64


def draw_doc_lengths(key, part):
    key = jax.random.fold_in(key, 7)
    first, second = jax.random.split(key)
    lens = jax.random.randint(first, (ROWS,), LEN // 8, LEN + 1)
    pick = jax.random.randint(second, (ROWS // ROWS_DEV, 1), 0, ROWS_DEV)
    grid = lens.reshape(ROWS // ROWS_DEV, ROWS_DEV)
    grid = jnp.where(jnp.arange(ROWS_DEV)[None, :] == pick, LEN, grid)
    return grid.reshape(ROWS).astype(jnp.int32)


def set_ends(values, stream_key, low, top_value):
    longest = values.shape.index(max(values.shape))
    spots = []
    for shift in (0, 1):
        where = [jax.random.randint(jax.random.fold_in(stream_key, axis), (), 0, length) for axis, length in enumerate(values.shape)]
        where[longest] = (where[longest] + shift) % values.shape[longest]
        spots.append(tuple(where))
    return values.at[spots[0]].set(low).at[spots[1]].set(top_value)


def strengthened(result, stream_key, source, target, blocks, factor):
    owner, partner = [(jnp.arange(result.shape[axis_at]) // (result.shape[axis_at] // blocks)).reshape([-1 if axis == axis_at else 1 for axis in range(result.ndim)]) for axis_at in (source, target)]
    chosen = jax.random.permutation(stream_key, blocks)[partner]
    strong = (owner == chosen) | (owner == (partner + blocks // 2) % blocks)
    return jnp.where(strong, factor * result, result)


def block_scale(rng, dims, cuts, least, top_value):
    def one(position, blocks):
        steps = jax.random.uniform(jax.random.fold_in(jax.random.fold_in(rng, 6), position), (blocks,), jnp.float32, least / len(cuts), top_value / len(cuts))
        return jnp.repeat(jnp.exp(steps), dims[position] // blocks).reshape((-1,) + (1,) * (len(dims) - position - 1))

    level = one(*cuts[0])
    for cut in cuts[1:]:
        level = level * one(*cut)
    return level


def scatter_about(key, extent, width, most, cuts=(), kind=jnp.bfloat16):
    entries = width * jax.random.normal(key, extent, jnp.float32)
    if cuts:
        entries = entries * block_scale(key, extent, cuts, -0.22, 0.18)
    return jnp.clip(entries, -most, most).astype(kind)


def noise_with(stream_key, dims, spread, reach, shards, heavy, held_as=jnp.bfloat16):
    result = spread * jax.random.normal(stream_key, dims, jnp.float32)
    if shards:
        result = result * block_scale(stream_key, dims, shards, -0.22, 0.18)
    return jnp.clip(strengthened(result, jax.random.fold_in(stream_key, 3), *heavy), -reach, reach).astype(held_as)


def setup_inputs(seed: int = 0) -> dict:
    splits = jax.random.split(jax.random.key(seed), 14)
    return {
        "tokens": noise_with(splits[0], (ROWS, LEN, D), 1.0, 6.0, ((0, 16), (1, 2)), (0, 2, 16, 2.0)),
        "doc_lengths": draw_doc_lengths(jax.random.fold_in(splits[13], 71), 0),
        "rel_buckets": set_ends(jax.random.randint(splits[2], (2 * LEN - 1,), 0, NB), jax.random.fold_in(splits[2], 1), 0, NB - 1).astype(jnp.int32),
        "w_query": scatter_about(splits[3], (D, D), (D * HD // 4) ** -0.5, 0.0546875, ((0, 32),)),
        "w_key": scatter_about(splits[4], (D, D), D ** -0.5, 0.21875, ((0, 32),)),
        "w_value": scatter_about(splits[5], (D, D), D ** -0.5, 0.21875, ((0, 32),)),
        "w_output": scatter_about(splits[6], (D, D), (D // 16) ** -0.5, 0.875, ((0, 32),)),
        "w_inner": scatter_about(splits[7], (D, FF), D ** -0.5, 0.21875, ((0, 32),)),
        "w_outer": scatter_about(splits[8], (FF, D), FF ** -0.5, 0.109375, ((0, 32),)),
        "attn_gain": jnp.clip(1.0 + 0.1 * jax.random.normal(splits[9], (D,), jnp.float32), 0.5, 1.5).astype(jnp.bfloat16),
        "ffn_gain": jnp.clip(1.0 + 0.1 * jax.random.normal(splits[10], (D,), jnp.float32), 0.5, 1.5).astype(jnp.bfloat16),
        "bias_table": scatter_about(splits[11], (NB, H), 1.0, 4.0),
        "out_grad": scatter_about(splits[12], (ROWS, LEN, D), 1.0, 6.0, ((0, 16), (1, 2))),
    }


@jax.custom_vjp
def low(v):
    return lax.optimization_barrier(v.astype(jnp.bfloat16)).astype(jnp.float32)

@jax.custom_vjp
def low_back(v):
    return v

def low_keep(v):
    return (low(v), None)

def low_pass(kept, grad):
    return (grad,)

def back_keep(v):
    return (v, None)

def back_low(kept, grad):
    return (low(grad),)
low.defvjp(low_keep, low_pass)
low_back.defvjp(back_keep, back_low)
EPS = 1e-06
NEG = -1000000000.0
HIGH = lax.Precision.HIGHEST

def normed(h, gain):
    return h * lax.rsqrt(lax.optimization_barrier(jnp.mean(h * h, axis=-1, keepdims=True)) + EPS) * gain

def matmul(a, b):
    return jnp.einsum('btd,de->bte', a, b, precision=HIGH)

def forward(x, wq, wk, wv, wo, wi, wf, g1, g2, table, doc_lengths, rel_buckets):
    place = jnp.arange(LEN, dtype=jnp.int32)
    offset = place[None, :] - place[:, None] + (LEN - 1)
    bias = jnp.transpose(table[rel_buckets[offset]], (2, 0, 1))

    def block(args):
        xb, lens = args
        count = xb.shape[0]
        n1 = low(normed(xb, g1))
        q = low_back(low(matmul(n1, wq))).reshape(count, LEN, H, HD)
        k = low_back(low(matmul(n1, wk))).reshape(count, LEN, H, HD)
        v = low_back(low(matmul(n1, wv))).reshape(count, LEN, H, HD)
        s = jnp.einsum('bqhd,bkhd->bhqk', q, k, precision=HIGH) + bias[None]
        valid = place[None, :] < lens[:, None]
        s = jnp.where(valid[:, None, None, :], s, NEG)
        s = low_back(s)
        top = lax.optimization_barrier(jnp.max(s, axis=-1, keepdims=True))
        expo = jnp.exp(s - top)
        p = expo / lax.optimization_barrier(jnp.sum(expo, axis=-1, keepdims=True))
        pb = low(p)
        o = jnp.einsum('bhqk,bkhd->bqhd', pb, v, precision=HIGH).reshape(count, LEN, D)
        o = low_back(low(o))
        h1 = xb + low_back(matmul(o, wo))
        n2 = low(normed(h1, g2))
        u = low_back(matmul(n2, wi))
        a = low(jax.nn.gelu(u))
        return h1 + low_back(matmul(a, wf))
    groups = ROWS // 8
    ys = lax.map(jax.checkpoint(block), (x.reshape(groups, 8, LEN, D), doc_lengths.reshape(groups, 8)))
    return ys.reshape(ROWS, LEN, D)

def reference(tokens, doc_lengths, rel_buckets, w_query, w_key, w_value, w_output, w_inner, w_outer, attn_gain, ffn_gain, bias_table, out_grad):
    floats = [a.astype(jnp.float32) for a in (tokens, w_query, w_key, w_value, w_output, w_inner, w_outer, attn_gain, ffn_gain, bias_table)]

    def run(x, wq, wk, wv, wo, wi, wf, g1, g2, table):
        return forward(x, wq, wk, wv, wo, wi, wf, g1, g2, table, doc_lengths, rel_buckets)
    out, pull = jax.vjp(run, *floats)
    grads = pull(out_grad.astype(jnp.float32))
    return (out.astype(jnp.bfloat16), grads[0], grads[1], grads[2], grads[3], grads[4], grads[5], grads[6], grads[7], grads[8], grads[9])
```

```python
import functools

import jax
import jax.numpy as jnp
from jax import lax
from jax.experimental import pallas as pl
from jax.experimental.pallas import tpu as pltpu
from jax.sharding import PartitionSpec as P

MB = 2


EPS = 1e-06
NEG = -1000000000.0
HIGH = lax.Precision.HIGHEST


def normed(h, gain):
    return h * lax.rsqrt(jnp.mean(h * h, axis=-1, keepdims=True) + EPS) * gain


def fetch(shards):
    return (
        lax.all_gather(shards[0], ("seq", "rows"), axis=0, tiled=True),
        lax.all_gather(shards[1], ("seq", "rows"), axis=0, tiled=True),
        lax.all_gather(shards[2], ("seq", "rows"), axis=0, tiled=True),
        lax.all_gather(shards[3], ("seq", "rows"), axis=0, tiled=True),
        lax.all_gather(shards[4], ("seq", "rows"), axis=0, tiled=True),
        lax.all_gather(shards[5], ("seq", "rows"), axis=0, tiled=True),
        lax.all_gather(shards[6], ("seq", "rows"), axis=0, tiled=True),
        lax.all_gather(shards[7], ("seq", "rows"), axis=0, tiled=True),
    )


def local(
    tokens,
    doc_lengths,
    rel_buckets,
    w_query,
    w_key,
    w_value,
    w_output,
    w_inner,
    w_outer,
    attn_gain,
    ffn_gain,
    bias_table,
    out_grad,
):
    f32 = jnp.float32
    bf16 = jnp.bfloat16
    rows_dev, span, width = tokens.shape
    n_bins, heads = bias_table.shape
    head_dim = width // heads
    seq_count = lax.axis_size("seq")
    seq_place = lax.axis_index("seq")
    total = span * seq_count
    q_start = seq_place * span
    per = rows_dev // MB
    flat_rows = per * span
    shards = (w_query, w_key, w_value, w_output, w_inner, w_outer, attn_gain, ffn_gain)
    table = bias_table.astype(f32)
    k_pos = jnp.arange(total, dtype=jnp.int32)
    onehot = (rel_buckets[:, None] == jnp.arange(n_bins, dtype=jnp.int32)[None, :]).astype(f32)
    rel_bias = jnp.dot(onehot, table, precision=HIGH)
    spread = jnp.concatenate([rel_bias.T, jnp.zeros((heads, 1), f32)], axis=1)
    tiled = jnp.tile(spread, (1, total))
    full_bias = tiled[:, : total * (2 * total - 1)].reshape(heads, total, 2 * total - 1)[
        :, :, total - 1 :
    ]
    bias = lax.dynamic_slice_in_dim(full_bias, q_start, span, 1)
    ff_width = w_inner.shape[1]
    grad_wq = jnp.zeros((width, width), f32)
    grad_wk = jnp.zeros((width, width), f32)
    grad_wv = jnp.zeros((width, width), f32)
    grad_wo = jnp.zeros((width, width), f32)
    grad_wi = jnp.zeros((width, ff_width), f32)
    grad_wf = jnp.zeros((ff_width, width), f32)
    grad_g1 = jnp.zeros((width,), f32)
    grad_g2 = jnp.zeros((width,), f32)
    grad_bias = jnp.zeros((heads, span, total), f32)
    outputs = []
    input_grads = []
    for batch in range(MB):
        whole = fetch(shards)
        wq, wk, wv, wo, wi, wf, gain_one, gain_two = whole
        g1 = gain_one.astype(f32)
        g2 = gain_two.astype(f32)
        first = batch * per
        xflat = tokens[first : first + per].astype(f32).reshape(flat_rows, width)
        lens = doc_lengths[first : first + per]
        upstream = out_grad[first : first + per].reshape(flat_rows, width)
        n1 = normed(xflat, g1).astype(bf16)
        query = jnp.dot(n1, wq, preferred_element_type=f32).astype(bf16)
        key_local = jnp.dot(n1, wk, preferred_element_type=f32).astype(bf16)
        value_local = jnp.dot(n1, wv, preferred_element_type=f32).astype(bf16)
        keys_all, values_all = (
            lax.all_gather(key_local.reshape(per, span, width), "seq", axis=1, tiled=True),
            lax.all_gather(value_local.reshape(per, span, width), "seq", axis=1, tiled=True),
        )
        q4 = query.reshape(per, span, heads, head_dim)
        k4 = keys_all.reshape(per, total, heads, head_dim)
        v4 = values_all.reshape(per, total, heads, head_dim)
        valid = k_pos[None, :] < lens[:, None]

        def scores():
            raw = jnp.einsum("bqhd,bkhd->bhqk", q4, k4, preferred_element_type=f32) + bias[None]
            return jnp.where(valid[:, None, None, :], raw, NEG)

        first_scores = scores()
        top = jnp.max(first_scores, axis=-1, keepdims=True)
        expo = jnp.exp(first_scores - top)
        denom = jnp.sum(expo, axis=-1, keepdims=True)
        probs_low = (expo / denom).astype(bf16)
        mixed = jnp.einsum("bhqk,bkhd->bqhd", probs_low, v4, preferred_element_type=f32)
        mixed = mixed.reshape(flat_rows, width).astype(bf16)
        h1 = xflat + jnp.dot(mixed, wo, preferred_element_type=f32)
        n2 = normed(h1, g2).astype(bf16)
        inner = jnp.dot(n2, wi, preferred_element_type=f32)
        act_full, gelu_pull = jax.vjp(jax.nn.gelu, inner)
        act = act_full.astype(bf16)
        result = h1 + jnp.dot(act, wf, preferred_element_type=f32)
        outputs.append(result.astype(bf16).reshape(per, span, width))
        grad_wf = grad_wf + jnp.einsum("tf,td->fd", act, upstream, preferred_element_type=f32)
        d_act = jnp.einsum("td,fd->tf", upstream, wf, preferred_element_type=f32)
        d_inner = gelu_pull(d_act)[0].astype(bf16)
        grad_wi = grad_wi + jnp.einsum("td,tf->df", n2, d_inner, preferred_element_type=f32)
        d_n2 = jnp.einsum("tf,df->td", d_inner, wi, preferred_element_type=f32)
        norm_pull = jax.vjp(normed, h1, g2)[1]
        dh_part, dg_two = norm_pull(d_n2)
        grad_g2 = grad_g2 + dg_two
        dh1 = upstream.astype(f32) + dh_part
        d_attn = dh1.astype(bf16)
        grad_wo = grad_wo + jnp.einsum("td,te->de", mixed, d_attn, preferred_element_type=f32)
        d_mixed = jnp.einsum("te,de->td", d_attn, wo, preferred_element_type=f32).astype(bf16)
        dm4 = d_mixed.reshape(per, span, heads, head_dim)
        probs = jnp.exp(scores() - top) / denom
        d_probs = jnp.einsum("bqhd,bkhd->bhqk", dm4, v4, preferred_element_type=f32)
        value_terms = jnp.einsum("bhqk,bqhd->bkhd", probs_low, dm4, preferred_element_type=f32)
        delta = jnp.sum(probs * d_probs, axis=-1, keepdims=True)
        d_scores = (probs * (d_probs - delta)).astype(bf16)
        grad_bias = grad_bias + jnp.sum(d_scores.astype(f32), axis=0)
        d_query = jnp.einsum("bhqk,bkhd->bqhd", d_scores, k4, preferred_element_type=f32)
        d_query = d_query.reshape(flat_rows, width).astype(bf16)
        key_terms = jnp.einsum("bhqk,bqhd->bkhd", d_scores, q4, preferred_element_type=f32)
        key_share, value_share = (
            lax.psum_scatter(
                key_terms.reshape(per, total, width), "seq", scatter_dimension=1, tiled=True
            ),
            lax.psum_scatter(
                value_terms.reshape(per, total, width), "seq", scatter_dimension=1, tiled=True
            ),
        )
        d_key = key_share.reshape(flat_rows, width).astype(bf16)
        d_value = value_share.reshape(flat_rows, width).astype(bf16)
        grad_wq = grad_wq + jnp.einsum("td,te->de", n1, d_query, preferred_element_type=f32)
        grad_wk = grad_wk + jnp.einsum("td,te->de", n1, d_key, preferred_element_type=f32)
        grad_wv = grad_wv + jnp.einsum("td,te->de", n1, d_value, preferred_element_type=f32)
        d_n1 = jnp.einsum("te,de->td", d_query, wq, preferred_element_type=f32)
        d_n1 = d_n1 + jnp.einsum("te,de->td", d_key, wk, preferred_element_type=f32)
        d_n1 = d_n1 + jnp.einsum("te,de->td", d_value, wv, preferred_element_type=f32)
        first_pull = jax.vjp(normed, xflat, g1)[1]
        dx_part, dg_one = first_pull(d_n1)
        grad_g1 = grad_g1 + dg_one
        input_grads.append((dh1 + dx_part).reshape(per, span, width))
    owned = (
        lax.psum_scatter(grad_wq, ("seq", "rows"), scatter_dimension=0, tiled=True),
        lax.psum_scatter(grad_wk, ("seq", "rows"), scatter_dimension=0, tiled=True),
        lax.psum_scatter(grad_wv, ("seq", "rows"), scatter_dimension=0, tiled=True),
        lax.psum_scatter(grad_wo, ("seq", "rows"), scatter_dimension=0, tiled=True),
        lax.psum_scatter(grad_wi, ("seq", "rows"), scatter_dimension=0, tiled=True),
        lax.psum_scatter(grad_wf, ("seq", "rows"), scatter_dimension=0, tiled=True),
        lax.psum_scatter(grad_g1, ("seq", "rows"), scatter_dimension=0, tiled=True),
        lax.psum_scatter(grad_g2, ("seq", "rows"), scatter_dimension=0, tiled=True),
    )
    grad_full = lax.dynamic_update_slice_in_dim(
        jnp.zeros((heads, total, total), f32), grad_bias, q_start, 1
    )
    widened = jnp.pad(grad_full, ((0, 0), (0, 0), (total - 1, 0)))
    folded = jnp.pad(widened.reshape(heads, total * (2 * total - 1)), ((0, 0), (0, total)))
    rel_grad = jnp.sum(folded.reshape(heads, total, 2 * total), axis=1)[:, : 2 * total - 1]
    table_local = jnp.dot(onehot.T, rel_grad.T, precision=HIGH)
    table_grad = lax.psum(table_local, ("seq", "rows"))
    result_rows = jnp.concatenate(outputs, axis=0)
    grad_rows = jnp.concatenate(input_grads, axis=0)
    return (
        result_rows,
        grad_rows,
        owned[0],
        owned[1],
        owned[2],
        owned[3],
        owned[4],
        owned[5],
        owned[6],
        owned[7],
        table_grad,
    )


MESH_ID = pl.DeviceIdType.MESH
HBM = pl.BlockSpec(memory_space=pl.ANY)
VMEM = pl.BlockSpec(memory_space=pltpu.VMEM)
SMEM = pl.BlockSpec(memory_space=pltpu.SMEM)
BF = jnp.bfloat16
F32 = jnp.float32
NX, NZ, NY, NC = 2, 4, 2, 2


def rcopy(src, dst, send, recv, to):
    return pltpu.make_async_remote_copy(
        src_ref=src, dst_ref=dst, send_sem=send, recv_sem=recv, device_id=to, device_id_type=MESH_ID
    )


class Place:
    def __init__(self):
        self.x = lax.axis_index("seq")
        r = lax.axis_index("rows")
        self.c = lax.rem(r, 2)
        self.y = lax.rem(r // 2, 2)
        self.z = r // 4
        self.core = self.at(self.x, self.y, self.z, 1 - self.c)
        self.xn = self.at(1 - self.x, self.y, self.z, self.c)
        self.yn = self.at(self.x, 1 - self.y, self.z, self.c)
        self.zp = [None] + [self.at(self.x, self.y, self.zz(j), self.c) for j in range(1, NZ)]

    def at(self, x, y, z, c):
        return (x, z * 4 + y * 2 + c)

    def zz(self, j):
        return lax.rem(self.z + j, NZ)

    def barrier(self):
        sem = pltpu.get_barrier_semaphore()
        peers = [self.core, self.xn, self.yn] + self.zp[1:]
        for p in peers:
            pl.semaphore_signal(sem, inc=1, device_id=p, device_id_type=MESH_ID)
        pl.semaphore_wait(sem, len(peers))


class GatherXZY:
    def __init__(self, me, w, ss, rr, dd):
        self.me, self.w, self.ss, self.rr, self.dd = me, w, ss, rr, dd
        self.nh = w.shape[-1] // 2

    def ref(self, x, z, y, c):
        cols = pl.ds(pl.multiple_of(c * self.nh, 128), self.nh)
        return self.w.at[x, z, y, :, cols]

    def pair(self, z, y, c):
        cols = pl.ds(pl.multiple_of(c * self.nh, 128), self.nh)
        return self.w.at[:, z, y, :, cols]

    def send(self, ref, s, recv, to):
        rcopy(ref, ref, self.ss.at[s], recv, to).start()

    def got(self, ref, recv):
        rcopy(ref, ref, self.ss.at[0], recv, self.me.core).wait_recv()

    def start(self):
        m = self.me
        self.send(self.ref(m.x, m.z, m.y, m.c), 0, self.rr.at[0], m.xn)

    def step_x(self):
        m = self.me
        self.got(self.ref(1 - m.x, m.z, m.y, m.c), self.rr.at[0])
        p = self.pair(m.z, m.y, m.c)
        for j in range(1, NZ):
            self.send(p, j, self.rr.at[NZ - j], m.zp[j])
        self.send(p, 4, self.rr.at[4], m.yn)
        self.send(p, 8, self.dd.at[0], m.core)

    def step_z(self, j):
        m = self.me
        p = self.pair(m.zz(j), m.y, m.c)
        self.got(p, self.rr.at[j])
        self.send(p, 4 + j, self.rr.at[4 + j], m.yn)
        self.send(p, 8 + j, self.dd.at[j], m.core)

    def step_y(self, j):
        m = self.me
        p = self.pair(m.zz(j), 1 - m.y, m.c)
        self.got(p, self.rr.at[4 + j])
        self.send(p, 12 + j, self.dd.at[4 + j], m.core)

    def done(self):
        m = self.me
        for j in range(NZ):
            self.got(self.pair(m.zz(j), m.y, 1 - m.c), self.dd.at[j])
        for j in range(NZ):
            self.got(self.pair(m.zz(j), 1 - m.y, 1 - m.c), self.dd.at[4 + j])

    def sent(self):
        m = self.me
        one = self.ref(m.x, m.z, m.y, m.c)
        rcopy(one, one, self.ss.at[0], self.rr.at[0], m.core).wait_send()
        p = self.pair(m.z, m.y, m.c)
        for s in range(1, 16):
            rcopy(p, p, self.ss.at[s], self.rr.at[0], m.core).wait_send()


class GatherZYX:
    def __init__(self, me, w, ss, rr, dd):
        self.me, self.w, self.ss, self.rr, self.dd = me, w, ss, rr, dd

    def send(self, ref, s, recv, to):
        rcopy(ref, ref, self.ss.at[s], recv, to).start()

    def got(self, ref, recv):
        rcopy(ref, ref, self.ss.at[0], recv, self.me.core).wait_recv()

    def start(self):
        m = self.me
        own = self.w.at[m.x, m.z, m.y, m.c]
        for j in range(1, NZ):
            self.send(own, j - 1, self.rr.at[NZ - j - 1], m.zp[j])
        self.send(own, 3, self.rr.at[3], m.yn)

    def step_z(self, j):
        m = self.me
        b = self.w.at[m.x, m.zz(j), m.y, m.c]
        self.got(b, self.rr.at[j - 1])
        self.send(b, 5 + j, self.rr.at[3 + j], m.yn)

    def step_y(self, j):
        m = self.me
        self.got(self.w.at[m.x, m.zz(j), 1 - m.y, m.c], self.rr.at[3 + j])
        p = self.w.at[m.x, m.zz(j), :, m.c]
        self.send(p, 4 if j == 0 else 8 + j, self.rr.at[7 + j], m.xn)
        self.send(p, 5 if j == 0 else 11 + j, self.dd.at[j], m.core)

    def step_x(self, j):
        m = self.me
        p = self.w.at[1 - m.x, m.zz(j), :, m.c]
        self.got(p, self.rr.at[7 + j])
        self.send(p, 15 + j, self.dd.at[4 + j], m.core)

    def done(self):
        m = self.me
        for j in range(NZ):
            self.got(self.w.at[m.x, m.zz(j), :, 1 - m.c], self.dd.at[j])
        for j in range(NZ):
            self.got(self.w.at[1 - m.x, m.zz(j), :, 1 - m.c], self.dd.at[4 + j])

    def sent(self):
        m = self.me
        one = self.w.at[m.x, m.z, m.y, m.c]
        p = self.w.at[m.x, m.z, :, m.c]
        for s in range(19):
            r = one if s in (0, 1, 2, 3, 6, 7, 8) else p
            rcopy(r, r, self.ss.at[s], self.rr.at[0], m.core).wait_send()


def own_block(me, mine, theirs, w, nh):
    cols = pl.ds(pl.multiple_of(me.c * nh, 128), nh)
    a = mine[:, cols].astype(F32)[:24]
    b = theirs[...].astype(F32)[:24]
    first = jnp.where(me.c == 0, a, b)
    second = jnp.where(me.c == 0, b, a)
    w[me.x, me.z, me.y, :, cols] = jnp.concatenate([first, second], axis=0).astype(BF)


def forward_kernel(
    tok, gin, pa, pb, pd, relb, table, lens,
    wa_o, wb_o, wd_o, x_o, g_o, n1_o, qkv_o, o_o,
    WA, WB, WD, X, N1, QKV, O, RA, RB, M, R,
    ts, tr, tl, gs, gr, gl, es, er,
    as_, ar, ad, bs, br, bd, ds_, dr, dd, os_,
):
    me = Place()
    x, y, z, c = me.x, me.y, me.z, me.c
    length = X.shape[1] * X.shape[2]
    span = X.shape[2]
    width = X.shape[3]
    na, nb = RA.shape[1], RB.shape[1]
    heads = M.shape[0]
    hd = width // heads
    gath_a = GatherXZY(me, WA, as_, ar, ad)
    gath_b = GatherXZY(me, WB, bs, br, bd)
    gath_d = GatherZYX(me, WD, ds_, dr, dd)
    me.barrier()
    ea = rcopy(pa.at[:, pl.ds(pl.multiple_of((1 - c) * na, 128), na)], RA, es.at[0], er.at[0], me.core)
    eb = rcopy(pb.at[:, pl.ds(pl.multiple_of((1 - c) * nb, 128), nb)], RB, es.at[1], er.at[1], me.core)
    ea.start()
    eb.start()
    tok_r = [rcopy(tok.at[2 * (1 - x) + i], X.at[i, x], ts.at[i], tr.at[i], me.xn) for i in range(2)]
    tok_in = [rcopy(X.at[i, 1 - x], X.at[i, 1 - x], ts.at[i], tr.at[i], me.xn) for i in range(2)]
    tok_l = [pltpu.make_async_copy(tok.at[2 * x + i], X.at[i, x], tl.at[i]) for i in range(2)]
    g_r = rcopy(gin.at[pl.ds(2 * (1 - x), 2)], g_o.at[:, x], gs, gr, me.xn)
    g_in = rcopy(g_o.at[:, 1 - x], g_o.at[:, 1 - x], gs, gr, me.xn)
    g_l = pltpu.make_async_copy(gin.at[pl.ds(2 * x, 2)], g_o.at[:, x], gl)
    ea.wait_recv()
    own_block(me, pa, RA, WA, na)
    gath_a.start()
    for i in range(2):
        tok_r[i].start()
        tok_l[i].start()
    eb.wait_recv()
    own_block(me, pb, RB, WB, nb)
    WD[x, z, y, c] = pd[...]
    cols = relb.shape[1]
    kinds = table.shape[0]
    hot = (lax.broadcasted_iota(jnp.int32, (kinds, cols), 0) == relb[...]).astype(BF)
    R[...] = lax.dot_general(table[...], hot, (((0,), (0,)), ((), ())), preferred_element_type=F32)

    def make_bias(h, carry):
        row = jnp.broadcast_to(R[pl.ds(h, 1), :], (128, cols))
        strip = pltpu.roll(row, cols - 127, 1, stride=1, stride_axis=0)
        M[h] = strip[:, : M.shape[2]]
        return carry

    lax.fori_loop(0, heads, make_bias, 0)
    gath_a.step_x()
    for j in range(1, NZ):
        gath_a.step_z(j)
    for j in range(NZ):
        gath_a.step_y(j)
    gath_b.start()
    gath_d.start()
    g_r.start()
    g_l.start()
    gath_a.done()
    gain = jnp.transpose(WA[:, :, :, :, 0:128].reshape(width, 128).astype(F32))[0:1, :]
    for i in range(2):
        tok_l[i].wait()
        tok_in[i].wait_recv()
        for half in range(2):
            xf = X[i, half].astype(F32)
            scale = lax.rsqrt(jnp.mean(xf * xf, axis=-1, keepdims=True) + EPS)
            N1[pl.ds(i * length + half * span, span), :] = (xf * scale * gain).astype(BF)
        for n in range(3):
            w = WA[:, :, :, :, 256 + n * width : 256 + (n + 1) * width].reshape(width, width)
            QKV[pl.ds(i * length, length), n * width : (n + 1) * width] = jnp.dot(
                N1[pl.ds(i * length, length), :], w, preferred_element_type=F32
            ).astype(BF)
        if i == 0:
            gath_b.step_x()
            gath_d.step_y(0)
    pairs = heads // 2
    low = lax.broadcasted_iota(jnp.int32, (1, 128), 1) < hd
    kpos = lax.broadcasted_iota(jnp.int32, (1, length), 1)
    comm = {
        1: lambda: gath_b.step_z(1), 2: lambda: gath_d.step_z(1), 3: lambda: gath_b.step_y(0),
        5: lambda: gath_b.step_z(2), 6: lambda: gath_d.step_z(2), 8: lambda: gath_b.step_z(3),
        9: lambda: gath_d.step_z(3), 10: lambda: gath_d.step_x(0), 11: lambda: gath_b.step_y(1),
    }

    def attend(t, carry):
        i = t // pairs
        p = lax.rem(t, pairs)
        rows = pl.ds(pl.multiple_of(i * length, length), length)
        k = QKV[rows, pl.ds(pl.multiple_of(width + p * 128, 128), 128)]
        v = QKV[rows, pl.ds(pl.multiple_of(2 * width + p * 128, 128), 128)]
        valid = kpos < lens[2 * x + i]
        zero = jnp.zeros((), BF)
        for qb in range(length // 256):
            qrows = pl.ds(pl.multiple_of(i * length + qb * 256, 256), 256)
            q = QKV[qrows, pl.ds(pl.multiple_of(p * 128, 128), 128)]
            outs = []
            for h in range(2):
                qm = jnp.where(low if h == 0 else jnp.logical_not(low), q, zero)
                s = lax.dot_general(qm, k, (((1,), (1,)), ((), ())), preferred_element_type=F32)
                strips = [
                    M[2 * p + h, :, 128 * (3 - a) : 128 * (3 - a) + length] for a in (2 * qb, 2 * qb + 1)
                ]
                s = jnp.where(valid, s + jnp.concatenate(strips, axis=0), NEG)
                top = jnp.max(s, axis=-1, keepdims=True)
                e = jnp.exp(s - top)
                inv = 1.0 / jnp.sum(e, axis=-1, keepdims=True)
                outs.append(jnp.dot((e * inv).astype(BF), v, preferred_element_type=F32))
            O[qrows, pl.ds(pl.multiple_of(p * 128, 128), 128)] = jnp.where(low, outs[0], outs[1]).astype(BF)
        for at, step in comm.items():
            pl.when(t == at)(step)
        return carry

    lax.fori_loop(0, 2 * pairs, attend, 0)
    gath_d.step_y(1)
    gath_d.step_y(2)
    gath_d.step_x(1)
    gath_b.step_y(2)
    gath_d.step_y(3)
    gath_d.step_x(2)
    gath_b.step_y(3)
    gath_d.step_x(3)
    gath_b.done()
    gath_d.done()
    outs = [(WA, wa_o), (WB, wb_o), (WD, wd_o), (X, x_o), (N1, n1_o), (QKV, qkv_o), (O, o_o)]
    copies = [pltpu.make_async_copy(a, b, os_.at[n]) for n, (a, b) in enumerate(outs)]
    for cp in copies:
        cp.start()
    g_l.wait()
    g_in.wait_recv()
    g_r.wait_send()
    ea.wait_send()
    eb.wait_send()
    for t in tok_r:
        t.wait_send()
    gath_a.sent()
    gath_b.sent()
    gath_d.sent()
    for cp in copies:
        cp.wait()


def forward_call(tok, gin, pa, pb, pd, relb, table, lens, heads):
    rows_dev, span, width = tok.shape
    length = 2 * span
    mine = rows_dev // 2
    flat = mine * length
    dma = pltpu.SemaphoreType.DMA
    na, nb = pa.shape[1] // 2, pb.shape[1] // 2
    wa = (NX, NZ, NY, 48, 2 * na)
    wb = (NX, NZ, NY, 48, 2 * nb)
    wd = (NX, NZ, NY, NC) + pd.shape
    xs = (mine, 2, span, width)
    sds = lambda s: jax.ShapeDtypeStruct(s, BF)
    return pl.pallas_call(
        forward_kernel,
        out_shape=[sds(wa), sds(wb), sds(wd), sds(xs), sds(xs), sds((flat, width)), sds((flat, 3 * width)), sds((flat, width))],
        in_specs=[HBM, HBM, VMEM, VMEM, VMEM, VMEM, VMEM, SMEM],
        out_specs=[HBM] * 8,
        scratch_shapes=[
            pltpu.VMEM(wa, BF), pltpu.VMEM(wb, BF), pltpu.VMEM(wd, BF), pltpu.VMEM(xs, BF),
            pltpu.VMEM((flat, width), BF), pltpu.VMEM((flat, 3 * width), BF), pltpu.VMEM((flat, width), BF),
            pltpu.VMEM((32, na), BF), pltpu.VMEM((32, nb), BF),
            pltpu.VMEM((heads, 128, 896), F32), pltpu.VMEM((128, relb.shape[1]), F32),
            dma((2,)), dma((2,)), dma((2,)), dma, dma, dma, dma((2,)), dma((2,)),
            dma((16,)), dma((8,)), dma((8,)), dma((16,)), dma((8,)), dma((8,)),
            dma((19,)), dma((11,)), dma((8,)), dma((8,)),
        ],
        compiler_params=pltpu.CompilerParams(
            collective_id=0, has_side_effects=True, vmem_limit_bytes=56 * 1024 * 1024
        ),
        name="gather_attend",
    )(tok, gin, pa, pb, pd, relb, table, lens)


def fast(
    tokens, doc_lengths, rel_buckets, w_query, w_key, w_value, w_output, w_inner, w_outer,
    attn_gain, ffn_gain, bias_table, out_grad,
):
    rows_dev, span, width = tokens.shape
    n_bins, heads = bias_table.shape
    hd = width // heads
    length = 2 * span
    mine = rows_dev // 2
    flat = mine * length
    seq = lax.axis_index("seq")
    wide = lambda g: jnp.broadcast_to(g[:, None], (g.shape[0], 128))
    pad8 = lambda a: jnp.pad(a, ((0, 8), (0, 0)))
    pa = pad8(jnp.concatenate([wide(attn_gain), wide(ffn_gain), w_query, w_key, w_value], axis=1))
    pb = pad8(jnp.concatenate([w_output, w_inner], axis=1))
    relb = jnp.pad(rel_buckets, (0, 1))[None, :]
    table = jnp.pad(bias_table, ((0, 0), (0, 128 - heads)))
    wa, wb, wd, xs, g, n1, qkv, o = forward_call(
        tokens, out_grad, pa, pb, w_outer, relb, table, doc_lengths, heads
    )
    wa = wa.reshape(width, -1)
    wb = wb.reshape(width, -1)
    wf = wd.reshape(-1, width)
    g1 = wa[:, 0].astype(F32)
    g2 = wa[:, 128].astype(F32)
    wq, wk, wv = (wa[:, 256 + n * width : 256 + (n + 1) * width] for n in range(3))
    wo, wi = wb[:, :width], wb[:, width:]
    xflat = xs.reshape(flat, width).astype(F32)
    upstream = g.reshape(flat, width)
    h1 = xflat + jnp.dot(o, wo, preferred_element_type=F32)
    n2 = normed(h1, g2).astype(BF)
    inner = jnp.dot(n2, wi, preferred_element_type=F32)
    act_full, gelu_pull = jax.vjp(jax.nn.gelu, inner)
    act = act_full.astype(BF)
    result = (h1 + jnp.dot(act, wf, preferred_element_type=F32)).astype(BF)
    grad_wf = jnp.einsum("tf,td->fd", act, upstream, preferred_element_type=F32)
    d_act = jnp.einsum("td,fd->tf", upstream, wf, preferred_element_type=F32)
    d_inner = gelu_pull(d_act)[0].astype(BF)
    grad_wi = jnp.einsum("td,tf->df", n2, d_inner, preferred_element_type=F32)
    d_n2 = jnp.einsum("tf,df->td", d_inner, wi, preferred_element_type=F32)
    dh_part, grad_g2 = jax.vjp(normed, h1, g2)[1](d_n2)
    dh1 = upstream.astype(F32) + dh_part
    d_attn = dh1.astype(BF)
    grad_wo = jnp.einsum("td,te->de", o, d_attn, preferred_element_type=F32)
    d_mixed = jnp.einsum("te,de->td", d_attn, wo, preferred_element_type=F32).astype(BF)
    split = lambda a: a.reshape(mine, length, heads, hd)
    q4, k4, v4 = (split(qkv[:, n * width : (n + 1) * width]) for n in range(3))
    dm4 = split(d_mixed)
    onehot = (rel_buckets[:, None] == jnp.arange(n_bins, dtype=jnp.int32)[None, :]).astype(F32)
    rel_bias = jnp.dot(onehot, bias_table.astype(F32), precision=HIGH)
    spread = jnp.concatenate([rel_bias.T, jnp.zeros((heads, 1), F32)], axis=1)
    tiled = jnp.tile(spread, (1, length))
    bias = tiled[:, : length * (2 * length - 1)].reshape(heads, length, 2 * length - 1)[:, :, length - 1 :]
    lens = lax.dynamic_slice_in_dim(doc_lengths, seq * mine, mine)
    valid = jnp.arange(length, dtype=jnp.int32)[None, :] < lens[:, None]
    raw = jnp.einsum("bqhd,bkhd->bhqk", q4, k4, preferred_element_type=F32) + bias[None]
    probs = jax.nn.softmax(jnp.where(valid[:, None, None, :], raw, NEG), axis=-1)
    low = probs.astype(BF)
    d_probs = jnp.einsum("bqhd,bkhd->bhqk", dm4, v4, preferred_element_type=F32)
    d_value = jnp.einsum("bhqk,bqhd->bkhd", low, dm4, preferred_element_type=F32)
    delta = jnp.sum(probs * d_probs, axis=-1, keepdims=True)
    d_scores = (probs * (d_probs - delta)).astype(BF)
    grad_bias = jnp.sum(d_scores.astype(F32), axis=0)
    d_query = jnp.einsum("bhqk,bkhd->bqhd", d_scores, k4, preferred_element_type=F32)
    d_key = jnp.einsum("bhqk,bqhd->bkhd", d_scores, q4, preferred_element_type=F32)
    dq, dk, dv = (a.reshape(flat, width).astype(BF) for a in (d_query, d_key, d_value))
    grads = [jnp.einsum("td,te->de", n1, d, preferred_element_type=F32) for d in (dq, dk, dv)]
    d_n1 = sum(jnp.einsum("te,de->td", d, w, preferred_element_type=F32) for d, w in ((dq, wq), (dk, wk), (dv, wv)))
    dx_part, grad_g1 = jax.vjp(normed, xflat, g1)[1](d_n1)
    dx = dh1 + dx_part
    n_dev = lax.axis_size("seq") * lax.axis_size("rows")
    parts = grads + [grad_wo, grad_wi, grad_wf]
    owned = [lax.psum_scatter(a, ("seq", "rows"), scatter_dimension=0, tiled=True) for a in parts]
    widened = jnp.pad(grad_bias, ((0, 0), (0, 0), (length - 1, 0)))
    folded = jnp.pad(widened.reshape(heads, length * (2 * length - 1)), ((0, 0), (0, length)))
    rel_grad = jnp.sum(folded.reshape(heads, length, 2 * length), axis=1)[:, : 2 * length - 1]
    table_local = jnp.dot(onehot.T, rel_grad.T, precision=HIGH)
    small = lax.psum(
        jnp.concatenate([table_local.reshape(-1), grad_g1, grad_g2]), ("seq", "rows")
    )
    cut = n_bins * heads
    me = seq * lax.axis_size("rows") + lax.axis_index("rows")
    gg = small[cut:].reshape(2, n_dev, -1)[:, me]

    def home(a):
        a = a.reshape(mine, 2, span, width)
        keep = lax.dynamic_index_in_dim(a, seq, 1, keepdims=False)
        away = lax.dynamic_index_in_dim(a, 1 - seq, 1, keepdims=False)
        came = lax.ppermute(away, "seq", [(0, 1), (1, 0)])
        return jnp.where(seq == 0, jnp.concatenate([keep, came]), jnp.concatenate([came, keep]))

    return (
        home(result), home(dx), *owned, gg[0], gg[1], small[:cut].reshape(n_bins, heads),
    )


def solution(mesh):
    split = P(("seq", "rows"), None)
    rows = P("rows", "seq", None)
    in_specs = (rows, P("rows"), P()) + (split,) * 6 + (P(("seq", "rows")),) * 2 + (P(), rows)
    out_specs = (rows, rows) + (split,) * 6 + (P(("seq", "rows")),) * 2 + (P(),)
    shape = (mesh.shape["seq"], mesh.shape["rows"])
    program = fast if shape == (NX, NZ * NY * NC) else local
    return jax.shard_map(program, mesh=mesh, in_specs=in_specs, out_specs=out_specs, check_vma=False)
```

```python
import functools

import jax
import jax.numpy as jnp
from jax import lax
from jax.experimental import pallas as pl
from jax.experimental.pallas import tpu as pltpu
from jax.sharding import PartitionSpec as P

MB = 2


EPS = 1e-06
NEG = -1000000000.0
HIGH = lax.Precision.HIGHEST


def normed(h, gain):
    return h * lax.rsqrt(jnp.mean(h * h, axis=-1, keepdims=True) + EPS) * gain


def fetch(shards):
    return (
        lax.all_gather(shards[0], ("seq", "rows"), axis=0, tiled=True),
        lax.all_gather(shards[1], ("seq", "rows"), axis=0, tiled=True),
        lax.all_gather(shards[2], ("seq", "rows"), axis=0, tiled=True),
        lax.all_gather(shards[3], ("seq", "rows"), axis=0, tiled=True),
        lax.all_gather(shards[4], ("seq", "rows"), axis=0, tiled=True),
        lax.all_gather(shards[5], ("seq", "rows"), axis=0, tiled=True),
        lax.all_gather(shards[6], ("seq", "rows"), axis=0, tiled=True),
        lax.all_gather(shards[7], ("seq", "rows"), axis=0, tiled=True),
    )


def local(
    tokens,
    doc_lengths,
    rel_buckets,
    w_query,
    w_key,
    w_value,
    w_output,
    w_inner,
    w_outer,
    attn_gain,
    ffn_gain,
    bias_table,
    out_grad,
):
    f32 = jnp.float32
    bf16 = jnp.bfloat16
    rows_dev, span, width = tokens.shape
    n_bins, heads = bias_table.shape
    head_dim = width // heads
    seq_count = lax.axis_size("seq")
    seq_place = lax.axis_index("seq")
    total = span * seq_count
    q_start = seq_place * span
    per = rows_dev // MB
    flat_rows = per * span
    shards = (w_query, w_key, w_value, w_output, w_inner, w_outer, attn_gain, ffn_gain)
    table = bias_table.astype(f32)
    k_pos = jnp.arange(total, dtype=jnp.int32)
    onehot = (rel_buckets[:, None] == jnp.arange(n_bins, dtype=jnp.int32)[None, :]).astype(f32)
    rel_bias = jnp.dot(onehot, table, precision=HIGH)
    spread = jnp.concatenate([rel_bias.T, jnp.zeros((heads, 1), f32)], axis=1)
    tiled = jnp.tile(spread, (1, total))
    full_bias = tiled[:, : total * (2 * total - 1)].reshape(heads, total, 2 * total - 1)[
        :, :, total - 1 :
    ]
    bias = lax.dynamic_slice_in_dim(full_bias, q_start, span, 1)
    ff_width = w_inner.shape[1]
    grad_wq = jnp.zeros((width, width), f32)
    grad_wk = jnp.zeros((width, width), f32)
    grad_wv = jnp.zeros((width, width), f32)
    grad_wo = jnp.zeros((width, width), f32)
    grad_wi = jnp.zeros((width, ff_width), f32)
    grad_wf = jnp.zeros((ff_width, width), f32)
    grad_g1 = jnp.zeros((width,), f32)
    grad_g2 = jnp.zeros((width,), f32)
    grad_bias = jnp.zeros((heads, span, total), f32)
    outputs = []
    input_grads = []
    for batch in range(MB):
        whole = fetch(shards)
        wq, wk, wv, wo, wi, wf, gain_one, gain_two = whole
        g1 = gain_one.astype(f32)
        g2 = gain_two.astype(f32)
        first = batch * per
        xflat = tokens[first : first + per].astype(f32).reshape(flat_rows, width)
        lens = doc_lengths[first : first + per]
        upstream = out_grad[first : first + per].reshape(flat_rows, width)
        n1 = normed(xflat, g1).astype(bf16)
        query = jnp.dot(n1, wq, preferred_element_type=f32).astype(bf16)
        key_local = jnp.dot(n1, wk, preferred_element_type=f32).astype(bf16)
        value_local = jnp.dot(n1, wv, preferred_element_type=f32).astype(bf16)
        keys_all, values_all = (
            lax.all_gather(key_local.reshape(per, span, width), "seq", axis=1, tiled=True),
            lax.all_gather(value_local.reshape(per, span, width), "seq", axis=1, tiled=True),
        )
        q4 = query.reshape(per, span, heads, head_dim)
        k4 = keys_all.reshape(per, total, heads, head_dim)
        v4 = values_all.reshape(per, total, heads, head_dim)
        valid = k_pos[None, :] < lens[:, None]

        def scores():
            raw = jnp.einsum("bqhd,bkhd->bhqk", q4, k4, preferred_element_type=f32) + bias[None]
            return jnp.where(valid[:, None, None, :], raw, NEG)

        first_scores = scores()
        top = jnp.max(first_scores, axis=-1, keepdims=True)
        expo = jnp.exp(first_scores - top)
        denom = jnp.sum(expo, axis=-1, keepdims=True)
        probs_low = (expo / denom).astype(bf16)
        mixed = jnp.einsum("bhqk,bkhd->bqhd", probs_low, v4, preferred_element_type=f32)
        mixed = mixed.reshape(flat_rows, width).astype(bf16)
        h1 = xflat + jnp.dot(mixed, wo, preferred_element_type=f32)
        n2 = normed(h1, g2).astype(bf16)
        inner = jnp.dot(n2, wi, preferred_element_type=f32)
        act_full, gelu_pull = jax.vjp(jax.nn.gelu, inner)
        act = act_full.astype(bf16)
        result = h1 + jnp.dot(act, wf, preferred_element_type=f32)
        outputs.append(result.astype(bf16).reshape(per, span, width))
        grad_wf = grad_wf + jnp.einsum("tf,td->fd", act, upstream, preferred_element_type=f32)
        d_act = jnp.einsum("td,fd->tf", upstream, wf, preferred_element_type=f32)
        d_inner = gelu_pull(d_act)[0].astype(bf16)
        grad_wi = grad_wi + jnp.einsum("td,tf->df", n2, d_inner, preferred_element_type=f32)
        d_n2 = jnp.einsum("tf,df->td", d_inner, wi, preferred_element_type=f32)
        norm_pull = jax.vjp(normed, h1, g2)[1]
        dh_part, dg_two = norm_pull(d_n2)
        grad_g2 = grad_g2 + dg_two
        dh1 = upstream.astype(f32) + dh_part
        d_attn = dh1.astype(bf16)
        grad_wo = grad_wo + jnp.einsum("td,te->de", mixed, d_attn, preferred_element_type=f32)
        d_mixed = jnp.einsum("te,de->td", d_attn, wo, preferred_element_type=f32).astype(bf16)
        dm4 = d_mixed.reshape(per, span, heads, head_dim)
        probs = jnp.exp(scores() - top) / denom
        d_probs = jnp.einsum("bqhd,bkhd->bhqk", dm4, v4, preferred_element_type=f32)
        value_terms = jnp.einsum("bhqk,bqhd->bkhd", probs_low, dm4, preferred_element_type=f32)
        delta = jnp.sum(probs * d_probs, axis=-1, keepdims=True)
        d_scores = (probs * (d_probs - delta)).astype(bf16)
        grad_bias = grad_bias + jnp.sum(d_scores.astype(f32), axis=0)
        d_query = jnp.einsum("bhqk,bkhd->bqhd", d_scores, k4, preferred_element_type=f32)
        d_query = d_query.reshape(flat_rows, width).astype(bf16)
        key_terms = jnp.einsum("bhqk,bqhd->bkhd", d_scores, q4, preferred_element_type=f32)
        key_share, value_share = (
            lax.psum_scatter(
                key_terms.reshape(per, total, width), "seq", scatter_dimension=1, tiled=True
            ),
            lax.psum_scatter(
                value_terms.reshape(per, total, width), "seq", scatter_dimension=1, tiled=True
            ),
        )
        d_key = key_share.reshape(flat_rows, width).astype(bf16)
        d_value = value_share.reshape(flat_rows, width).astype(bf16)
        grad_wq = grad_wq + jnp.einsum("td,te->de", n1, d_query, preferred_element_type=f32)
        grad_wk = grad_wk + jnp.einsum("td,te->de", n1, d_key, preferred_element_type=f32)
        grad_wv = grad_wv + jnp.einsum("td,te->de", n1, d_value, preferred_element_type=f32)
        d_n1 = jnp.einsum("te,de->td", d_query, wq, preferred_element_type=f32)
        d_n1 = d_n1 + jnp.einsum("te,de->td", d_key, wk, preferred_element_type=f32)
        d_n1 = d_n1 + jnp.einsum("te,de->td", d_value, wv, preferred_element_type=f32)
        first_pull = jax.vjp(normed, xflat, g1)[1]
        dx_part, dg_one = first_pull(d_n1)
        grad_g1 = grad_g1 + dg_one
        input_grads.append((dh1 + dx_part).reshape(per, span, width))
    owned = (
        lax.psum_scatter(grad_wq, ("seq", "rows"), scatter_dimension=0, tiled=True),
        lax.psum_scatter(grad_wk, ("seq", "rows"), scatter_dimension=0, tiled=True),
        lax.psum_scatter(grad_wv, ("seq", "rows"), scatter_dimension=0, tiled=True),
        lax.psum_scatter(grad_wo, ("seq", "rows"), scatter_dimension=0, tiled=True),
        lax.psum_scatter(grad_wi, ("seq", "rows"), scatter_dimension=0, tiled=True),
        lax.psum_scatter(grad_wf, ("seq", "rows"), scatter_dimension=0, tiled=True),
        lax.psum_scatter(grad_g1, ("seq", "rows"), scatter_dimension=0, tiled=True),
        lax.psum_scatter(grad_g2, ("seq", "rows"), scatter_dimension=0, tiled=True),
    )
    grad_full = lax.dynamic_update_slice_in_dim(
        jnp.zeros((heads, total, total), f32), grad_bias, q_start, 1
    )
    widened = jnp.pad(grad_full, ((0, 0), (0, 0), (total - 1, 0)))
    folded = jnp.pad(widened.reshape(heads, total * (2 * total - 1)), ((0, 0), (0, total)))
    rel_grad = jnp.sum(folded.reshape(heads, total, 2 * total), axis=1)[:, : 2 * total - 1]
    table_local = jnp.dot(onehot.T, rel_grad.T, precision=HIGH)
    table_grad = lax.psum(table_local, ("seq", "rows"))
    result_rows = jnp.concatenate(outputs, axis=0)
    grad_rows = jnp.concatenate(input_grads, axis=0)
    return (
        result_rows,
        grad_rows,
        owned[0],
        owned[1],
        owned[2],
        owned[3],
        owned[4],
        owned[5],
        owned[6],
        owned[7],
        table_grad,
    )


MESH_ID = pl.DeviceIdType.MESH
HBM = pl.BlockSpec(memory_space=pl.ANY)
VMEM = pl.BlockSpec(memory_space=pltpu.VMEM)
SMEM = pl.BlockSpec(memory_space=pltpu.SMEM)
BF = jnp.bfloat16
F32 = jnp.float32
NX, NZ, NY, NC = 2, 4, 2, 2


def rcopy(src, dst, send, recv, to):
    return pltpu.make_async_remote_copy(
        src_ref=src, dst_ref=dst, send_sem=send, recv_sem=recv, device_id=to, device_id_type=MESH_ID
    )


class Place:
    def __init__(self):
        self.x = lax.axis_index("seq")
        r = lax.axis_index("rows")
        self.c = lax.rem(r, 2)
        self.y = lax.rem(r // 2, 2)
        self.z = r // 4
        self.core = self.at(self.x, self.y, self.z, 1 - self.c)
        self.xn = self.at(1 - self.x, self.y, self.z, self.c)
        self.yn = self.at(self.x, 1 - self.y, self.z, self.c)
        self.zp = [None] + [self.at(self.x, self.y, self.zz(j), self.c) for j in range(1, NZ)]

    def at(self, x, y, z, c):
        return (x, z * 4 + y * 2 + c)

    def zz(self, j):
        return lax.rem(self.z + j, NZ)

    def barrier(self):
        sem = pltpu.get_barrier_semaphore()
        peers = [self.core, self.xn, self.yn] + self.zp[1:]
        for p in peers:
            pl.semaphore_signal(sem, inc=1, device_id=p, device_id_type=MESH_ID)
        pl.semaphore_wait(sem, len(peers))


class GatherXZY:
    def __init__(self, me, w, ss, rr, dd):
        self.me, self.w, self.ss, self.rr, self.dd = me, w, ss, rr, dd
        self.nh = w.shape[-1] // 2

    def ref(self, x, z, y, c):
        cols = pl.ds(pl.multiple_of(c * self.nh, 128), self.nh)
        return self.w.at[x, z, y, :, cols]

    def pair(self, z, y, c):
        cols = pl.ds(pl.multiple_of(c * self.nh, 128), self.nh)
        return self.w.at[:, z, y, :, cols]

    def send(self, ref, s, recv, to):
        rcopy(ref, ref, self.ss.at[s], recv, to).start()

    def got(self, ref, recv):
        rcopy(ref, ref, self.ss.at[0], recv, self.me.core).wait_recv()

    def start(self):
        m = self.me
        self.send(self.ref(m.x, m.z, m.y, m.c), 0, self.rr.at[0], m.xn)

    def step_x(self):
        m = self.me
        self.got(self.ref(1 - m.x, m.z, m.y, m.c), self.rr.at[0])
        p = self.pair(m.z, m.y, m.c)
        for j in range(1, NZ):
            self.send(p, j, self.rr.at[NZ - j], m.zp[j])
        self.send(p, 4, self.rr.at[4], m.yn)
        self.send(p, 8, self.dd.at[0], m.core)

    def step_z(self, j):
        m = self.me
        p = self.pair(m.zz(j), m.y, m.c)
        self.got(p, self.rr.at[j])
        self.send(p, 4 + j, self.rr.at[4 + j], m.yn)
        self.send(p, 8 + j, self.dd.at[j], m.core)

    def step_y(self, j):
        m = self.me
        p = self.pair(m.zz(j), 1 - m.y, m.c)
        self.got(p, self.rr.at[4 + j])
        self.send(p, 12 + j, self.dd.at[4 + j], m.core)

    def done(self):
        m = self.me
        for j in range(NZ):
            self.got(self.pair(m.zz(j), m.y, 1 - m.c), self.dd.at[j])
        for j in range(NZ):
            self.got(self.pair(m.zz(j), 1 - m.y, 1 - m.c), self.dd.at[4 + j])

    def sent(self):
        m = self.me
        one = self.ref(m.x, m.z, m.y, m.c)
        rcopy(one, one, self.ss.at[0], self.rr.at[0], m.core).wait_send()
        p = self.pair(m.z, m.y, m.c)
        for s in range(1, 16):
            rcopy(p, p, self.ss.at[s], self.rr.at[0], m.core).wait_send()


class GatherZYX:
    def __init__(self, me, w, ss, rr, dd):
        self.me, self.w, self.ss, self.rr, self.dd = me, w, ss, rr, dd

    def send(self, ref, s, recv, to):
        rcopy(ref, ref, self.ss.at[s], recv, to).start()

    def got(self, ref, recv):
        rcopy(ref, ref, self.ss.at[0], recv, self.me.core).wait_recv()

    def start(self):
        m = self.me
        own = self.w.at[m.x, m.z, m.y, m.c]
        for j in range(1, NZ):
            self.send(own, j - 1, self.rr.at[NZ - j - 1], m.zp[j])
        self.send(own, 3, self.rr.at[3], m.yn)

    def step_z(self, j):
        m = self.me
        b = self.w.at[m.x, m.zz(j), m.y, m.c]
        self.got(b, self.rr.at[j - 1])
        self.send(b, 5 + j, self.rr.at[3 + j], m.yn)

    def step_y(self, j):
        m = self.me
        self.got(self.w.at[m.x, m.zz(j), 1 - m.y, m.c], self.rr.at[3 + j])
        p = self.w.at[m.x, m.zz(j), :, m.c]
        self.send(p, 4 if j == 0 else 8 + j, self.rr.at[7 + j], m.xn)
        self.send(p, 5 if j == 0 else 11 + j, self.dd.at[j], m.core)

    def step_x(self, j):
        m = self.me
        p = self.w.at[1 - m.x, m.zz(j), :, m.c]
        self.got(p, self.rr.at[7 + j])
        self.send(p, 15 + j, self.dd.at[4 + j], m.core)

    def done(self):
        m = self.me
        for j in range(NZ):
            self.got(self.w.at[m.x, m.zz(j), :, 1 - m.c], self.dd.at[j])
        for j in range(NZ):
            self.got(self.w.at[1 - m.x, m.zz(j), :, 1 - m.c], self.dd.at[4 + j])

    def sent(self):
        m = self.me
        one = self.w.at[m.x, m.z, m.y, m.c]
        p = self.w.at[m.x, m.z, :, m.c]
        for s in range(19):
            r = one if s in (0, 1, 2, 3, 6, 7, 8) else p
            rcopy(r, r, self.ss.at[s], self.rr.at[0], m.core).wait_send()


def own_block(me, mine, theirs, w, nh):
    cols = pl.ds(pl.multiple_of(me.c * nh, 128), nh)
    a = mine[:, cols].astype(F32)[:24]
    b = theirs[...].astype(F32)[:24]
    first = jnp.where(me.c == 0, a, b)
    second = jnp.where(me.c == 0, b, a)
    w[me.x, me.z, me.y, :, cols] = jnp.concatenate([first, second], axis=0).astype(BF)


class Piece:
    def __init__(self, index, rows, first):
        self.index, self.slot, self.rows = index, index % 2, rows
        cut = rows // 2 if rows // 2 % 16 == 0 else rows // 2 + 8
        self.subs = ((0, cut, first[0]), (cut, rows - cut, first[1]))


class Reduce:
    def __init__(self, me, acc, a1, a2, a3, cs, cr, s1s, s1r, s2s, s2r, s3s, s3r, fin, finr, sems):
        self.me = me
        self.acc, self.a1, self.a2, self.a3, self.cs, self.cr = acc, a1, a2, a3, cs, cr
        self.s1s, self.s1r, self.s2s, self.s2r, self.s3s, self.s3r = s1s, s1r, s2s, s2r, s3s, s3r
        self.fin, self.finr = fin, finr
        (self.c_s, self.c_r, self.a_s, self.a_r, self.b_s, self.b_r, self.z_s, self.z_r, self.f_s, self.f_r) = sems

    def near(self, axis):
        return self.me.xn if axis == "x" else self.me.yn

    def core_copy(self, p):
        s, n = p.slot, p.rows
        return rcopy(
            self.cs.at[:, :, :, 0:n], self.cr.at[s, :, :, :, 0:n], self.c_s.at[s], self.c_r.at[s], self.me.core
        )

    def one_copy(self, p, k):
        s, (_, n, axis) = p.slot, p.subs[k]
        return rcopy(
            self.s1s.at[k, :, :, 0:n], self.s1r.at[s, k, :, :, 0:n], self.a_s.at[s, k], self.a_r.at[s, k], self.near(axis)
        )

    def two_copy(self, p, k):
        s, (_, n, axis) = p.slot, p.subs[k]
        to = self.near("y" if axis == "x" else "x")
        return rcopy(self.s2s.at[k, :, 0:n], self.s2r.at[s, k, :, 0:n], self.b_s.at[s, k], self.b_r.at[s, k], to)

    def z_copy(self, p, j):
        s, n = p.slot, p.rows
        return rcopy(
            self.s3s.at[j, 0:n], self.s3r.at[s, NZ - j, 0:n], self.z_s.at[s, j], self.z_r.at[s, NZ - j], self.me.zp[j]
        )

    def fin_copy(self, p):
        i, n = p.index, p.rows // 2
        return rcopy(
            self.fin.at[i, 1 - self.me.c, 0:n], self.finr.at[i, 0:n], self.f_s.at[i], self.f_r.at[i], self.me.core
        )

    def send_core(self, p):
        self.core_copy(p).start()

    def h1(self, p, old):
        me, s, n = self.me, p.slot, p.rows
        self.core_copy(p).wait_recv()
        for k, (lo, n, axis) in enumerate(p.subs):
            if old is not None:
                self.one_copy(old, k).wait_send()
            rows = pl.ds(lo, n)

            def body(q, carry):
                a, zq = q // NZ, lax.rem(q, NZ)
                if axis == "x":
                    keep, away = (me.x, a, zq, rows), (1 - me.x, a, zq, rows)
                else:
                    keep, away = (a, me.y, zq, rows), (a, 1 - me.y, zq, rows)
                self.a1[k, a, zq, 0:n] = self.acc[keep] + self.cr[(s,) + keep].astype(F32)
                self.s1s[k, a, zq, 0:n] = (self.acc[away] + self.cr[(s,) + away].astype(F32)).astype(BF)
                return carry

            lax.fori_loop(0, 2 * NZ, body, 0)
            self.one_copy(p, k).start()

    def h2(self, p, old):
        me, s = self.me, p.slot
        for k, (lo, n, axis) in enumerate(p.subs):
            self.one_copy(p, k).wait_recv()
            if old is not None:
                self.two_copy(old, k).wait_send()
            b = me.y if axis == "x" else me.x

            def body(zq, carry):
                self.a2[k, zq, 0:n] = self.a1[k, b, zq, 0:n] + self.s1r[s, k, b, zq, 0:n].astype(F32)
                self.s2s[k, zq, 0:n] = (
                    self.a1[k, 1 - b, zq, 0:n] + self.s1r[s, k, 1 - b, zq, 0:n].astype(F32)
                ).astype(BF)
                return carry

            lax.fori_loop(0, NZ, body, 0)
            self.two_copy(p, k).start()

    def h3(self, p, old):
        me, s = self.me, p.slot
        for k in range(2):
            self.two_copy(p, k).wait_recv()
        for j in range(1, NZ):
            if old is not None:
                self.z_copy(old, j).wait_send()
        for k, (lo, n, _) in enumerate(p.subs):
            rows = pl.ds(lo, n)
            for j in range(NZ):
                zq = me.zz(j)
                v = self.a2[k, zq, 0:n] + self.s2r[s, k, zq, 0:n].astype(F32)
                if j == 0:
                    self.a3[rows] = v
                else:
                    self.s3s[j, rows] = v.astype(BF)
        for j in range(1, NZ):
            self.z_copy(p, j).start()

    def h4(self, p):
        me, s, n, i = self.me, p.slot, p.rows, p.index
        for j in range(1, NZ):
            self.z_copy(p, NZ - j).wait_recv()
        total = self.a3[0:n]
        for j in range(1, NZ):
            total = total + self.s3r[s, j, 0:n].astype(F32)
        for cd in range(NC):
            if p.groups is None:
                half = n // 2
                self.fin[i, cd, 0:half] = total[half * cd : half * cd + half]
            else:
                for g in range(p.groups):
                    self.fin[i, cd, 24 * g : 24 * g + 24] = total[48 * g + 24 * cd : 48 * g + 24 * cd + 24]
        self.fin_copy(p).start()


def norm_back(h, gain, up):
    r = lax.rsqrt(jnp.mean(h * h, axis=-1, keepdims=True) + EPS)
    hr = h * r
    w = up * gain
    dgain = jnp.sum(up * hr, axis=0, keepdims=True)
    return r * (w - hr * jnp.mean(w * hr, axis=-1, keepdims=True)), dgain


def layer_kernel(
    tok, gin, pa, pb, pd, relb, table, lens,
    act_o, dx_o, gq_o, gk_o, gv_o, go_o, gi_o, gf_o, sm_o,
    WA, WB, WD, X, G, N2, QKV, O, H1, ACT, DU, T, M, MACC, LSE, R, RG, RA, RB,
    ACC, A1, A2, A3, CS, CR, S1S, S1R, S2S, S2R, S3S, S3R, FIN, FINR, SM, SMR, ZB, DG,
    ts, tr, tl, gs, gr, gl, es, er, as_, ar, ad, bs, br, bd, ds_, dr, dd, ys, yr, yl, xs_, xr, xl,
    c_s, c_r, a_s, a_r, b_s, b_r, z_s, z_r, f_s, f_r, ms, mr,
):
    me = Place()
    x, y, z, c = me.x, me.y, me.z, me.c
    mine, span, width = X.shape[0], X.shape[2], X.shape[3]
    length = 2 * span
    flat = mine * length
    ff = DU.shape[1]
    na, nb = RA.shape[1], RB.shape[1]
    hd = 64
    YB = O
    pairs = width // hd // 2
    gath_a = GatherXZY(me, WA, as_, ar, ad)
    gath_b = GatherXZY(me, WB, bs, br, bd)
    gath_d = GatherZYX(me, WD, ds_, dr, dd)
    me.barrier()
    ea = rcopy(pa.at[:, pl.ds(pl.multiple_of((1 - c) * na, 128), na)], RA, es.at[0], er.at[0], me.core)
    eb = rcopy(pb.at[:, pl.ds(pl.multiple_of((1 - c) * nb, 128), nb)], RB, es.at[1], er.at[1], me.core)
    ea.start()
    eb.start()
    tok_r = [rcopy(tok.at[2 * (1 - x) + i], X.at[i, x], ts.at[i], tr.at[i], me.xn) for i in range(mine)]
    tok_in = [rcopy(X.at[i, 1 - x], X.at[i, 1 - x], ts.at[i], tr.at[i], me.xn) for i in range(mine)]
    tok_l = [pltpu.make_async_copy(tok.at[2 * x + i], X.at[i, x], tl.at[i]) for i in range(mine)]
    g_r = rcopy(gin.at[pl.ds(2 * (1 - x), 2)], G.at[:, x], gs, gr, me.xn)
    g_in = rcopy(G.at[:, 1 - x], G.at[:, 1 - x], gs, gr, me.xn)
    g_l = pltpu.make_async_copy(gin.at[pl.ds(2 * x, 2)], G.at[:, x], gl)
    ea.wait_recv()
    own_block(me, pa, RA, WA, na)
    gath_a.start()
    for i in range(mine):
        tok_r[i].start()
        tok_l[i].start()
    g_l.start()
    eb.wait_recv()
    own_block(me, pb, RB, WB, nb)
    WD[x, z, y, c] = pd[...]
    cols = relb.shape[1]
    kinds = table.shape[0]
    hot = (lax.broadcasted_iota(jnp.int32, (kinds, cols), 0) == relb[...]).astype(BF)
    R[...] = lax.dot_general(table[...], hot, (((0,), (0,)), ((), ())), preferred_element_type=F32)[0:16]
    gath_a.step_x()
    gath_b.start()
    gath_d.start()
    for j in range(1, NZ):
        gath_a.step_z(j)
    gath_b.step_x()
    for j in range(NZ):
        gath_a.step_y(j)
    gath_d.step_y(0)
    g_r.start()
    gath_a.done()

    def gain_row(k):
        return jnp.transpose(WA[:, :, :, :, 128 * k : 128 * k + 128].reshape(width, 128).astype(F32))[0:1, :]

    gain1 = gain_row(0)

    def row_slice(i):
        return pl.ds(pl.multiple_of(i * length, length), length)

    for i in range(mine):
        tok_l[i].wait()
        tok_in[i].wait_recv()
        for half in range(2):
            xf = X[i, half].astype(F32)
            scale = lax.rsqrt(jnp.mean(xf * xf, axis=-1, keepdims=True) + EPS)
            N2[pl.ds(i * length + half * span, span), :] = (xf * scale * gain1).astype(BF)
        for n in range(3):
            w = WA[:, :, :, :, 256 + n * width : 256 + (n + 1) * width].reshape(width, width)
            QKV[row_slice(i), n * width : (n + 1) * width] = jnp.dot(
                N2[row_slice(i), :], w, preferred_element_type=F32
            ).astype(BF)
    low = lax.broadcasted_iota(jnp.int32, (1, 128), 1) < hd
    lane = lax.broadcasted_iota(jnp.int32, (1, 128), 1)
    kpos = lax.broadcasted_iota(jnp.int32, (1, length), 1)
    zero = jnp.zeros((), BF)
    blocks = length // 128

    def strips(p):
        for h in range(2):
            row = jnp.broadcast_to(R[pl.ds(2 * p + h, 1), :], (128, cols))
            M[h] = pltpu.roll(row, cols - 127, 1, stride=1, stride_axis=0)[:, : M.shape[2]]

    def bias_of(h, qb):
        return jnp.concatenate(
            [M[h, :, 128 * (blocks - 1 - a) : 128 * (blocks - 1 - a) + length] for a in (2 * qb, 2 * qb + 1)], axis=0
        )

    def half_of(h, v):
        return jnp.where(low if h == 0 else jnp.logical_not(low), v, zero)

    def lanes(n, p):
        return pl.ds(pl.multiple_of(n * width + p * 128, 128), 128)

    nt = (((1,), (1,)), ((), ()))
    tn = (((0,), (0,)), ((), ()))

    def mm(a, b, dims):
        return lax.dot_general(a, b, dims, preferred_element_type=F32)

    comm = {
        0: (lambda: gath_b.step_z(1), lambda: gath_d.step_z(1)),
        1: (lambda: gath_b.step_z(2), lambda: gath_d.step_z(2)),
        2: (lambda: gath_b.step_z(3), lambda: gath_d.step_z(3)),
        3: (lambda: gath_b.step_y(0), lambda: gath_d.step_y(1)),
        5: (lambda: gath_b.step_y(1), lambda: gath_d.step_y(2)),
        7: (lambda: gath_b.step_y(2), lambda: gath_d.step_y(3)),
        8: (lambda: gath_b.step_y(3),),
        9: (lambda: gath_d.step_x(0),),
        10: (lambda: gath_d.step_x(1),),
        11: (lambda: gath_d.step_x(2),),
    }

    def attend(t, carry):
        p, i = t // mine, lax.rem(t, mine)
        pl.when(i == 0)(lambda: strips(p))
        k = QKV[row_slice(i), lanes(1, p)]
        v = QKV[row_slice(i), lanes(2, p)]
        valid = kpos < lens[2 * x + i]
        for qb in range(length // 256):
            rows = pl.ds(pl.multiple_of(i * length + qb * 256, 256), 256)
            q = QKV[rows, lanes(0, p)]
            outs = []
            for h in range(2):
                s = mm(half_of(h, q), k, nt)
                s = jnp.where(valid, s + bias_of(h, qb), NEG)
                top = jnp.max(s, axis=-1, keepdims=True)
                e = jnp.exp(s - top)
                total = jnp.sum(e, axis=-1, keepdims=True)
                LSE[rows, :] = jnp.where(lane == 2 * p + h, top + jnp.log(total), LSE[rows, :])
                outs.append(jnp.dot((e * (1.0 / total)).astype(BF), v, preferred_element_type=F32))
            O[i, qb, :, lanes(0, p)] = jnp.where(low, outs[0], outs[1]).astype(BF)
        for at, steps in comm.items():
            @pl.when(t == at)
            def _():
                for step in steps:
                    step()
        return carry

    LSE[...] = jnp.zeros_like(LSE)
    lax.fori_loop(0, mine * pairs, attend, 0)
    gath_d.step_x(3)
    gath_b.done()
    gath_d.done()
    g_l.wait()
    g_in.wait_recv()

    gain2 = gain_row(1)
    DG[...] = jnp.zeros_like(DG)
    c0, c1 = 0.7978845608028654, 0.044715

    T[...] = jnp.transpose(O[...].reshape(flat, width))

    def ffn(i, carry):
        wo = WB[:, :, :, :, 0:width].reshape(width, width)
        for half in range(2):
            hrows = pl.ds(pl.multiple_of(i * length + half * span, span), span)
            h1 = X[i, half].astype(F32) + jnp.dot(O[i, half], wo, preferred_element_type=F32)
            H1[i, half] = h1
            r = lax.rsqrt(jnp.mean(h1 * h1, axis=-1, keepdims=True) + EPS)
            N2[hrows, :] = (h1 * r * gain2).astype(BF)

        def chunk(f, carry):
            fcols = pl.ds(pl.multiple_of(f * width, width), width)
            wi = WB[:, :, :, :, pl.ds(pl.multiple_of(width + f * width, width), width)].reshape(width, width)
            wf = WD[f // 2, pl.ds(2 * lax.rem(f, 2), 2)].reshape(width, width)
            for half in range(2):
                hrows = pl.ds(pl.multiple_of(i * length + half * span, span), span)
                u = jnp.dot(N2[hrows, :], wi, preferred_element_type=F32)
                da = mm(G[i, half], wf, nt)
                sq = u * u
                t = jnp.tanh(u * (c0 + (c0 * c1) * sq))
                cdf = 0.5 + 0.5 * t
                ACT[hrows, fcols] = (u * cdf).astype(BF)
                slope = cdf + (0.5 * u) * (1.0 - t * t) * (c0 + (3.0 * c0 * c1) * sq)
                DU[hrows, fcols] = (da * slope).astype(BF)
            return carry

        lax.fori_loop(0, ff // width, chunk, 0)
        for half in range(2):
            hrows = pl.ds(pl.multiple_of(i * length + half * span, span), span)
            out = jnp.dot(ACT[hrows, :], WD[...].reshape(ff, width), preferred_element_type=F32)
            YB[i, half] = (H1[i, half] + out).astype(BF)
        for half in range(2):
            hrows = pl.ds(pl.multiple_of(i * length + half * span, span), span)
            dn2 = mm(DU[hrows, :], WB[:, :, :, :, width:].reshape(width, ff), nt)
            dh, dgain = norm_back(H1[i, half], gain2, dn2)
            DG[1:2, :] = DG[1:2, :] + dgain
            H1[i, half] = G[i, half].astype(F32) + dh
        rcopy(YB.at[i, 1 - x], act_o.at[2 * x + i], ys.at[i], yr.at[i], me.xn).start()
        pltpu.make_async_copy(YB.at[i, x], act_o.at[2 * x + i], yl.at[i]).start()
        return carry

    lax.fori_loop(0, mine, ffn, 0)

    red = Reduce(
        me, ACC, A1, A2, A3, CS, CR, S1S, S1R, S2S, S2R, S3S, S3R, FIN, FINR, (c_s, c_r, a_s, a_r, b_s, b_r, z_s, z_r, f_s, f_r)
    )
    pieces = []
    last = (ff // 1024) + (width // 256) + 4
    for n in range(last):
        rows = 192 if 0 < n < last - 3 else 144
        piece = Piece(n, rows, ("x", "y") if n < last - 3 else ("y", "y"))
        piece.groups = None if 0 < n <= width // 256 else rows // 48
        pieces.append(piece)

    def stages(n, lo, hi):
        at = lambda k: pieces[n - k] if lo <= n - k < hi else None
        old = lambda k: pieces[n - k - 1] if n - k - 1 >= 0 else None
        if at(4):
            red.h4(at(4))
        if at(3):
            red.h3(at(3), old(3))
        if at(2):
            red.h2(at(2), old(2))
        if at(1):
            red.h1(at(1), old(1))
        if at(0) and old(0):
            red.core_copy(old(0)).wait_send()

    def split(res):
        a, b = res[:, 0:128], res[:, 128:256]
        return jnp.where(c == 0, a, b), jnp.where(c == 0, b, a).astype(BF)

    def outer_piece(j):

        def body(q, carry):
            xq, zh = q // 2, lax.rem(q, 2)
            lhs = ACT[:, pl.ds(pl.multiple_of(q * 768, 768), 768)]
            rhs = G[:, :, :, 256 * j : 256 * j + 256].reshape(flat, 256)
            own, other = split(mm(lhs, rhs, tn))
            for b in range(4):
                at = (xq, b % 2, 2 * zh + b // 2)
                ACC[at] = own[192 * b : 192 * b + 192]
                CS[at] = other[192 * b : 192 * b + 192]
            return carry

        lax.fori_loop(0, 4, body, 0)

    def rows_piece(groups, rhs):
        def body(g, carry):
            own, other = split(jnp.dot(T[...], rhs(g), preferred_element_type=F32))
            at = pl.ds(pl.multiple_of(48 * g, 48), 48)
            for k in range(NX * NZ * NY):
                ACC[k // 8, k % 2, (k // 2) % 4, at] = own[48 * k : 48 * k + 48]
                CS[k // 8, k % 2, (k // 2) % 4, at] = other[48 * k : 48 * k + 48]
            return carry

        lax.fori_loop(0, groups, body, 0)

    early = last - 3
    rows_piece(3, lambda g: H1[:, :, :, pl.ds(pl.multiple_of(256 * g, 256), 256)].reshape(flat, 256).astype(BF))
    red.send_core(pieces[0])
    step = 1
    T[...] = jnp.transpose(N2[...])
    for j in range(width // 256):
        stages(step, 0, early)
        outer_piece(j)
        red.send_core(pieces[step])
        step += 1
    for j in range(ff // 1024):
        stages(step, 0, early)
        rows_piece(4, lambda g: DU[:, pl.ds(pl.multiple_of(1024 * j + 256 * g, 256), 256)])
        red.send_core(pieces[step])
        step += 1
    N2[...] = H1[...].reshape(flat, width).astype(BF)
    for i in range(mine):
        wo = WB[:, :, :, :, 0:width].reshape(width, width)
        G[i] = mm(N2[row_slice(i), :], wo, nt).astype(BF).reshape(2, span, width)

    def attend_back(t, carry):
        p, i = t // mine, lax.rem(t, mine)

        @pl.when(i == 0)
        def _():
            strips(p)
            MACC[...] = jnp.zeros_like(MACC)

        k = QKV[row_slice(i), lanes(1, p)]
        v = QKV[row_slice(i), lanes(2, p)]
        q = QKV[row_slice(i), lanes(0, p)]
        do = G[i, :, :, lanes(0, p)].reshape(length, 128)
        valid = kpos < lens[2 * x + i]
        dqs, dks, dvs = [], [], []
        for h in range(2):
            pbs, dss = [], []
            for qb in range(length // 256):
                rows = pl.ds(pl.multiple_of(i * length + qb * 256, 256), 256)
                cut = slice(256 * qb, 256 * qb + 256)
                lse = jnp.sum(jnp.where(lane == 2 * p + h, LSE[rows, :], 0.0), axis=-1, keepdims=True)
                s = mm(half_of(h, q[cut]), k, nt)
                pr = jnp.exp(jnp.where(valid, s + bias_of(h, qb), NEG) - lse)
                e = pr * mm(half_of(h, do[cut]), v, nt)
                ds = (e - pr * jnp.sum(e, axis=-1, keepdims=True)).astype(BF)
                for a in range(2):
                    at = 128 * (blocks - 1 - 2 * qb - a)
                    MACC[h, :, at : at + length] = MACC[h, :, at : at + length] + ds[128 * a : 128 * a + 128].astype(F32)
                pbs.append(pr.astype(BF))
                dss.append(ds)
            pb_, ds_all = jnp.concatenate(pbs, axis=0), jnp.concatenate(dss, axis=0)
            dqs.append(jnp.dot(ds_all, k, preferred_element_type=F32))
            dks.append(mm(ds_all, q, tn))
            dvs.append(mm(pb_, do, tn))
        for n, parts in enumerate((dqs, dks, dvs)):
            ACT[row_slice(i), lanes(n, p)] = jnp.where(low, parts[0], parts[1]).astype(BF)

        @pl.when(i == mine - 1)
        def _():
            for h in range(2):
                part = jnp.zeros((8, cols), F32)
                for a in range(16):
                    part = part + pltpu.roll(MACC[h, 8 * a : 8 * a + 8, :], (cols - 8 * a) % cols, 1)
                line = part[0:1]
                for a in range(1, 8):
                    line = line + pltpu.roll(part[a : a + 1], cols - a, 1)
                RG[pl.ds(2 * p + h, 1), :] = pltpu.roll(line, 127, 1)

        for at in range(4):
            pl.when(t == 2 * at + 1)(lambda n=at: stages(early + n, 0, early))
        return carry

    y_out = [
        rcopy(YB.at[i, 1 - x], act_o.at[2 * (1 - x) + i], ys.at[i], yr.at[i], me.xn) for i in range(mine)
    ]
    for i in range(mine):
        y_out[i].wait_recv()
        y_out[i].wait_send()
    RG[...] = jnp.zeros_like(RG)
    MACC[...] = jnp.zeros_like(MACC)
    lax.fori_loop(0, mine * pairs, attend_back, 0)

    for i in range(mine):
        for half in range(2):
            xf = X[i, half].astype(F32)
            scale = lax.rsqrt(jnp.mean(xf * xf, axis=-1, keepdims=True) + EPS)
            N2[pl.ds(i * length + half * span, span), :] = (xf * scale * gain1).astype(BF)
    T[...] = jnp.transpose(N2[...])
    for n in range(3):
        stages(step, early, last)
        rows_piece(3, lambda g: ACT[:, pl.ds(pl.multiple_of(n * width + 256 * g, 256), 256)])
        red.send_core(pieces[step])
        step += 1
    dx_r = [rcopy(X.at[i, 1 - x], YB.at[i, x], xs_.at[i], xr.at[i], me.xn) for i in range(mine)]
    dx_l = [pltpu.make_async_copy(H1.at[i, x], dx_o.at[2 * x + i], xl.at[i]) for i in range(mine)]
    dx_f = [pltpu.make_async_copy(H1.at[i, 1 - x], dx_o.at[2 * (1 - x) + i], xl.at[mine + i]) for i in range(mine)]
    for i in range(mine):
        for half in range(2):
            hrows = pl.ds(i * length + half * span, span)
            dn1 = mm(ACT[hrows, 0 : 3 * width], WA[:, :, :, :, 256:].reshape(width, 3 * width), nt)
            dh, dgain = norm_back(X[i, half].astype(F32), gain1, dn1)
            DG[0:1, :] = DG[0:1, :] + dgain
            H1[i, half] = H1[i, half] + dh
        X[i, 1 - x] = H1[i, 1 - x].astype(BF)
        dx_r[i].start()
        dx_l[i].start()
        stages(step, early, last)
        step += 1
    for n in range(width // 128):
        SM[0, n : n + 1, :] = DG[0:1, 128 * n : 128 * n + 128]
        SM[0, 8 + n : 9 + n, :] = DG[1:2, 128 * n : 128 * n + 128]
    rest = jnp.concatenate([RG[...], jnp.zeros((112, cols), F32)], axis=0)
    spread = jnp.zeros((kinds, 128), F32)
    for _ in range(3):
        part = rest.astype(BF)
        rest = rest - part.astype(F32)
        spread = spread + mm(hot, part, nt)
    SM[0, 16 : 16 + kinds, :] = spread
    sm_copies = [
        rcopy(SM.at[k], SMR.at[k], ms.at[k], mr.at[k], to) for k, to in enumerate((me.core, me.xn, me.yn))
    ]
    sm_copies[0].start()
    stages(step, early, last)
    step += 1
    for k in range(3):
        sm_copies[k].wait_recv()
        SM[k + 1] = SM[k] + SMR[k]
        if k < 2:
            sm_copies[k + 1].start()
        if k == 0:
            stages(step, early, last)
            step += 1
    ZB[z] = SM[3]
    sm_z = [None] + [rcopy(SM.at[3], ZB.at[z], ms.at[2 + j], mr.at[6 - j], me.zp[j]) for j in range(1, NZ)]
    for j in range(1, NZ):
        sm_z[j].start()
    for i in range(mine):
        rcopy(X.at[i, 1 - x], YB.at[i, 1 - x], xs_.at[i], xr.at[i], me.xn).wait_recv()
        H1[i, 1 - x] = YB[i, 1 - x].astype(F32)
        dx_f[i].start()
    outs = (go_o, gq_o, gk_o, gv_o)
    for p in pieces:
        red.fin_copy(p).wait_recv()
        for src, core in ((FIN.at[p.index, c], c), (FINR.at[p.index], 1 - c)):
            if p.groups is None:
                gf_o[:, pl.ds(pl.multiple_of(256 * (p.index - 1) + 128 * core, 128), 128)] = src[0:96]
                continue
            if p.groups == 4:
                dst, base = gi_o, 1024 * (p.index - 1 - width // 256)
            else:
                dst, base = outs[max(0, p.index - early + 1)], 0
            for g in range(p.groups):
                dst[:, pl.ds(pl.multiple_of(base + 256 * g + 128 * core, 128), 128)] = src[24 * g : 24 * g + 24]
    for j in range(1, NZ):
        rcopy(SM.at[3], ZB.at[me.zz(j)], ms.at[2 + j], mr.at[2 + j], me.zp[j]).wait_recv()
    sm_o[...] = ZB[0] + ZB[1] + ZB[2] + ZB[3]
    ea.wait_send()
    eb.wait_send()
    g_r.wait_send()
    for k in range(3):
        sm_copies[k].wait_send()
    for j in range(1, NZ):
        sm_z[j].wait_send()
    for g in (gath_a, gath_b, gath_d):
        g.sent()
    for i in range(mine):
        tok_r[i].wait_send()
        pltpu.make_async_copy(YB.at[i, x], act_o.at[2 * x + i], yl.at[i]).wait()
        dx_r[i].wait_send()
        dx_l[i].wait()
        dx_f[i].wait()
    for p in pieces[-1:]:
        red.core_copy(p).wait_send()
        for k in range(2):
            red.one_copy(p, k).wait_send()
            red.two_copy(p, k).wait_send()
        for j in range(1, NZ):
            red.z_copy(p, j).wait_send()
    for p in pieces:
        red.fin_copy(p).wait_send()


def layer_call(tok, gin, pa, pb, pd, relb, table, lens, heads):
    rows_dev, span, width = tok.shape
    length = 2 * span
    mine = rows_dev // 2
    flat = mine * length
    dma = pltpu.SemaphoreType.DMA
    na, nb = pa.shape[1] // 2, pb.shape[1] // 2
    ff = pb.shape[1] - width
    count = width // 256 + ff // 1024 + 4
    wa = (NX, NZ, NY, 48, 2 * na)
    wb = (NX, NZ, NY, 48, 2 * nb)
    wd = (NX, NZ, NY, NC) + pd.shape
    xs = (mine, 2, span, width)
    block = (192, 128)
    bf = lambda *s: pltpu.VMEM(s, BF)
    f32 = lambda *s: pltpu.VMEM(s, F32)
    out = lambda *s: jax.ShapeDtypeStruct(s, F32)
    shard = pa.shape[0] - 8
    return pl.pallas_call(
        layer_kernel,
        out_shape=[jax.ShapeDtypeStruct(tok.shape, BF), out(*tok.shape)]
        + [out(shard, width)] * 4 + [out(shard, ff), out(*pd.shape), out(48, 128)],
        in_specs=[HBM, HBM, VMEM, VMEM, VMEM, VMEM, VMEM, SMEM],
        out_specs=[HBM, HBM] + [VMEM] * 7,
        scratch_shapes=[
            bf(*wa), bf(*wb), bf(*wd), bf(*xs), bf(*xs), bf(flat, width), bf(flat, 3 * width), bf(*xs), f32(*xs),
             bf(flat, ff), bf(flat, ff), bf(width, flat), f32(2, 128, 896), f32(2, 128, 1024),
            f32(flat, 128), f32(16, relb.shape[1]), f32(16, relb.shape[1]), bf(32, na), bf(32, nb),
            f32(NX, NY, NZ, *block), f32(2, 2, NZ, 96, 128), f32(2, NZ, 96, 128), f32(*block), bf(NX, NY, NZ, *block), bf(2, NX, NY, NZ, *block),
            bf(2, 2, NZ, 96, 128), bf(2, 2, 2, NZ, 96, 128), bf(2, NZ, 96, 128), bf(2, 2, NZ, 96, 128),
            bf(NZ, *block), bf(2, NZ, *block), f32(count, NC, 96, 128), f32(count, 96, 128),
            f32(4, 48, 128), f32(3, 48, 128), f32(NZ, 48, 128), f32(8, width),
            dma((2,)), dma((2,)), dma((2,)), dma, dma, dma, dma((2,)), dma((2,)),
            dma((16,)), dma((8,)), dma((8,)), dma((16,)), dma((8,)), dma((8,)), dma((19,)), dma((11,)), dma((8,)),
            dma((2,)), dma((2,)), dma((2,)), dma((2,)), dma((2,)), dma((4,)),
            dma((2,)), dma((2,)), dma((2, 2)), dma((2, 2)), dma((2, 2)), dma((2, 2)), dma((2, NZ)), dma((2, NZ)),
            dma((count,)), dma((count,)), dma((6,)), dma((6,)),
        ],
        compiler_params=pltpu.CompilerParams(
            collective_id=0, has_side_effects=True, vmem_limit_bytes=VMEM_LIMIT
        ),
        name="layer",
    )(tok, gin, pa, pb, pd, relb, table, lens)


VMEM_LIMIT = 63 * 1024 * 1024 + 512 * 1024


def fast(
    tokens, doc_lengths, rel_buckets, w_query, w_key, w_value, w_output, w_inner, w_outer,
    attn_gain, ffn_gain, bias_table, out_grad,
):
    n_bins, heads = bias_table.shape
    wide = lambda g: jnp.broadcast_to(g[:, None], (g.shape[0], 128))
    pad8 = lambda a: jnp.pad(a, ((0, 8), (0, 0)))
    pa = pad8(jnp.concatenate([wide(attn_gain), wide(ffn_gain), w_query, w_key, w_value], axis=1))
    pb = pad8(jnp.concatenate([w_output, w_inner], axis=1))
    relb = jnp.pad(rel_buckets, (0, 1))[None, :]
    table = jnp.pad(bias_table, ((0, 0), (0, 128 - heads)))
    act, dx, gq, gk, gv, go, gi, gf, small = layer_call(
        tokens, out_grad, pa, pb, w_outer, relb, table, doc_lengths, heads
    )
    me = lax.axis_index("seq") * lax.axis_size("rows") + lax.axis_index("rows")
    cut = attn_gain.shape[0]
    gains = [lax.dynamic_slice_in_dim(small[8 * k : 8 * k + 6].reshape(-1), me * cut, cut) for k in range(2)]
    return act, dx, gq, gk, gv, go, gi, gf, gains[0], gains[1], small[16 : 16 + n_bins, :heads]


def solution(mesh):
    split = P(("seq", "rows"), None)
    rows = P("rows", "seq", None)
    in_specs = (rows, P("rows"), P()) + (split,) * 6 + (P(("seq", "rows")),) * 2 + (P(), rows)
    out_specs = (rows, rows) + (split,) * 6 + (P(("seq", "rows")),) * 2 + (P(),)
    shape = (mesh.shape["seq"], mesh.shape["rows"])
    program = fast if shape == (NX, NZ * NY * NC) else local
    return jax.shard_map(program, mesh=mesh, in_specs=in_specs, out_specs=out_specs, check_vma=False)
```

```python
import functools

import jax
import jax.numpy as jnp
from jax import lax
from jax.experimental import pallas as pl
from jax.experimental.pallas import tpu as pltpu
from jax.sharding import PartitionSpec as P

MB = 2


EPS = 1e-06
NEG = -1000000000.0
HIGH = lax.Precision.HIGHEST


def normed(h, gain):
    return h * lax.rsqrt(jnp.mean(h * h, axis=-1, keepdims=True) + EPS) * gain


def fetch(shards):
    return (
        lax.all_gather(shards[0], ("seq", "rows"), axis=0, tiled=True),
        lax.all_gather(shards[1], ("seq", "rows"), axis=0, tiled=True),
        lax.all_gather(shards[2], ("seq", "rows"), axis=0, tiled=True),
        lax.all_gather(shards[3], ("seq", "rows"), axis=0, tiled=True),
        lax.all_gather(shards[4], ("seq", "rows"), axis=0, tiled=True),
        lax.all_gather(shards[5], ("seq", "rows"), axis=0, tiled=True),
        lax.all_gather(shards[6], ("seq", "rows"), axis=0, tiled=True),
        lax.all_gather(shards[7], ("seq", "rows"), axis=0, tiled=True),
    )


def local(
    tokens,
    doc_lengths,
    rel_buckets,
    w_query,
    w_key,
    w_value,
    w_output,
    w_inner,
    w_outer,
    attn_gain,
    ffn_gain,
    bias_table,
    out_grad,
):
    f32 = jnp.float32
    bf16 = jnp.bfloat16
    rows_dev, span, width = tokens.shape
    n_bins, heads = bias_table.shape
    head_dim = width // heads
    seq_count = lax.axis_size("seq")
    seq_place = lax.axis_index("seq")
    total = span * seq_count
    q_start = seq_place * span
    per = rows_dev // MB
    flat_rows = per * span
    shards = (w_query, w_key, w_value, w_output, w_inner, w_outer, attn_gain, ffn_gain)
    table = bias_table.astype(f32)
    k_pos = jnp.arange(total, dtype=jnp.int32)
    onehot = (rel_buckets[:, None] == jnp.arange(n_bins, dtype=jnp.int32)[None, :]).astype(f32)
    rel_bias = jnp.dot(onehot, table, precision=HIGH)
    spread = jnp.concatenate([rel_bias.T, jnp.zeros((heads, 1), f32)], axis=1)
    tiled = jnp.tile(spread, (1, total))
    full_bias = tiled[:, : total * (2 * total - 1)].reshape(heads, total, 2 * total - 1)[
        :, :, total - 1 :
    ]
    bias = lax.dynamic_slice_in_dim(full_bias, q_start, span, 1)
    ff_width = w_inner.shape[1]
    grad_wq = jnp.zeros((width, width), f32)
    grad_wk = jnp.zeros((width, width), f32)
    grad_wv = jnp.zeros((width, width), f32)
    grad_wo = jnp.zeros((width, width), f32)
    grad_wi = jnp.zeros((width, ff_width), f32)
    grad_wf = jnp.zeros((ff_width, width), f32)
    grad_g1 = jnp.zeros((width,), f32)
    grad_g2 = jnp.zeros((width,), f32)
    grad_bias = jnp.zeros((heads, span, total), f32)
    outputs = []
    input_grads = []
    for batch in range(MB):
        whole = fetch(shards)
        wq, wk, wv, wo, wi, wf, gain_one, gain_two = whole
        g1 = gain_one.astype(f32)
        g2 = gain_two.astype(f32)
        first = batch * per
        xflat = tokens[first : first + per].astype(f32).reshape(flat_rows, width)
        lens = doc_lengths[first : first + per]
        upstream = out_grad[first : first + per].reshape(flat_rows, width)
        n1 = normed(xflat, g1).astype(bf16)
        query = jnp.dot(n1, wq, preferred_element_type=f32).astype(bf16)
        key_local = jnp.dot(n1, wk, preferred_element_type=f32).astype(bf16)
        value_local = jnp.dot(n1, wv, preferred_element_type=f32).astype(bf16)
        keys_all, values_all = (
            lax.all_gather(key_local.reshape(per, span, width), "seq", axis=1, tiled=True),
            lax.all_gather(value_local.reshape(per, span, width), "seq", axis=1, tiled=True),
        )
        q4 = query.reshape(per, span, heads, head_dim)
        k4 = keys_all.reshape(per, total, heads, head_dim)
        v4 = values_all.reshape(per, total, heads, head_dim)
        valid = k_pos[None, :] < lens[:, None]

        def scores():
            raw = jnp.einsum("bqhd,bkhd->bhqk", q4, k4, preferred_element_type=f32) + bias[None]
            return jnp.where(valid[:, None, None, :], raw, NEG)

        first_scores = scores()
        top = jnp.max(first_scores, axis=-1, keepdims=True)
        expo = jnp.exp(first_scores - top)
        denom = jnp.sum(expo, axis=-1, keepdims=True)
        probs_low = (expo / denom).astype(bf16)
        mixed = jnp.einsum("bhqk,bkhd->bqhd", probs_low, v4, preferred_element_type=f32)
        mixed = mixed.reshape(flat_rows, width).astype(bf16)
        h1 = xflat + jnp.dot(mixed, wo, preferred_element_type=f32)
        n2 = normed(h1, g2).astype(bf16)
        inner = jnp.dot(n2, wi, preferred_element_type=f32)
        act_full, gelu_pull = jax.vjp(jax.nn.gelu, inner)
        act = act_full.astype(bf16)
        result = h1 + jnp.dot(act, wf, preferred_element_type=f32)
        outputs.append(result.astype(bf16).reshape(per, span, width))
        grad_wf = grad_wf + jnp.einsum("tf,td->fd", act, upstream, preferred_element_type=f32)
        d_act = jnp.einsum("td,fd->tf", upstream, wf, preferred_element_type=f32)
        d_inner = gelu_pull(d_act)[0].astype(bf16)
        grad_wi = grad_wi + jnp.einsum("td,tf->df", n2, d_inner, preferred_element_type=f32)
        d_n2 = jnp.einsum("tf,df->td", d_inner, wi, preferred_element_type=f32)
        norm_pull = jax.vjp(normed, h1, g2)[1]
        dh_part, dg_two = norm_pull(d_n2)
        grad_g2 = grad_g2 + dg_two
        dh1 = upstream.astype(f32) + dh_part
        d_attn = dh1.astype(bf16)
        grad_wo = grad_wo + jnp.einsum("td,te->de", mixed, d_attn, preferred_element_type=f32)
        d_mixed = jnp.einsum("te,de->td", d_attn, wo, preferred_element_type=f32).astype(bf16)
        dm4 = d_mixed.reshape(per, span, heads, head_dim)
        probs = jnp.exp(scores() - top) / denom
        d_probs = jnp.einsum("bqhd,bkhd->bhqk", dm4, v4, preferred_element_type=f32)
        value_terms = jnp.einsum("bhqk,bqhd->bkhd", probs_low, dm4, preferred_element_type=f32)
        delta = jnp.sum(probs * d_probs, axis=-1, keepdims=True)
        d_scores = (probs * (d_probs - delta)).astype(bf16)
        grad_bias = grad_bias + jnp.sum(d_scores.astype(f32), axis=0)
        d_query = jnp.einsum("bhqk,bkhd->bqhd", d_scores, k4, preferred_element_type=f32)
        d_query = d_query.reshape(flat_rows, width).astype(bf16)
        key_terms = jnp.einsum("bhqk,bqhd->bkhd", d_scores, q4, preferred_element_type=f32)
        key_share, value_share = (
            lax.psum_scatter(
                key_terms.reshape(per, total, width), "seq", scatter_dimension=1, tiled=True
            ),
            lax.psum_scatter(
                value_terms.reshape(per, total, width), "seq", scatter_dimension=1, tiled=True
            ),
        )
        d_key = key_share.reshape(flat_rows, width).astype(bf16)
        d_value = value_share.reshape(flat_rows, width).astype(bf16)
        grad_wq = grad_wq + jnp.einsum("td,te->de", n1, d_query, preferred_element_type=f32)
        grad_wk = grad_wk + jnp.einsum("td,te->de", n1, d_key, preferred_element_type=f32)
        grad_wv = grad_wv + jnp.einsum("td,te->de", n1, d_value, preferred_element_type=f32)
        d_n1 = jnp.einsum("te,de->td", d_query, wq, preferred_element_type=f32)
        d_n1 = d_n1 + jnp.einsum("te,de->td", d_key, wk, preferred_element_type=f32)
        d_n1 = d_n1 + jnp.einsum("te,de->td", d_value, wv, preferred_element_type=f32)
        first_pull = jax.vjp(normed, xflat, g1)[1]
        dx_part, dg_one = first_pull(d_n1)
        grad_g1 = grad_g1 + dg_one
        input_grads.append((dh1 + dx_part).reshape(per, span, width))
    owned = (
        lax.psum_scatter(grad_wq, ("seq", "rows"), scatter_dimension=0, tiled=True),
        lax.psum_scatter(grad_wk, ("seq", "rows"), scatter_dimension=0, tiled=True),
        lax.psum_scatter(grad_wv, ("seq", "rows"), scatter_dimension=0, tiled=True),
        lax.psum_scatter(grad_wo, ("seq", "rows"), scatter_dimension=0, tiled=True),
        lax.psum_scatter(grad_wi, ("seq", "rows"), scatter_dimension=0, tiled=True),
        lax.psum_scatter(grad_wf, ("seq", "rows"), scatter_dimension=0, tiled=True),
        lax.psum_scatter(grad_g1, ("seq", "rows"), scatter_dimension=0, tiled=True),
        lax.psum_scatter(grad_g2, ("seq", "rows"), scatter_dimension=0, tiled=True),
    )
    grad_full = lax.dynamic_update_slice_in_dim(
        jnp.zeros((heads, total, total), f32), grad_bias, q_start, 1
    )
    widened = jnp.pad(grad_full, ((0, 0), (0, 0), (total - 1, 0)))
    folded = jnp.pad(widened.reshape(heads, total * (2 * total - 1)), ((0, 0), (0, total)))
    rel_grad = jnp.sum(folded.reshape(heads, total, 2 * total), axis=1)[:, : 2 * total - 1]
    table_local = jnp.dot(onehot.T, rel_grad.T, precision=HIGH)
    table_grad = lax.psum(table_local, ("seq", "rows"))
    result_rows = jnp.concatenate(outputs, axis=0)
    grad_rows = jnp.concatenate(input_grads, axis=0)
    return (
        result_rows,
        grad_rows,
        owned[0],
        owned[1],
        owned[2],
        owned[3],
        owned[4],
        owned[5],
        owned[6],
        owned[7],
        table_grad,
    )


MESH_ID = pl.DeviceIdType.MESH
HBM = pl.BlockSpec(memory_space=pl.ANY)
VMEM = pl.BlockSpec(memory_space=pltpu.VMEM)
SMEM = pl.BlockSpec(memory_space=pltpu.SMEM)
BF = jnp.bfloat16
F32 = jnp.float32
NX, NZ, NY, NC = 2, 4, 2, 2


def rcopy(src, dst, send, recv, to):
    return pltpu.make_async_remote_copy(
        src_ref=src, dst_ref=dst, send_sem=send, recv_sem=recv, device_id=to, device_id_type=MESH_ID
    )


class Place:
    def __init__(self):
        self.x = lax.axis_index("seq")
        r = lax.axis_index("rows")
        self.c = lax.rem(r, 2)
        self.y = lax.rem(r // 2, 2)
        self.z = r // 4
        self.core = self.at(self.x, self.y, self.z, 1 - self.c)
        self.xn = self.at(1 - self.x, self.y, self.z, self.c)
        self.yn = self.at(self.x, 1 - self.y, self.z, self.c)
        self.zp = [None] + [self.at(self.x, self.y, self.zz(j), self.c) for j in range(1, NZ)]

    def at(self, x, y, z, c):
        return (x, z * 4 + y * 2 + c)

    def zz(self, j):
        return lax.rem(self.z + j, NZ)

    def barrier(self):
        sem = pltpu.get_barrier_semaphore()
        peers = [self.core, self.xn, self.yn] + self.zp[1:]
        for p in peers:
            pl.semaphore_signal(sem, inc=1, device_id=p, device_id_type=MESH_ID)
        pl.semaphore_wait(sem, len(peers))


class GatherXZY:
    def __init__(self, me, w, ss, rr, dd):
        self.me, self.w, self.ss, self.rr, self.dd = me, w, ss, rr, dd
        self.nh = w.shape[-1] // 2

    def ref(self, x, z, y, c):
        cols = pl.ds(pl.multiple_of(c * self.nh, 128), self.nh)
        return self.w.at[x, z, y, :, cols]

    def pair(self, z, y, c):
        cols = pl.ds(pl.multiple_of(c * self.nh, 128), self.nh)
        return self.w.at[:, z, y, :, cols]

    def send(self, ref, s, recv, to):
        rcopy(ref, ref, self.ss.at[s], recv, to).start()

    def got(self, ref, recv):
        rcopy(ref, ref, self.ss.at[0], recv, self.me.core).wait_recv()

    def start(self):
        m = self.me
        self.send(self.ref(m.x, m.z, m.y, m.c), 0, self.rr.at[0], m.xn)

    def step_x(self):
        m = self.me
        self.got(self.ref(1 - m.x, m.z, m.y, m.c), self.rr.at[0])
        p = self.pair(m.z, m.y, m.c)
        for j in range(1, NZ):
            self.send(p, j, self.rr.at[NZ - j], m.zp[j])
        self.send(p, 4, self.rr.at[4], m.yn)
        self.send(p, 8, self.dd.at[0], m.core)

    def step_z(self, j):
        m = self.me
        p = self.pair(m.zz(j), m.y, m.c)
        self.got(p, self.rr.at[j])
        self.send(p, 4 + j, self.rr.at[4 + j], m.yn)
        self.send(p, 8 + j, self.dd.at[j], m.core)

    def step_y(self, j):
        m = self.me
        p = self.pair(m.zz(j), 1 - m.y, m.c)
        self.got(p, self.rr.at[4 + j])
        self.send(p, 12 + j, self.dd.at[4 + j], m.core)

    def done(self):
        m = self.me
        for j in range(NZ):
            self.got(self.pair(m.zz(j), m.y, 1 - m.c), self.dd.at[j])
        for j in range(NZ):
            self.got(self.pair(m.zz(j), 1 - m.y, 1 - m.c), self.dd.at[4 + j])

    def sent(self):
        m = self.me
        one = self.ref(m.x, m.z, m.y, m.c)
        rcopy(one, one, self.ss.at[0], self.rr.at[0], m.core).wait_send()
        p = self.pair(m.z, m.y, m.c)
        for s in range(1, 16):
            rcopy(p, p, self.ss.at[s], self.rr.at[0], m.core).wait_send()


class GatherZYX:
    def __init__(self, me, w, ss, rr, dd):
        self.me, self.w, self.ss, self.rr, self.dd = me, w, ss, rr, dd

    def send(self, ref, s, recv, to):
        rcopy(ref, ref, self.ss.at[s], recv, to).start()

    def got(self, ref, recv):
        rcopy(ref, ref, self.ss.at[0], recv, self.me.core).wait_recv()

    def start(self):
        m = self.me
        own = self.w.at[m.x, m.z, m.y, m.c]
        for j in range(1, NZ):
            self.send(own, j - 1, self.rr.at[NZ - j - 1], m.zp[j])
        self.send(own, 3, self.rr.at[3], m.yn)

    def step_z(self, j):
        m = self.me
        b = self.w.at[m.x, m.zz(j), m.y, m.c]
        self.got(b, self.rr.at[j - 1])
        self.send(b, 5 + j, self.rr.at[3 + j], m.yn)

    def step_y(self, j):
        m = self.me
        self.got(self.w.at[m.x, m.zz(j), 1 - m.y, m.c], self.rr.at[3 + j])
        p = self.w.at[m.x, m.zz(j), :, m.c]
        self.send(p, 4 if j == 0 else 8 + j, self.rr.at[7 + j], m.xn)
        self.send(p, 5 if j == 0 else 11 + j, self.dd.at[j], m.core)

    def step_x(self, j):
        m = self.me
        p = self.w.at[1 - m.x, m.zz(j), :, m.c]
        self.got(p, self.rr.at[7 + j])
        self.send(p, 15 + j, self.dd.at[4 + j], m.core)

    def done_near(self):
        m = self.me
        for j in range(NZ):
            self.got(self.w.at[m.x, m.zz(j), :, 1 - m.c], self.dd.at[j])

    def done_far(self):
        m = self.me
        for j in range(NZ):
            self.got(self.w.at[1 - m.x, m.zz(j), :, 1 - m.c], self.dd.at[4 + j])

    def sent(self):
        m = self.me
        one = self.w.at[m.x, m.z, m.y, m.c]
        p = self.w.at[m.x, m.z, :, m.c]
        for s in range(19):
            r = one if s in (0, 1, 2, 3, 6, 7, 8) else p
            rcopy(r, r, self.ss.at[s], self.rr.at[0], m.core).wait_send()


def own_block(me, mine, theirs, w, nh):
    cols = pl.ds(pl.multiple_of(me.c * nh, 128), nh)
    a = mine[...].astype(F32)[:24]
    b = theirs[...].astype(F32)[:24]
    first = jnp.where(me.c == 0, a, b)
    second = jnp.where(me.c == 0, b, a)
    w[me.x, me.z, me.y, :, cols] = jnp.concatenate([first, second], axis=0).astype(BF)


class Piece:
    def __init__(self, index, rows, first):
        self.index, self.slot, self.rows = index, index % 2, rows
        cut = rows // 2 if rows // 2 % 16 == 0 else rows // 2 + 8
        self.subs = ((0, cut, first[0]), (cut, rows - cut, first[1]))


def acc_rows(x, y, z, lo, n):
    return pl.ds(pl.multiple_of(((x * NY + y) * NZ + z) * 192 + lo, 8), n)


class Reduce:
    def __init__(self, me, acc, a1, a2, a3, cs, cr, s1s, s1r, s2s, s2r, s3s, s3r, fin, finr, keep, sems):
        self.me = me
        self.acc, self.a1, self.a2, self.a3, self.cs, self.cr = acc, a1, a2, a3, cs, cr
        self.s1s, self.s1r, self.s2s, self.s2r, self.s3s, self.s3r = s1s, s1r, s2s, s2r, s3s, s3r
        self.fin, self.finr = fin, finr
        self.keep = keep
        (self.c_s, self.c_r, self.a_s, self.a_r, self.b_s, self.b_r, self.z_s, self.z_r, self.f_s, self.f_r) = sems

    def near(self, axis):
        return self.me.xn if axis == "x" else self.me.yn

    def core_copy(self, p):
        s, n = p.slot, p.rows
        return rcopy(
            self.cs.at[:, :, :, 0:n], self.cr.at[s, :, :, :, 0:n], self.c_s.at[s], self.c_r.at[s], self.me.core
        )

    def one_copy(self, p, k):
        s, (_, n, axis) = p.slot, p.subs[k]
        return rcopy(
            self.s1s.at[k, :, :, 0:n], self.s1r.at[s, k, :, :, 0:n], self.a_s.at[s, k], self.a_r.at[s, k], self.near(axis)
        )

    def two_copy(self, p, k):
        s, (_, n, axis) = p.slot, p.subs[k]
        to = self.near("y" if axis == "x" else "x")
        return rcopy(self.s2s.at[k, :, 0:n], self.s2r.at[s, k, :, 0:n], self.b_s.at[s, k], self.b_r.at[s, k], to)

    def z_copy(self, p, j):
        s, n = p.slot, p.rows
        return rcopy(
            self.s3s.at[j, 0:n], self.s3r.at[s, NZ - j, 0:n], self.z_s.at[s, j], self.z_r.at[s, NZ - j], self.me.zp[j]
        )

    def fin_copy(self, p):
        i, n = p.index, p.rows // 2
        return rcopy(
            self.fin.at[i, 0:n], self.finr.at[i, 0:n], self.f_s.at[i], self.f_r.at[i], self.me.core
        )

    def send_core(self, p):
        self.core_copy(p).start()

    def h1(self, p, old):
        me, s, n = self.me, p.slot, p.rows
        self.core_copy(p).wait_recv()
        for k, (lo, n, axis) in enumerate(p.subs):
            if old is not None:
                self.one_copy(old, k).wait_send()
            rows = pl.ds(lo, n)

            def body(q, carry):
                a, zq = q // NZ, lax.rem(q, NZ)
                if axis == "x":
                    keep, away = (me.x, a, zq, rows), (1 - me.x, a, zq, rows)
                else:
                    keep, away = (a, me.y, zq, rows), (a, 1 - me.y, zq, rows)
                held = [self.acc[acc_rows(*at[:3], lo, n), :] for at in (keep, away)]
                self.a1[k, a, zq, 0:n] = held[0] + self.cr[(s,) + keep].astype(F32)
                self.s1s[k, a, zq, 0:n] = (held[1] + self.cr[(s,) + away].astype(F32)).astype(BF)
                return carry

            lax.fori_loop(0, 2 * NZ, body, 0)
            self.one_copy(p, k).start()

    def h2(self, p, old):
        me, s = self.me, p.slot
        for k, (lo, n, axis) in enumerate(p.subs):
            self.one_copy(p, k).wait_recv()
            if old is not None:
                self.two_copy(old, k).wait_send()
            b = me.y if axis == "x" else me.x

            def body(zq, carry):
                self.a2[k, zq, 0:n] = self.a1[k, b, zq, 0:n] + self.s1r[s, k, b, zq, 0:n].astype(F32)
                self.s2s[k, zq, 0:n] = (
                    self.a1[k, 1 - b, zq, 0:n] + self.s1r[s, k, 1 - b, zq, 0:n].astype(F32)
                ).astype(BF)
                return carry

            lax.fori_loop(0, NZ, body, 0)
            self.two_copy(p, k).start()

    def h3(self, p, old):
        me, s = self.me, p.slot
        for k in range(2):
            self.two_copy(p, k).wait_recv()
        for j in range(1, NZ):
            if old is not None:
                self.z_copy(old, j).wait_send()
        for k, (lo, n, _) in enumerate(p.subs):
            rows = pl.ds(lo, n)
            for j in range(NZ):
                zq = me.zz(j)
                v = self.a2[k, zq, 0:n] + self.s2r[s, k, zq, 0:n].astype(F32)
                if j == 0:
                    self.a3[rows] = v
                else:
                    self.s3s[j, rows] = v.astype(BF)
        for j in range(1, NZ):
            self.z_copy(p, j).start()

    def h4(self, p):
        me, s, n, i = self.me, p.slot, p.rows, p.index
        for j in range(1, NZ):
            self.z_copy(p, NZ - j).wait_recv()
        total = self.a3[0:n]
        for j in range(1, NZ):
            total = total + self.s3r[s, j, 0:n].astype(F32)
        if p.groups is None:
            a, b = total[0 : n // 2], total[n // 2 :]
        else:
            a, b = (
                jnp.concatenate([total[48 * g + 24 * k : 48 * g + 24 * k + 24] for g in range(p.groups)], axis=0)
                for k in range(NC)
            )
        self.fin[i, 0 : n // 2] = jnp.where(me.c == 0, b, a)
        self.keep(p, jnp.where(me.c == 0, a, b), me.c)
        self.fin_copy(p).start()


def norm_back(h, gain, up):
    r = lax.rsqrt(jnp.mean(h * h, axis=-1, keepdims=True) + EPS)
    hr = h * r
    w = up * gain
    dgain = jnp.sum(up * hr, axis=0, keepdims=True)
    return r * (w - hr * jnp.mean(w * hr, axis=-1, keepdims=True)), dgain


def layer_kernel(
    tok, gin, gains, wq, wk, wv, wo, wi, pd, relb, table, lens,
    act_o, dx_o, gq_o, gk_o, gv_o, go_o, gi_o, gf_o, sm_o,
    WA, WB, WD, X, G, N2, QKV, O, H1, ACT, DU, T, M, MACC, LSE, R, RG,
    ACC, A1, A2, A3, CS, CR, S1S, S1R, S2S, S2R, S3S, S3R, FIN, FINR, SM, SMR, ZB, DG,
    ts, tr, tl, gs, gr, gl, es, er, as_, ar, ad, bs, br, bd, ds_, dr, dd, ys, yr, yl, xs_, xr, xl,
    c_s, c_r, a_s, a_r, b_s, b_r, z_s, z_r, f_s, f_r, ms, mr,
):
    me = Place()
    x, y, z, c = me.x, me.y, me.z, me.c
    mine, span, width = X.shape[0], X.shape[2], X.shape[3]
    length = 2 * span
    flat = mine * length
    ff = DU.shape[1]
    na, nb = WA.shape[4] // 2, WB.shape[4] // 2
    PA, PB = DU.at[pl.ds(32 * c, 32), 0:na], DU.at[pl.ds(64 + 32 * c, 32), 0:nb]
    RA, RB = DU.at[128:160, 0:na], DU.at[160:192, 0:nb]
    hd = 64
    YB = N2
    pairs = width // hd // 2
    gath_a = GatherXZY(me, WA, as_, ar, ad)
    gath_b = GatherXZY(me, WB, bs, br, bd)
    gath_d = GatherZYX(me, WD, ds_, dr, dd)

    def pack(first, n, parts):
        filled = [
            jnp.concatenate([p[...].astype(F32), jnp.zeros((32 - p.shape[0], p.shape[1]), F32)], axis=0) for p in parts
        ]
        filled = jnp.concatenate(filled, axis=1).astype(BF)
        for half in range(2):
            DU[first + 32 * half : first + 32 * half + 32, 0:n] = filled[:, n * half : n * half + n]

    pack(0, na, (gains, wq, wk, wv))
    me.barrier()
    ea = rcopy(DU.at[pl.ds(32 * (1 - c), 32), 0:na], RA, es.at[0], er.at[0], me.core)
    eb = rcopy(DU.at[pl.ds(64 + 32 * (1 - c), 32), 0:nb], RB, es.at[1], er.at[1], me.core)
    ea.start()
    pack(64, nb, (wo, wi))
    eb.start()
    tok_r = [rcopy(tok.at[2 * (1 - x) + i], X.at[i, x], ts.at[i], tr.at[i], me.xn) for i in range(mine)]
    tok_in = [rcopy(X.at[i, 1 - x], X.at[i, 1 - x], ts.at[i], tr.at[i], me.xn) for i in range(mine)]
    tok_l = [pltpu.make_async_copy(tok.at[2 * x + i], X.at[i, x], tl.at[i]) for i in range(mine)]
    g_r = rcopy(gin.at[pl.ds(2 * (1 - x), 2)], G.at[:, x], gs, gr, me.xn)
    g_in = rcopy(G.at[:, 1 - x], G.at[:, 1 - x], gs, gr, me.xn)
    g_l = pltpu.make_async_copy(gin.at[pl.ds(2 * x, 2)], G.at[:, x], gl)
    ea.wait_recv()
    own_block(me, PA, RA, WA, na)
    gath_a.start()
    for i in range(mine):
        tok_r[i].start()
        tok_l[i].start()
    g_l.start()
    eb.wait_recv()
    own_block(me, PB, RB, WB, nb)
    WD[x, z, y, c] = pd[...]
    cols = relb.shape[1]
    kinds = table.shape[0]
    hot = (lax.broadcasted_iota(jnp.int32, (kinds, cols), 0) == relb[...]).astype(BF)
    R[...] = lax.dot_general(table[...], hot, (((0,), (0,)), ((), ())), preferred_element_type=F32)[0:16]
    gath_a.step_x()
    gath_b.start()
    gath_d.start()
    for j in range(1, NZ):
        gath_a.step_z(j)
    gath_b.step_x()
    for j in range(NZ):
        gath_a.step_y(j)
    gath_d.step_y(0)
    g_r.start()
    gath_a.done()

    def gain_row(k):
        return jnp.transpose(WA[:, :, :, :, 128 * k : 128 * k + 128].reshape(width, 128).astype(F32))[0:1, :]

    gain1 = gain_row(0)

    def row_slice(i):
        return pl.ds(pl.multiple_of(i * length, length), length)

    def first_norm(i):
        for half in range(2):
            xf = X[i, half].astype(F32)
            scale = lax.rsqrt(jnp.mean(xf * xf, axis=-1, keepdims=True) + EPS)
            N2[i, half] = (xf * scale * gain1).astype(BF)

    for i in range(mine):
        tok_l[i].wait()
        tok_in[i].wait_recv()
        first_norm(i)
        for n in range(3):
            w = WA[:, :, :, :, 256 + n * width : 256 + (n + 1) * width].reshape(width, width)
            QKV[row_slice(i), n * width : (n + 1) * width] = jnp.dot(
                N2[i].reshape(length, width), w, preferred_element_type=F32
            ).astype(BF)
    low = lax.broadcasted_iota(jnp.int32, (1, 128), 1) < hd
    lane = lax.broadcasted_iota(jnp.int32, (1, 128), 1)
    kpos = lax.broadcasted_iota(jnp.int32, (length, 128), 0)
    blocks = length // 128

    def strips(p):
        for h in range(2):
            row = jnp.broadcast_to(R[pl.ds(2 * p + h, 1), :], (128, cols))
            M[h] = pltpu.roll(row, cols - 127, 1, stride=1, stride_axis=0)[:, : M.shape[2]]

    def bias_of(h):
        return jnp.concatenate(
            [M[h, :, 128 * (blocks - 1 - a) : 128 * (blocks - 1 - a) + length] for a in range(blocks)], axis=0
        )

    own = (low, jnp.logical_not(low))
    spare = (hd, 0)
    ones = [(lane == spare[h]).astype(F32).astype(BF) for h in range(2)]
    none = jnp.zeros((), BF)

    def masked_keys(h, k, count):
        pad = jnp.where((lane == spare[h]) & (kpos >= count), NEG, 0.0).astype(BF)
        return jnp.where(own[h], k, pad)

    def lanes(n, p):
        return pl.ds(pl.multiple_of(n * width + p * 128, 128), 128)

    nt = (((1,), (1,)), ((), ()))
    tn = (((0,), (0,)), ((), ()))

    def mm(a, b, dims):
        return lax.dot_general(a, b, dims, preferred_element_type=F32)

    comm = {
        0: (lambda: gath_b.step_z(1), lambda: gath_d.step_z(1)),
        1: (lambda: gath_b.step_z(2), lambda: gath_d.step_z(2)),
        2: (lambda: gath_b.step_z(3), lambda: gath_d.step_z(3)),
        3: (lambda: gath_b.step_y(0), lambda: gath_d.step_y(1)),
        5: (lambda: gath_b.step_y(1), lambda: gath_d.step_y(2)),
        7: (lambda: gath_b.step_y(2), lambda: gath_d.step_y(3)),
        8: (lambda: gath_b.step_y(3),),
        9: (lambda: gath_d.step_x(0),),
        10: (lambda: gath_d.step_x(1),),
        11: (lambda: gath_d.step_x(2),),
    }

    def attend(t, carry):
        p, i = t // mine, lax.rem(t, mine)
        pl.when(i == 0)(lambda: strips(p))
        rows = row_slice(i)
        q, k, v = QKV[rows, lanes(0, p)], QKV[rows, lanes(1, p)], QKV[rows, lanes(2, p)]
        outs = []
        for h in range(2):
            s = mm(jnp.where(own[h], q, ones[h]), masked_keys(h, k, lens[2 * x + i]), nt) + bias_of(h)
            top = jnp.max(s, axis=-1, keepdims=True)
            e = jnp.exp(s - top)
            total = jnp.sum(e, axis=-1, keepdims=True)
            LSE[rows, :] = jnp.where(lane == 2 * p + h, top + jnp.log(total), LSE[rows, :])
            outs.append(jnp.dot((e * (1.0 / total)).astype(BF), v, preferred_element_type=F32))
        O[i, :, :, lanes(0, p)] = jnp.where(low, outs[0], outs[1]).astype(BF).reshape(2, span, 128)
        for at, steps in comm.items():
            @pl.when(t == at)
            def _():
                for step in steps:
                    step()
        return carry

    LSE[...] = jnp.zeros_like(LSE)
    lax.fori_loop(0, mine * pairs, attend, 0)
    ea.wait_send()
    eb.wait_send()
    gath_d.step_x(3)
    gath_b.done()
    gath_d.done_near()
    g_l.wait()
    g_in.wait_recv()

    gain2 = gain_row(1)
    DG[...] = jnp.zeros_like(DG)
    c0, c1 = 0.7978845608028654, 0.044715

    def dn_set(v):
        for n in range(width // 128):
            ACC[length * n : length * n + length, :] = v[:, 128 * n : 128 * n + 128]

    def dn_get(lo, n):
        return jnp.concatenate([ACC[length * k + lo : length * k + lo + n, :] for k in range(width // 128)], axis=1)

    def dn_add(v):
        for n in range(width // 128):
            at = slice(length * n, length * n + length)
            ACC[at, :] = ACC[at, :] + v[:, 128 * n : 128 * n + 128]

    wo_all = lambda: WB[:, :, :, :, 0:width].reshape(width, width)
    for i in range(mine):
        h1 = X[i].reshape(length, width).astype(F32) + jnp.dot(
            O[i].reshape(length, width), wo_all(), preferred_element_type=F32
        )
        H1[i] = h1.reshape(2, span, width)
        r = lax.rsqrt(jnp.mean(h1 * h1, axis=-1, keepdims=True) + EPS)
        N2[i] = (h1 * r * gain2).astype(BF).reshape(2, span, width)

    def chunk(n, carry):
        pl.when(n == 2)(gath_d.done_far)
        f = lax.rem(2 * x + n, 4)

        def one_row(i, carry):
            n2, g = N2[i].reshape(length, width), G[i].reshape(length, width)
            for part in range(3):
                fcols = pl.ds(pl.multiple_of(f * width + 256 * part, 256), 256)
                wcols = pl.ds(pl.multiple_of(width + f * width + 256 * part, 256), 256)
                wi_part = WB[:, :, :, :, wcols].reshape(width, 256)
                wf_part = WD[f // 2, pl.ds(2 * lax.rem(f, 2), 2)].reshape(width, width)[256 * part : 256 * part + 256]
                u = jnp.dot(n2, wi_part, preferred_element_type=F32)
                da = mm(g, wf_part, nt)
                sq = u * u
                t = jnp.tanh(u * (c0 + (c0 * c1) * sq))
                cdf = 0.5 + 0.5 * t
                ACT[row_slice(i), fcols] = (u * cdf).astype(BF)
                slope = cdf + (0.5 * u) * (1.0 - t * t) * (c0 + (3.0 * c0 * c1) * sq)
                DU[row_slice(i), fcols] = (da * slope).astype(BF)
            return carry

        return lax.fori_loop(0, mine, one_row, carry)

    lax.fori_loop(0, ff // width, chunk, 0)
    T[...] = jnp.transpose(N2[...].reshape(flat, width))

    def result(t, carry):
        i, f = t // 4, lax.rem(t, 4)
        a = ACT[row_slice(i), pl.ds(pl.multiple_of(f * width, width), width)]
        wf = WD[f // 2, pl.ds(2 * lax.rem(f, 2), 2)].reshape(width, width)
        out = jnp.dot(a, wf, preferred_element_type=F32)

        @pl.when(f == 0)
        def _():
            dn_set(H1[i].reshape(length, width) + out)

        @pl.when(f > 0)
        def _():
            dn_add(out)

        @pl.when(f == 3)
        def _():
            YB[i] = dn_get(0, length).astype(BF).reshape(2, span, width)

        return carry

    lax.fori_loop(0, 4 * mine, result, 0)
    y_out = [
        rcopy(YB.at[i, 1 - x], act_o.at[2 * (1 - x) + i], ys.at[i], yr.at[i], me.xn) for i in range(mine)
    ]
    y_loc = [pltpu.make_async_copy(YB.at[i, x], act_o.at[2 * x + i], yl.at[i]) for i in range(mine)]
    for i in range(mine):
        rcopy(YB.at[i, 1 - x], act_o.at[2 * x + i], ys.at[i], yr.at[i], me.xn).start()
        y_loc[i].start()

    def back(t, carry):
        i, f = t // 4, lax.rem(t, 4)
        du = DU[row_slice(i), pl.ds(pl.multiple_of(f * width, width), width)]
        wi_part = WB[:, :, :, :, pl.ds(pl.multiple_of((f + 1) * width, width), width)].reshape(width, width)
        out = mm(du, wi_part, nt)

        @pl.when(f == 0)
        def _():
            dn_set(out)

        @pl.when(f > 0)
        def _():
            dn_add(out)

        @pl.when(f == 3)
        def _():
            for half in range(2):
                dh, dgain = norm_back(H1[i, half], gain2, dn_get(span * half, span))
                DG[1:2, :] = DG[1:2, :] + dgain
                H1[i, half] = G[i, half].astype(F32) + dh

        return carry

    lax.fori_loop(0, 4 * mine, back, 0)

    def keep(p, value, core):
        if p.groups is None:
            gf_o[:, pl.ds(pl.multiple_of(256 * p.index + 128 * core, 128), 128)] = value
            return
        for g in range(p.groups):
            if p.groups == 4:
                dst, base = gi_o, 1024 * (p.index - width // 256) + 256 * g
            elif p.index == last - 4:
                dst, base = go_o, 256 * g
            else:
                dst, base = (gq_o, gk_o, gv_o)[g], 256 * (p.index - last + 3)
            dst[:, pl.ds(pl.multiple_of(base + 128 * core, 128), 128)] = value[24 * g : 24 * g + 24]

    red = Reduce(
        me, ACC, A1, A2, A3, CS, CR, S1S, S1R, S2S, S2R, S3S, S3R, FIN, FINR, keep, (c_s, c_r, a_s, a_r, b_s, b_r, z_s, z_r, f_s, f_r)
    )
    pieces = []
    last = (ff // 1024) + (width // 256) + 4
    for n in range(last):
        rows = 192 if n < last - 4 else 144
        piece = Piece(n, rows, ("x", "y") if n < last - 1 else ("x", "x"))
        piece.groups = None if n < width // 256 else rows // 48
        pieces.append(piece)

    def stages(n, lo, hi):
        at = lambda k: pieces[n - k] if lo <= n - k < hi else None
        old = lambda k: pieces[n - k - 1] if n - k - 1 >= 0 else None
        if at(4):
            red.h4(at(4))
        if at(3):
            red.h3(at(3), old(3))
        if at(2):
            red.h2(at(2), old(2))
        if at(1):
            red.h1(at(1), old(1))
        if at(0) and old(0):
            red.core_copy(old(0)).wait_send()

    def split(res):
        a, b = res[:, 0:128], res[:, 128:256]
        return jnp.where(c == 0, a, b), jnp.where(c == 0, b, a).astype(BF)

    def outer_piece(j):

        def body(q, carry):
            xq, zh = q // 2, lax.rem(q, 2)
            lhs = ACT[:, pl.ds(pl.multiple_of(q * 768, 768), 768)]
            rhs = G[:, :, :, 256 * j : 256 * j + 256].reshape(flat, 256)
            own, other = split(mm(lhs, rhs, tn))
            for b in range(4):
                at = (xq, b % 2, 2 * zh + b // 2)
                ACC[acc_rows(*at, 0, 192), :] = own[192 * b : 192 * b + 192]
                CS[at] = other[192 * b : 192 * b + 192]
            return carry

        lax.fori_loop(0, 4, body, 0)

    def rows_piece(groups, rhs):
        def body(g, carry):
            own, other = split(jnp.dot(T[...], rhs(g), preferred_element_type=F32))
            at = pl.ds(pl.multiple_of(48 * g, 48), 48)
            for k in range(NX * NZ * NY):
                ACC[acc_rows(k // 8, k % 2, (k // 2) % 4, 48 * g, 48), :] = own[48 * k : 48 * k + 48]
                CS[k // 8, k % 2, (k // 2) % 4, at] = other[48 * k : 48 * k + 48]
            return carry

        lax.fori_loop(0, groups, body, 0)

    early = last - 3
    step = 0
    for j in range(width // 256):
        stages(step, 0, early)
        outer_piece(j)
        red.send_core(pieces[step])
        step += 1
    for j in range(ff // 1024):
        stages(step, 0, early)
        rows_piece(4, lambda g: DU[:, pl.ds(pl.multiple_of(1024 * j + 256 * g, 256), 256)])
        red.send_core(pieces[step])
        step += 1
    stages(step, 0, early)
    T[...] = jnp.transpose(O[...].reshape(flat, width))
    rows_piece(3, lambda g: H1[:, :, :, pl.ds(pl.multiple_of(256 * g, 256), 256)].reshape(flat, 256).astype(BF))
    red.send_core(pieces[step])
    step += 1
    for i in range(mine):
        dab = H1[i].reshape(length, width).astype(BF)
        G[i] = mm(dab, wo_all(), nt).astype(BF).reshape(2, span, width)
    for i in range(mine):
        y_out[i].wait_recv()
        y_out[i].wait_send()
        y_loc[i].wait()
    for i in range(mine):
        first_norm(i)
    T[...] = jnp.transpose(N2[...].reshape(flat, width))

    def attend_back(t, carry):
        p, i = t // mine, lax.rem(t, mine)

        @pl.when(i == 0)
        def _():
            strips(p)
            MACC[...] = jnp.zeros_like(MACC)

        rows = row_slice(i)
        q, k, v = QKV[rows, lanes(0, p)], QKV[rows, lanes(1, p)], QKV[rows, lanes(2, p)]
        do = G[i, :, :, lanes(0, p)].reshape(length, 128)
        prod = do.astype(F32) * O[i, :, :, lanes(0, p)].reshape(length, 128).astype(F32)
        dqs, dks, dvs = [], [], []
        for h in range(2):
            lse = jnp.sum(jnp.where(lane == 2 * p + h, LSE[rows, :], 0.0), axis=-1, keepdims=True)
            delta = jnp.sum(jnp.where(own[h], prod, 0.0), axis=-1, keepdims=True)
            s = mm(jnp.where(own[h], q, ones[h]), masked_keys(h, k, lens[2 * x + i]), nt) + bias_of(h)
            pr = jnp.exp(s - lse)
            ds = pr * (mm(jnp.where(own[h], do, none), v, nt) - delta)
            for a in range(blocks):
                at = 128 * (blocks - 1 - a)
                MACC[h, :, at : at + length] = MACC[h, :, at : at + length] + ds[128 * a : 128 * a + 128]
            low_p, low_ds = pr.astype(BF), ds.astype(BF)
            dqs.append(jnp.dot(low_ds, k, preferred_element_type=F32))
            dks.append(mm(low_ds, q, tn))
            dvs.append(mm(low_p, do, tn))
        for n, parts in enumerate((dqs, dks, dvs)):
            ACT[rows, lanes(n, p)] = jnp.where(low, parts[0], parts[1]).astype(BF)

        @pl.when(i == mine - 1)
        def _():
            for h in range(2):
                part = jnp.zeros((8, cols), F32)
                for a in range(16):
                    part = part + pltpu.roll(MACC[h, 8 * a : 8 * a + 8, :], (cols - 8 * a) % cols, 1)
                line = part[0:1]
                for a in range(1, 8):
                    line = line + pltpu.roll(part[a : a + 1], cols - a, 1)
                RG[pl.ds(2 * p + h, 1), :] = pltpu.roll(line, 127, 1)

        for n in range(4):
            pl.when(t == n)(lambda n=n: stages(early + n, 0, early))
        for m in range(2):
            @pl.when(t == 4 * m + 3)
            def _():
                red.core_copy(pieces[early + m - 1]).wait_send()
                rows_piece(3, lambda g: ACT[:, pl.ds(pl.multiple_of(g * width + 256 * m, 256), 256)])
                red.send_core(pieces[early + m])

            for n in range(1, 5):
                pl.when(t == 4 * m + 3 + n)(lambda m=m, n=n: stages(early + m + n, early + m, early + m + 1))
        return carry

    RG[...] = jnp.zeros_like(RG)
    MACC[...] = jnp.zeros_like(MACC)
    lax.fori_loop(0, mine * pairs, attend_back, 0)

    step = last - 1
    red.core_copy(pieces[step - 1]).wait_send()
    rows_piece(3, lambda g: ACT[:, pl.ds(pl.multiple_of(g * width + 512, 256), 256)])
    red.send_core(pieces[step])
    step += 1
    early = last - 1
    stages(step, early, last)
    step += 1
    landing = lambda i: DU.at[pl.ds(i * span, span), 0:width]
    dx_r = [rcopy(X.at[i, 1 - x], landing(i), xs_.at[i], xr.at[i], me.xn) for i in range(mine)]
    dx_l = [pltpu.make_async_copy(H1.at[i, x], dx_o.at[2 * x + i], xl.at[i]) for i in range(mine)]
    dx_f = [pltpu.make_async_copy(H1.at[i, 1 - x], dx_o.at[2 * (1 - x) + i], xl.at[mine + i]) for i in range(mine)]
    for i in range(mine):
        for n in range(3):
            out = mm(
                ACT[row_slice(i), n * width : (n + 1) * width],
                WA[:, :, :, :, 256 + n * width : 256 + (n + 1) * width].reshape(width, width),
                nt,
            )
            (dn_set if n == 0 else dn_add)(out)
        for half in range(2):
            dh, dgain = norm_back(X[i, half].astype(F32), gain1, dn_get(span * half, span))
            DG[0:1, :] = DG[0:1, :] + dgain
            H1[i, half] = H1[i, half] + dh
        X[i, 1 - x] = H1[i, 1 - x].astype(BF)
        dx_r[i].start()
        dx_l[i].start()
        stages(step, early, last)
        step += 1
    for n in range(width // 128):
        SM[0, n : n + 1, :] = DG[0:1, 128 * n : 128 * n + 128]
        SM[0, 8 + n : 9 + n, :] = DG[1:2, 128 * n : 128 * n + 128]
    rest = jnp.concatenate([RG[...], jnp.zeros((112, cols), F32)], axis=0)
    spread = jnp.zeros((kinds, 128), F32)
    for _ in range(3):
        part = rest.astype(BF)
        rest = rest - part.astype(F32)
        spread = spread + mm(hot, part, nt)
    SM[0, 16 : 16 + kinds, :] = spread
    sm_copies = [
        rcopy(SM.at[k], SMR.at[k], ms.at[k], mr.at[k], to) for k, to in enumerate((me.core, me.xn, me.yn))
    ]
    sm_copies[0].start()
    stages(step, early, last)
    step += 1
    for k in range(3):
        sm_copies[k].wait_recv()
        SM[k + 1] = SM[k] + SMR[k]
        if k < 2:
            sm_copies[k + 1].start()
    ZB[z] = SM[3]
    sm_z = [None] + [rcopy(SM.at[3], ZB.at[z], ms.at[2 + j], mr.at[6 - j], me.zp[j]) for j in range(1, NZ)]
    for j in range(1, NZ):
        sm_z[j].start()
    for i in range(mine):
        dx_r[i].wait_recv()
        H1[i, 1 - x] = DU[pl.ds(i * span, span), 0:width].astype(F32)
        dx_f[i].start()
    for p in pieces:
        red.fin_copy(p).wait_recv()
        keep(p, FINR[p.index, 0 : p.rows // 2], 1 - c)
    for j in range(1, NZ):
        rcopy(SM.at[3], ZB.at[me.zz(j)], ms.at[2 + j], mr.at[2 + j], me.zp[j]).wait_recv()
    sm_o[...] = ZB[0] + ZB[1] + ZB[2] + ZB[3]
    g_r.wait_send()
    for k in range(3):
        sm_copies[k].wait_send()
    for j in range(1, NZ):
        sm_z[j].wait_send()
    for g in (gath_a, gath_b, gath_d):
        g.sent()
    for i in range(mine):
        tok_r[i].wait_send()
        dx_r[i].wait_send()
        dx_l[i].wait()
        dx_f[i].wait()
    for p in pieces[-1:]:
        red.core_copy(p).wait_send()
        for k in range(2):
            red.one_copy(p, k).wait_send()
            red.two_copy(p, k).wait_send()
        for j in range(1, NZ):
            red.z_copy(p, j).wait_send()
    for p in pieces:
        red.fin_copy(p).wait_send()


def layer_call(tok, gin, gains, wq, wk, wv, wo, wi, pd, relb, table, lens, heads):
    rows_dev, span, width = tok.shape
    length = 2 * span
    mine = rows_dev // 2
    flat = mine * length
    dma = pltpu.SemaphoreType.DMA
    ff = wi.shape[1]
    na, nb = (gains.shape[1] + 3 * width) // 2, (width + ff) // 2
    count = width // 256 + ff // 1024 + 4
    wa = (NX, NZ, NY, 48, 2 * na)
    wb = (NX, NZ, NY, 48, 2 * nb)
    wd = (NX, NZ, NY, NC) + pd.shape
    xs = (mine, 2, span, width)
    block = (192, 128)
    bf = lambda *s: pltpu.VMEM(s, BF)
    f32 = lambda *s: pltpu.VMEM(s, F32)
    out = lambda *s: jax.ShapeDtypeStruct(s, F32)
    shard = wq.shape[0]
    return pl.pallas_call(
        layer_kernel,
        out_shape=[jax.ShapeDtypeStruct(tok.shape, BF), out(*tok.shape)]
        + [out(shard, width)] * 4 + [out(shard, ff), out(*pd.shape), out(48, 128)],
        in_specs=[HBM, HBM] + [VMEM] * 9 + [SMEM],
        out_specs=[HBM, HBM] + [VMEM] * 7,
        scratch_shapes=[
            bf(*wa), bf(*wb), bf(*wd), bf(*xs), bf(*xs), bf(*xs), bf(flat, 3 * width), bf(*xs), f32(*xs),
             bf(flat, ff), bf(flat, ff), bf(width, flat), f32(2, 128, 896), f32(2, 128, 1024),
            f32(flat, 128), f32(16, relb.shape[1]), f32(16, relb.shape[1]),
            f32(NX * NY * NZ * 192, 128), f32(2, 2, NZ, 96, 128), f32(2, NZ, 96, 128), f32(*block), bf(NX, NY, NZ, *block), bf(2, NX, NY, NZ, *block),
            bf(2, 2, NZ, 96, 128), bf(2, 2, 2, NZ, 96, 128), bf(2, NZ, 96, 128), bf(2, 2, NZ, 96, 128),
            bf(NZ, *block), bf(2, NZ, *block), f32(count, 96, 128), f32(count, 96, 128),
            f32(4, 48, 128), f32(3, 48, 128), f32(NZ, 48, 128), f32(8, width),
            dma((2,)), dma((2,)), dma((2,)), dma, dma, dma, dma((2,)), dma((2,)),
            dma((16,)), dma((8,)), dma((8,)), dma((16,)), dma((8,)), dma((8,)), dma((19,)), dma((11,)), dma((8,)),
            dma((2,)), dma((2,)), dma((2,)), dma((2,)), dma((2,)), dma((4,)),
            dma((2,)), dma((2,)), dma((2, 2)), dma((2, 2)), dma((2, 2)), dma((2, 2)), dma((2, NZ)), dma((2, NZ)),
            dma((count,)), dma((count,)), dma((6,)), dma((6,)),
        ],
        compiler_params=pltpu.CompilerParams(
            collective_id=0, has_side_effects=True, vmem_limit_bytes=VMEM_LIMIT
        ),
        name="layer",
    )(tok, gin, gains, wq, wk, wv, wo, wi, pd, relb, table, lens)


VMEM_LIMIT = 67_000_000


def fast(
    tokens, doc_lengths, rel_buckets, w_query, w_key, w_value, w_output, w_inner, w_outer,
    attn_gain, ffn_gain, bias_table, out_grad,
):
    n_bins, heads = bias_table.shape
    wide = lambda g: jnp.broadcast_to(g[:, None], (g.shape[0], 128))
    gains = jnp.concatenate([wide(attn_gain), wide(ffn_gain)], axis=1)
    relb = jnp.pad(rel_buckets, (0, 1))[None, :]
    table = jnp.pad(bias_table, ((0, 0), (0, 128 - heads)))
    act, dx, gq, gk, gv, go, gi, gf, small = layer_call(
        tokens, out_grad, gains, w_query, w_key, w_value, w_output, w_inner, w_outer, relb, table, doc_lengths, heads
    )
    me = lax.axis_index("seq") * lax.axis_size("rows") + lax.axis_index("rows")
    cut = attn_gain.shape[0]
    gains = [lax.dynamic_slice_in_dim(small[8 * k : 8 * k + 6].reshape(-1), me * cut, cut) for k in range(2)]
    return act, dx, gq, gk, gv, go, gi, gf, gains[0], gains[1], small[16 : 16 + n_bins, :heads]


def solution(mesh):
    split = P(("seq", "rows"), None)
    rows = P("rows", "seq", None)
    in_specs = (rows, P("rows"), P()) + (split,) * 6 + (P(("seq", "rows")),) * 2 + (P(), rows)
    out_specs = (rows, rows) + (split,) * 6 + (P(("seq", "rows")),) * 2 + (P(),)
    shape = (mesh.shape["seq"], mesh.shape["rows"])
    program = fast if shape == (NX, NZ * NY * NC) else local
    return jax.shard_map(program, mesh=mesh, in_specs=in_specs, out_specs=out_specs, check_vma=False)
```

```python
import functools

import jax
import jax.numpy as jnp
from jax import lax
from jax.experimental import pallas as pl
from jax.experimental.pallas import tpu as pltpu
from jax.sharding import PartitionSpec as P

MB = 2


EPS = 1e-06
NEG = -1000000000.0
HIGH = lax.Precision.HIGHEST


def normed(h, gain):
    return h * lax.rsqrt(jnp.mean(h * h, axis=-1, keepdims=True) + EPS) * gain


def fetch(shards):
    return (
        lax.all_gather(shards[0], ("seq", "rows"), axis=0, tiled=True),
        lax.all_gather(shards[1], ("seq", "rows"), axis=0, tiled=True),
        lax.all_gather(shards[2], ("seq", "rows"), axis=0, tiled=True),
        lax.all_gather(shards[3], ("seq", "rows"), axis=0, tiled=True),
        lax.all_gather(shards[4], ("seq", "rows"), axis=0, tiled=True),
        lax.all_gather(shards[5], ("seq", "rows"), axis=0, tiled=True),
        lax.all_gather(shards[6], ("seq", "rows"), axis=0, tiled=True),
        lax.all_gather(shards[7], ("seq", "rows"), axis=0, tiled=True),
    )


def local(
    tokens,
    doc_lengths,
    rel_buckets,
    w_query,
    w_key,
    w_value,
    w_output,
    w_inner,
    w_outer,
    attn_gain,
    ffn_gain,
    bias_table,
    out_grad,
):
    f32 = jnp.float32
    bf16 = jnp.bfloat16
    rows_dev, span, width = tokens.shape
    n_bins, heads = bias_table.shape
    head_dim = width // heads
    seq_count = lax.axis_size("seq")
    seq_place = lax.axis_index("seq")
    total = span * seq_count
    q_start = seq_place * span
    per = rows_dev // MB
    flat_rows = per * span
    shards = (w_query, w_key, w_value, w_output, w_inner, w_outer, attn_gain, ffn_gain)
    table = bias_table.astype(f32)
    k_pos = jnp.arange(total, dtype=jnp.int32)
    onehot = (rel_buckets[:, None] == jnp.arange(n_bins, dtype=jnp.int32)[None, :]).astype(f32)
    rel_bias = jnp.dot(onehot, table, precision=HIGH)
    spread = jnp.concatenate([rel_bias.T, jnp.zeros((heads, 1), f32)], axis=1)
    tiled = jnp.tile(spread, (1, total))
    full_bias = tiled[:, : total * (2 * total - 1)].reshape(heads, total, 2 * total - 1)[
        :, :, total - 1 :
    ]
    bias = lax.dynamic_slice_in_dim(full_bias, q_start, span, 1)
    ff_width = w_inner.shape[1]
    grad_wq = jnp.zeros((width, width), f32)
    grad_wk = jnp.zeros((width, width), f32)
    grad_wv = jnp.zeros((width, width), f32)
    grad_wo = jnp.zeros((width, width), f32)
    grad_wi = jnp.zeros((width, ff_width), f32)
    grad_wf = jnp.zeros((ff_width, width), f32)
    grad_g1 = jnp.zeros((width,), f32)
    grad_g2 = jnp.zeros((width,), f32)
    grad_bias = jnp.zeros((heads, span, total), f32)
    outputs = []
    input_grads = []
    for batch in range(MB):
        whole = fetch(shards)
        wq, wk, wv, wo, wi, wf, gain_one, gain_two = whole
        g1 = gain_one.astype(f32)
        g2 = gain_two.astype(f32)
        first = batch * per
        xflat = tokens[first : first + per].astype(f32).reshape(flat_rows, width)
        lens = doc_lengths[first : first + per]
        upstream = out_grad[first : first + per].reshape(flat_rows, width)
        n1 = normed(xflat, g1).astype(bf16)
        query = jnp.dot(n1, wq, preferred_element_type=f32).astype(bf16)
        key_local = jnp.dot(n1, wk, preferred_element_type=f32).astype(bf16)
        value_local = jnp.dot(n1, wv, preferred_element_type=f32).astype(bf16)
        keys_all, values_all = (
            lax.all_gather(key_local.reshape(per, span, width), "seq", axis=1, tiled=True),
            lax.all_gather(value_local.reshape(per, span, width), "seq", axis=1, tiled=True),
        )
        q4 = query.reshape(per, span, heads, head_dim)
        k4 = keys_all.reshape(per, total, heads, head_dim)
        v4 = values_all.reshape(per, total, heads, head_dim)
        valid = k_pos[None, :] < lens[:, None]

        def scores():
            raw = jnp.einsum("bqhd,bkhd->bhqk", q4, k4, preferred_element_type=f32) + bias[None]
            return jnp.where(valid[:, None, None, :], raw, NEG)

        first_scores = scores()
        top = jnp.max(first_scores, axis=-1, keepdims=True)
        expo = jnp.exp(first_scores - top)
        denom = jnp.sum(expo, axis=-1, keepdims=True)
        probs_low = (expo / denom).astype(bf16)
        mixed = jnp.einsum("bhqk,bkhd->bqhd", probs_low, v4, preferred_element_type=f32)
        mixed = mixed.reshape(flat_rows, width).astype(bf16)
        h1 = xflat + jnp.dot(mixed, wo, preferred_element_type=f32)
        n2 = normed(h1, g2).astype(bf16)
        inner = jnp.dot(n2, wi, preferred_element_type=f32)
        act_full, gelu_pull = jax.vjp(jax.nn.gelu, inner)
        act = act_full.astype(bf16)
        result = h1 + jnp.dot(act, wf, preferred_element_type=f32)
        outputs.append(result.astype(bf16).reshape(per, span, width))
        grad_wf = grad_wf + jnp.einsum("tf,td->fd", act, upstream, preferred_element_type=f32)
        d_act = jnp.einsum("td,fd->tf", upstream, wf, preferred_element_type=f32)
        d_inner = gelu_pull(d_act)[0].astype(bf16)
        grad_wi = grad_wi + jnp.einsum("td,tf->df", n2, d_inner, preferred_element_type=f32)
        d_n2 = jnp.einsum("tf,df->td", d_inner, wi, preferred_element_type=f32)
        norm_pull = jax.vjp(normed, h1, g2)[1]
        dh_part, dg_two = norm_pull(d_n2)
        grad_g2 = grad_g2 + dg_two
        dh1 = upstream.astype(f32) + dh_part
        d_attn = dh1.astype(bf16)
        grad_wo = grad_wo + jnp.einsum("td,te->de", mixed, d_attn, preferred_element_type=f32)
        d_mixed = jnp.einsum("te,de->td", d_attn, wo, preferred_element_type=f32).astype(bf16)
        dm4 = d_mixed.reshape(per, span, heads, head_dim)
        probs = jnp.exp(scores() - top) / denom
        d_probs = jnp.einsum("bqhd,bkhd->bhqk", dm4, v4, preferred_element_type=f32)
        value_terms = jnp.einsum("bhqk,bqhd->bkhd", probs_low, dm4, preferred_element_type=f32)
        delta = jnp.sum(probs * d_probs, axis=-1, keepdims=True)
        d_scores = (probs * (d_probs - delta)).astype(bf16)
        grad_bias = grad_bias + jnp.sum(d_scores.astype(f32), axis=0)
        d_query = jnp.einsum("bhqk,bkhd->bqhd", d_scores, k4, preferred_element_type=f32)
        d_query = d_query.reshape(flat_rows, width).astype(bf16)
        key_terms = jnp.einsum("bhqk,bqhd->bkhd", d_scores, q4, preferred_element_type=f32)
        key_share, value_share = (
            lax.psum_scatter(
                key_terms.reshape(per, total, width), "seq", scatter_dimension=1, tiled=True
            ),
            lax.psum_scatter(
                value_terms.reshape(per, total, width), "seq", scatter_dimension=1, tiled=True
            ),
        )
        d_key = key_share.reshape(flat_rows, width).astype(bf16)
        d_value = value_share.reshape(flat_rows, width).astype(bf16)
        grad_wq = grad_wq + jnp.einsum("td,te->de", n1, d_query, preferred_element_type=f32)
        grad_wk = grad_wk + jnp.einsum("td,te->de", n1, d_key, preferred_element_type=f32)
        grad_wv = grad_wv + jnp.einsum("td,te->de", n1, d_value, preferred_element_type=f32)
        d_n1 = jnp.einsum("te,de->td", d_query, wq, preferred_element_type=f32)
        d_n1 = d_n1 + jnp.einsum("te,de->td", d_key, wk, preferred_element_type=f32)
        d_n1 = d_n1 + jnp.einsum("te,de->td", d_value, wv, preferred_element_type=f32)
        first_pull = jax.vjp(normed, xflat, g1)[1]
        dx_part, dg_one = first_pull(d_n1)
        grad_g1 = grad_g1 + dg_one
        input_grads.append((dh1 + dx_part).reshape(per, span, width))
    owned = (
        lax.psum_scatter(grad_wq, ("seq", "rows"), scatter_dimension=0, tiled=True),
        lax.psum_scatter(grad_wk, ("seq", "rows"), scatter_dimension=0, tiled=True),
        lax.psum_scatter(grad_wv, ("seq", "rows"), scatter_dimension=0, tiled=True),
        lax.psum_scatter(grad_wo, ("seq", "rows"), scatter_dimension=0, tiled=True),
        lax.psum_scatter(grad_wi, ("seq", "rows"), scatter_dimension=0, tiled=True),
        lax.psum_scatter(grad_wf, ("seq", "rows"), scatter_dimension=0, tiled=True),
        lax.psum_scatter(grad_g1, ("seq", "rows"), scatter_dimension=0, tiled=True),
        lax.psum_scatter(grad_g2, ("seq", "rows"), scatter_dimension=0, tiled=True),
    )
    grad_full = lax.dynamic_update_slice_in_dim(
        jnp.zeros((heads, total, total), f32), grad_bias, q_start, 1
    )
    widened = jnp.pad(grad_full, ((0, 0), (0, 0), (total - 1, 0)))
    folded = jnp.pad(widened.reshape(heads, total * (2 * total - 1)), ((0, 0), (0, total)))
    rel_grad = jnp.sum(folded.reshape(heads, total, 2 * total), axis=1)[:, : 2 * total - 1]
    table_local = jnp.dot(onehot.T, rel_grad.T, precision=HIGH)
    table_grad = lax.psum(table_local, ("seq", "rows"))
    result_rows = jnp.concatenate(outputs, axis=0)
    grad_rows = jnp.concatenate(input_grads, axis=0)
    return (
        result_rows,
        grad_rows,
        owned[0],
        owned[1],
        owned[2],
        owned[3],
        owned[4],
        owned[5],
        owned[6],
        owned[7],
        table_grad,
    )


MESH_ID = pl.DeviceIdType.MESH
HBM = pl.BlockSpec(memory_space=pl.ANY)
VMEM = pl.BlockSpec(memory_space=pltpu.VMEM)
SMEM = pl.BlockSpec(memory_space=pltpu.SMEM)
BF = jnp.bfloat16
F32 = jnp.float32
NX, NZ, NY, NC = 2, 4, 2, 2


def rcopy(src, dst, send, recv, to):
    return pltpu.make_async_remote_copy(
        src_ref=src, dst_ref=dst, send_sem=send, recv_sem=recv, device_id=to, device_id_type=MESH_ID
    )


class Place:
    def __init__(self):
        self.x = lax.axis_index("seq")
        r = lax.axis_index("rows")
        self.c = lax.rem(r, 2)
        self.y = lax.rem(r // 2, 2)
        self.z = r // 4
        self.core = self.at(self.x, self.y, self.z, 1 - self.c)
        self.xn = self.at(1 - self.x, self.y, self.z, self.c)
        self.yn = self.at(self.x, 1 - self.y, self.z, self.c)
        self.zp = [None] + [self.at(self.x, self.y, self.zz(j), self.c) for j in range(1, NZ)]

    def at(self, x, y, z, c):
        return (x, z * 4 + y * 2 + c)

    def zz(self, j):
        return lax.rem(self.z + j, NZ)

    def barrier(self):
        sem = pltpu.get_barrier_semaphore()
        peers = [self.core, self.xn, self.yn] + self.zp[1:]
        for p in peers:
            pl.semaphore_signal(sem, inc=1, device_id=p, device_id_type=MESH_ID)
        pl.semaphore_wait(sem, len(peers))


class GatherXZY:
    def __init__(self, me, w, ss, rr, dd):
        self.me, self.w, self.ss, self.rr, self.dd = me, w, ss, rr, dd
        self.nh = w.shape[-1] // 2

    def ref(self, x, z, y, c):
        cols = pl.ds(pl.multiple_of(c * self.nh, 128), self.nh)
        return self.w.at[x, z, y, :, cols]

    def pair(self, z, y, c):
        cols = pl.ds(pl.multiple_of(c * self.nh, 128), self.nh)
        return self.w.at[:, z, y, :, cols]

    def send(self, ref, s, recv, to):
        rcopy(ref, ref, self.ss.at[s], recv, to).start()

    def got(self, ref, recv):
        rcopy(ref, ref, self.ss.at[0], recv, self.me.core).wait_recv()

    def start(self):
        m = self.me
        self.send(self.ref(m.x, m.z, m.y, m.c), 0, self.rr.at[0], m.xn)

    def step_x(self):
        m = self.me
        self.got(self.ref(1 - m.x, m.z, m.y, m.c), self.rr.at[0])
        p = self.pair(m.z, m.y, m.c)
        for j in range(1, NZ):
            self.send(p, j, self.rr.at[NZ - j], m.zp[j])
        self.send(p, 4, self.rr.at[4], m.yn)
        self.send(p, 8, self.dd.at[0], m.core)

    def step_z(self, j):
        m = self.me
        p = self.pair(m.zz(j), m.y, m.c)
        self.got(p, self.rr.at[j])
        self.send(p, 4 + j, self.rr.at[4 + j], m.yn)
        self.send(p, 8 + j, self.dd.at[j], m.core)

    def step_y(self, j):
        m = self.me
        p = self.pair(m.zz(j), 1 - m.y, m.c)
        self.got(p, self.rr.at[4 + j])
        self.send(p, 12 + j, self.dd.at[4 + j], m.core)

    def done(self):
        m = self.me
        for j in range(NZ):
            self.got(self.pair(m.zz(j), m.y, 1 - m.c), self.dd.at[j])
        for j in range(NZ):
            self.got(self.pair(m.zz(j), 1 - m.y, 1 - m.c), self.dd.at[4 + j])

    def sent(self):
        m = self.me
        one = self.ref(m.x, m.z, m.y, m.c)
        rcopy(one, one, self.ss.at[0], self.rr.at[0], m.core).wait_send()
        p = self.pair(m.z, m.y, m.c)
        for s in range(1, 16):
            rcopy(p, p, self.ss.at[s], self.rr.at[0], m.core).wait_send()


class GatherZYX:
    def __init__(self, me, w, ss, rr, dd):
        self.me, self.w, self.ss, self.rr, self.dd = me, w, ss, rr, dd

    def send(self, ref, s, recv, to):
        rcopy(ref, ref, self.ss.at[s], recv, to).start()

    def got(self, ref, recv):
        rcopy(ref, ref, self.ss.at[0], recv, self.me.core).wait_recv()

    def start(self):
        m = self.me
        own = self.w.at[m.x, m.z, m.y, m.c]
        for j in range(1, NZ):
            self.send(own, j - 1, self.rr.at[NZ - j - 1], m.zp[j])
        self.send(own, 3, self.rr.at[3], m.yn)

    def step_z(self, j):
        m = self.me
        b = self.w.at[m.x, m.zz(j), m.y, m.c]
        self.got(b, self.rr.at[j - 1])
        self.send(b, 5 + j, self.rr.at[3 + j], m.yn)

    def step_y(self, j):
        m = self.me
        self.got(self.w.at[m.x, m.zz(j), 1 - m.y, m.c], self.rr.at[3 + j])
        p = self.w.at[m.x, m.zz(j), :, m.c]
        self.send(p, 4 if j == 0 else 8 + j, self.rr.at[7 + j], m.xn)
        self.send(p, 5 if j == 0 else 11 + j, self.dd.at[j], m.core)

    def step_x(self, j):
        m = self.me
        p = self.w.at[1 - m.x, m.zz(j), :, m.c]
        self.got(p, self.rr.at[7 + j])
        self.send(p, 15 + j, self.dd.at[4 + j], m.core)

    def done_near(self):
        m = self.me
        for j in range(NZ):
            self.got(self.w.at[m.x, m.zz(j), :, 1 - m.c], self.dd.at[j])

    def done_far(self):
        m = self.me
        for j in range(NZ):
            self.got(self.w.at[1 - m.x, m.zz(j), :, 1 - m.c], self.dd.at[4 + j])

    def sent(self):
        m = self.me
        one = self.w.at[m.x, m.z, m.y, m.c]
        p = self.w.at[m.x, m.z, :, m.c]
        for s in range(19):
            r = one if s in (0, 1, 2, 3, 6, 7, 8) else p
            rcopy(r, r, self.ss.at[s], self.rr.at[0], m.core).wait_send()


def own_block(me, mine, theirs, w, nh):
    cols = pl.ds(pl.multiple_of(me.c * nh, 128), nh)
    a = mine[...].astype(F32)[:24]
    b = theirs[...].astype(F32)[:24]
    first = jnp.where(me.c == 0, a, b)
    second = jnp.where(me.c == 0, b, a)
    w[me.x, me.z, me.y, :, cols] = jnp.concatenate([first, second], axis=0).astype(BF)


class Piece:
    def __init__(self, index, rows, first):
        self.index, self.slot, self.rows = index, index % 2, rows
        cut = rows // 2 if rows // 2 % 16 == 0 else rows // 2 + 8
        self.subs = ((0, cut, first[0]), (cut, rows - cut, first[1]))


def acc_rows(x, y, z, lo, n):
    return pl.ds(pl.multiple_of(((x * NY + y) * NZ + z) * 192 + lo, 8), n)


class Reduce:
    def __init__(self, me, acc, a1, a2, a3, cs, cr, s1s, s1r, s2s, s2r, s3s, s3r, fin, finr, keep, sems):
        self.me = me
        self.acc, self.a1, self.a2, self.a3, self.cs, self.cr = acc, a1, a2, a3, cs, cr
        self.s1s, self.s1r, self.s2s, self.s2r, self.s3s, self.s3r = s1s, s1r, s2s, s2r, s3s, s3r
        self.fin, self.finr = fin, finr
        self.keep = keep
        (self.c_s, self.c_r, self.a_s, self.a_r, self.b_s, self.b_r, self.z_s, self.z_r, self.f_s, self.f_r) = sems

    def near(self, axis):
        return self.me.xn if axis == "x" else self.me.yn

    def core_copy(self, p):
        s, n = p.slot, p.rows
        return rcopy(
            self.cs.at[:, :, :, 0:n], self.cr.at[s, :, :, :, 0:n], self.c_s.at[s], self.c_r.at[s], self.me.core
        )

    def one_copy(self, p, k):
        s, (_, n, axis) = p.slot, p.subs[k]
        return rcopy(
            self.s1s.at[k, :, :, 0:n], self.s1r.at[s, k, :, :, 0:n], self.a_s.at[s, k], self.a_r.at[s, k], self.near(axis)
        )

    def two_copy(self, p, k):
        s, (_, n, axis) = p.slot, p.subs[k]
        to = self.near("y" if axis == "x" else "x")
        return rcopy(self.s2s.at[k, :, 0:n], self.s2r.at[s, k, :, 0:n], self.b_s.at[s, k], self.b_r.at[s, k], to)

    def z_copy(self, p, j):
        s, n = p.slot, p.rows
        return rcopy(
            self.s3s.at[j, 0:n], self.s3r.at[s, NZ - j, 0:n], self.z_s.at[s, j], self.z_r.at[s, NZ - j], self.me.zp[j]
        )

    def fin_copy(self, p):
        i, n = p.index, p.rows // 2
        return rcopy(
            self.fin.at[i, 0:n], self.finr.at[i, 0:n], self.f_s.at[i], self.f_r.at[i], self.me.core
        )

    def send_core(self, p):
        self.core_copy(p).start()

    def h1(self, p, old):
        me, s, n = self.me, p.slot, p.rows
        self.core_copy(p).wait_recv()
        for k, (lo, n, axis) in enumerate(p.subs):
            if old is not None:
                self.one_copy(old, k).wait_send()
            rows = pl.ds(lo, n)

            def body(q, carry):
                a, zq = q // NZ, lax.rem(q, NZ)
                if axis == "x":
                    keep, away = (me.x, a, zq, rows), (1 - me.x, a, zq, rows)
                else:
                    keep, away = (a, me.y, zq, rows), (a, 1 - me.y, zq, rows)
                held = [self.acc[acc_rows(*at[:3], lo, n), :] for at in (keep, away)]
                self.a1[k, a, zq, 0:n] = held[0] + self.cr[(s,) + keep].astype(F32)
                self.s1s[k, a, zq, 0:n] = (held[1] + self.cr[(s,) + away].astype(F32)).astype(BF)
                return carry

            lax.fori_loop(0, 2 * NZ, body, 0)
            self.one_copy(p, k).start()

    def h2(self, p, old):
        me, s = self.me, p.slot
        for k, (lo, n, axis) in enumerate(p.subs):
            self.one_copy(p, k).wait_recv()
            if old is not None:
                self.two_copy(old, k).wait_send()
            b = me.y if axis == "x" else me.x

            def body(zq, carry):
                self.a2[k, zq, 0:n] = self.a1[k, b, zq, 0:n] + self.s1r[s, k, b, zq, 0:n].astype(F32)
                self.s2s[k, zq, 0:n] = (
                    self.a1[k, 1 - b, zq, 0:n] + self.s1r[s, k, 1 - b, zq, 0:n].astype(F32)
                ).astype(BF)
                return carry

            lax.fori_loop(0, NZ, body, 0)
            self.two_copy(p, k).start()

    def h3(self, p, old):
        me, s = self.me, p.slot
        for k in range(2):
            self.two_copy(p, k).wait_recv()
        for j in range(1, NZ):
            if old is not None:
                self.z_copy(old, j).wait_send()
        for k, (lo, n, _) in enumerate(p.subs):
            rows = pl.ds(lo, n)
            for j in range(NZ):
                zq = me.zz(j)
                v = self.a2[k, zq, 0:n] + self.s2r[s, k, zq, 0:n].astype(F32)
                if j == 0:
                    self.a3[rows] = v
                else:
                    self.s3s[j, rows] = v.astype(BF)
        for j in range(1, NZ):
            self.z_copy(p, j).start()

    def h4(self, p):
        me, s, n, i = self.me, p.slot, p.rows, p.index
        for j in range(1, NZ):
            self.z_copy(p, NZ - j).wait_recv()
        total = self.a3[0:n]
        for j in range(1, NZ):
            total = total + self.s3r[s, j, 0:n].astype(F32)
        if p.groups is None:
            a, b = total[0 : n // 2], total[n // 2 :]
        else:
            a, b = (
                jnp.concatenate([total[48 * g + 24 * k : 48 * g + 24 * k + 24] for g in range(p.groups)], axis=0)
                for k in range(NC)
            )
        self.fin[i, 0 : n // 2] = jnp.where(me.c == 0, b, a)
        self.keep(p, jnp.where(me.c == 0, a, b), me.c)
        self.fin_copy(p).start()


def norm_back(h, gain, up):
    r = lax.rsqrt(jnp.mean(h * h, axis=-1, keepdims=True) + EPS)
    hr = h * r
    w = up * gain
    dgain = jnp.sum(up * hr, axis=0, keepdims=True)
    return r * (w - hr * jnp.mean(w * hr, axis=-1, keepdims=True)), dgain


def layer_kernel(
    tok, gin, gains, wq, wk, wv, wo, wi, pd, relb, table, lens,
    act_o, dx_o, gq_o, gk_o, gv_o, go_o, gi_o, gf_o, sm_o,
    WA, WB, WD, X, G, N2, QKV, O, H1, ACT, DU, T, M, MACC, LSE, R, RG,
    ACC, A1, A2, A3, CS, CR, S1S, S1R, S2S, S2R, S3S, S3R, FIN, FINR, SM, SMR, ZB, DG,
    ts, tr, tl, gs, gr, gl, es, er, as_, ar, ad, bs, br, bd, ds_, dr, dd, ys, yr, yl, xs_, xr, xl,
    c_s, c_r, a_s, a_r, b_s, b_r, z_s, z_r, f_s, f_r, ms, mr,
):
    me = Place()
    x, y, z, c = me.x, me.y, me.z, me.c
    mine, span, width = X.shape[0], X.shape[2], X.shape[3]
    length = 2 * span
    flat = mine * length
    ff = DU.shape[1]
    na, nb = WA.shape[4] // 2, WB.shape[4] // 2
    PA, PB = DU.at[pl.ds(32 * c, 32), 0:na], DU.at[pl.ds(64 + 32 * c, 32), 0:nb]
    RA, RB = DU.at[128:160, 0:na], DU.at[160:192, 0:nb]
    hd = 64
    YB = N2
    pairs = width // hd // 2
    gath_a = GatherXZY(me, WA, as_, ar, ad)
    gath_b = GatherXZY(me, WB, bs, br, bd)
    gath_d = GatherZYX(me, WD, ds_, dr, dd)

    def pack(first, n, parts):
        filled = [
            jnp.concatenate([p[...].astype(F32), jnp.zeros((32 - p.shape[0], p.shape[1]), F32)], axis=0) for p in parts
        ]
        filled = jnp.concatenate(filled, axis=1).astype(BF)
        for half in range(2):
            DU[first + 32 * half : first + 32 * half + 32, 0:n] = filled[:, n * half : n * half + n]

    pack(0, na, (gains, wq, wk, wv))
    me.barrier()
    ea = rcopy(DU.at[pl.ds(32 * (1 - c), 32), 0:na], RA, es.at[0], er.at[0], me.core)
    eb = rcopy(DU.at[pl.ds(64 + 32 * (1 - c), 32), 0:nb], RB, es.at[1], er.at[1], me.core)
    ea.start()
    pack(64, nb, (wo, wi))
    eb.start()
    tok_r = [rcopy(tok.at[2 * (1 - x) + i], X.at[i, x], ts.at[i], tr.at[i], me.xn) for i in range(mine)]
    tok_in = [rcopy(X.at[i, 1 - x], X.at[i, 1 - x], ts.at[i], tr.at[i], me.xn) for i in range(mine)]
    tok_l = [pltpu.make_async_copy(tok.at[2 * x + i], X.at[i, x], tl.at[i]) for i in range(mine)]
    g_r = rcopy(gin.at[pl.ds(2 * (1 - x), 2)], G.at[:, x], gs, gr, me.xn)
    g_in = rcopy(G.at[:, 1 - x], G.at[:, 1 - x], gs, gr, me.xn)
    g_l = pltpu.make_async_copy(gin.at[pl.ds(2 * x, 2)], G.at[:, x], gl)
    ea.wait_recv()
    own_block(me, PA, RA, WA, na)
    gath_a.start()
    for i in range(mine):
        tok_r[i].start()
        tok_l[i].start()
    g_l.start()
    eb.wait_recv()
    own_block(me, PB, RB, WB, nb)
    WD[x, z, y, c] = pd[...]
    cols = relb.shape[1]
    kinds = table.shape[0]
    hot = (lax.broadcasted_iota(jnp.int32, (kinds, cols), 0) == relb[...]).astype(BF)
    R[...] = lax.dot_general(table[...], hot, (((0,), (0,)), ((), ())), preferred_element_type=F32)[0:16]
    gath_a.step_x()
    gath_b.start()
    gath_d.start()
    for j in range(1, NZ):
        gath_a.step_z(j)
    gath_b.step_x()
    for j in range(NZ):
        gath_a.step_y(j)
    gath_d.step_y(0)
    g_r.start()
    gath_a.done()

    def gain_row(k):
        return jnp.transpose(WA[:, :, :, :, 128 * k : 128 * k + 128].reshape(width, 128).astype(F32))[0:1, :]

    gain1 = gain_row(0)

    def row_slice(i):
        return pl.ds(pl.multiple_of(i * length, length), length)

    def first_norm(i):
        for half in range(2):
            xf = X[i, half].astype(F32)
            scale = lax.rsqrt(jnp.mean(xf * xf, axis=-1, keepdims=True) + EPS)
            N2[i, half] = (xf * scale * gain1).astype(BF)

    for i in range(mine):
        tok_l[i].wait()
        tok_in[i].wait_recv()
        first_norm(i)
        for n in range(3):
            w = WA[:, :, :, :, 256 + n * width : 256 + (n + 1) * width].reshape(width, width)
            QKV[row_slice(i), n * width : (n + 1) * width] = jnp.dot(
                N2[i].reshape(length, width), w, preferred_element_type=F32
            ).astype(BF)
    low = lax.broadcasted_iota(jnp.int32, (1, 128), 1) < hd
    lane = lax.broadcasted_iota(jnp.int32, (1, 128), 1)
    kpos = lax.broadcasted_iota(jnp.int32, (length, 128), 0)
    blocks = length // 128

    def strips(p):
        for h in range(2):
            row = jnp.broadcast_to(R[pl.ds(2 * p + h, 1), :], (128, cols))
            M[h] = pltpu.roll(row, cols - 127, 1, stride=1, stride_axis=0)[:, : M.shape[2]]

    def bias_of(h):
        return jnp.concatenate(
            [M[h, :, 128 * (blocks - 1 - a) : 128 * (blocks - 1 - a) + length] for a in range(blocks)], axis=0
        )

    own = (low, jnp.logical_not(low))
    spare = (hd, 0)
    ones = [(lane == spare[h]).astype(F32).astype(BF) for h in range(2)]
    none = jnp.zeros((), BF)

    def masked_keys(h, k, count):
        pad = jnp.where((lane == spare[h]) & (kpos >= count), NEG, 0.0).astype(BF)
        return jnp.where(own[h], k, pad)

    def lanes(n, p):
        return pl.ds(pl.multiple_of(n * width + p * 128, 128), 128)

    nt = (((1,), (1,)), ((), ()))
    tn = (((0,), (0,)), ((), ()))

    def mm(a, b, dims):
        return lax.dot_general(a, b, dims, preferred_element_type=F32)

    comm = {
        0: (lambda: gath_b.step_z(1), lambda: gath_d.step_z(1)),
        1: (lambda: gath_b.step_z(2), lambda: gath_d.step_z(2)),
        2: (lambda: gath_b.step_z(3), lambda: gath_d.step_z(3)),
        3: (lambda: gath_b.step_y(0), lambda: gath_d.step_y(1)),
        5: (lambda: gath_b.step_y(1), lambda: gath_d.step_y(2)),
        7: (lambda: gath_b.step_y(2), lambda: gath_d.step_y(3)),
        8: (lambda: gath_b.step_y(3),),
        9: (lambda: gath_d.step_x(0),),
        10: (lambda: gath_d.step_x(1),),
        11: (lambda: gath_d.step_x(2),),
    }

    def attend(t, carry):
        p, i = t // mine, lax.rem(t, mine)
        pl.when(i == 0)(lambda: strips(p))
        rows = row_slice(i)
        q, k, v = QKV[rows, lanes(0, p)], QKV[rows, lanes(1, p)], QKV[rows, lanes(2, p)]
        outs = []
        for h in range(2):
            s = mm(jnp.where(own[h], q, ones[h]), masked_keys(h, k, lens[2 * x + i]), nt) + bias_of(h)
            top = jnp.max(s, axis=-1, keepdims=True)
            e = jnp.exp(s - top)
            total = jnp.sum(e, axis=-1, keepdims=True)
            LSE[rows, :] = jnp.where(lane == 2 * p + h, top + jnp.log(total), LSE[rows, :])
            outs.append(jnp.dot((e * (1.0 / total)).astype(BF), v, preferred_element_type=F32))
        O[i, :, :, lanes(0, p)] = jnp.where(low, outs[0], outs[1]).astype(BF).reshape(2, span, 128)
        for at, steps in comm.items():
            @pl.when(t == at)
            def _():
                for step in steps:
                    step()
        return carry

    LSE[...] = jnp.zeros_like(LSE)
    lax.fori_loop(0, mine * pairs, attend, 0)
    ea.wait_send()
    eb.wait_send()
    gath_d.step_x(3)
    gath_b.done()
    gath_d.done_near()
    g_l.wait()
    g_in.wait_recv()

    gain2 = gain_row(1)
    DG[...] = jnp.zeros_like(DG)
    c0, c1 = 0.7978845608028654, 0.044715

    def dn_set(v):
        for n in range(width // 128):
            ACC[length * n : length * n + length, :] = v[:, 128 * n : 128 * n + 128]

    def dn_get(lo, n):
        return jnp.concatenate([ACC[length * k + lo : length * k + lo + n, :] for k in range(width // 128)], axis=1)

    def dn_add(v):
        for n in range(width // 128):
            at = slice(length * n, length * n + length)
            ACC[at, :] = ACC[at, :] + v[:, 128 * n : 128 * n + 128]

    wo_all = lambda: WB[:, :, :, :, 0:width].reshape(width, width)
    for i in range(mine):
        h1 = X[i].reshape(length, width).astype(F32) + jnp.dot(
            O[i].reshape(length, width), wo_all(), preferred_element_type=F32
        )
        H1[i] = h1.reshape(2, span, width)
        r = lax.rsqrt(jnp.mean(h1 * h1, axis=-1, keepdims=True) + EPS)
        N2[i] = (h1 * r * gain2).astype(BF).reshape(2, span, width)

    def chunk(n, carry):
        pl.when(n == 2)(gath_d.done_far)
        f = lax.rem(2 * x + n, 4)

        def one_row(i, carry):
            n2, g = N2[i].reshape(length, width), G[i].reshape(length, width)
            for part in range(3):
                fcols = pl.ds(pl.multiple_of(f * width + 256 * part, 256), 256)
                wcols = pl.ds(pl.multiple_of(width + f * width + 256 * part, 256), 256)
                wi_part = WB[:, :, :, :, wcols].reshape(width, 256)
                wf_part = WD[f // 2, pl.ds(2 * lax.rem(f, 2), 2)].reshape(width, width)[256 * part : 256 * part + 256]
                u = jnp.dot(n2, wi_part, preferred_element_type=F32)
                da = mm(g, wf_part, nt)
                sq = u * u
                t = jnp.tanh(u * (c0 + (c0 * c1) * sq))
                cdf = 0.5 + 0.5 * t
                ACT[row_slice(i), fcols] = (u * cdf).astype(BF)
                slope = cdf + (0.5 * u) * (1.0 - t * t) * (c0 + (3.0 * c0 * c1) * sq)
                DU[row_slice(i), fcols] = (da * slope).astype(BF)
            return carry

        return lax.fori_loop(0, mine, one_row, carry)

    lax.fori_loop(0, ff // width, chunk, 0)
    def keep(p, value, core):
        if p.groups is None:
            gf_o[:, pl.ds(pl.multiple_of(256 * p.part + 128 * core, 128), 128)] = value
            return
        for g in range(p.groups):
            if p.kind == "i":
                dst, base = gi_o, 1024 * p.part + 256 * g
            elif p.kind == "o":
                dst, base = go_o, 256 * g
            else:
                dst, base = (gq_o, gk_o, gv_o)[g], 256 * p.part
            dst[:, pl.ds(pl.multiple_of(base + 128 * core, 128), 128)] = value[24 * g : 24 * g + 24]

    red = Reduce(
        me, ACC, A1, A2, A3, CS, CR, S1S, S1R, S2S, S2R, S3S, S3R, FIN, FINR, keep, (c_s, c_r, a_s, a_r, b_s, b_r, z_s, z_r, f_s, f_r)
    )
    pieces = []
    kinds_of = [("f", 0), ("f", 1), ("f", 2), ("i", 0), ("i", 1), ("i", 2), ("o", 0), ("qkv", 0), ("qkv", 1), ("qkv", 2)]
    made_at = [0, 2, 4, 5, 6, 7, 8, 9, 13, 17]
    last = len(kinds_of)
    for n in range(last):
        kind, part = kinds_of[n]
        piece = Piece(n, 144 if kind in ("o", "qkv") else 192, ("x", "y") if n < last - 1 else ("x", "x"))
        piece.kind, piece.part = kind, part
        piece.groups = None if kind == "f" else piece.rows // 48
        pieces.append(piece)

    def stages(n):
        def at(k):
            return pieces[made_at.index(n - k)] if n - k in made_at else None

        def old(p):
            return pieces[p.index - 1] if p.index else None

        if at(4):
            red.h4(at(4))
        if at(3):
            red.h3(at(3), old(at(3)))
        if at(2):
            red.h2(at(2), old(at(2)))
        if at(1):
            red.h1(at(1), old(at(1)))
        if at(0):
            if old(at(0)):
                red.core_copy(old(at(0))).wait_send()
            produce(at(0))

    def split(res):
        a, b = res[:, 0:128], res[:, 128:256]
        return jnp.where(c == 0, a, b), jnp.where(c == 0, b, a).astype(BF)

    def outer_piece(j):

        def body(q, carry):
            xq, zh = q // 2, lax.rem(q, 2)
            lhs = ACT[:, pl.ds(pl.multiple_of(q * 768, 768), 768)]
            rhs = G[:, :, :, 256 * j : 256 * j + 256].reshape(flat, 256)
            own, other = split(mm(lhs, rhs, tn))
            for b in range(4):
                at = (xq, b % 2, 2 * zh + b // 2)
                ACC[acc_rows(*at, 0, 192), :] = own[192 * b : 192 * b + 192]
                CS[at] = other[192 * b : 192 * b + 192]
            return carry

        lax.fori_loop(0, 4, body, 0)

    def rows_piece(groups, rhs):
        def body(g, carry):
            own, other = split(jnp.dot(T[...], rhs(g), preferred_element_type=F32))
            at = pl.ds(pl.multiple_of(48 * g, 48), 48)
            for k in range(NX * NZ * NY):
                ACC[acc_rows(k // 8, k % 2, (k // 2) % 4, 48 * g, 48), :] = own[48 * k : 48 * k + 48]
                CS[k // 8, k % 2, (k // 2) % 4, at] = other[48 * k : 48 * k + 48]
            return carry

        lax.fori_loop(0, groups, body, 0)

    def produce(p):
        if p.kind == "f":
            outer_piece(p.part)
        elif p.kind == "i":
            rows_piece(4, lambda g: DU[:, pl.ds(pl.multiple_of(1024 * p.part + 256 * g, 256), 256)])
        elif p.kind == "o":
            T[...] = jnp.transpose(O[...].reshape(flat, width))
            rows_piece(3, lambda g: H1[:, :, :, pl.ds(pl.multiple_of(256 * g, 256), 256)].reshape(flat, 256).astype(BF))
        else:
            if p.part == 0:
                for i in range(mine):
                    y_out[i].wait_recv()
                    y_out[i].wait_send()
                    y_loc[i].wait()
                for i in range(mine):
                    first_norm(i)
                T[...] = jnp.transpose(N2[...].reshape(flat, width))
            rows_piece(3, lambda g: QKV[:, pl.ds(pl.multiple_of(g * width + 256 * p.part, 256), 256)])
        red.send_core(p)

    stages(0)
    T[...] = jnp.transpose(N2[...].reshape(flat, width))
    stages(1)

    def result(t, carry):
        i, f = t // 4, lax.rem(t, 4)
        a = ACT[row_slice(i), pl.ds(pl.multiple_of(f * width, width), width)]
        wf = WD[f // 2, pl.ds(2 * lax.rem(f, 2), 2)].reshape(width, width)
        out = jnp.dot(a, wf, preferred_element_type=F32)

        @pl.when(f == 0)
        def _():
            dn_set(H1[i].reshape(length, width) + out)

        @pl.when(f > 0)
        def _():
            dn_add(out)

        @pl.when(f == 3)
        def _():
            YB[i] = dn_get(0, length).astype(BF).reshape(2, span, width)

        return carry

    lax.fori_loop(0, 4 * mine, result, 0)
    y_out = [
        rcopy(YB.at[i, 1 - x], act_o.at[2 * (1 - x) + i], ys.at[i], yr.at[i], me.xn) for i in range(mine)
    ]
    y_loc = [pltpu.make_async_copy(YB.at[i, x], act_o.at[2 * x + i], yl.at[i]) for i in range(mine)]
    for i in range(mine):
        rcopy(YB.at[i, 1 - x], act_o.at[2 * x + i], ys.at[i], yr.at[i], me.xn).start()
        y_loc[i].start()

    stages(2)
    stages(3)

    def back(t, carry):
        i, f = t // 4, lax.rem(t, 4)
        du = DU[row_slice(i), pl.ds(pl.multiple_of(f * width, width), width)]
        wi_part = WB[:, :, :, :, pl.ds(pl.multiple_of((f + 1) * width, width), width)].reshape(width, width)
        out = mm(du, wi_part, nt)

        @pl.when(f == 0)
        def _():
            dn_set(out)

        @pl.when(f > 0)
        def _():
            dn_add(out)

        @pl.when(f == 3)
        def _():
            for half in range(2):
                dh, dgain = norm_back(H1[i, half], gain2, dn_get(span * half, span))
                DG[1:2, :] = DG[1:2, :] + dgain
                H1[i, half] = G[i, half].astype(F32) + dh

        return carry

    lax.fori_loop(0, 4 * mine, back, 0)

    stages(4)
    for i in range(mine):
        dab = H1[i].reshape(length, width).astype(BF)
        G[i] = mm(dab, wo_all(), nt).astype(BF).reshape(2, span, width)
    def attend_back(t, carry):
        p, i = t // mine, lax.rem(t, mine)

        @pl.when(i == 0)
        def _():
            strips(p)
            MACC[...] = jnp.zeros_like(MACC)

        rows = row_slice(i)
        q, k, v = QKV[rows, lanes(0, p)], QKV[rows, lanes(1, p)], QKV[rows, lanes(2, p)]
        do = G[i, :, :, lanes(0, p)].reshape(length, 128)
        prod = do.astype(F32) * O[i, :, :, lanes(0, p)].reshape(length, 128).astype(F32)
        dqs, dks, dvs = [], [], []
        for h in range(2):
            lse = jnp.sum(jnp.where(lane == 2 * p + h, LSE[rows, :], 0.0), axis=-1, keepdims=True)
            delta = jnp.sum(jnp.where(own[h], prod, 0.0), axis=-1, keepdims=True)
            s = mm(jnp.where(own[h], q, ones[h]), masked_keys(h, k, lens[2 * x + i]), nt) + bias_of(h)
            pr = jnp.exp(s - lse)
            ds = pr * (mm(jnp.where(own[h], do, none), v, nt) - delta)
            for a in range(blocks):
                at = 128 * (blocks - 1 - a)
                MACC[h, :, at : at + length] = MACC[h, :, at : at + length] + ds[128 * a : 128 * a + 128]
            low_p, low_ds = pr.astype(BF), ds.astype(BF)
            dqs.append(jnp.dot(low_ds, k, preferred_element_type=F32))
            dks.append(mm(low_ds, q, tn))
            dvs.append(mm(low_p, do, tn))
        for n, parts in enumerate((dqs, dks, dvs)):
            QKV[rows, lanes(n, p)] = jnp.where(low, parts[0], parts[1]).astype(BF)

        @pl.when(i == mine - 1)
        def _():
            for h in range(2):
                part = jnp.zeros((8, cols), F32)
                for a in range(16):
                    part = part + pltpu.roll(MACC[h, 8 * a : 8 * a + 8, :], (cols - 8 * a) % cols, 1)
                line = part[0:1]
                for a in range(1, 8):
                    line = line + pltpu.roll(part[a : a + 1], cols - a, 1)
                RG[pl.ds(2 * p + h, 1), :] = pltpu.roll(line, 127, 1)

        for n in range(mine * pairs):
            @pl.when(t == n)
            def _():
                stages(5 + n)

        return carry

    RG[...] = jnp.zeros_like(RG)
    MACC[...] = jnp.zeros_like(MACC)
    lax.fori_loop(0, mine * pairs, attend_back, 0)

    stages(17)
    stages(18)
    landing = lambda i: DU.at[pl.ds(i * span, span), 0:width]
    dx_r = [rcopy(X.at[i, 1 - x], landing(i), xs_.at[i], xr.at[i], me.xn) for i in range(mine)]
    dx_l = [pltpu.make_async_copy(H1.at[i, x], dx_o.at[2 * x + i], xl.at[i]) for i in range(mine)]
    dx_f = [pltpu.make_async_copy(H1.at[i, 1 - x], dx_o.at[2 * (1 - x) + i], xl.at[mine + i]) for i in range(mine)]
    for i in range(mine):
        for n in range(3):
            out = mm(
                QKV[row_slice(i), n * width : (n + 1) * width],
                WA[:, :, :, :, 256 + n * width : 256 + (n + 1) * width].reshape(width, width),
                nt,
            )
            (dn_set if n == 0 else dn_add)(out)
        for half in range(2):
            dh, dgain = norm_back(X[i, half].astype(F32), gain1, dn_get(span * half, span))
            DG[0:1, :] = DG[0:1, :] + dgain
            H1[i, half] = H1[i, half] + dh
        X[i, 1 - x] = H1[i, 1 - x].astype(BF)
        dx_r[i].start()
        dx_l[i].start()
        stages(19 + i)
    for n in range(width // 128):
        SM[0, n : n + 1, :] = DG[0:1, 128 * n : 128 * n + 128]
        SM[0, 8 + n : 9 + n, :] = DG[1:2, 128 * n : 128 * n + 128]
    rest = jnp.concatenate([RG[...], jnp.zeros((112, cols), F32)], axis=0)
    spread = jnp.zeros((kinds, 128), F32)
    for _ in range(3):
        part = rest.astype(BF)
        rest = rest - part.astype(F32)
        spread = spread + mm(hot, part, nt)
    SM[0, 16 : 16 + kinds, :] = spread
    sm_copies = [
        rcopy(SM.at[k], SMR.at[k], ms.at[k], mr.at[k], to) for k, to in enumerate((me.core, me.xn, me.yn))
    ]
    sm_copies[0].start()
    stages(21)
    for k in range(3):
        sm_copies[k].wait_recv()
        SM[k + 1] = SM[k] + SMR[k]
        if k < 2:
            sm_copies[k + 1].start()
    ZB[z] = SM[3]
    sm_z = [None] + [rcopy(SM.at[3], ZB.at[z], ms.at[2 + j], mr.at[6 - j], me.zp[j]) for j in range(1, NZ)]
    for j in range(1, NZ):
        sm_z[j].start()
    for i in range(mine):
        dx_r[i].wait_recv()
        H1[i, 1 - x] = DU[pl.ds(i * span, span), 0:width].astype(F32)
        dx_f[i].start()
    for p in pieces:
        red.fin_copy(p).wait_recv()
        keep(p, FINR[p.index, 0 : p.rows // 2], 1 - c)
    for j in range(1, NZ):
        rcopy(SM.at[3], ZB.at[me.zz(j)], ms.at[2 + j], mr.at[2 + j], me.zp[j]).wait_recv()
    sm_o[...] = ZB[0] + ZB[1] + ZB[2] + ZB[3]
    g_r.wait_send()
    for k in range(3):
        sm_copies[k].wait_send()
    for j in range(1, NZ):
        sm_z[j].wait_send()
    for g in (gath_a, gath_b, gath_d):
        g.sent()
    for i in range(mine):
        tok_r[i].wait_send()
        dx_r[i].wait_send()
        dx_l[i].wait()
        dx_f[i].wait()
    for p in pieces[-1:]:
        red.core_copy(p).wait_send()
        for k in range(2):
            red.one_copy(p, k).wait_send()
            red.two_copy(p, k).wait_send()
        for j in range(1, NZ):
            red.z_copy(p, j).wait_send()
    for p in pieces:
        red.fin_copy(p).wait_send()


def layer_call(tok, gin, gains, wq, wk, wv, wo, wi, pd, relb, table, lens, heads):
    rows_dev, span, width = tok.shape
    length = 2 * span
    mine = rows_dev // 2
    flat = mine * length
    dma = pltpu.SemaphoreType.DMA
    ff = wi.shape[1]
    na, nb = (gains.shape[1] + 3 * width) // 2, (width + ff) // 2
    count = width // 256 + ff // 1024 + 4
    wa = (NX, NZ, NY, 48, 2 * na)
    wb = (NX, NZ, NY, 48, 2 * nb)
    wd = (NX, NZ, NY, NC) + pd.shape
    xs = (mine, 2, span, width)
    block = (192, 128)
    bf = lambda *s: pltpu.VMEM(s, BF)
    f32 = lambda *s: pltpu.VMEM(s, F32)
    out = lambda *s: jax.ShapeDtypeStruct(s, F32)
    shard = wq.shape[0]
    return pl.pallas_call(
        layer_kernel,
        out_shape=[jax.ShapeDtypeStruct(tok.shape, BF), out(*tok.shape)]
        + [out(shard, width)] * 4 + [out(shard, ff), out(*pd.shape), out(48, 128)],
        in_specs=[HBM, HBM] + [VMEM] * 9 + [SMEM],
        out_specs=[HBM, HBM] + [VMEM] * 7,
        scratch_shapes=[
            bf(*wa), bf(*wb), bf(*wd), bf(*xs), bf(*xs), bf(*xs), bf(flat, 3 * width), bf(*xs), f32(*xs),
             bf(flat, ff), bf(flat, ff), bf(width, flat), f32(2, 128, 896), f32(2, 128, 1024),
            f32(flat, 128), f32(16, relb.shape[1]), f32(16, relb.shape[1]),
            f32(NX * NY * NZ * 192, 128), f32(2, 2, NZ, 96, 128), f32(2, NZ, 96, 128), f32(*block), bf(NX, NY, NZ, *block), bf(2, NX, NY, NZ, *block),
            bf(2, 2, NZ, 96, 128), bf(2, 2, 2, NZ, 96, 128), bf(2, NZ, 96, 128), bf(2, 2, NZ, 96, 128),
            bf(NZ, *block), bf(2, NZ, *block), f32(count, 96, 128), f32(count, 96, 128),
            f32(4, 48, 128), f32(3, 48, 128), f32(NZ, 48, 128), f32(8, width),
            dma((2,)), dma((2,)), dma((2,)), dma, dma, dma, dma((2,)), dma((2,)),
            dma((16,)), dma((8,)), dma((8,)), dma((16,)), dma((8,)), dma((8,)), dma((19,)), dma((11,)), dma((8,)),
            dma((2,)), dma((2,)), dma((2,)), dma((2,)), dma((2,)), dma((4,)),
            dma((2,)), dma((2,)), dma((2, 2)), dma((2, 2)), dma((2, 2)), dma((2, 2)), dma((2, NZ)), dma((2, NZ)),
            dma((count,)), dma((count,)), dma((6,)), dma((6,)),
        ],
        compiler_params=pltpu.CompilerParams(
            collective_id=0, has_side_effects=True, vmem_limit_bytes=VMEM_LIMIT
        ),
        name="layer",
    )(tok, gin, gains, wq, wk, wv, wo, wi, pd, relb, table, lens)


VMEM_LIMIT = 67_000_000


def fast(
    tokens, doc_lengths, rel_buckets, w_query, w_key, w_value, w_output, w_inner, w_outer,
    attn_gain, ffn_gain, bias_table, out_grad,
):
    n_bins, heads = bias_table.shape
    wide = lambda g: jnp.broadcast_to(g[:, None], (g.shape[0], 128))
    gains = jnp.concatenate([wide(attn_gain), wide(ffn_gain)], axis=1)
    relb = jnp.pad(rel_buckets, (0, 1))[None, :]
    table = jnp.pad(bias_table, ((0, 0), (0, 128 - heads)))
    act, dx, gq, gk, gv, go, gi, gf, small = layer_call(
        tokens, out_grad, gains, w_query, w_key, w_value, w_output, w_inner, w_outer, relb, table, doc_lengths, heads
    )
    me = lax.axis_index("seq") * lax.axis_size("rows") + lax.axis_index("rows")
    cut = attn_gain.shape[0]
    gains = [lax.dynamic_slice_in_dim(small[8 * k : 8 * k + 6].reshape(-1), me * cut, cut) for k in range(2)]
    return act, dx, gq, gk, gv, go, gi, gf, gains[0], gains[1], small[16 : 16 + n_bins, :heads]


def solution(mesh):
    split = P(("seq", "rows"), None)
    rows = P("rows", "seq", None)
    in_specs = (rows, P("rows"), P()) + (split,) * 6 + (P(("seq", "rows")),) * 2 + (P(), rows)
    out_specs = (rows, rows) + (split,) * 6 + (P(("seq", "rows")),) * 2 + (P(),)
    shape = (mesh.shape["seq"], mesh.shape["rows"])
    program = fast if shape == (NX, NZ * NY * NC) else local
    return jax.shard_map(program, mesh=mesh, in_specs=in_specs, out_specs=out_specs, check_vma=False)
```

```python
import functools

import jax
import jax.numpy as jnp
from jax import lax
from jax.experimental import pallas as pl
from jax.experimental.pallas import tpu as pltpu
from jax.sharding import PartitionSpec as P

MB = 2


EPS = 1e-06
NEG = -1000000000.0
HIGH = lax.Precision.HIGHEST


def normed(h, gain):
    return h * lax.rsqrt(jnp.mean(h * h, axis=-1, keepdims=True) + EPS) * gain


def fetch(shards):
    return (
        lax.all_gather(shards[0], ("seq", "rows"), axis=0, tiled=True),
        lax.all_gather(shards[1], ("seq", "rows"), axis=0, tiled=True),
        lax.all_gather(shards[2], ("seq", "rows"), axis=0, tiled=True),
        lax.all_gather(shards[3], ("seq", "rows"), axis=0, tiled=True),
        lax.all_gather(shards[4], ("seq", "rows"), axis=0, tiled=True),
        lax.all_gather(shards[5], ("seq", "rows"), axis=0, tiled=True),
        lax.all_gather(shards[6], ("seq", "rows"), axis=0, tiled=True),
        lax.all_gather(shards[7], ("seq", "rows"), axis=0, tiled=True),
    )


def local(
    tokens,
    doc_lengths,
    rel_buckets,
    w_query,
    w_key,
    w_value,
    w_output,
    w_inner,
    w_outer,
    attn_gain,
    ffn_gain,
    bias_table,
    out_grad,
):
    f32 = jnp.float32
    bf16 = jnp.bfloat16
    rows_dev, span, width = tokens.shape
    n_bins, heads = bias_table.shape
    head_dim = width // heads
    seq_count = lax.axis_size("seq")
    seq_place = lax.axis_index("seq")
    total = span * seq_count
    q_start = seq_place * span
    per = rows_dev // MB
    flat_rows = per * span
    shards = (w_query, w_key, w_value, w_output, w_inner, w_outer, attn_gain, ffn_gain)
    table = bias_table.astype(f32)
    k_pos = jnp.arange(total, dtype=jnp.int32)
    onehot = (rel_buckets[:, None] == jnp.arange(n_bins, dtype=jnp.int32)[None, :]).astype(f32)
    rel_bias = jnp.dot(onehot, table, precision=HIGH)
    spread = jnp.concatenate([rel_bias.T, jnp.zeros((heads, 1), f32)], axis=1)
    tiled = jnp.tile(spread, (1, total))
    full_bias = tiled[:, : total * (2 * total - 1)].reshape(heads, total, 2 * total - 1)[
        :, :, total - 1 :
    ]
    bias = lax.dynamic_slice_in_dim(full_bias, q_start, span, 1)
    ff_width = w_inner.shape[1]
    grad_wq = jnp.zeros((width, width), f32)
    grad_wk = jnp.zeros((width, width), f32)
    grad_wv = jnp.zeros((width, width), f32)
    grad_wo = jnp.zeros((width, width), f32)
    grad_wi = jnp.zeros((width, ff_width), f32)
    grad_wf = jnp.zeros((ff_width, width), f32)
    grad_g1 = jnp.zeros((width,), f32)
    grad_g2 = jnp.zeros((width,), f32)
    grad_bias = jnp.zeros((heads, span, total), f32)
    outputs = []
    input_grads = []
    for batch in range(MB):
        whole = fetch(shards)
        wq, wk, wv, wo, wi, wf, gain_one, gain_two = whole
        g1 = gain_one.astype(f32)
        g2 = gain_two.astype(f32)
        first = batch * per
        xflat = tokens[first : first + per].astype(f32).reshape(flat_rows, width)
        lens = doc_lengths[first : first + per]
        upstream = out_grad[first : first + per].reshape(flat_rows, width)
        n1 = normed(xflat, g1).astype(bf16)
        query = jnp.dot(n1, wq, preferred_element_type=f32).astype(bf16)
        key_local = jnp.dot(n1, wk, preferred_element_type=f32).astype(bf16)
        value_local = jnp.dot(n1, wv, preferred_element_type=f32).astype(bf16)
        keys_all, values_all = (
            lax.all_gather(key_local.reshape(per, span, width), "seq", axis=1, tiled=True),
            lax.all_gather(value_local.reshape(per, span, width), "seq", axis=1, tiled=True),
        )
        q4 = query.reshape(per, span, heads, head_dim)
        k4 = keys_all.reshape(per, total, heads, head_dim)
        v4 = values_all.reshape(per, total, heads, head_dim)
        valid = k_pos[None, :] < lens[:, None]

        def scores():
            raw = jnp.einsum("bqhd,bkhd->bhqk", q4, k4, preferred_element_type=f32) + bias[None]
            return jnp.where(valid[:, None, None, :], raw, NEG)

        first_scores = scores()
        top = jnp.max(first_scores, axis=-1, keepdims=True)
        expo = jnp.exp(first_scores - top)
        denom = jnp.sum(expo, axis=-1, keepdims=True)
        probs_low = (expo / denom).astype(bf16)
        mixed = jnp.einsum("bhqk,bkhd->bqhd", probs_low, v4, preferred_element_type=f32)
        mixed = mixed.reshape(flat_rows, width).astype(bf16)
        h1 = xflat + jnp.dot(mixed, wo, preferred_element_type=f32)
        n2 = normed(h1, g2).astype(bf16)
        inner = jnp.dot(n2, wi, preferred_element_type=f32)
        act_full, gelu_pull = jax.vjp(jax.nn.gelu, inner)
        act = act_full.astype(bf16)
        result = h1 + jnp.dot(act, wf, preferred_element_type=f32)
        outputs.append(result.astype(bf16).reshape(per, span, width))
        grad_wf = grad_wf + jnp.einsum("tf,td->fd", act, upstream, preferred_element_type=f32)
        d_act = jnp.einsum("td,fd->tf", upstream, wf, preferred_element_type=f32)
        d_inner = gelu_pull(d_act)[0].astype(bf16)
        grad_wi = grad_wi + jnp.einsum("td,tf->df", n2, d_inner, preferred_element_type=f32)
        d_n2 = jnp.einsum("tf,df->td", d_inner, wi, preferred_element_type=f32)
        norm_pull = jax.vjp(normed, h1, g2)[1]
        dh_part, dg_two = norm_pull(d_n2)
        grad_g2 = grad_g2 + dg_two
        dh1 = upstream.astype(f32) + dh_part
        d_attn = dh1.astype(bf16)
        grad_wo = grad_wo + jnp.einsum("td,te->de", mixed, d_attn, preferred_element_type=f32)
        d_mixed = jnp.einsum("te,de->td", d_attn, wo, preferred_element_type=f32).astype(bf16)
        dm4 = d_mixed.reshape(per, span, heads, head_dim)
        probs = jnp.exp(scores() - top) / denom
        d_probs = jnp.einsum("bqhd,bkhd->bhqk", dm4, v4, preferred_element_type=f32)
        value_terms = jnp.einsum("bhqk,bqhd->bkhd", probs_low, dm4, preferred_element_type=f32)
        delta = jnp.sum(probs * d_probs, axis=-1, keepdims=True)
        d_scores = (probs * (d_probs - delta)).astype(bf16)
        grad_bias = grad_bias + jnp.sum(d_scores.astype(f32), axis=0)
        d_query = jnp.einsum("bhqk,bkhd->bqhd", d_scores, k4, preferred_element_type=f32)
        d_query = d_query.reshape(flat_rows, width).astype(bf16)
        key_terms = jnp.einsum("bhqk,bqhd->bkhd", d_scores, q4, preferred_element_type=f32)
        key_share, value_share = (
            lax.psum_scatter(
                key_terms.reshape(per, total, width), "seq", scatter_dimension=1, tiled=True
            ),
            lax.psum_scatter(
                value_terms.reshape(per, total, width), "seq", scatter_dimension=1, tiled=True
            ),
        )
        d_key = key_share.reshape(flat_rows, width).astype(bf16)
        d_value = value_share.reshape(flat_rows, width).astype(bf16)
        grad_wq = grad_wq + jnp.einsum("td,te->de", n1, d_query, preferred_element_type=f32)
        grad_wk = grad_wk + jnp.einsum("td,te->de", n1, d_key, preferred_element_type=f32)
        grad_wv = grad_wv + jnp.einsum("td,te->de", n1, d_value, preferred_element_type=f32)
        d_n1 = jnp.einsum("te,de->td", d_query, wq, preferred_element_type=f32)
        d_n1 = d_n1 + jnp.einsum("te,de->td", d_key, wk, preferred_element_type=f32)
        d_n1 = d_n1 + jnp.einsum("te,de->td", d_value, wv, preferred_element_type=f32)
        first_pull = jax.vjp(normed, xflat, g1)[1]
        dx_part, dg_one = first_pull(d_n1)
        grad_g1 = grad_g1 + dg_one
        input_grads.append((dh1 + dx_part).reshape(per, span, width))
    owned = (
        lax.psum_scatter(grad_wq, ("seq", "rows"), scatter_dimension=0, tiled=True),
        lax.psum_scatter(grad_wk, ("seq", "rows"), scatter_dimension=0, tiled=True),
        lax.psum_scatter(grad_wv, ("seq", "rows"), scatter_dimension=0, tiled=True),
        lax.psum_scatter(grad_wo, ("seq", "rows"), scatter_dimension=0, tiled=True),
        lax.psum_scatter(grad_wi, ("seq", "rows"), scatter_dimension=0, tiled=True),
        lax.psum_scatter(grad_wf, ("seq", "rows"), scatter_dimension=0, tiled=True),
        lax.psum_scatter(grad_g1, ("seq", "rows"), scatter_dimension=0, tiled=True),
        lax.psum_scatter(grad_g2, ("seq", "rows"), scatter_dimension=0, tiled=True),
    )
    grad_full = lax.dynamic_update_slice_in_dim(
        jnp.zeros((heads, total, total), f32), grad_bias, q_start, 1
    )
    widened = jnp.pad(grad_full, ((0, 0), (0, 0), (total - 1, 0)))
    folded = jnp.pad(widened.reshape(heads, total * (2 * total - 1)), ((0, 0), (0, total)))
    rel_grad = jnp.sum(folded.reshape(heads, total, 2 * total), axis=1)[:, : 2 * total - 1]
    table_local = jnp.dot(onehot.T, rel_grad.T, precision=HIGH)
    table_grad = lax.psum(table_local, ("seq", "rows"))
    result_rows = jnp.concatenate(outputs, axis=0)
    grad_rows = jnp.concatenate(input_grads, axis=0)
    return (
        result_rows,
        grad_rows,
        owned[0],
        owned[1],
        owned[2],
        owned[3],
        owned[4],
        owned[5],
        owned[6],
        owned[7],
        table_grad,
    )


MESH_ID = pl.DeviceIdType.MESH
HBM = pl.BlockSpec(memory_space=pl.ANY)
VMEM = pl.BlockSpec(memory_space=pltpu.VMEM)
SMEM = pl.BlockSpec(memory_space=pltpu.SMEM)
BF = jnp.bfloat16
F32 = jnp.float32
NX, NZ, NY, NC = 2, 4, 2, 2


def rcopy(src, dst, send, recv, to):
    return pltpu.make_async_remote_copy(
        src_ref=src, dst_ref=dst, send_sem=send, recv_sem=recv, device_id=to, device_id_type=MESH_ID
    )


class Place:
    def __init__(self):
        self.x = lax.axis_index("seq")
        r = lax.axis_index("rows")
        self.c = lax.rem(r, 2)
        self.y = lax.rem(r // 2, 2)
        self.z = r // 4
        self.core = self.at(self.x, self.y, self.z, 1 - self.c)
        self.xn = self.at(1 - self.x, self.y, self.z, self.c)
        self.yn = self.at(self.x, 1 - self.y, self.z, self.c)
        self.zp = [None] + [self.at(self.x, self.y, self.zz(j), self.c) for j in range(1, NZ)]

    def at(self, x, y, z, c):
        return (x, z * 4 + y * 2 + c)

    def zz(self, j):
        return lax.rem(self.z + j, NZ)

    def barrier(self):
        sem = pltpu.get_barrier_semaphore()
        peers = [self.core, self.xn, self.yn] + self.zp[1:]
        for p in peers:
            pl.semaphore_signal(sem, inc=1, device_id=p, device_id_type=MESH_ID)
        pl.semaphore_wait(sem, len(peers))


class GatherXZY:
    def __init__(self, me, w, base, nh, ss, rr, dd):
        self.me, self.w, self.ss, self.rr, self.dd = me, w, ss, rr, dd
        self.base, self.nh = base, nh

    def cols(self, plane, c):
        return pl.ds(pl.multiple_of(self.base(plane) + c * self.nh, 128), self.nh)

    def ref(self, x, z, y, c, plane):
        return self.w.at[x, z, y, :, self.cols(plane, c)]

    def pair(self, z, y, c):
        return self.w.at[:, z, y, :, self.cols(self.me.x, c)]

    def send(self, ref, s, recv, to):
        rcopy(ref, ref, self.ss.at[s], recv, to).start()

    def got(self, ref, recv):
        rcopy(ref, ref, self.ss.at[0], recv, self.me.core).wait_recv()

    def start(self):
        m = self.me
        self.send(self.ref(m.x, m.z, m.y, m.c, 1 - m.x), 0, self.rr.at[0], m.xn)

    def step_x(self):
        m = self.me
        self.got(self.ref(1 - m.x, m.z, m.y, m.c, m.x), self.rr.at[0])
        p = self.pair(m.z, m.y, m.c)
        for j in range(1, NZ):
            self.send(p, j, self.rr.at[NZ - j], m.zp[j])
        self.send(p, 4, self.rr.at[4], m.yn)
        self.send(p, 8, self.dd.at[0], m.core)

    def step_z(self, j):
        m = self.me
        p = self.pair(m.zz(j), m.y, m.c)
        self.got(p, self.rr.at[j])
        self.send(p, 4 + j, self.rr.at[4 + j], m.yn)
        self.send(p, 8 + j, self.dd.at[j], m.core)

    def step_y(self, j):
        m = self.me
        p = self.pair(m.zz(j), 1 - m.y, m.c)
        self.got(p, self.rr.at[4 + j])
        self.send(p, 12 + j, self.dd.at[4 + j], m.core)

    def done(self):
        m = self.me
        for j in range(NZ):
            self.got(self.pair(m.zz(j), m.y, 1 - m.c), self.dd.at[j])
        for j in range(NZ):
            self.got(self.pair(m.zz(j), 1 - m.y, 1 - m.c), self.dd.at[4 + j])

    def sent(self):
        m = self.me
        one = self.ref(m.x, m.z, m.y, m.c, m.x)
        rcopy(one, one, self.ss.at[0], self.rr.at[0], m.core).wait_send()
        p = self.pair(m.z, m.y, m.c)
        for s in range(1, 16):
            rcopy(p, p, self.ss.at[s], self.rr.at[0], m.core).wait_send()


class GatherZYX:
    def __init__(self, me, w, ss, rr, dd):
        self.me, self.w, self.ss, self.rr, self.dd = me, w, ss, rr, dd

    def send(self, ref, s, recv, to):
        rcopy(ref, ref, self.ss.at[s], recv, to).start()

    def got(self, ref, recv):
        rcopy(ref, ref, self.ss.at[0], recv, self.me.core).wait_recv()

    def start(self):
        m = self.me
        own = self.w.at[m.x, m.z, m.y, m.c]
        for j in range(1, NZ):
            self.send(own, j - 1, self.rr.at[NZ - j - 1], m.zp[j])
        self.send(own, 3, self.rr.at[3], m.yn)

    def step_z(self, j):
        m = self.me
        b = self.w.at[m.x, m.zz(j), m.y, m.c]
        self.got(b, self.rr.at[j - 1])
        self.send(b, 5 + j, self.rr.at[3 + j], m.yn)

    def step_y(self, j):
        m = self.me
        self.got(self.w.at[m.x, m.zz(j), 1 - m.y, m.c], self.rr.at[3 + j])
        p = self.w.at[m.x, m.zz(j), :, m.c]
        self.send(p, 4 if j == 0 else 8 + j, self.rr.at[7 + j], m.xn)
        self.send(p, 5 if j == 0 else 11 + j, self.dd.at[j], m.core)

    def step_x(self, j):
        m = self.me
        p = self.w.at[1 - m.x, m.zz(j), :, m.c]
        self.got(p, self.rr.at[7 + j])
        self.send(p, 15 + j, self.dd.at[4 + j], m.core)

    def done_near(self):
        m = self.me
        for j in range(NZ):
            self.got(self.w.at[m.x, m.zz(j), :, 1 - m.c], self.dd.at[j])

    def done_far(self):
        m = self.me
        for j in range(NZ):
            self.got(self.w.at[1 - m.x, m.zz(j), :, 1 - m.c], self.dd.at[4 + j])

    def sent(self):
        m = self.me
        one = self.w.at[m.x, m.z, m.y, m.c]
        p = self.w.at[m.x, m.z, :, m.c]
        for s in range(19):
            r = one if s in (0, 1, 2, 3, 6, 7, 8) else p
            rcopy(r, r, self.ss.at[s], self.rr.at[0], m.core).wait_send()


def own_block(me, mine, theirs, w, parts):
    a = mine[...].astype(F32)[:24]
    b = theirs[...].astype(F32)[:24]
    first = jnp.where(me.c == 0, a, b)
    second = jnp.where(me.c == 0, b, a)
    both = jnp.concatenate([first, second], axis=0).astype(BF)
    at = 0
    for n, base in parts:
        w[me.x, me.z, me.y, :, pl.ds(pl.multiple_of(base, 128), n)] = both[:, at : at + n]
        at += n


class Piece:
    def __init__(self, index, rows, first):
        self.index, self.slot, self.rows = index, index % 2, rows
        cut = rows // 2 if rows // 2 % 16 == 0 else rows // 2 + 8
        self.subs = ((0, cut, first[0]), (cut, rows - cut, first[1]))


def acc_rows(x, y, z, lo, n):
    return pl.ds(pl.multiple_of(((x * NY + y) * NZ + z) * 192 + lo, 8), n)


class Reduce:
    def __init__(self, me, acc, a1, a2, a3, cs, cr, s1s, s1r, s2s, s2r, s3s, s3r, fin, finr, keep, sems):
        self.me = me
        self.acc, self.a1, self.a2, self.a3, self.cs, self.cr = acc, a1, a2, a3, cs, cr
        self.s1s, self.s1r, self.s2s, self.s2r, self.s3s, self.s3r = s1s, s1r, s2s, s2r, s3s, s3r
        self.fin, self.finr = fin, finr
        self.keep = keep
        (self.c_s, self.c_r, self.a_s, self.a_r, self.b_s, self.b_r, self.z_s, self.z_r, self.f_s, self.f_r) = sems

    def near(self, axis):
        return self.me.xn if axis == "x" else self.me.yn

    def core_copy(self, p):
        s, n = p.slot, p.rows
        return rcopy(
            self.cs.at[:, :, :, 0:n], self.cr.at[s, :, :, :, 0:n], self.c_s.at[s], self.c_r.at[s], self.me.core
        )

    def one_copy(self, p, k):
        s, (_, n, axis) = p.slot, p.subs[k]
        return rcopy(
            self.s1s.at[k, :, :, 0:n], self.s1r.at[s, k, :, :, 0:n], self.a_s.at[s, k], self.a_r.at[s, k], self.near(axis)
        )

    def two_copy(self, p, k):
        s, (_, n, axis) = p.slot, p.subs[k]
        to = self.near("y" if axis == "x" else "x")
        return rcopy(self.s2s.at[k, :, 0:n], self.s2r.at[s, k, :, 0:n], self.b_s.at[s, k], self.b_r.at[s, k], to)

    def z_copy(self, p, j):
        s, n = p.slot, p.rows
        return rcopy(
            self.s3s.at[j, 0:n], self.s3r.at[s, NZ - j, 0:n], self.z_s.at[s, j], self.z_r.at[s, NZ - j], self.me.zp[j]
        )

    def fin_copy(self, p):
        i, n = p.index, p.rows // 2
        return rcopy(
            self.fin.at[i, 0:n], self.finr.at[i, 0:n], self.f_s.at[i], self.f_r.at[i], self.me.core
        )

    def send_core(self, p):
        self.core_copy(p).start()

    def h1(self, p, old):
        me, s, n = self.me, p.slot, p.rows
        self.core_copy(p).wait_recv()
        for k, (lo, n, axis) in enumerate(p.subs):
            if old is not None:
                self.one_copy(old, k).wait_send()
            rows = pl.ds(lo, n)

            def body(q, carry):
                a, zq = q // NZ, lax.rem(q, NZ)
                if axis == "x":
                    keep, away = (me.x, a, zq, rows), (1 - me.x, a, zq, rows)
                else:
                    keep, away = (a, me.y, zq, rows), (a, 1 - me.y, zq, rows)
                held = [self.acc[acc_rows(*at[:3], lo, n), :] for at in (keep, away)]
                self.a1[k, a, zq, 0:n] = held[0] + self.cr[(s,) + keep].astype(F32)
                self.s1s[k, a, zq, 0:n] = (held[1] + self.cr[(s,) + away].astype(F32)).astype(BF)
                return carry

            lax.fori_loop(0, 2 * NZ, body, 0)
            self.one_copy(p, k).start()

    def h2(self, p, old):
        me, s = self.me, p.slot
        for k, (lo, n, axis) in enumerate(p.subs):
            self.one_copy(p, k).wait_recv()
            if old is not None:
                self.two_copy(old, k).wait_send()
            b = me.y if axis == "x" else me.x

            def body(zq, carry):
                self.a2[k, zq, 0:n] = self.a1[k, b, zq, 0:n] + self.s1r[s, k, b, zq, 0:n].astype(F32)
                self.s2s[k, zq, 0:n] = (
                    self.a1[k, 1 - b, zq, 0:n] + self.s1r[s, k, 1 - b, zq, 0:n].astype(F32)
                ).astype(BF)
                return carry

            lax.fori_loop(0, NZ, body, 0)
            self.two_copy(p, k).start()

    def h3(self, p, old):
        me, s = self.me, p.slot
        for k in range(2):
            self.two_copy(p, k).wait_recv()
        for j in range(1, NZ):
            if old is not None:
                self.z_copy(old, j).wait_send()
        for k, (lo, n, _) in enumerate(p.subs):
            rows = pl.ds(lo, n)
            for j in range(NZ):
                zq = me.zz(j)
                v = self.a2[k, zq, 0:n] + self.s2r[s, k, zq, 0:n].astype(F32)
                if j == 0:
                    self.a3[rows] = v
                else:
                    self.s3s[j, rows] = v.astype(BF)
        for j in range(1, NZ):
            self.z_copy(p, j).start()

    def h4(self, p):
        me, s, n, i = self.me, p.slot, p.rows, p.index
        for j in range(1, NZ):
            self.z_copy(p, NZ - j).wait_recv()
        total = self.a3[0:n]
        for j in range(1, NZ):
            total = total + self.s3r[s, j, 0:n].astype(F32)
        if p.groups is None:
            a, b = total[0 : n // 2], total[n // 2 :]
        else:
            a, b = (
                jnp.concatenate([total[48 * g + 24 * k : 48 * g + 24 * k + 24] for g in range(p.groups)], axis=0)
                for k in range(NC)
            )
        self.fin[i, 0 : n // 2] = jnp.where(me.c == 0, b, a)
        self.keep(p, jnp.where(me.c == 0, a, b), me.c)
        self.fin_copy(p).start()


def norm_back(h, gain, up):
    r = lax.rsqrt(jnp.mean(h * h, axis=-1, keepdims=True) + EPS)
    hr = h * r
    w = up * gain
    dgain = jnp.sum(up * hr, axis=0, keepdims=True)
    return r * (w - hr * jnp.mean(w * hr, axis=-1, keepdims=True)), dgain


def layer_kernel(
    tok, gin, gains, wq, wk, wv, wo, wi, pd, relb, table, lens,
    act_o, dx_o, gq_o, gk_o, gv_o, go_o, gi_o, gf_o, sm_o,
    WA, WB, WD, X, G, N2, QKV, O, H1, ACT, DU, T, M, MACC, LSE, R, RG,
    ACC, A1, A2, A3, CS, CR, S1S, S1R, S2S, S2R, S3S, S3R, FIN, FINR, SM, SMR, ZB, DG,
    ts, tr, tl, gs, gr, gl, es, er, as_, ar, ad, os_, or_, od, bs, br, bd, b2s, b2r, b2d, ds_, dr, dd, ys, yr, yl, xs_, xr, xl,
    c_s, c_r, a_s, a_r, b_s, b_r, z_s, z_r, f_s, f_r, ms, mr,
):
    me = Place()
    x, y, z, c = me.x, me.y, me.z, me.c
    mine, span, width = X.shape[0], X.shape[2], X.shape[3]
    length = 2 * span
    flat = mine * length
    ff = DU.shape[1]
    na, nb = WA.shape[4] // 2, WB.shape[4] // 2
    PA, PB = DU.at[pl.ds(32 * c, 32), 0:na], DU.at[pl.ds(64 + 32 * c, 32), 0:nb]
    RA, RB = DU.at[128:160, 0:na], DU.at[160:192, 0:nb]
    hd = 64
    YB = N2
    pairs = width // hd // 2
    half_ff, half_w = ff // 2, width // 2
    gath_a = GatherXZY(me, WA, lambda plane: 0, na, as_, ar, ad)
    gath_o = GatherXZY(me, WB, lambda plane: 0, half_w, os_, or_, od)
    gath_1 = GatherXZY(me, WB, lambda plane: width + half_ff * plane, half_ff // 2, bs, br, bd)
    gath_2 = GatherXZY(me, WB, lambda plane: width + half_ff * (1 - plane), half_ff // 2, b2s, b2r, b2d)
    gath_d = GatherZYX(me, WD, ds_, dr, dd)

    def pack(first, n, parts):
        filled = [
            jnp.concatenate([p.astype(F32), jnp.zeros((32 - p.shape[0], p.shape[1]), F32)], axis=0) for p in parts
        ]
        DU[first : first + 32, 0:n] = jnp.concatenate(filled, axis=1).astype(BF)

    quarter = half_ff // 2
    pack(0, na, (gains[...], wq[...], wk[:, 0 : na - gains.shape[1] - width]))
    pack(32, na, (wk[:, na - gains.shape[1] - width :], wv[...]))
    me.barrier()
    ea = rcopy(DU.at[pl.ds(32 * (1 - c), 32), 0:na], RA, es.at[0], er.at[0], me.core)
    eb = rcopy(DU.at[pl.ds(64 + 32 * (1 - c), 32), 0:nb], RB, es.at[1], er.at[1], me.core)
    ea.start()
    for k in range(2):
        first = wi[:, quarter * k : quarter * k + quarter]
        second = wi[:, half_ff + quarter * k : half_ff + quarter * k + quarter]
        pack(64 + 32 * k, nb, (wo[:, half_w * k : half_w * k + half_w], first, second))
    eb.start()
    tok_r = [rcopy(tok.at[2 * (1 - x) + i], X.at[i, x], ts.at[i], tr.at[i], me.xn) for i in range(mine)]
    tok_in = [rcopy(X.at[i, 1 - x], X.at[i, 1 - x], ts.at[i], tr.at[i], me.xn) for i in range(mine)]
    tok_l = [pltpu.make_async_copy(tok.at[2 * x + i], X.at[i, x], tl.at[i]) for i in range(mine)]
    g_r = rcopy(gin.at[pl.ds(2 * (1 - x), 2)], G.at[:, x], gs, gr, me.xn)
    g_in = rcopy(G.at[:, 1 - x], G.at[:, 1 - x], gs, gr, me.xn)
    g_l = pltpu.make_async_copy(gin.at[pl.ds(2 * x, 2)], G.at[:, x], gl)
    ea.wait_recv()
    own_block(me, PA, RA, WA, ((na, c * na),))
    gath_a.start()
    for i in range(mine):
        tok_r[i].start()
        tok_l[i].start()
    g_l.start()
    eb.wait_recv()
    own_block(
        me, PB, RB, WB,
        ((half_w, c * half_w), (quarter, width + c * quarter), (quarter, width + half_ff + c * quarter)),
    )
    WD[x, z, y, c] = pd[...]
    cols = relb.shape[1]
    kinds = table.shape[0]
    hot = (lax.broadcasted_iota(jnp.int32, (kinds, cols), 0) == relb[...]).astype(BF)
    R[...] = lax.dot_general(table[...], hot, (((0,), (0,)), ((), ())), preferred_element_type=F32)[0:16]
    gath_a.step_x()
    gath_o.start()
    gath_1.start()
    gath_d.start()
    for j in range(1, NZ):
        gath_a.step_z(j)
    gath_o.step_x()
    gath_1.step_x()
    for j in range(NZ):
        gath_a.step_y(j)
    gath_d.step_y(0)
    gath_2.start()
    g_r.start()
    gath_a.done()

    def gain_row(k):
        return jnp.transpose(WA[:, :, :, :, 128 * k : 128 * k + 128].reshape(width, 128).astype(F32))[0:1, :]

    gain1 = gain_row(0)

    def row_slice(i):
        return pl.ds(pl.multiple_of(i * length, length), length)

    def first_norm(i):
        for half in range(2):
            xf = X[i, half].astype(F32)
            scale = lax.rsqrt(jnp.mean(xf * xf, axis=-1, keepdims=True) + EPS)
            N2[i, half] = (xf * scale * gain1).astype(BF)

    for i in range(mine):
        tok_l[i].wait()
        tok_in[i].wait_recv()
        first_norm(i)
        for n in range(3):
            w = WA[:, :, :, :, 256 + n * width : 256 + (n + 1) * width].reshape(width, width)
            QKV[row_slice(i), n * width : (n + 1) * width] = jnp.dot(
                N2[i].reshape(length, width), w, preferred_element_type=F32
            ).astype(BF)
        for g in (gath_o, gath_1, gath_d):
            g.step_z(i + 1)
    low = lax.broadcasted_iota(jnp.int32, (1, 128), 1) < hd
    lane = lax.broadcasted_iota(jnp.int32, (1, 128), 1)
    kpos = lax.broadcasted_iota(jnp.int32, (length, 128), 0)
    blocks = length // 128

    def strips(p):
        for h in range(2):
            row = jnp.broadcast_to(R[pl.ds(2 * p + h, 1), :], (128, cols))
            M[h] = pltpu.roll(row, cols - 127, 1, stride=1, stride_axis=0)[:, : M.shape[2]]

    def bias_of(h):
        return jnp.concatenate(
            [M[h, :, 128 * (blocks - 1 - a) : 128 * (blocks - 1 - a) + length] for a in range(blocks)], axis=0
        )

    own = (low, jnp.logical_not(low))
    spare = (hd, 0)
    ones = [(lane == spare[h]).astype(F32).astype(BF) for h in range(2)]
    none = jnp.zeros((), BF)

    def masked_keys(h, k, count):
        pad = jnp.where((lane == spare[h]) & (kpos >= count), NEG, 0.0).astype(BF)
        return jnp.where(own[h], k, pad)

    def lanes(n, p):
        return pl.ds(pl.multiple_of(n * width + p * 128, 128), 128)

    nt = (((1,), (1,)), ((), ()))
    tn = (((0,), (0,)), ((), ()))

    def mm(a, b, dims):
        return lax.dot_general(a, b, dims, preferred_element_type=F32)

    o_, b1, b2, d_ = gath_o, gath_1, gath_2, gath_d
    comm = {
        0: ((o_.step_z, 3), (b1.step_z, 3), (d_.step_z, 3)),
        1: ((o_.step_y, 0), (b1.step_y, 0), (d_.step_y, 1)),
        2: ((lambda j: b2.step_x(), 0), (o_.step_y, 1), (b1.step_y, 1), (d_.step_y, 2)),
        3: ((o_.step_y, 2), (b1.step_y, 2), (d_.step_y, 3)),
        4: ((o_.step_y, 3), (b1.step_y, 3)),
        5: ((b2.step_z, 1), (d_.step_x, 0)),
        6: ((b2.step_z, 2),),
        7: ((b2.step_z, 3), (d_.step_x, 1)),
        8: ((b2.step_y, 0),),
        9: ((d_.step_x, 2),),
        10: ((b2.step_y, 1),),
        11: ((d_.step_x, 3),),
    }

    def attend(t, carry):
        p, i = t // mine, lax.rem(t, mine)
        pl.when(i == 0)(lambda: strips(p))
        rows = row_slice(i)
        q, k, v = QKV[rows, lanes(0, p)], QKV[rows, lanes(1, p)], QKV[rows, lanes(2, p)]
        outs = []
        for h in range(2):
            s = mm(jnp.where(own[h], q, ones[h]), masked_keys(h, k, lens[2 * x + i]), nt) + bias_of(h)
            top = jnp.max(s, axis=-1, keepdims=True)
            e = jnp.exp(s - top)
            total = jnp.sum(e, axis=-1, keepdims=True)
            LSE[rows, :] = jnp.where(lane == 2 * p + h, top + jnp.log(total), LSE[rows, :])
            outs.append(jnp.dot((e * (1.0 / total)).astype(BF), v, preferred_element_type=F32))
        O[i, :, :, lanes(0, p)] = jnp.where(low, outs[0], outs[1]).astype(BF).reshape(2, span, 128)
        for at, steps in comm.items():
            @pl.when(t == at)
            def _():
                for step, j in steps:
                    step(j)
        return carry

    LSE[...] = jnp.zeros_like(LSE)
    lax.fori_loop(0, mine * pairs, attend, 0)
    ea.wait_send()
    eb.wait_send()
    gath_o.done()
    gath_1.done()
    gath_d.done_near()
    g_l.wait()
    g_in.wait_recv()

    gain2 = gain_row(1)
    DG[...] = jnp.zeros_like(DG)
    c0, c1 = 0.7978845608028654, 0.044715

    def dn_set(v):
        for n in range(width // 128):
            ACC[length * n : length * n + length, :] = v[:, 128 * n : 128 * n + 128]

    def dn_get(lo, n):
        return jnp.concatenate([ACC[length * k + lo : length * k + lo + n, :] for k in range(width // 128)], axis=1)

    def dn_add(v):
        for n in range(width // 128):
            at = slice(length * n, length * n + length)
            ACC[at, :] = ACC[at, :] + v[:, 128 * n : 128 * n + 128]

    wo_all = lambda: WB[:, :, :, :, 0:width].reshape(width, width)
    for i in range(mine):
        h1 = X[i].reshape(length, width).astype(F32) + jnp.dot(
            O[i].reshape(length, width), wo_all(), preferred_element_type=F32
        )
        H1[i] = h1.reshape(2, span, width)
        r = lax.rsqrt(jnp.mean(h1 * h1, axis=-1, keepdims=True) + EPS)
        N2[i] = (h1 * r * gain2).astype(BF).reshape(2, span, width)

    def chunk(n, carry):
        @pl.when(n == 2)
        def _():
            gath_2.done()
            gath_d.done_far()

        f = lax.rem(2 * x + n, 4)

        def one_row(i, carry):
            pl.when((n == 0) & (i == 0))(lambda: gath_2.step_y(2))
            pl.when((n == 0) & (i == 1))(lambda: gath_2.step_y(3))
            n2, g = N2[i].reshape(length, width), G[i].reshape(length, width)
            for part in range(3):
                fcols = pl.ds(pl.multiple_of(f * width + 256 * part, 256), 256)
                wcols = pl.ds(pl.multiple_of(width + f * width + 256 * part, 256), 256)
                wi_part = WB[:, :, :, :, wcols].reshape(width, 256)
                wf_part = WD[f // 2, pl.ds(2 * lax.rem(f, 2), 2)].reshape(width, width)[256 * part : 256 * part + 256]
                u = jnp.dot(n2, wi_part, preferred_element_type=F32)
                da = mm(g, wf_part, nt)
                sq = u * u
                t = jnp.tanh(u * (c0 + (c0 * c1) * sq))
                cdf = 0.5 + 0.5 * t
                ACT[row_slice(i), fcols] = (u * cdf).astype(BF)
                slope = cdf + (0.5 * u) * (1.0 - t * t) * (c0 + (3.0 * c0 * c1) * sq)
                DU[row_slice(i), fcols] = (da * slope).astype(BF)
            return carry

        return lax.fori_loop(0, mine, one_row, carry)

    lax.fori_loop(0, ff // width, chunk, 0)
    def keep(p, value, core):
        if p.groups is None:
            gf_o[:, pl.ds(pl.multiple_of(256 * p.part + 128 * core, 128), 128)] = value
            return
        for g in range(p.groups):
            if p.kind == "i":
                dst, base = gi_o, 1024 * p.part + 256 * g
            elif p.kind == "o":
                dst, base = go_o, 256 * g
            else:
                dst, base = (gq_o, gk_o, gv_o)[g], 256 * p.part
            dst[:, pl.ds(pl.multiple_of(base + 128 * core, 128), 128)] = value[24 * g : 24 * g + 24]

    red = Reduce(
        me, ACC, A1, A2, A3, CS, CR, S1S, S1R, S2S, S2R, S3S, S3R, FIN, FINR, keep, (c_s, c_r, a_s, a_r, b_s, b_r, z_s, z_r, f_s, f_r)
    )
    pieces = []
    kinds_of = [("f", 0), ("f", 1), ("f", 2), ("i", 0), ("i", 1), ("i", 2), ("o", 0), ("qkv", 0), ("qkv", 1), ("qkv", 2)]
    made_at = [0, 2, 4, 5, 6, 7, 8, 13, 15, 17]
    last = len(kinds_of)
    for n in range(last):
        kind, part = kinds_of[n]
        piece = Piece(n, 144 if kind in ("o", "qkv") else 192, ("y", "y") if n < last - 1 else ("x", "x"))
        piece.kind, piece.part = kind, part
        piece.groups = None if kind == "f" else piece.rows // 48
        pieces.append(piece)

    def stages(n):
        def at(k):
            return pieces[made_at.index(n - k)] if n - k in made_at else None

        def old(p):
            return pieces[p.index - 1] if p.index else None

        if at(4):
            red.h4(at(4))
        if at(3):
            red.h3(at(3), old(at(3)))
        if at(2):
            red.h2(at(2), old(at(2)))
        if at(1):
            red.h1(at(1), old(at(1)))
        if at(0):
            if old(at(0)):
                red.core_copy(old(at(0))).wait_send()
            produce(at(0))

    def split(res):
        a, b = res[:, 0:128], res[:, 128:256]
        return jnp.where(c == 0, a, b), jnp.where(c == 0, b, a).astype(BF)

    def outer_piece(j):

        def body(q, carry):
            xq, zh = q // 2, lax.rem(q, 2)
            lhs = ACT[:, pl.ds(pl.multiple_of(q * 768, 768), 768)]
            rhs = G[:, :, :, 256 * j : 256 * j + 256].reshape(flat, 256)
            own, other = split(mm(lhs, rhs, tn))
            for b in range(4):
                at = (xq, b % 2, 2 * zh + b // 2)
                ACC[acc_rows(*at, 0, 192), :] = own[192 * b : 192 * b + 192]
                CS[at] = other[192 * b : 192 * b + 192]
            return carry

        lax.fori_loop(0, 4, body, 0)

    def rows_piece(groups, rhs):
        def body(g, carry):
            own, other = split(jnp.dot(T[...], rhs(g), preferred_element_type=F32))
            at = pl.ds(pl.multiple_of(48 * g, 48), 48)
            for k in range(NX * NZ * NY):
                ACC[acc_rows(k // 8, k % 2, (k // 2) % 4, 48 * g, 48), :] = own[48 * k : 48 * k + 48]
                CS[k // 8, k % 2, (k // 2) % 4, at] = other[48 * k : 48 * k + 48]
            return carry

        lax.fori_loop(0, groups, body, 0)

    def produce(p):
        if p.kind == "f":
            outer_piece(p.part)
        elif p.kind == "i":
            rows_piece(4, lambda g: DU[:, pl.ds(pl.multiple_of(1024 * p.part + 256 * g, 256), 256)])
        elif p.kind == "o":
            T[...] = jnp.transpose(O[...].reshape(flat, width))
            rows_piece(3, lambda g: H1[:, :, :, pl.ds(pl.multiple_of(256 * g, 256), 256)].reshape(flat, 256).astype(BF))
        else:
            rows_piece(3, lambda g: QKV[:, pl.ds(pl.multiple_of(g * width + 256 * p.part, 256), 256)])
        red.send_core(p)

    stages(0)
    T[...] = jnp.transpose(N2[...].reshape(flat, width))
    stages(1)

    def result(t, carry):
        i, f = t // 4, lax.rem(t, 4)
        a = ACT[row_slice(i), pl.ds(pl.multiple_of(f * width, width), width)]
        wf = WD[f // 2, pl.ds(2 * lax.rem(f, 2), 2)].reshape(width, width)
        out = jnp.dot(a, wf, preferred_element_type=F32)

        @pl.when(f == 0)
        def _():
            dn_set(H1[i].reshape(length, width) + out)

        @pl.when(f > 0)
        def _():
            dn_add(out)

        @pl.when(f == 3)
        def _():
            YB[i] = dn_get(0, length).astype(BF).reshape(2, span, width)

        return carry

    lax.fori_loop(0, 4 * mine, result, 0)
    y_out = [
        rcopy(YB.at[i, 1 - x], act_o.at[2 * (1 - x) + i], ys.at[i], yr.at[i], me.xn) for i in range(mine)
    ]
    y_loc = [pltpu.make_async_copy(YB.at[i, x], act_o.at[2 * x + i], yl.at[i]) for i in range(mine)]
    for i in range(mine):
        rcopy(YB.at[i, 1 - x], act_o.at[2 * x + i], ys.at[i], yr.at[i], me.xn).start()
        y_loc[i].start()

    stages(2)
    stages(3)

    def back(t, carry):
        i, f = t // 4, lax.rem(t, 4)
        du = DU[row_slice(i), pl.ds(pl.multiple_of(f * width, width), width)]
        wi_part = WB[:, :, :, :, pl.ds(pl.multiple_of((f + 1) * width, width), width)].reshape(width, width)
        out = mm(du, wi_part, nt)

        @pl.when(f == 0)
        def _():
            dn_set(out)

        @pl.when(f > 0)
        def _():
            dn_add(out)

        @pl.when(f == 3)
        def _():
            for half in range(2):
                dh, dgain = norm_back(H1[i, half], gain2, dn_get(span * half, span))
                DG[1:2, :] = DG[1:2, :] + dgain
                H1[i, half] = G[i, half].astype(F32) + dh

        return carry

    lax.fori_loop(0, 4 * mine, back, 0)

    stages(4)
    for i in range(mine):
        dab = H1[i].reshape(length, width).astype(BF)
        G[i] = mm(dab, wo_all(), nt).astype(BF).reshape(2, span, width)
    landing = lambda i: DU.at[pl.ds(i * span, span), 0:width]
    dx_r = [rcopy(X.at[i, 1 - x], landing(i), xs_.at[i], xr.at[i], me.xn) for i in range(mine)]
    dx_l = [pltpu.make_async_copy(H1.at[i, x], dx_o.at[2 * x + i], xl.at[i]) for i in range(mine)]
    dx_f = [pltpu.make_async_copy(H1.at[i, 1 - x], dx_o.at[2 * (1 - x) + i], xl.at[mine + i]) for i in range(mine)]

    def input_grad(i):
        for n in range(3):
            out = mm(
                QKV[row_slice(i), n * width : (n + 1) * width],
                WA[:, :, :, :, 256 + n * width : 256 + (n + 1) * width].reshape(width, width),
                nt,
            )
            (dn_set if n == 0 else dn_add)(out)
        for half in range(2):
            dh, dgain = norm_back(X[i, half].astype(F32), gain1, dn_get(span * half, span))
            DG[0:1, :] = DG[0:1, :] + dgain
            H1[i, half] = H1[i, half] + dh
        X[i, 1 - x] = H1[i, 1 - x].astype(BF)
        dx_r[i].start()
        dx_l[i].start()

    def norm_again():
        for i in range(mine):
            y_out[i].wait_recv()
            y_out[i].wait_send()
            y_loc[i].wait()
        for i in range(mine):
            first_norm(i)
        T[...] = jnp.transpose(N2[...].reshape(flat, width))

    def attend_back(t, carry):
        i, p = t // pairs, lax.rem(t, pairs)
        strips(p)
        MACC[...] = jnp.zeros_like(MACC)
        rows = row_slice(i)
        q, k, v = QKV[rows, lanes(0, p)], QKV[rows, lanes(1, p)], QKV[rows, lanes(2, p)]
        do = G[i, :, :, lanes(0, p)].reshape(length, 128)
        prod = do.astype(F32) * O[i, :, :, lanes(0, p)].reshape(length, 128).astype(F32)
        dqs, dks, dvs = [], [], []
        for h in range(2):
            lse = jnp.sum(jnp.where(lane == 2 * p + h, LSE[rows, :], 0.0), axis=-1, keepdims=True)
            delta = jnp.sum(jnp.where(own[h], prod, 0.0), axis=-1, keepdims=True)
            s = mm(jnp.where(own[h], q, ones[h]), masked_keys(h, k, lens[2 * x + i]), nt) + bias_of(h)
            pr = jnp.exp(s - lse)
            ds = pr * (mm(jnp.where(own[h], do, none), v, nt) - delta)
            for a in range(blocks):
                at = 128 * (blocks - 1 - a)
                MACC[h, :, at : at + length] = MACC[h, :, at : at + length] + ds[128 * a : 128 * a + 128]
            low_p, low_ds = pr.astype(BF), ds.astype(BF)
            dqs.append(jnp.dot(low_ds, k, preferred_element_type=F32))
            dks.append(mm(low_ds, q, tn))
            dvs.append(mm(low_p, do, tn))
        for n, parts in enumerate((dqs, dks, dvs)):
            QKV[rows, lanes(n, p)] = jnp.where(low, parts[0], parts[1]).astype(BF)

        for h in range(2):
            part = jnp.zeros((8, cols), F32)
            for a in range(16):
                part = part + pltpu.roll(MACC[h, 8 * a : 8 * a + 8, :], (cols - 8 * a) % cols, 1)
            line = part[0:1]
            for a in range(1, 8):
                line = line + pltpu.roll(part[a : a + 1], cols - a, 1)
            at = pl.ds(2 * p + h, 1)
            RG[at, :] = RG[at, :] + pltpu.roll(line, 127, 1)

        for n in range(mine * pairs):
            @pl.when(t == n)
            def _():
                stages(5 + n)
                if n == pairs - 1:
                    norm_again()
                if n == pairs:
                    input_grad(0)

        return carry

    RG[...] = jnp.zeros_like(RG)
    MACC[...] = jnp.zeros_like(MACC)
    lax.fori_loop(0, mine * pairs, attend_back, 0)

    stages(17)
    stages(18)
    input_grad(1)
    stages(19)
    stages(20)
    for n in range(width // 128):
        SM[0, n : n + 1, :] = DG[0:1, 128 * n : 128 * n + 128]
        SM[0, 8 + n : 9 + n, :] = DG[1:2, 128 * n : 128 * n + 128]
    rest = jnp.concatenate([RG[...], jnp.zeros((112, cols), F32)], axis=0)
    spread = jnp.zeros((kinds, 128), F32)
    for _ in range(3):
        part = rest.astype(BF)
        rest = rest - part.astype(F32)
        spread = spread + mm(hot, part, nt)
    SM[0, 16 : 16 + kinds, :] = spread
    sm_copies = [
        rcopy(SM.at[k], SMR.at[k], ms.at[k], mr.at[k], to) for k, to in enumerate((me.core, me.xn, me.yn))
    ]
    sm_copies[0].start()
    stages(21)
    for k in range(3):
        sm_copies[k].wait_recv()
        SM[k + 1] = SM[k] + SMR[k]
        if k < 2:
            sm_copies[k + 1].start()
    ZB[z] = SM[3]
    sm_z = [None] + [rcopy(SM.at[3], ZB.at[z], ms.at[2 + j], mr.at[6 - j], me.zp[j]) for j in range(1, NZ)]
    for j in range(1, NZ):
        sm_z[j].start()
    for i in range(mine):
        dx_r[i].wait_recv()
        H1[i, 1 - x] = DU[pl.ds(i * span, span), 0:width].astype(F32)
        dx_f[i].start()
    for p in pieces:
        red.fin_copy(p).wait_recv()
        keep(p, FINR[p.index, 0 : p.rows // 2], 1 - c)
    for j in range(1, NZ):
        rcopy(SM.at[3], ZB.at[me.zz(j)], ms.at[2 + j], mr.at[2 + j], me.zp[j]).wait_recv()
    sm_o[...] = ZB[0] + ZB[1] + ZB[2] + ZB[3]
    g_r.wait_send()
    for k in range(3):
        sm_copies[k].wait_send()
    for j in range(1, NZ):
        sm_z[j].wait_send()
    for g in (gath_a, gath_o, gath_1, gath_2, gath_d):
        g.sent()
    for i in range(mine):
        tok_r[i].wait_send()
        dx_r[i].wait_send()
        dx_l[i].wait()
        dx_f[i].wait()
    for p in pieces[-1:]:
        red.core_copy(p).wait_send()
        for k in range(2):
            red.one_copy(p, k).wait_send()
            red.two_copy(p, k).wait_send()
        for j in range(1, NZ):
            red.z_copy(p, j).wait_send()
    for p in pieces:
        red.fin_copy(p).wait_send()


def layer_call(tok, gin, gains, wq, wk, wv, wo, wi, pd, relb, table, lens, heads):
    rows_dev, span, width = tok.shape
    length = 2 * span
    mine = rows_dev // 2
    flat = mine * length
    dma = pltpu.SemaphoreType.DMA
    ff = wi.shape[1]
    na, nb = (gains.shape[1] + 3 * width) // 2, (width + ff) // 2
    count = width // 256 + ff // 1024 + 4
    wa = (NX, NZ, NY, 48, 2 * na)
    wb = (NX, NZ, NY, 48, 2 * nb)
    wd = (NX, NZ, NY, NC) + pd.shape
    xs = (mine, 2, span, width)
    block = (192, 128)
    bf = lambda *s: pltpu.VMEM(s, BF)
    f32 = lambda *s: pltpu.VMEM(s, F32)
    out = lambda *s: jax.ShapeDtypeStruct(s, F32)
    shard = wq.shape[0]
    return pl.pallas_call(
        layer_kernel,
        out_shape=[jax.ShapeDtypeStruct(tok.shape, BF), out(*tok.shape)]
        + [out(shard, width)] * 4 + [out(shard, ff), out(*pd.shape), out(48, 128)],
        in_specs=[HBM, HBM] + [VMEM] * 9 + [SMEM],
        out_specs=[HBM, HBM] + [VMEM] * 7,
        scratch_shapes=[
            bf(*wa), bf(*wb), bf(*wd), bf(*xs), bf(*xs), bf(*xs), bf(flat, 3 * width), bf(*xs), f32(*xs),
             bf(flat, ff), bf(flat, ff), bf(width, flat), f32(2, 128, 896), f32(2, 128, 1024),
            f32(flat, 128), f32(16, relb.shape[1]), f32(16, relb.shape[1]),
            f32(NX * NY * NZ * 192, 128), f32(2, 2, NZ, 96, 128), f32(2, NZ, 96, 128), f32(*block), bf(NX, NY, NZ, *block), bf(2, NX, NY, NZ, *block),
            bf(2, 2, NZ, 96, 128), bf(2, 2, 2, NZ, 96, 128), bf(2, NZ, 96, 128), bf(2, 2, NZ, 96, 128),
            bf(NZ, *block), bf(2, NZ, *block), f32(count, 96, 128), f32(count, 96, 128),
            f32(4, 48, 128), f32(3, 48, 128), f32(NZ, 48, 128), f32(8, width),
            dma((2,)), dma((2,)), dma((2,)), dma, dma, dma, dma((2,)), dma((2,)),
            *[dma((n,)) for _ in range(4) for n in (16, 8, 8)], dma((19,)), dma((11,)), dma((8,)),
            dma((2,)), dma((2,)), dma((2,)), dma((2,)), dma((2,)), dma((4,)),
            dma((2,)), dma((2,)), dma((2, 2)), dma((2, 2)), dma((2, 2)), dma((2, 2)), dma((2, NZ)), dma((2, NZ)),
            dma((count,)), dma((count,)), dma((6,)), dma((6,)),
        ],
        compiler_params=pltpu.CompilerParams(
            collective_id=0, has_side_effects=True, vmem_limit_bytes=VMEM_LIMIT
        ),
        name="layer",
    )(tok, gin, gains, wq, wk, wv, wo, wi, pd, relb, table, lens)


VMEM_LIMIT = 67_000_000


def fast(
    tokens, doc_lengths, rel_buckets, w_query, w_key, w_value, w_output, w_inner, w_outer,
    attn_gain, ffn_gain, bias_table, out_grad,
):
    n_bins, heads = bias_table.shape
    wide = lambda g: jnp.broadcast_to(g[:, None], (g.shape[0], 128))
    gains = jnp.concatenate([wide(attn_gain), wide(ffn_gain)], axis=1)
    relb = jnp.pad(rel_buckets, (0, 1))[None, :]
    table = jnp.pad(bias_table, ((0, 0), (0, 128 - heads)))
    act, dx, gq, gk, gv, go, gi, gf, small = layer_call(
        tokens, out_grad, gains, w_query, w_key, w_value, w_output, w_inner, w_outer, relb, table, doc_lengths, heads
    )
    me = lax.axis_index("seq") * lax.axis_size("rows") + lax.axis_index("rows")
    cut = attn_gain.shape[0]
    gains = [lax.dynamic_slice_in_dim(small[8 * k : 8 * k + 6].reshape(-1), me * cut, cut) for k in range(2)]
    return act, dx, gq, gk, gv, go, gi, gf, gains[0], gains[1], small[16 : 16 + n_bins, :heads]


def solution(mesh):
    split = P(("seq", "rows"), None)
    rows = P("rows", "seq", None)
    in_specs = (rows, P("rows"), P()) + (split,) * 6 + (P(("seq", "rows")),) * 2 + (P(), rows)
    out_specs = (rows, rows) + (split,) * 6 + (P(("seq", "rows")),) * 2 + (P(),)
    shape = (mesh.shape["seq"], mesh.shape["rows"])
    program = fast if shape == (NX, NZ * NY * NC) else local
    return jax.shard_map(program, mesh=mesh, in_specs=in_specs, out_specs=out_specs, check_vma=False)
```

```python
import functools

import jax
import jax.numpy as jnp
from jax import lax
from jax.experimental import pallas as pl
from jax.experimental.pallas import tpu as pltpu
from jax.sharding import PartitionSpec as P

MB = 2


EPS = 1e-06
NEG = -1000000000.0
HIGH = lax.Precision.HIGHEST


def normed(h, gain):
    return h * lax.rsqrt(jnp.mean(h * h, axis=-1, keepdims=True) + EPS) * gain


def fetch(shards):
    return (
        lax.all_gather(shards[0], ("seq", "rows"), axis=0, tiled=True),
        lax.all_gather(shards[1], ("seq", "rows"), axis=0, tiled=True),
        lax.all_gather(shards[2], ("seq", "rows"), axis=0, tiled=True),
        lax.all_gather(shards[3], ("seq", "rows"), axis=0, tiled=True),
        lax.all_gather(shards[4], ("seq", "rows"), axis=0, tiled=True),
        lax.all_gather(shards[5], ("seq", "rows"), axis=0, tiled=True),
        lax.all_gather(shards[6], ("seq", "rows"), axis=0, tiled=True),
        lax.all_gather(shards[7], ("seq", "rows"), axis=0, tiled=True),
    )


def local(
    tokens,
    doc_lengths,
    rel_buckets,
    w_query,
    w_key,
    w_value,
    w_output,
    w_inner,
    w_outer,
    attn_gain,
    ffn_gain,
    bias_table,
    out_grad,
):
    f32 = jnp.float32
    bf16 = jnp.bfloat16
    rows_dev, span, width = tokens.shape
    n_bins, heads = bias_table.shape
    head_dim = width // heads
    seq_count = lax.axis_size("seq")
    seq_place = lax.axis_index("seq")
    total = span * seq_count
    q_start = seq_place * span
    per = rows_dev // MB
    flat_rows = per * span
    shards = (w_query, w_key, w_value, w_output, w_inner, w_outer, attn_gain, ffn_gain)
    table = bias_table.astype(f32)
    k_pos = jnp.arange(total, dtype=jnp.int32)
    onehot = (rel_buckets[:, None] == jnp.arange(n_bins, dtype=jnp.int32)[None, :]).astype(f32)
    rel_bias = jnp.dot(onehot, table, precision=HIGH)
    spread = jnp.concatenate([rel_bias.T, jnp.zeros((heads, 1), f32)], axis=1)
    tiled = jnp.tile(spread, (1, total))
    full_bias = tiled[:, : total * (2 * total - 1)].reshape(heads, total, 2 * total - 1)[
        :, :, total - 1 :
    ]
    bias = lax.dynamic_slice_in_dim(full_bias, q_start, span, 1)
    ff_width = w_inner.shape[1]
    grad_wq = jnp.zeros((width, width), f32)
    grad_wk = jnp.zeros((width, width), f32)
    grad_wv = jnp.zeros((width, width), f32)
    grad_wo = jnp.zeros((width, width), f32)
    grad_wi = jnp.zeros((width, ff_width), f32)
    grad_wf = jnp.zeros((ff_width, width), f32)
    grad_g1 = jnp.zeros((width,), f32)
    grad_g2 = jnp.zeros((width,), f32)
    grad_bias = jnp.zeros((heads, span, total), f32)
    outputs = []
    input_grads = []
    for batch in range(MB):
        whole = fetch(shards)
        wq, wk, wv, wo, wi, wf, gain_one, gain_two = whole
        g1 = gain_one.astype(f32)
        g2 = gain_two.astype(f32)
        first = batch * per
        xflat = tokens[first : first + per].astype(f32).reshape(flat_rows, width)
        lens = doc_lengths[first : first + per]
        upstream = out_grad[first : first + per].reshape(flat_rows, width)
        n1 = normed(xflat, g1).astype(bf16)
        query = jnp.dot(n1, wq, preferred_element_type=f32).astype(bf16)
        key_local = jnp.dot(n1, wk, preferred_element_type=f32).astype(bf16)
        value_local = jnp.dot(n1, wv, preferred_element_type=f32).astype(bf16)
        keys_all, values_all = (
            lax.all_gather(key_local.reshape(per, span, width), "seq", axis=1, tiled=True),
            lax.all_gather(value_local.reshape(per, span, width), "seq", axis=1, tiled=True),
        )
        q4 = query.reshape(per, span, heads, head_dim)
        k4 = keys_all.reshape(per, total, heads, head_dim)
        v4 = values_all.reshape(per, total, heads, head_dim)
        valid = k_pos[None, :] < lens[:, None]

        def scores():
            raw = jnp.einsum("bqhd,bkhd->bhqk", q4, k4, preferred_element_type=f32) + bias[None]
            return jnp.where(valid[:, None, None, :], raw, NEG)

        first_scores = scores()
        top = jnp.max(first_scores, axis=-1, keepdims=True)
        expo = jnp.exp(first_scores - top)
        denom = jnp.sum(expo, axis=-1, keepdims=True)
        probs_low = (expo / denom).astype(bf16)
        mixed = jnp.einsum("bhqk,bkhd->bqhd", probs_low, v4, preferred_element_type=f32)
        mixed = mixed.reshape(flat_rows, width).astype(bf16)
        h1 = xflat + jnp.dot(mixed, wo, preferred_element_type=f32)
        n2 = normed(h1, g2).astype(bf16)
        inner = jnp.dot(n2, wi, preferred_element_type=f32)
        act_full, gelu_pull = jax.vjp(jax.nn.gelu, inner)
        act = act_full.astype(bf16)
        result = h1 + jnp.dot(act, wf, preferred_element_type=f32)
        outputs.append(result.astype(bf16).reshape(per, span, width))
        grad_wf = grad_wf + jnp.einsum("tf,td->fd", act, upstream, preferred_element_type=f32)
        d_act = jnp.einsum("td,fd->tf", upstream, wf, preferred_element_type=f32)
        d_inner = gelu_pull(d_act)[0].astype(bf16)
        grad_wi = grad_wi + jnp.einsum("td,tf->df", n2, d_inner, preferred_element_type=f32)
        d_n2 = jnp.einsum("tf,df->td", d_inner, wi, preferred_element_type=f32)
        norm_pull = jax.vjp(normed, h1, g2)[1]
        dh_part, dg_two = norm_pull(d_n2)
        grad_g2 = grad_g2 + dg_two
        dh1 = upstream.astype(f32) + dh_part
        d_attn = dh1.astype(bf16)
        grad_wo = grad_wo + jnp.einsum("td,te->de", mixed, d_attn, preferred_element_type=f32)
        d_mixed = jnp.einsum("te,de->td", d_attn, wo, preferred_element_type=f32).astype(bf16)
        dm4 = d_mixed.reshape(per, span, heads, head_dim)
        probs = jnp.exp(scores() - top) / denom
        d_probs = jnp.einsum("bqhd,bkhd->bhqk", dm4, v4, preferred_element_type=f32)
        value_terms = jnp.einsum("bhqk,bqhd->bkhd", probs_low, dm4, preferred_element_type=f32)
        delta = jnp.sum(probs * d_probs, axis=-1, keepdims=True)
        d_scores = (probs * (d_probs - delta)).astype(bf16)
        grad_bias = grad_bias + jnp.sum(d_scores.astype(f32), axis=0)
        d_query = jnp.einsum("bhqk,bkhd->bqhd", d_scores, k4, preferred_element_type=f32)
        d_query = d_query.reshape(flat_rows, width).astype(bf16)
        key_terms = jnp.einsum("bhqk,bqhd->bkhd", d_scores, q4, preferred_element_type=f32)
        key_share, value_share = (
            lax.psum_scatter(
                key_terms.reshape(per, total, width), "seq", scatter_dimension=1, tiled=True
            ),
            lax.psum_scatter(
                value_terms.reshape(per, total, width), "seq", scatter_dimension=1, tiled=True
            ),
        )
        d_key = key_share.reshape(flat_rows, width).astype(bf16)
        d_value = value_share.reshape(flat_rows, width).astype(bf16)
        grad_wq = grad_wq + jnp.einsum("td,te->de", n1, d_query, preferred_element_type=f32)
        grad_wk = grad_wk + jnp.einsum("td,te->de", n1, d_key, preferred_element_type=f32)
        grad_wv = grad_wv + jnp.einsum("td,te->de", n1, d_value, preferred_element_type=f32)
        d_n1 = jnp.einsum("te,de->td", d_query, wq, preferred_element_type=f32)
        d_n1 = d_n1 + jnp.einsum("te,de->td", d_key, wk, preferred_element_type=f32)
        d_n1 = d_n1 + jnp.einsum("te,de->td", d_value, wv, preferred_element_type=f32)
        first_pull = jax.vjp(normed, xflat, g1)[1]
        dx_part, dg_one = first_pull(d_n1)
        grad_g1 = grad_g1 + dg_one
        input_grads.append((dh1 + dx_part).reshape(per, span, width))
    owned = (
        lax.psum_scatter(grad_wq, ("seq", "rows"), scatter_dimension=0, tiled=True),
        lax.psum_scatter(grad_wk, ("seq", "rows"), scatter_dimension=0, tiled=True),
        lax.psum_scatter(grad_wv, ("seq", "rows"), scatter_dimension=0, tiled=True),
        lax.psum_scatter(grad_wo, ("seq", "rows"), scatter_dimension=0, tiled=True),
        lax.psum_scatter(grad_wi, ("seq", "rows"), scatter_dimension=0, tiled=True),
        lax.psum_scatter(grad_wf, ("seq", "rows"), scatter_dimension=0, tiled=True),
        lax.psum_scatter(grad_g1, ("seq", "rows"), scatter_dimension=0, tiled=True),
        lax.psum_scatter(grad_g2, ("seq", "rows"), scatter_dimension=0, tiled=True),
    )
    grad_full = lax.dynamic_update_slice_in_dim(
        jnp.zeros((heads, total, total), f32), grad_bias, q_start, 1
    )
    widened = jnp.pad(grad_full, ((0, 0), (0, 0), (total - 1, 0)))
    folded = jnp.pad(widened.reshape(heads, total * (2 * total - 1)), ((0, 0), (0, total)))
    rel_grad = jnp.sum(folded.reshape(heads, total, 2 * total), axis=1)[:, : 2 * total - 1]
    table_local = jnp.dot(onehot.T, rel_grad.T, precision=HIGH)
    table_grad = lax.psum(table_local, ("seq", "rows"))
    result_rows = jnp.concatenate(outputs, axis=0)
    grad_rows = jnp.concatenate(input_grads, axis=0)
    return (
        result_rows,
        grad_rows,
        owned[0],
        owned[1],
        owned[2],
        owned[3],
        owned[4],
        owned[5],
        owned[6],
        owned[7],
        table_grad,
    )


MESH_ID = pl.DeviceIdType.MESH
HBM = pl.BlockSpec(memory_space=pl.ANY)
VMEM = pl.BlockSpec(memory_space=pltpu.VMEM)
SMEM = pl.BlockSpec(memory_space=pltpu.SMEM)
BF = jnp.bfloat16
F32 = jnp.float32
NX, NZ, NY, NC = 2, 4, 2, 2


def rcopy(src, dst, send, recv, to):
    return pltpu.make_async_remote_copy(
        src_ref=src, dst_ref=dst, send_sem=send, recv_sem=recv, device_id=to, device_id_type=MESH_ID
    )


class Place:
    def __init__(self):
        self.x = lax.axis_index("seq")
        r = lax.axis_index("rows")
        self.c = lax.rem(r, 2)
        self.y = lax.rem(r // 2, 2)
        self.z = r // 4
        self.core = self.at(self.x, self.y, self.z, 1 - self.c)
        self.xn = self.at(1 - self.x, self.y, self.z, self.c)
        self.yn = self.at(self.x, 1 - self.y, self.z, self.c)
        self.zp = [None] + [self.at(self.x, self.y, self.zz(j), self.c) for j in range(1, NZ)]

    def at(self, x, y, z, c):
        return (x, z * 4 + y * 2 + c)

    def zz(self, j):
        return lax.rem(self.z + j, NZ)

    def barrier(self):
        sem = pltpu.get_barrier_semaphore()
        peers = [self.core, self.xn, self.yn] + self.zp[1:]
        for p in peers:
            pl.semaphore_signal(sem, inc=1, device_id=p, device_id_type=MESH_ID)
        pl.semaphore_wait(sem, len(peers))


class GatherXZY:
    def __init__(self, me, w, base, nh, ss, rr, dd):
        self.me, self.w, self.ss, self.rr, self.dd = me, w, ss, rr, dd
        self.base, self.nh = base, nh

    def cols(self, plane, c):
        return pl.ds(pl.multiple_of(self.base(plane) + c * self.nh, 128), self.nh)

    def ref(self, x, z, y, c, plane):
        return self.w.at[x, z, y, :, self.cols(plane, c)]

    def pair(self, z, y, c):
        return self.w.at[:, z, y, :, self.cols(self.me.x, c)]

    def send(self, ref, s, recv, to):
        rcopy(ref, ref, self.ss.at[s], recv, to).start()

    def got(self, ref, recv):
        rcopy(ref, ref, self.ss.at[0], recv, self.me.core).wait_recv()

    def start(self):
        m = self.me
        self.send(self.ref(m.x, m.z, m.y, m.c, 1 - m.x), 0, self.rr.at[0], m.xn)

    def step_x(self):
        m = self.me
        self.got(self.ref(1 - m.x, m.z, m.y, m.c, m.x), self.rr.at[0])
        p = self.pair(m.z, m.y, m.c)
        for j in range(1, NZ):
            self.send(p, j, self.rr.at[NZ - j], m.zp[j])
        self.send(p, 4, self.rr.at[4], m.yn)
        self.send(p, 8, self.dd.at[0], m.core)

    def step_z(self, j):
        m = self.me
        p = self.pair(m.zz(j), m.y, m.c)
        self.got(p, self.rr.at[j])
        self.send(p, 4 + j, self.rr.at[4 + j], m.yn)
        self.send(p, 8 + j, self.dd.at[j], m.core)

    def step_y(self, j):
        m = self.me
        p = self.pair(m.zz(j), 1 - m.y, m.c)
        self.got(p, self.rr.at[4 + j])
        self.send(p, 12 + j, self.dd.at[4 + j], m.core)

    def done(self):
        m = self.me
        for j in range(NZ):
            self.got(self.pair(m.zz(j), m.y, 1 - m.c), self.dd.at[j])
        for j in range(NZ):
            self.got(self.pair(m.zz(j), 1 - m.y, 1 - m.c), self.dd.at[4 + j])

    def sent(self):
        m = self.me
        one = self.ref(m.x, m.z, m.y, m.c, m.x)
        rcopy(one, one, self.ss.at[0], self.rr.at[0], m.core).wait_send()
        p = self.pair(m.z, m.y, m.c)
        for s in range(1, 16):
            rcopy(p, p, self.ss.at[s], self.rr.at[0], m.core).wait_send()


class GatherZYX:
    def __init__(self, me, w, ss, rr, dd):
        self.me, self.w, self.ss, self.rr, self.dd = me, w, ss, rr, dd

    def send(self, ref, s, recv, to):
        rcopy(ref, ref, self.ss.at[s], recv, to).start()

    def got(self, ref, recv):
        rcopy(ref, ref, self.ss.at[0], recv, self.me.core).wait_recv()

    def start(self):
        m = self.me
        own = self.w.at[m.x, m.z, m.y, m.c]
        for j in range(1, NZ):
            self.send(own, j - 1, self.rr.at[NZ - j - 1], m.zp[j])
        self.send(own, 3, self.rr.at[3], m.yn)

    def step_z(self, j):
        m = self.me
        b = self.w.at[m.x, m.zz(j), m.y, m.c]
        self.got(b, self.rr.at[j - 1])
        self.send(b, 5 + j, self.rr.at[3 + j], m.yn)

    def step_y(self, j):
        m = self.me
        self.got(self.w.at[m.x, m.zz(j), 1 - m.y, m.c], self.rr.at[3 + j])
        p = self.w.at[m.x, m.zz(j), :, m.c]
        self.send(p, 4 if j == 0 else 8 + j, self.rr.at[7 + j], m.xn)
        self.send(p, 5 if j == 0 else 11 + j, self.dd.at[j], m.core)

    def step_x(self, j):
        m = self.me
        p = self.w.at[1 - m.x, m.zz(j), :, m.c]
        self.got(p, self.rr.at[7 + j])
        self.send(p, 15 + j, self.dd.at[4 + j], m.core)

    def done_near(self):
        m = self.me
        for j in range(NZ):
            self.got(self.w.at[m.x, m.zz(j), :, 1 - m.c], self.dd.at[j])

    def done_far(self):
        m = self.me
        for j in range(NZ):
            self.got(self.w.at[1 - m.x, m.zz(j), :, 1 - m.c], self.dd.at[4 + j])

    def sent(self):
        m = self.me
        one = self.w.at[m.x, m.z, m.y, m.c]
        p = self.w.at[m.x, m.z, :, m.c]
        for s in range(19):
            r = one if s in (0, 1, 2, 3, 6, 7, 8) else p
            rcopy(r, r, self.ss.at[s], self.rr.at[0], m.core).wait_send()


def own_block(me, mine, theirs, w, parts):
    a = mine[...].astype(F32)[:24]
    b = theirs[...].astype(F32)[:24]
    first = jnp.where(me.c == 0, a, b)
    second = jnp.where(me.c == 0, b, a)
    both = jnp.concatenate([first, second], axis=0).astype(BF)
    at = 0
    for n, base in parts:
        w[me.x, me.z, me.y, :, pl.ds(pl.multiple_of(base, 128), n)] = both[:, at : at + n]
        at += n


class Piece:
    def __init__(self, index, rows, first):
        self.index, self.slot, self.rows = index, index % 2, rows
        cut = rows // 2 if rows // 2 % 16 == 0 else rows // 2 + 8
        self.subs = ((0, cut, first[0]), (cut, rows - cut, first[1]))


def acc_rows(x, y, z, lo, n):
    return pl.ds(pl.multiple_of(((x * NY + y) * NZ + z) * 192 + lo, 8), n)


class Reduce:
    def __init__(self, me, acc, a1, a2, a3, cs, cr, s1s, s1r, s2s, s2r, s3s, s3r, fin, finr, keep, sems):
        self.me = me
        self.acc, self.a1, self.a2, self.a3, self.cs, self.cr = acc, a1, a2, a3, cs, cr
        self.s1s, self.s1r, self.s2s, self.s2r, self.s3s, self.s3r = s1s, s1r, s2s, s2r, s3s, s3r
        self.fin, self.finr = fin, finr
        self.keep = keep
        (self.c_s, self.c_r, self.a_s, self.a_r, self.b_s, self.b_r, self.z_s, self.z_r, self.f_s, self.f_r) = sems

    def near(self, axis):
        return self.me.xn if axis == "x" else self.me.yn

    def core_copy(self, p):
        s, n = p.slot, p.rows
        return rcopy(
            self.cs.at[:, :, :, 0:n], self.cr.at[s, :, :, :, 0:n], self.c_s.at[s], self.c_r.at[s], self.me.core
        )

    def one_copy(self, p, k):
        s, (_, n, axis) = p.slot, p.subs[k]
        return rcopy(
            self.s1s.at[k, :, :, 0:n], self.s1r.at[s, k, :, :, 0:n], self.a_s.at[s, k], self.a_r.at[s, k], self.near(axis)
        )

    def two_copy(self, p, k):
        s, (_, n, axis) = p.slot, p.subs[k]
        to = self.near("y" if axis == "x" else "x")
        return rcopy(self.s2s.at[k, :, 0:n], self.s2r.at[s, k, :, 0:n], self.b_s.at[s, k], self.b_r.at[s, k], to)

    def z_copy(self, p, j):
        s, n = p.slot, p.rows
        return rcopy(
            self.s3s.at[j, 0:n], self.s3r.at[s, NZ - j, 0:n], self.z_s.at[s, j], self.z_r.at[s, NZ - j], self.me.zp[j]
        )

    def fin_copy(self, p):
        i, n = p.index, p.rows // 2
        return rcopy(
            self.fin.at[i, 0:n], self.finr.at[i, 0:n], self.f_s.at[i], self.f_r.at[i], self.me.core
        )

    def send_core(self, p):
        self.core_copy(p).start()

    def h1(self, p, old):
        me, s, n = self.me, p.slot, p.rows
        self.core_copy(p).wait_recv()
        for k, (lo, n, axis) in enumerate(p.subs):
            if old is not None:
                self.one_copy(old, k).wait_send()
            rows = pl.ds(lo, n)

            def body(q, carry):
                a, zq = q // NZ, lax.rem(q, NZ)
                if axis == "x":
                    keep, away = (me.x, a, zq, rows), (1 - me.x, a, zq, rows)
                else:
                    keep, away = (a, me.y, zq, rows), (a, 1 - me.y, zq, rows)
                held = [self.acc[acc_rows(*at[:3], lo, n), :] for at in (keep, away)]
                self.a1[k, a, zq, 0:n] = held[0] + self.cr[(s,) + keep].astype(F32)
                self.s1s[k, a, zq, 0:n] = (held[1] + self.cr[(s,) + away].astype(F32)).astype(BF)
                return carry

            lax.fori_loop(0, 2 * NZ, body, 0)
            self.one_copy(p, k).start()

    def h2(self, p, old):
        me, s = self.me, p.slot
        for k, (lo, n, axis) in enumerate(p.subs):
            self.one_copy(p, k).wait_recv()
            if old is not None:
                self.two_copy(old, k).wait_send()
            b = me.y if axis == "x" else me.x

            def body(zq, carry):
                self.a2[k, zq, 0:n] = self.a1[k, b, zq, 0:n] + self.s1r[s, k, b, zq, 0:n].astype(F32)
                self.s2s[k, zq, 0:n] = (
                    self.a1[k, 1 - b, zq, 0:n] + self.s1r[s, k, 1 - b, zq, 0:n].astype(F32)
                ).astype(BF)
                return carry

            lax.fori_loop(0, NZ, body, 0)
            self.two_copy(p, k).start()

    def h3(self, p, old):
        me, s = self.me, p.slot
        for k in range(2):
            self.two_copy(p, k).wait_recv()
        for j in range(1, NZ):
            if old is not None:
                self.z_copy(old, j).wait_send()
        for k, (lo, n, _) in enumerate(p.subs):
            rows = pl.ds(lo, n)
            for j in range(NZ):
                zq = me.zz(j)
                v = self.a2[k, zq, 0:n] + self.s2r[s, k, zq, 0:n].astype(F32)
                if j == 0:
                    self.a3[rows] = v
                else:
                    self.s3s[j, rows] = v.astype(BF)
        for j in range(1, NZ):
            self.z_copy(p, j).start()

    def h4(self, p):
        me, s, n, i = self.me, p.slot, p.rows, p.index
        for j in range(1, NZ):
            self.z_copy(p, NZ - j).wait_recv()
        total = self.a3[0:n]
        for j in range(1, NZ):
            total = total + self.s3r[s, j, 0:n].astype(F32)
        if p.groups is None:
            a, b = total[0 : n // 2], total[n // 2 :]
        else:
            a, b = (
                jnp.concatenate([total[48 * g + 24 * k : 48 * g + 24 * k + 24] for g in range(p.groups)], axis=0)
                for k in range(NC)
            )
        self.fin[i, 0 : n // 2] = jnp.where(me.c == 0, b, a)
        self.keep(p, jnp.where(me.c == 0, a, b), me.c)
        self.fin_copy(p).start()


def norm_back(h, gain, up):
    r = lax.rsqrt(jnp.mean(h * h, axis=-1, keepdims=True) + EPS)
    hr = h * r
    w = up * gain
    dgain = jnp.sum(up * hr, axis=0, keepdims=True)
    return r * (w - hr * jnp.mean(w * hr, axis=-1, keepdims=True)), dgain


def layer_kernel(
    tok, gin, gains, wq, wk, wv, wo, wi, pd, relb, table, lens,
    act_o, dx_o, gq_o, gk_o, gv_o, go_o, gi_o, gf_o, sm_o,
    WA, WB, WD, X, G, N2, QKV, O, H1, ACT, DU, T, M, MACC, LSE, R, RG,
    ACC, A1, A2, A3, CS, CR, S1S, S1R, S2S, S2R, S3S, S3R, FIN, FINR, SM, SMR, ZB, DG,
    ts, tr, tl, gs, gr, gl, es, er, as_, ar, ad, a2s, a2r, a2d, os_, or_, od, bs, br, bd, b2s, b2r, b2d, ds_, dr, dd, ys, yr, yl, xs_, xr, xl,
    c_s, c_r, a_s, a_r, b_s, b_r, z_s, z_r, f_s, f_r, ms, mr,
):
    me = Place()
    x, y, z, c = me.x, me.y, me.z, me.c
    mine, span, width = X.shape[0], X.shape[2], X.shape[3]
    length = 2 * span
    flat = mine * length
    ff = DU.shape[1]
    na, nb = WA.shape[4] // 2, WB.shape[4] // 2
    PA, PB = DU.at[pl.ds(32 * c, 32), 0:na], DU.at[pl.ds(64 + 32 * c, 32), 0:nb]
    RA, RB = DU.at[128:160, 0:na], DU.at[160:192, 0:nb]
    hd = 64
    YB = N2
    pairs = width // hd // 2
    half_ff, half_w = ff // 2, width // 2
    n1, n2_ = (256 + 3 * 256) // 2, 3 * (width - 256) // 2
    gath_a = GatherXZY(me, WA, lambda plane: 0, n1, as_, ar, ad)
    gath_e = GatherXZY(me, WA, lambda plane: 2 * n1, n2_, a2s, a2r, a2d)
    gath_o = GatherXZY(me, WB, lambda plane: 0, half_w, os_, or_, od)
    gath_1 = GatherXZY(me, WB, lambda plane: width + half_ff * plane, half_ff // 2, bs, br, bd)
    gath_2 = GatherXZY(me, WB, lambda plane: width + half_ff * (1 - plane), half_ff // 2, b2s, b2r, b2d)
    gath_d = GatherZYX(me, WD, ds_, dr, dd)

    def pack(first, n, parts):
        filled = [
            jnp.concatenate([p.astype(F32), jnp.zeros((32 - p.shape[0], p.shape[1]), F32)], axis=0) for p in parts
        ]
        DU[first : first + 32, 0:n] = jnp.concatenate(filled, axis=1).astype(BF)

    quarter = half_ff // 2
    part = width - 256
    pack(0, na, (gains[...], wq[:, 0:256], wq[:, 256:], wk[:, 256 : 256 + part // 2]))
    pack(32, na, (wk[:, 0:256], wv[:, 0:256], wk[:, 256 + part // 2 :], wv[:, 256:]))
    me.barrier()
    ea = rcopy(DU.at[pl.ds(32 * (1 - c), 32), 0:na], RA, es.at[0], er.at[0], me.core)
    eb = rcopy(DU.at[pl.ds(64 + 32 * (1 - c), 32), 0:nb], RB, es.at[1], er.at[1], me.core)
    ea.start()
    for k in range(2):
        first = wi[:, quarter * k : quarter * k + quarter]
        second = wi[:, half_ff + quarter * k : half_ff + quarter * k + quarter]
        pack(64 + 32 * k, nb, (wo[:, half_w * k : half_w * k + half_w], first, second))
    eb.start()
    tok_r = [rcopy(tok.at[2 * (1 - x) + i], X.at[i, x], ts.at[i], tr.at[i], me.xn) for i in range(mine)]
    tok_in = [rcopy(X.at[i, 1 - x], X.at[i, 1 - x], ts.at[i], tr.at[i], me.xn) for i in range(mine)]
    tok_l = [pltpu.make_async_copy(tok.at[2 * x + i], X.at[i, x], tl.at[i]) for i in range(mine)]
    g_r = rcopy(gin.at[pl.ds(2 * (1 - x), 2)], G.at[:, x], gs, gr, me.xn)
    g_in = rcopy(G.at[:, 1 - x], G.at[:, 1 - x], gs, gr, me.xn)
    g_l = pltpu.make_async_copy(gin.at[pl.ds(2 * x, 2)], G.at[:, x], gl)
    ea.wait_recv()
    own_block(me, PA, RA, WA, ((n1, c * n1), (n2_, 2 * n1 + c * n2_)))
    gath_a.start()
    for i in range(mine):
        tok_r[i].start()
        tok_l[i].start()
    g_l.start()
    eb.wait_recv()
    own_block(
        me, PB, RB, WB,
        ((half_w, c * half_w), (quarter, width + c * quarter), (quarter, width + half_ff + c * quarter)),
    )
    WD[x, z, y, c] = pd[...]
    cols = relb.shape[1]
    kinds = table.shape[0]
    hot = (lax.broadcasted_iota(jnp.int32, (kinds, cols), 0) == relb[...]).astype(BF)
    R[...] = lax.dot_general(table[...], hot, (((0,), (0,)), ((), ())), preferred_element_type=F32)[0:16]
    gath_a.step_x()
    gath_e.start()
    gath_o.start()
    gath_1.start()
    gath_d.start()
    for j in range(1, NZ):
        gath_a.step_z(j)
    gath_e.step_x()
    for j in range(NZ):
        gath_a.step_y(j)
    gath_o.step_x()
    gath_1.step_x()
    gath_d.step_y(0)
    for j in range(1, NZ):
        gath_e.step_z(j)
    gath_a.done()

    def gain_row(k):
        return jnp.transpose(WA[:, :, :, :, 128 * k : 128 * k + 128].reshape(width, 128).astype(F32))[0:1, :]

    gain1 = gain_row(0)

    def row_slice(i):
        return pl.ds(pl.multiple_of(i * length, length), length)

    def first_norm(i):
        for half in range(2):
            xf = X[i, half].astype(F32)
            scale = lax.rsqrt(jnp.mean(xf * xf, axis=-1, keepdims=True) + EPS)
            N2[i, half] = (xf * scale * gain1).astype(BF)

    def project(i, first, count):
        for n in range(count):
            lo = (first + n) * width
            QKV[row_slice(i), lo : lo + width] = jnp.dot(
                N2[i].reshape(length, width),
                WA[:, :, :, :, 256 + lo : 256 + lo + width].reshape(width, width),
                preferred_element_type=F32,
            ).astype(BF)

    for i in range(mine):
        tok_l[i].wait()
        tok_in[i].wait_recv()
        first_norm(i)
        project(i, 0, 1)
    gath_2.start()
    g_r.start()
    low = lax.broadcasted_iota(jnp.int32, (1, 128), 1) < hd
    lane = lax.broadcasted_iota(jnp.int32, (1, 128), 1)
    kpos = lax.broadcasted_iota(jnp.int32, (length, 128), 0)
    blocks = length // 128

    def strips(p):
        for h in range(2):
            row = jnp.broadcast_to(R[pl.ds(2 * p + h, 1), :], (128, cols))
            M[h] = pltpu.roll(row, cols - 127, 1, stride=1, stride_axis=0)[:, : M.shape[2]]

    def bias_of(h):
        return jnp.concatenate(
            [M[h, :, 128 * (blocks - 1 - a) : 128 * (blocks - 1 - a) + length] for a in range(blocks)], axis=0
        )

    own = (low, jnp.logical_not(low))
    spare = (hd, 0)
    ones = [(lane == spare[h]).astype(F32).astype(BF) for h in range(2)]
    none = jnp.zeros((), BF)

    def masked_keys(h, k, count):
        pad = jnp.where((lane == spare[h]) & (kpos >= count), NEG, 0.0).astype(BF)
        return jnp.where(own[h], k, pad)

    def lanes(n, p):
        at = jnp.where(p < 2, n * 256 + p * 128, width + n * (width - 256) + (p - 2) * 128)
        return pl.ds(pl.multiple_of(at, 128), 128)

    def wide_lanes(p):
        return pl.ds(pl.multiple_of(p * 128, 128), 128)

    nt = (((1,), (1,)), ((), ()))
    tn = (((0,), (0,)), ((), ()))

    def mm(a, b, dims):
        return lax.dot_general(a, b, dims, preferred_element_type=F32)

    o_, b1, b2, d_, e_ = gath_o, gath_1, gath_2, gath_d, gath_e
    comm = {
        0: ((e_.step_y, 0), (e_.step_y, 1)),
        1: ((e_.step_y, 2), (e_.step_y, 3)),
        2: ((o_.step_z, 1), (b1.step_z, 1), (d_.step_z, 1)),
        3: ((o_.step_z, 2), (b1.step_z, 2), (d_.step_z, 2)),
        4: ((o_.step_z, 3), (b1.step_z, 3), (d_.step_z, 3), (lambda j: b2.step_x(), 0)),
        5: ((o_.step_y, 0), (b1.step_y, 0), (d_.step_y, 1)),
        6: ((o_.step_y, 1), (b1.step_y, 1), (d_.step_y, 2)),
        7: ((o_.step_y, 2), (b1.step_y, 2), (d_.step_y, 3)),
        8: ((o_.step_y, 3), (b1.step_y, 3), (d_.step_x, 0), (b2.step_z, 1)),
        9: ((b2.step_z, 2), (d_.step_x, 1)),
        10: ((b2.step_z, 3), (b2.step_y, 0), (d_.step_x, 2)),
        11: ((b2.step_y, 1), (d_.step_x, 3)),
    }

    def attend(t, carry):
        p, i = t // mine, lax.rem(t, mine)
        pl.when(i == 0)(lambda: strips(p))
        rows = row_slice(i)
        q, k, v = QKV[rows, lanes(0, p)], QKV[rows, lanes(1, p)], QKV[rows, lanes(2, p)]
        outs = []
        for h in range(2):
            s = mm(jnp.where(own[h], q, ones[h]), masked_keys(h, k, lens[2 * x + i]), nt) + bias_of(h)
            top = jnp.max(s, axis=-1, keepdims=True)
            e = jnp.exp(s - top)
            total = jnp.sum(e, axis=-1, keepdims=True)
            LSE[rows, :] = jnp.where(lane == 2 * p + h, top + jnp.log(total), LSE[rows, :])
            outs.append(jnp.dot((e * (1.0 / total)).astype(BF), v, preferred_element_type=F32))
        O[i, :, :, wide_lanes(p)] = jnp.where(low, outs[0], outs[1]).astype(BF).reshape(2, span, 128)
        for at, steps in comm.items():
            @pl.when(t == at)
            def _():
                for step, j in steps:
                    step(j)
        return carry

    LSE[...] = jnp.zeros_like(LSE)
    lax.fori_loop(0, 2 * mine, attend, 0)
    gath_e.done()
    for i in range(mine):
        project(i, 1, 2)
    lax.fori_loop(2 * mine, mine * pairs, attend, 0)
    ea.wait_send()
    eb.wait_send()
    gath_o.done()
    gath_1.done()
    gath_d.done_near()
    g_l.wait()
    g_in.wait_recv()

    gain2 = gain_row(1)
    DG[...] = jnp.zeros_like(DG)
    c0, c1 = 0.7978845608028654, 0.044715

    def dn_set(v):
        for n in range(width // 128):
            ACC[length * n : length * n + length, :] = v[:, 128 * n : 128 * n + 128]

    def dn_get(lo, n):
        return jnp.concatenate([ACC[length * k + lo : length * k + lo + n, :] for k in range(width // 128)], axis=1)

    def dn_add(v):
        for n in range(width // 128):
            at = slice(length * n, length * n + length)
            ACC[at, :] = ACC[at, :] + v[:, 128 * n : 128 * n + 128]

    wo_all = lambda: WB[:, :, :, :, 0:width].reshape(width, width)
    for i in range(mine):
        h1 = X[i].reshape(length, width).astype(F32) + jnp.dot(
            O[i].reshape(length, width), wo_all(), preferred_element_type=F32
        )
        H1[i] = h1.reshape(2, span, width)
        r = lax.rsqrt(jnp.mean(h1 * h1, axis=-1, keepdims=True) + EPS)
        N2[i] = (h1 * r * gain2).astype(BF).reshape(2, span, width)

    def chunk(n, carry):
        @pl.when(n == 2)
        def _():
            gath_2.done()
            gath_d.done_far()

        f = lax.rem(2 * x + n, 4)

        def one_row(i, carry):
            pl.when((n == 0) & (i == 0))(lambda: gath_2.step_y(2))
            pl.when((n == 0) & (i == 1))(lambda: gath_2.step_y(3))
            n2, g = N2[i].reshape(length, width), G[i].reshape(length, width)
            for part in range(3):
                fcols = pl.ds(pl.multiple_of(f * width + 256 * part, 256), 256)
                wcols = pl.ds(pl.multiple_of(width + f * width + 256 * part, 256), 256)
                wi_part = WB[:, :, :, :, wcols].reshape(width, 256)
                wf_part = WD[f // 2, pl.ds(2 * lax.rem(f, 2), 2)].reshape(width, width)[256 * part : 256 * part + 256]
                u = jnp.dot(n2, wi_part, preferred_element_type=F32)
                da = mm(g, wf_part, nt)
                sq = u * u
                t = jnp.tanh(u * (c0 + (c0 * c1) * sq))
                cdf = 0.5 + 0.5 * t
                ACT[row_slice(i), fcols] = (u * cdf).astype(BF)
                slope = cdf + (0.5 * u) * (1.0 - t * t) * (c0 + (3.0 * c0 * c1) * sq)
                DU[row_slice(i), fcols] = (da * slope).astype(BF)
            return carry

        return lax.fori_loop(0, mine, one_row, carry)

    lax.fori_loop(0, ff // width, chunk, 0)
    def keep(p, value, core):
        if p.groups is None:
            gf_o[:, pl.ds(pl.multiple_of(256 * p.part + 128 * core, 128), 128)] = value
            return
        for g in range(p.groups):
            if p.kind == "i":
                dst, base = gi_o, 1024 * p.part + 256 * g
            elif p.kind == "o":
                dst, base = go_o, 256 * g
            else:
                dst, base = (gq_o, gk_o, gv_o)[g], 256 * p.part
            dst[:, pl.ds(pl.multiple_of(base + 128 * core, 128), 128)] = value[24 * g : 24 * g + 24]

    red = Reduce(
        me, ACC, A1, A2, A3, CS, CR, S1S, S1R, S2S, S2R, S3S, S3R, FIN, FINR, keep, (c_s, c_r, a_s, a_r, b_s, b_r, z_s, z_r, f_s, f_r)
    )
    pieces = []
    kinds_of = [("f", 0), ("f", 1), ("f", 2), ("i", 0), ("i", 1), ("i", 2), ("o", 0), ("qkv", 0), ("qkv", 1), ("qkv", 2)]
    made_at = [0, 2, 4, 5, 6, 7, 8, 13, 15, 17]
    last = len(kinds_of)
    for n in range(last):
        kind, part = kinds_of[n]
        piece = Piece(n, 144 if kind in ("o", "qkv") else 192, ("y", "y") if n < last - 1 else ("x", "x"))
        piece.kind, piece.part = kind, part
        piece.groups = None if kind == "f" else piece.rows // 48
        pieces.append(piece)

    def stages(n):
        def at(k):
            return pieces[made_at.index(n - k)] if n - k in made_at else None

        def old(p):
            return pieces[p.index - 1] if p.index else None

        if at(4):
            red.h4(at(4))
        if at(3):
            red.h3(at(3), old(at(3)))
        if at(2):
            red.h2(at(2), old(at(2)))
        if at(1):
            red.h1(at(1), old(at(1)))
        if at(0):
            if old(at(0)):
                red.core_copy(old(at(0))).wait_send()
            produce(at(0))

    def split(res):
        a, b = res[:, 0:128], res[:, 128:256]
        return jnp.where(c == 0, a, b), jnp.where(c == 0, b, a).astype(BF)

    def outer_piece(j):

        def body(q, carry):
            xq, zh = q // 2, lax.rem(q, 2)
            lhs = ACT[:, pl.ds(pl.multiple_of(q * 768, 768), 768)]
            rhs = G[:, :, :, 256 * j : 256 * j + 256].reshape(flat, 256)
            own, other = split(mm(lhs, rhs, tn))
            for b in range(4):
                at = (xq, b % 2, 2 * zh + b // 2)
                ACC[acc_rows(*at, 0, 192), :] = own[192 * b : 192 * b + 192]
                CS[at] = other[192 * b : 192 * b + 192]
            return carry

        lax.fori_loop(0, 4, body, 0)

    def rows_piece(groups, rhs):
        def body(g, carry):
            own, other = split(jnp.dot(T[...], rhs(g), preferred_element_type=F32))
            at = pl.ds(pl.multiple_of(48 * g, 48), 48)
            for k in range(NX * NZ * NY):
                ACC[acc_rows(k // 8, k % 2, (k // 2) % 4, 48 * g, 48), :] = own[48 * k : 48 * k + 48]
                CS[k // 8, k % 2, (k // 2) % 4, at] = other[48 * k : 48 * k + 48]
            return carry

        lax.fori_loop(0, groups, body, 0)

    def produce(p):
        if p.kind == "f":
            outer_piece(p.part)
        elif p.kind == "i":
            rows_piece(4, lambda g: DU[:, pl.ds(pl.multiple_of(1024 * p.part + 256 * g, 256), 256)])
        elif p.kind == "o":
            T[...] = jnp.transpose(O[...].reshape(flat, width))
            rows_piece(3, lambda g: H1[:, :, :, pl.ds(pl.multiple_of(256 * g, 256), 256)].reshape(flat, 256).astype(BF))
        else:
            base, wide = (0, 256) if p.part == 0 else (width + 256 * (p.part - 1), width - 256)
            rows_piece(3, lambda g: QKV[:, pl.ds(pl.multiple_of(base + g * wide, 256), 256)])
        red.send_core(p)

    stages(0)
    T[...] = jnp.transpose(N2[...].reshape(flat, width))
    stages(1)

    def result(t, carry):
        i, f = t // 4, lax.rem(t, 4)
        a = ACT[row_slice(i), pl.ds(pl.multiple_of(f * width, width), width)]
        wf = WD[f // 2, pl.ds(2 * lax.rem(f, 2), 2)].reshape(width, width)
        out = jnp.dot(a, wf, preferred_element_type=F32)

        @pl.when(f == 0)
        def _():
            dn_set(H1[i].reshape(length, width) + out)

        @pl.when(f > 0)
        def _():
            dn_add(out)

        @pl.when(f == 3)
        def _():
            YB[i] = dn_get(0, length).astype(BF).reshape(2, span, width)

        return carry

    lax.fori_loop(0, 4 * mine, result, 0)
    y_out = [
        rcopy(YB.at[i, 1 - x], act_o.at[2 * (1 - x) + i], ys.at[i], yr.at[i], me.xn) for i in range(mine)
    ]
    y_loc = [pltpu.make_async_copy(YB.at[i, x], act_o.at[2 * x + i], yl.at[i]) for i in range(mine)]
    for i in range(mine):
        rcopy(YB.at[i, 1 - x], act_o.at[2 * x + i], ys.at[i], yr.at[i], me.xn).start()
        y_loc[i].start()

    stages(2)
    stages(3)

    def back(t, carry):
        i, f = t // 4, lax.rem(t, 4)
        du = DU[row_slice(i), pl.ds(pl.multiple_of(f * width, width), width)]
        wi_part = WB[:, :, :, :, pl.ds(pl.multiple_of((f + 1) * width, width), width)].reshape(width, width)
        out = mm(du, wi_part, nt)

        @pl.when(f == 0)
        def _():
            dn_set(out)

        @pl.when(f > 0)
        def _():
            dn_add(out)

        @pl.when(f == 3)
        def _():
            for half in range(2):
                dh, dgain = norm_back(H1[i, half], gain2, dn_get(span * half, span))
                DG[1:2, :] = DG[1:2, :] + dgain
                H1[i, half] = G[i, half].astype(F32) + dh

        return carry

    lax.fori_loop(0, 4 * mine, back, 0)

    stages(4)
    for i in range(mine):
        dab = H1[i].reshape(length, width).astype(BF)
        G[i] = mm(dab, wo_all(), nt).astype(BF).reshape(2, span, width)
    landing = lambda i: DU.at[pl.ds(i * span, span), 0:width]
    dx_r = [rcopy(X.at[i, 1 - x], landing(i), xs_.at[i], xr.at[i], me.xn) for i in range(mine)]
    dx_l = [pltpu.make_async_copy(H1.at[i, x], dx_o.at[2 * x + i], xl.at[i]) for i in range(mine)]
    dx_f = [pltpu.make_async_copy(H1.at[i, 1 - x], dx_o.at[2 * (1 - x) + i], xl.at[mine + i]) for i in range(mine)]

    def input_grad(i):
        for n in range(3):
            out = mm(
                QKV[row_slice(i), n * width : (n + 1) * width],
                WA[:, :, :, :, 256 + n * width : 256 + (n + 1) * width].reshape(width, width),
                nt,
            )
            (dn_set if n == 0 else dn_add)(out)
        for half in range(2):
            dh, dgain = norm_back(X[i, half].astype(F32), gain1, dn_get(span * half, span))
            DG[0:1, :] = DG[0:1, :] + dgain
            H1[i, half] = H1[i, half] + dh
        X[i, 1 - x] = H1[i, 1 - x].astype(BF)
        dx_r[i].start()
        dx_l[i].start()

    def norm_again():
        for i in range(mine):
            y_out[i].wait_recv()
            y_out[i].wait_send()
            y_loc[i].wait()
        for i in range(mine):
            first_norm(i)
        T[...] = jnp.transpose(N2[...].reshape(flat, width))

    def attend_back(t, carry):
        i, p = t // pairs, lax.rem(t, pairs)
        strips(p)
        MACC[...] = jnp.zeros_like(MACC)
        rows = row_slice(i)
        q, k, v = QKV[rows, lanes(0, p)], QKV[rows, lanes(1, p)], QKV[rows, lanes(2, p)]
        do = G[i, :, :, wide_lanes(p)].reshape(length, 128)
        prod = do.astype(F32) * O[i, :, :, wide_lanes(p)].reshape(length, 128).astype(F32)
        dqs, dks, dvs = [], [], []
        for h in range(2):
            lse = jnp.sum(jnp.where(lane == 2 * p + h, LSE[rows, :], 0.0), axis=-1, keepdims=True)
            delta = jnp.sum(jnp.where(own[h], prod, 0.0), axis=-1, keepdims=True)
            s = mm(jnp.where(own[h], q, ones[h]), masked_keys(h, k, lens[2 * x + i]), nt) + bias_of(h)
            pr = jnp.exp(s - lse)
            ds = pr * (mm(jnp.where(own[h], do, none), v, nt) - delta)
            for a in range(blocks):
                at = 128 * (blocks - 1 - a)
                MACC[h, :, at : at + length] = MACC[h, :, at : at + length] + ds[128 * a : 128 * a + 128]
            low_p, low_ds = pr.astype(BF), ds.astype(BF)
            dqs.append(jnp.dot(low_ds, k, preferred_element_type=F32))
            dks.append(mm(low_ds, q, tn))
            dvs.append(mm(low_p, do, tn))
        for n, parts in enumerate((dqs, dks, dvs)):
            QKV[rows, lanes(n, p)] = jnp.where(low, parts[0], parts[1]).astype(BF)

        for h in range(2):
            part = jnp.zeros((8, cols), F32)
            for a in range(16):
                part = part + pltpu.roll(MACC[h, 8 * a : 8 * a + 8, :], (cols - 8 * a) % cols, 1)
            line = part[0:1]
            for a in range(1, 8):
                line = line + pltpu.roll(part[a : a + 1], cols - a, 1)
            at = pl.ds(2 * p + h, 1)
            RG[at, :] = RG[at, :] + pltpu.roll(line, 127, 1)

        for n in range(mine * pairs):
            @pl.when(t == n)
            def _():
                stages(5 + n)
                if n == pairs - 1:
                    norm_again()
                if n == pairs:
                    input_grad(0)

        return carry

    RG[...] = jnp.zeros_like(RG)
    MACC[...] = jnp.zeros_like(MACC)
    lax.fori_loop(0, mine * pairs, attend_back, 0)

    stages(17)
    stages(18)
    input_grad(1)
    stages(19)
    stages(20)
    for n in range(width // 128):
        SM[0, n : n + 1, :] = DG[0:1, 128 * n : 128 * n + 128]
        SM[0, 8 + n : 9 + n, :] = DG[1:2, 128 * n : 128 * n + 128]
    rest = jnp.concatenate([RG[...], jnp.zeros((112, cols), F32)], axis=0)
    spread = jnp.zeros((kinds, 128), F32)
    for _ in range(3):
        part = rest.astype(BF)
        rest = rest - part.astype(F32)
        spread = spread + mm(hot, part, nt)
    SM[0, 16 : 16 + kinds, :] = spread
    sm_copies = [
        rcopy(SM.at[k], SMR.at[k], ms.at[k], mr.at[k], to) for k, to in enumerate((me.core, me.xn, me.yn))
    ]
    sm_copies[0].start()
    stages(21)
    for k in range(3):
        sm_copies[k].wait_recv()
        SM[k + 1] = SM[k] + SMR[k]
        if k < 2:
            sm_copies[k + 1].start()
    ZB[z] = SM[3]
    sm_z = [None] + [rcopy(SM.at[3], ZB.at[z], ms.at[2 + j], mr.at[6 - j], me.zp[j]) for j in range(1, NZ)]
    for j in range(1, NZ):
        sm_z[j].start()
    for i in range(mine):
        dx_r[i].wait_recv()
        H1[i, 1 - x] = DU[pl.ds(i * span, span), 0:width].astype(F32)
        dx_f[i].start()
    for p in pieces:
        red.fin_copy(p).wait_recv()
        keep(p, FINR[p.index, 0 : p.rows // 2], 1 - c)
    for j in range(1, NZ):
        rcopy(SM.at[3], ZB.at[me.zz(j)], ms.at[2 + j], mr.at[2 + j], me.zp[j]).wait_recv()
    sm_o[...] = ZB[0] + ZB[1] + ZB[2] + ZB[3]
    g_r.wait_send()
    for k in range(3):
        sm_copies[k].wait_send()
    for j in range(1, NZ):
        sm_z[j].wait_send()
    for g in (gath_a, gath_e, gath_o, gath_1, gath_2, gath_d):
        g.sent()
    for i in range(mine):
        tok_r[i].wait_send()
        dx_r[i].wait_send()
        dx_l[i].wait()
        dx_f[i].wait()
    for p in pieces[-1:]:
        red.core_copy(p).wait_send()
        for k in range(2):
            red.one_copy(p, k).wait_send()
            red.two_copy(p, k).wait_send()
        for j in range(1, NZ):
            red.z_copy(p, j).wait_send()
    for p in pieces:
        red.fin_copy(p).wait_send()


def layer_call(tok, gin, gains, wq, wk, wv, wo, wi, pd, relb, table, lens, heads):
    rows_dev, span, width = tok.shape
    length = 2 * span
    mine = rows_dev // 2
    flat = mine * length
    dma = pltpu.SemaphoreType.DMA
    ff = wi.shape[1]
    na, nb = (gains.shape[1] + 3 * width) // 2, (width + ff) // 2
    count = width // 256 + ff // 1024 + 4
    wa = (NX, NZ, NY, 48, 2 * na)
    wb = (NX, NZ, NY, 48, 2 * nb)
    wd = (NX, NZ, NY, NC) + pd.shape
    xs = (mine, 2, span, width)
    block = (192, 128)
    bf = lambda *s: pltpu.VMEM(s, BF)
    f32 = lambda *s: pltpu.VMEM(s, F32)
    out = lambda *s: jax.ShapeDtypeStruct(s, F32)
    shard = wq.shape[0]
    return pl.pallas_call(
        layer_kernel,
        out_shape=[jax.ShapeDtypeStruct(tok.shape, BF), out(*tok.shape)]
        + [out(shard, width)] * 4 + [out(shard, ff), out(*pd.shape), out(48, 128)],
        in_specs=[HBM, HBM] + [VMEM] * 9 + [SMEM],
        out_specs=[HBM, HBM] + [VMEM] * 7,
        scratch_shapes=[
            bf(*wa), bf(*wb), bf(*wd), bf(*xs), bf(*xs), bf(*xs), bf(flat, 3 * width), bf(*xs), f32(*xs),
             bf(flat, ff), bf(flat, ff), bf(width, flat), f32(2, 128, 896), f32(2, 128, 1024),
            f32(flat, 128), f32(16, relb.shape[1]), f32(16, relb.shape[1]),
            f32(NX * NY * NZ * 192, 128), f32(2, 2, NZ, 96, 128), f32(2, NZ, 96, 128), f32(*block), bf(NX, NY, NZ, *block), bf(2, NX, NY, NZ, *block),
            bf(2, 2, NZ, 96, 128), bf(2, 2, 2, NZ, 96, 128), bf(2, NZ, 96, 128), bf(2, 2, NZ, 96, 128),
            bf(NZ, *block), bf(2, NZ, *block), f32(count, 96, 128), f32(count, 96, 128),
            f32(4, 48, 128), f32(3, 48, 128), f32(NZ, 48, 128), f32(8, width),
            dma((2,)), dma((2,)), dma((2,)), dma, dma, dma, dma((2,)), dma((2,)),
            *[dma((n,)) for _ in range(5) for n in (16, 8, 8)], dma((19,)), dma((11,)), dma((8,)),
            dma((2,)), dma((2,)), dma((2,)), dma((2,)), dma((2,)), dma((4,)),
            dma((2,)), dma((2,)), dma((2, 2)), dma((2, 2)), dma((2, 2)), dma((2, 2)), dma((2, NZ)), dma((2, NZ)),
            dma((count,)), dma((count,)), dma((6,)), dma((6,)),
        ],
        compiler_params=pltpu.CompilerParams(
            collective_id=0, has_side_effects=True, vmem_limit_bytes=VMEM_LIMIT, fuse_transposed_lhs_in_matmul=True
        ),
        name="layer",
    )(tok, gin, gains, wq, wk, wv, wo, wi, pd, relb, table, lens)


VMEM_LIMIT = 67_000_000


def close_kernel(n_dev, *refs):
    srcs, small, dsts = refs[:8], refs[8], refs[9:17]
    g1, g2, table, sems = refs[17:]
    copies = []
    for k, (a, b) in enumerate(zip(srcs, dsts)):
        for i in range(a.shape[0] if len(a.shape) == 3 else 1):
            view = (a.at[i], b.at[i]) if len(a.shape) == 3 else (a, b)
            copies.append(pltpu.make_async_copy(*view, sems.at[len(copies)]))
    for cp in copies:
        cp.start()
    me = lax.axis_index("seq") * lax.axis_size("rows") + lax.axis_index("rows")
    cut = g1.shape[1]
    width = cut * n_dev
    for k, out in enumerate((g1, g2)):
        row = jnp.concatenate([small[8 * k + j : 8 * k + j + 1, :] for j in range(width // 128)], axis=1)
        out[...] = pltpu.roll(row, lax.rem(width - me * cut, width), 1)[:, 0:cut]
    table[...] = small[16 : 16 + table.shape[0], 0 : table.shape[1]]
    for cp in copies:
        cp.wait()


def close_call(arrays, small, cut, n_bins, heads):
    n_dev = NX * NZ * NY * NC
    like = [jax.ShapeDtypeStruct(a.shape, a.dtype) for a in arrays]
    out = lambda *s: jax.ShapeDtypeStruct(s, F32)
    count = sum(a.shape[0] if a.ndim == 3 else 1 for a in arrays)
    res = pl.pallas_call(
        functools.partial(close_kernel, n_dev),
        out_shape=like + [out(1, cut), out(1, cut), out(n_bins, heads)],
        in_specs=[HBM] * 8 + [VMEM],
        out_specs=[HBM] * 8 + [VMEM] * 3,
        scratch_shapes=[pltpu.SemaphoreType.DMA((count,))],
        name="close",
    )(*arrays, small)
    return (*res[:8], res[8].reshape(-1), res[9].reshape(-1), res[10])


def fast(
    tokens, doc_lengths, rel_buckets, w_query, w_key, w_value, w_output, w_inner, w_outer,
    attn_gain, ffn_gain, bias_table, out_grad,
):
    n_bins, heads = bias_table.shape
    wide = lambda g: jnp.broadcast_to(g[:, None], (g.shape[0], 128))
    gains = jnp.concatenate([wide(attn_gain), wide(ffn_gain)], axis=1)
    relb = jnp.pad(rel_buckets, (0, 1))[None, :]
    table = jnp.pad(bias_table, ((0, 0), (0, 128 - heads)))
    act, dx, gq, gk, gv, go, gi, gf, small = layer_call(
        tokens, out_grad, gains, w_query, w_key, w_value, w_output, w_inner, w_outer, relb, table, doc_lengths, heads
    )
    return close_call((act, dx, gq, gk, gv, go, gi, gf), small, attn_gain.shape[0], n_bins, heads)


def solution(mesh):
    split = P(("seq", "rows"), None)
    rows = P("rows", "seq", None)
    in_specs = (rows, P("rows"), P()) + (split,) * 6 + (P(("seq", "rows")),) * 2 + (P(), rows)
    out_specs = (rows, rows) + (split,) * 6 + (P(("seq", "rows")),) * 2 + (P(),)
    shape = (mesh.shape["seq"], mesh.shape["rows"])
    program = fast if shape == (NX, NZ * NY * NC) else local
    return jax.shard_map(program, mesh=mesh, in_specs=in_specs, out_specs=out_specs, check_vma=False)
```

```python
import functools

import jax
import jax.numpy as jnp
from jax import lax
from jax.experimental import pallas as pl
from jax.experimental.pallas import tpu as pltpu
from jax.sharding import PartitionSpec as P

MB = 2


EPS = 1e-06
NEG = -1000000000.0
HIGH = lax.Precision.HIGHEST


def normed(h, gain):
    return h * lax.rsqrt(jnp.mean(h * h, axis=-1, keepdims=True) + EPS) * gain


def fetch(shards):
    return (
        lax.all_gather(shards[0], ("seq", "rows"), axis=0, tiled=True),
        lax.all_gather(shards[1], ("seq", "rows"), axis=0, tiled=True),
        lax.all_gather(shards[2], ("seq", "rows"), axis=0, tiled=True),
        lax.all_gather(shards[3], ("seq", "rows"), axis=0, tiled=True),
        lax.all_gather(shards[4], ("seq", "rows"), axis=0, tiled=True),
        lax.all_gather(shards[5], ("seq", "rows"), axis=0, tiled=True),
        lax.all_gather(shards[6], ("seq", "rows"), axis=0, tiled=True),
        lax.all_gather(shards[7], ("seq", "rows"), axis=0, tiled=True),
    )


def local(
    tokens,
    doc_lengths,
    rel_buckets,
    w_query,
    w_key,
    w_value,
    w_output,
    w_inner,
    w_outer,
    attn_gain,
    ffn_gain,
    bias_table,
    out_grad,
):
    f32 = jnp.float32
    bf16 = jnp.bfloat16
    rows_dev, span, width = tokens.shape
    n_bins, heads = bias_table.shape
    head_dim = width // heads
    seq_count = lax.axis_size("seq")
    seq_place = lax.axis_index("seq")
    total = span * seq_count
    q_start = seq_place * span
    per = rows_dev // MB
    flat_rows = per * span
    shards = (w_query, w_key, w_value, w_output, w_inner, w_outer, attn_gain, ffn_gain)
    table = bias_table.astype(f32)
    k_pos = jnp.arange(total, dtype=jnp.int32)
    onehot = (rel_buckets[:, None] == jnp.arange(n_bins, dtype=jnp.int32)[None, :]).astype(f32)
    rel_bias = jnp.dot(onehot, table, precision=HIGH)
    spread = jnp.concatenate([rel_bias.T, jnp.zeros((heads, 1), f32)], axis=1)
    tiled = jnp.tile(spread, (1, total))
    full_bias = tiled[:, : total * (2 * total - 1)].reshape(heads, total, 2 * total - 1)[
        :, :, total - 1 :
    ]
    bias = lax.dynamic_slice_in_dim(full_bias, q_start, span, 1)
    ff_width = w_inner.shape[1]
    grad_wq = jnp.zeros((width, width), f32)
    grad_wk = jnp.zeros((width, width), f32)
    grad_wv = jnp.zeros((width, width), f32)
    grad_wo = jnp.zeros((width, width), f32)
    grad_wi = jnp.zeros((width, ff_width), f32)
    grad_wf = jnp.zeros((ff_width, width), f32)
    grad_g1 = jnp.zeros((width,), f32)
    grad_g2 = jnp.zeros((width,), f32)
    grad_bias = jnp.zeros((heads, span, total), f32)
    outputs = []
    input_grads = []
    for batch in range(MB):
        whole = fetch(shards)
        wq, wk, wv, wo, wi, wf, gain_one, gain_two = whole
        g1 = gain_one.astype(f32)
        g2 = gain_two.astype(f32)
        first = batch * per
        xflat = tokens[first : first + per].astype(f32).reshape(flat_rows, width)
        lens = doc_lengths[first : first + per]
        upstream = out_grad[first : first + per].reshape(flat_rows, width)
        n1 = normed(xflat, g1).astype(bf16)
        query = jnp.dot(n1, wq, preferred_element_type=f32).astype(bf16)
        key_local = jnp.dot(n1, wk, preferred_element_type=f32).astype(bf16)
        value_local = jnp.dot(n1, wv, preferred_element_type=f32).astype(bf16)
        keys_all, values_all = (
            lax.all_gather(key_local.reshape(per, span, width), "seq", axis=1, tiled=True),
            lax.all_gather(value_local.reshape(per, span, width), "seq", axis=1, tiled=True),
        )
        q4 = query.reshape(per, span, heads, head_dim)
        k4 = keys_all.reshape(per, total, heads, head_dim)
        v4 = values_all.reshape(per, total, heads, head_dim)
        valid = k_pos[None, :] < lens[:, None]

        def scores():
            raw = jnp.einsum("bqhd,bkhd->bhqk", q4, k4, preferred_element_type=f32) + bias[None]
            return jnp.where(valid[:, None, None, :], raw, NEG)

        first_scores = scores()
        top = jnp.max(first_scores, axis=-1, keepdims=True)
        expo = jnp.exp(first_scores - top)
        denom = jnp.sum(expo, axis=-1, keepdims=True)
        probs_low = (expo / denom).astype(bf16)
        mixed = jnp.einsum("bhqk,bkhd->bqhd", probs_low, v4, preferred_element_type=f32)
        mixed = mixed.reshape(flat_rows, width).astype(bf16)
        h1 = xflat + jnp.dot(mixed, wo, preferred_element_type=f32)
        n2 = normed(h1, g2).astype(bf16)
        inner = jnp.dot(n2, wi, preferred_element_type=f32)
        act_full, gelu_pull = jax.vjp(jax.nn.gelu, inner)
        act = act_full.astype(bf16)
        result = h1 + jnp.dot(act, wf, preferred_element_type=f32)
        outputs.append(result.astype(bf16).reshape(per, span, width))
        grad_wf = grad_wf + jnp.einsum("tf,td->fd", act, upstream, preferred_element_type=f32)
        d_act = jnp.einsum("td,fd->tf", upstream, wf, preferred_element_type=f32)
        d_inner = gelu_pull(d_act)[0].astype(bf16)
        grad_wi = grad_wi + jnp.einsum("td,tf->df", n2, d_inner, preferred_element_type=f32)
        d_n2 = jnp.einsum("tf,df->td", d_inner, wi, preferred_element_type=f32)
        norm_pull = jax.vjp(normed, h1, g2)[1]
        dh_part, dg_two = norm_pull(d_n2)
        grad_g2 = grad_g2 + dg_two
        dh1 = upstream.astype(f32) + dh_part
        d_attn = dh1.astype(bf16)
        grad_wo = grad_wo + jnp.einsum("td,te->de", mixed, d_attn, preferred_element_type=f32)
        d_mixed = jnp.einsum("te,de->td", d_attn, wo, preferred_element_type=f32).astype(bf16)
        dm4 = d_mixed.reshape(per, span, heads, head_dim)
        probs = jnp.exp(scores() - top) / denom
        d_probs = jnp.einsum("bqhd,bkhd->bhqk", dm4, v4, preferred_element_type=f32)
        value_terms = jnp.einsum("bhqk,bqhd->bkhd", probs_low, dm4, preferred_element_type=f32)
        delta = jnp.sum(probs * d_probs, axis=-1, keepdims=True)
        d_scores = (probs * (d_probs - delta)).astype(bf16)
        grad_bias = grad_bias + jnp.sum(d_scores.astype(f32), axis=0)
        d_query = jnp.einsum("bhqk,bkhd->bqhd", d_scores, k4, preferred_element_type=f32)
        d_query = d_query.reshape(flat_rows, width).astype(bf16)
        key_terms = jnp.einsum("bhqk,bqhd->bkhd", d_scores, q4, preferred_element_type=f32)
        key_share, value_share = (
            lax.psum_scatter(
                key_terms.reshape(per, total, width), "seq", scatter_dimension=1, tiled=True
            ),
            lax.psum_scatter(
                value_terms.reshape(per, total, width), "seq", scatter_dimension=1, tiled=True
            ),
        )
        d_key = key_share.reshape(flat_rows, width).astype(bf16)
        d_value = value_share.reshape(flat_rows, width).astype(bf16)
        grad_wq = grad_wq + jnp.einsum("td,te->de", n1, d_query, preferred_element_type=f32)
        grad_wk = grad_wk + jnp.einsum("td,te->de", n1, d_key, preferred_element_type=f32)
        grad_wv = grad_wv + jnp.einsum("td,te->de", n1, d_value, preferred_element_type=f32)
        d_n1 = jnp.einsum("te,de->td", d_query, wq, preferred_element_type=f32)
        d_n1 = d_n1 + jnp.einsum("te,de->td", d_key, wk, preferred_element_type=f32)
        d_n1 = d_n1 + jnp.einsum("te,de->td", d_value, wv, preferred_element_type=f32)
        first_pull = jax.vjp(normed, xflat, g1)[1]
        dx_part, dg_one = first_pull(d_n1)
        grad_g1 = grad_g1 + dg_one
        input_grads.append((dh1 + dx_part).reshape(per, span, width))
    owned = (
        lax.psum_scatter(grad_wq, ("seq", "rows"), scatter_dimension=0, tiled=True),
        lax.psum_scatter(grad_wk, ("seq", "rows"), scatter_dimension=0, tiled=True),
        lax.psum_scatter(grad_wv, ("seq", "rows"), scatter_dimension=0, tiled=True),
        lax.psum_scatter(grad_wo, ("seq", "rows"), scatter_dimension=0, tiled=True),
        lax.psum_scatter(grad_wi, ("seq", "rows"), scatter_dimension=0, tiled=True),
        lax.psum_scatter(grad_wf, ("seq", "rows"), scatter_dimension=0, tiled=True),
        lax.psum_scatter(grad_g1, ("seq", "rows"), scatter_dimension=0, tiled=True),
        lax.psum_scatter(grad_g2, ("seq", "rows"), scatter_dimension=0, tiled=True),
    )
    grad_full = lax.dynamic_update_slice_in_dim(
        jnp.zeros((heads, total, total), f32), grad_bias, q_start, 1
    )
    widened = jnp.pad(grad_full, ((0, 0), (0, 0), (total - 1, 0)))
    folded = jnp.pad(widened.reshape(heads, total * (2 * total - 1)), ((0, 0), (0, total)))
    rel_grad = jnp.sum(folded.reshape(heads, total, 2 * total), axis=1)[:, : 2 * total - 1]
    table_local = jnp.dot(onehot.T, rel_grad.T, precision=HIGH)
    table_grad = lax.psum(table_local, ("seq", "rows"))
    result_rows = jnp.concatenate(outputs, axis=0)
    grad_rows = jnp.concatenate(input_grads, axis=0)
    return (
        result_rows,
        grad_rows,
        owned[0],
        owned[1],
        owned[2],
        owned[3],
        owned[4],
        owned[5],
        owned[6],
        owned[7],
        table_grad,
    )


MESH_ID = pl.DeviceIdType.MESH
HBM = pl.BlockSpec(memory_space=pl.ANY)
VMEM = pl.BlockSpec(memory_space=pltpu.VMEM)
SMEM = pl.BlockSpec(memory_space=pltpu.SMEM)
BF = jnp.bfloat16
F32 = jnp.float32
NX, NZ, NY, NC = 2, 4, 2, 2


def rcopy(src, dst, send, recv, to):
    return pltpu.make_async_remote_copy(
        src_ref=src, dst_ref=dst, send_sem=send, recv_sem=recv, device_id=to, device_id_type=MESH_ID
    )


class Place:
    def __init__(self):
        self.x = lax.axis_index("seq")
        r = lax.axis_index("rows")
        self.c = lax.rem(r, 2)
        self.y = lax.rem(r // 2, 2)
        self.z = r // 4
        self.core = self.at(self.x, self.y, self.z, 1 - self.c)
        self.xn = self.at(1 - self.x, self.y, self.z, self.c)
        self.yn = self.at(self.x, 1 - self.y, self.z, self.c)
        self.zp = [None] + [self.at(self.x, self.y, self.zz(j), self.c) for j in range(1, NZ)]

    def at(self, x, y, z, c):
        return (x, z * 4 + y * 2 + c)

    def zz(self, j):
        return lax.rem(self.z + j, NZ)

    def barrier(self):
        sem = pltpu.get_barrier_semaphore()
        peers = [self.core, self.xn, self.yn] + self.zp[1:]
        for p in peers:
            pl.semaphore_signal(sem, inc=1, device_id=p, device_id_type=MESH_ID)
        pl.semaphore_wait(sem, len(peers))


class GatherXZY:
    def __init__(self, me, w, base, nh, ss, rr, dd):
        self.me, self.w, self.ss, self.rr, self.dd = me, w, ss, rr, dd
        self.base, self.nh = base, nh

    def cols(self, plane, c):
        return pl.ds(pl.multiple_of(self.base(plane) + c * self.nh, 128), self.nh)

    def ref(self, x, z, y, c, plane):
        return self.w.at[x, z, y, :, self.cols(plane, c)]

    def pair(self, z, y, c):
        return self.w.at[:, z, y, :, self.cols(self.me.x, c)]

    def send(self, ref, s, recv, to):
        rcopy(ref, ref, self.ss.at[s], recv, to).start()

    def got(self, ref, recv):
        rcopy(ref, ref, self.ss.at[0], recv, self.me.core).wait_recv()

    def start(self):
        m = self.me
        self.send(self.ref(m.x, m.z, m.y, m.c, 1 - m.x), 0, self.rr.at[0], m.xn)

    def step_x(self):
        m = self.me
        self.got(self.ref(1 - m.x, m.z, m.y, m.c, m.x), self.rr.at[0])
        p = self.pair(m.z, m.y, m.c)
        for j in range(1, NZ):
            self.send(p, j, self.rr.at[NZ - j], m.zp[j])
        self.send(p, 4, self.rr.at[4], m.yn)
        self.send(p, 8, self.dd.at[0], m.core)

    def step_z(self, j):
        m = self.me
        p = self.pair(m.zz(j), m.y, m.c)
        self.got(p, self.rr.at[j])
        self.send(p, 4 + j, self.rr.at[4 + j], m.yn)
        self.send(p, 8 + j, self.dd.at[j], m.core)

    def step_y(self, j):
        m = self.me
        p = self.pair(m.zz(j), 1 - m.y, m.c)
        self.got(p, self.rr.at[4 + j])
        self.send(p, 12 + j, self.dd.at[4 + j], m.core)

    def done(self):
        m = self.me
        for j in range(NZ):
            self.got(self.pair(m.zz(j), m.y, 1 - m.c), self.dd.at[j])
        for j in range(NZ):
            self.got(self.pair(m.zz(j), 1 - m.y, 1 - m.c), self.dd.at[4 + j])

    def sent(self):
        m = self.me
        one = self.ref(m.x, m.z, m.y, m.c, m.x)
        rcopy(one, one, self.ss.at[0], self.rr.at[0], m.core).wait_send()
        p = self.pair(m.z, m.y, m.c)
        for s in range(1, 16):
            rcopy(p, p, self.ss.at[s], self.rr.at[0], m.core).wait_send()


class GatherZYX:
    def __init__(self, me, w, ss, rr, dd):
        self.me, self.w, self.ss, self.rr, self.dd = me, w, ss, rr, dd

    def send(self, ref, s, recv, to):
        rcopy(ref, ref, self.ss.at[s], recv, to).start()

    def got(self, ref, recv):
        rcopy(ref, ref, self.ss.at[0], recv, self.me.core).wait_recv()

    def start(self):
        m = self.me
        own = self.w.at[m.x, m.z, m.y, m.c]
        for j in range(1, NZ):
            self.send(own, j - 1, self.rr.at[NZ - j - 1], m.zp[j])
        self.send(own, 3, self.rr.at[3], m.yn)

    def step_z(self, j):
        m = self.me
        b = self.w.at[m.x, m.zz(j), m.y, m.c]
        self.got(b, self.rr.at[j - 1])
        self.send(b, 5 + j, self.rr.at[3 + j], m.yn)

    def step_y(self, j):
        m = self.me
        self.got(self.w.at[m.x, m.zz(j), 1 - m.y, m.c], self.rr.at[3 + j])
        p = self.w.at[m.x, m.zz(j), :, m.c]
        self.send(p, 4 if j == 0 else 8 + j, self.rr.at[7 + j], m.xn)
        self.send(p, 5 if j == 0 else 11 + j, self.dd.at[j], m.core)

    def step_x(self, j):
        m = self.me
        p = self.w.at[1 - m.x, m.zz(j), :, m.c]
        self.got(p, self.rr.at[7 + j])
        self.send(p, 15 + j, self.dd.at[4 + j], m.core)

    def done_near(self):
        m = self.me
        for j in range(NZ):
            self.got(self.w.at[m.x, m.zz(j), :, 1 - m.c], self.dd.at[j])

    def done_far(self):
        m = self.me
        for j in range(NZ):
            self.got(self.w.at[1 - m.x, m.zz(j), :, 1 - m.c], self.dd.at[4 + j])

    def sent(self):
        m = self.me
        one = self.w.at[m.x, m.z, m.y, m.c]
        p = self.w.at[m.x, m.z, :, m.c]
        for s in range(19):
            r = one if s in (0, 1, 2, 3, 6, 7, 8) else p
            rcopy(r, r, self.ss.at[s], self.rr.at[0], m.core).wait_send()


def own_block(me, mine, theirs, w, parts):
    a = mine[...].astype(F32)[:24]
    b = theirs[...].astype(F32)[:24]
    first = jnp.where(me.c == 0, a, b)
    second = jnp.where(me.c == 0, b, a)
    both = jnp.concatenate([first, second], axis=0).astype(BF)
    at = 0
    for n, base in parts:
        w[me.x, me.z, me.y, :, pl.ds(pl.multiple_of(base, 128), n)] = both[:, at : at + n]
        at += n


class Piece:
    def __init__(self, index, rows, first):
        self.index, self.slot, self.rows = index, index % 2, rows
        cut = rows // 2 if rows // 2 % 16 == 0 else rows // 2 + 8
        self.subs = ((0, cut, first[0]), (cut, rows - cut, first[1]))


def acc_rows(x, y, z, lo, n):
    return pl.ds(pl.multiple_of(((x * NY + y) * NZ + z) * 192 + lo, 8), n)


class Reduce:
    def __init__(self, me, acc, a1, a2, a3, cs, cr, s1s, s1r, s2s, s2r, s3s, s3r, fin, finr, keep, sems):
        self.me = me
        self.acc, self.a1, self.a2, self.a3, self.cs, self.cr = acc, a1, a2, a3, cs, cr
        self.s1s, self.s1r, self.s2s, self.s2r, self.s3s, self.s3r = s1s, s1r, s2s, s2r, s3s, s3r
        self.fin, self.finr = fin, finr
        self.keep = keep
        (self.c_s, self.c_r, self.a_s, self.a_r, self.b_s, self.b_r, self.z_s, self.z_r, self.f_s, self.f_r) = sems

    def near(self, axis):
        return self.me.xn if axis == "x" else self.me.yn

    def core_copy(self, p):
        s, n = p.slot, p.rows
        return rcopy(
            self.cs.at[:, :, :, 0:n], self.cr.at[s, :, :, :, 0:n], self.c_s.at[s], self.c_r.at[s], self.me.core
        )

    def one_copy(self, p, k):
        s, (_, n, axis) = p.slot, p.subs[k]
        return rcopy(
            self.s1s.at[k, :, :, 0:n], self.s1r.at[s, k, :, :, 0:n], self.a_s.at[s, k], self.a_r.at[s, k], self.near(axis)
        )

    def two_copy(self, p, k):
        s, (_, n, axis) = p.slot, p.subs[k]
        to = self.near("y" if axis == "x" else "x")
        return rcopy(self.s2s.at[k, :, 0:n], self.s2r.at[s, k, :, 0:n], self.b_s.at[s, k], self.b_r.at[s, k], to)

    def z_copy(self, p, j):
        s, n = p.slot, p.rows
        return rcopy(
            self.s3s.at[j, 0:n], self.s3r.at[s, NZ - j, 0:n], self.z_s.at[s, j], self.z_r.at[s, NZ - j], self.me.zp[j]
        )

    def fin_copy(self, p):
        i, n = p.index, p.rows // 2
        return rcopy(
            self.fin.at[i, 0:n], self.finr.at[i, 0:n], self.f_s.at[i], self.f_r.at[i], self.me.core
        )

    def send_core(self, p):
        self.core_copy(p).start()

    def h1(self, p, old):
        me, s, n = self.me, p.slot, p.rows
        self.core_copy(p).wait_recv()
        for k, (lo, n, axis) in enumerate(p.subs):
            if old is not None:
                self.one_copy(old, k).wait_send()
            rows = pl.ds(lo, n)

            def body(q, carry):
                a, zq = q // NZ, lax.rem(q, NZ)
                if axis == "x":
                    keep, away = (me.x, a, zq, rows), (1 - me.x, a, zq, rows)
                else:
                    keep, away = (a, me.y, zq, rows), (a, 1 - me.y, zq, rows)
                held = [self.acc[acc_rows(*at[:3], lo, n), :] for at in (keep, away)]
                self.a1[k, a, zq, 0:n] = held[0] + self.cr[(s,) + keep].astype(F32)
                self.s1s[k, a, zq, 0:n] = (held[1] + self.cr[(s,) + away].astype(F32)).astype(BF)
                return carry

            lax.fori_loop(0, 2 * NZ, body, 0)
            self.one_copy(p, k).start()

    def h2(self, p, old):
        me, s = self.me, p.slot
        for k, (lo, n, axis) in enumerate(p.subs):
            self.one_copy(p, k).wait_recv()
            if old is not None:
                self.two_copy(old, k).wait_send()
            b = me.y if axis == "x" else me.x

            def body(zq, carry):
                self.a2[k, zq, 0:n] = self.a1[k, b, zq, 0:n] + self.s1r[s, k, b, zq, 0:n].astype(F32)
                self.s2s[k, zq, 0:n] = (
                    self.a1[k, 1 - b, zq, 0:n] + self.s1r[s, k, 1 - b, zq, 0:n].astype(F32)
                ).astype(BF)
                return carry

            lax.fori_loop(0, NZ, body, 0)
            self.two_copy(p, k).start()

    def h3(self, p, old):
        me, s = self.me, p.slot
        for k in range(2):
            self.two_copy(p, k).wait_recv()
        for j in range(1, NZ):
            if old is not None:
                self.z_copy(old, j).wait_send()
        for k, (lo, n, _) in enumerate(p.subs):
            rows = pl.ds(lo, n)
            for j in range(NZ):
                zq = me.zz(j)
                v = self.a2[k, zq, 0:n] + self.s2r[s, k, zq, 0:n].astype(F32)
                if j == 0:
                    self.a3[rows] = v
                else:
                    self.s3s[j, rows] = v.astype(BF)
        for j in range(1, NZ):
            self.z_copy(p, j).start()

    def h4(self, p):
        me, s, n, i = self.me, p.slot, p.rows, p.index
        for j in range(1, NZ):
            self.z_copy(p, NZ - j).wait_recv()
        total = self.a3[0:n]
        for j in range(1, NZ):
            total = total + self.s3r[s, j, 0:n].astype(F32)
        if p.groups is None:
            a, b = total[0 : n // 2], total[n // 2 :]
        else:
            a, b = (
                jnp.concatenate([total[48 * g + 24 * k : 48 * g + 24 * k + 24] for g in range(p.groups)], axis=0)
                for k in range(NC)
            )
        self.fin[i, 0 : n // 2] = jnp.where(me.c == 0, b, a)
        self.keep(p, jnp.where(me.c == 0, a, b), me.c)
        self.fin_copy(p).start()


def norm_back(h, gain, up):
    r = lax.rsqrt(jnp.mean(h * h, axis=-1, keepdims=True) + EPS)
    hr = h * r
    w = up * gain
    dgain = jnp.sum(up * hr, axis=0, keepdims=True)
    return r * (w - hr * jnp.mean(w * hr, axis=-1, keepdims=True)), dgain


def layer_kernel(
    tok, gin, gains, wq, wk, wv, wo, wi, pd, relb, table, lens,
    act_o, dx_o, gq_o, gk_o, gv_o, go_o, gi_o, gf_o, sm_o,
    WA, WB, WD, X, G, N2, QKV, O, H1, ACT, DU, T, M, MACC, LSE, R, RG,
    ACC, A1, A2, A3, CS, CR, S1S, S1R, S2S, S2R, S3S, S3R, FIN, FINR, SM, SMR, ZB, DG,
    ts, tr, tl, gs, gr, gl, es, er, as_, ar, ad, a2s, a2r, a2d, os_, or_, od, bs, br, bd, b2s, b2r, b2d, ds_, dr, dd, ys, yr, yl, xs_, xr, xl,
    c_s, c_r, a_s, a_r, b_s, b_r, z_s, z_r, f_s, f_r, ms, mr,
):
    me = Place()
    x, y, z, c = me.x, me.y, me.z, me.c
    mine, span, width = X.shape[0], X.shape[2], X.shape[3]
    length = 2 * span
    flat = mine * length
    ff = DU.shape[1]
    na, nb = WA.shape[4] // 2, WB.shape[4] // 2
    PA, PB = DU.at[pl.ds(32 * c, 32), 0:na], DU.at[pl.ds(64 + 32 * c, 32), 0:nb]
    RA, RB = DU.at[128:160, 0:na], DU.at[160:192, 0:nb]
    hd = 64
    YB = N2
    pairs = width // hd // 2
    half_ff, half_w = ff // 2, width // 2
    n1, n2_ = (256 + 3 * 256) // 2, 3 * (width - 256) // 2
    gath_a = GatherXZY(me, WA, lambda plane: 0, n1, as_, ar, ad)
    gath_e = GatherXZY(me, WA, lambda plane: 2 * n1, n2_, a2s, a2r, a2d)
    gath_o = GatherXZY(me, WB, lambda plane: 0, half_w, os_, or_, od)
    gath_1 = GatherXZY(me, WB, lambda plane: width + half_ff * plane, half_ff // 2, bs, br, bd)
    gath_2 = GatherXZY(me, WB, lambda plane: width + half_ff * (1 - plane), half_ff // 2, b2s, b2r, b2d)
    gath_d = GatherZYX(me, WD, ds_, dr, dd)

    def pack(first, n, parts):
        filled = [
            jnp.concatenate([p.astype(F32), jnp.zeros((32 - p.shape[0], p.shape[1]), F32)], axis=0) for p in parts
        ]
        DU[first : first + 32, 0:n] = jnp.concatenate(filled, axis=1).astype(BF)

    quarter = half_ff // 2
    part = width - 256
    pack(0, na, (gains[...], wq[:, 0:256], wq[:, 256:], wk[:, 256 : 256 + part // 2]))
    pack(32, na, (wk[:, 0:256], wv[:, 0:256], wk[:, 256 + part // 2 :], wv[:, 256:]))
    me.barrier()
    ea = rcopy(DU.at[pl.ds(32 * (1 - c), 32), 0:na], RA, es.at[0], er.at[0], me.core)
    eb = rcopy(DU.at[pl.ds(64 + 32 * (1 - c), 32), 0:nb], RB, es.at[1], er.at[1], me.core)
    ea.start()
    for k in range(2):
        first = wi[:, quarter * k : quarter * k + quarter]
        second = wi[:, half_ff + quarter * k : half_ff + quarter * k + quarter]
        pack(64 + 32 * k, nb, (wo[:, half_w * k : half_w * k + half_w], first, second))
    eb.start()
    tok_r = [rcopy(tok.at[2 * (1 - x) + i], X.at[i, x], ts.at[i], tr.at[i], me.xn) for i in range(mine)]
    tok_in = [rcopy(X.at[i, 1 - x], X.at[i, 1 - x], ts.at[i], tr.at[i], me.xn) for i in range(mine)]
    tok_l = [pltpu.make_async_copy(tok.at[2 * x + i], X.at[i, x], tl.at[i]) for i in range(mine)]
    g_r = rcopy(gin.at[pl.ds(2 * (1 - x), 2)], G.at[:, x], gs, gr, me.xn)
    g_in = rcopy(G.at[:, 1 - x], G.at[:, 1 - x], gs, gr, me.xn)
    g_l = pltpu.make_async_copy(gin.at[pl.ds(2 * x, 2)], G.at[:, x], gl)
    ea.wait_recv()
    own_block(me, PA, RA, WA, ((n1, c * n1), (n2_, 2 * n1 + c * n2_)))
    gath_a.start()
    for i in range(mine):
        tok_r[i].start()
        tok_l[i].start()
    g_l.start()
    eb.wait_recv()
    own_block(
        me, PB, RB, WB,
        ((half_w, c * half_w), (quarter, width + c * quarter), (quarter, width + half_ff + c * quarter)),
    )
    WD[x, z, y, c] = pd[...]
    cols = relb.shape[1]
    kinds = table.shape[0]
    hot = (lax.broadcasted_iota(jnp.int32, (kinds, cols), 0) == relb[...]).astype(BF)
    R[...] = lax.dot_general(table[...], hot, (((0,), (0,)), ((), ())), preferred_element_type=F32)[0:16]
    gath_a.step_x()
    gath_e.start()
    gath_o.start()
    gath_1.start()
    gath_d.start()
    for j in range(1, NZ):
        gath_a.step_z(j)
    gath_e.step_x()
    for j in range(NZ):
        gath_a.step_y(j)
    gath_o.step_x()
    gath_1.step_x()
    gath_d.step_y(0)
    for j in range(1, NZ):
        gath_e.step_z(j)
    gath_a.done()

    def gain_row(k):
        return jnp.transpose(WA[:, :, :, :, 128 * k : 128 * k + 128].reshape(width, 128).astype(F32))[0:1, :]

    gain1 = gain_row(0)

    def row_slice(i):
        return pl.ds(pl.multiple_of(i * length, length), length)

    def first_norm(i):
        for half in range(2):
            xf = X[i, half].astype(F32)
            scale = lax.rsqrt(jnp.mean(xf * xf, axis=-1, keepdims=True) + EPS)
            N2[i, half] = (xf * scale * gain1).astype(BF)

    def project(i, first, count):
        for n in range(count):
            lo = (first + n) * width
            QKV[row_slice(i), lo : lo + width] = jnp.dot(
                N2[i].reshape(length, width),
                WA[:, :, :, :, 256 + lo : 256 + lo + width].reshape(width, width),
                preferred_element_type=F32,
            ).astype(BF)

    for i in range(mine):
        tok_l[i].wait()
        tok_in[i].wait_recv()
        first_norm(i)
        project(i, 0, 1)
    gath_2.start()
    g_r.start()
    low = lax.broadcasted_iota(jnp.int32, (1, 128), 1) < hd
    lane = lax.broadcasted_iota(jnp.int32, (1, 128), 1)
    kpos = lax.broadcasted_iota(jnp.int32, (length, 128), 0)
    blocks = length // 128

    def strips(p):
        for h in range(2):
            row = jnp.broadcast_to(R[pl.ds(2 * p + h, 1), :], (128, cols))
            M[h] = pltpu.roll(row, cols - 127, 1, stride=1, stride_axis=0)[:, : M.shape[2]]

    def bias_of(h):
        return jnp.concatenate(
            [M[h, :, 128 * (blocks - 1 - a) : 128 * (blocks - 1 - a) + length] for a in range(blocks)], axis=0
        )

    own = (low, jnp.logical_not(low))
    spare = (hd, 0)
    ones = [(lane == spare[h]).astype(F32).astype(BF) for h in range(2)]
    none = jnp.zeros((), BF)

    def masked_keys(h, k, count):
        pad = jnp.where((lane == spare[h]) & (kpos >= count), NEG, 0.0).astype(BF)
        return jnp.where(own[h], k, pad)

    def lanes(n, p):
        at = jnp.where(p < 2, n * 256 + p * 128, width + n * (width - 256) + (p - 2) * 128)
        return pl.ds(pl.multiple_of(at, 128), 128)

    def wide_lanes(p):
        return pl.ds(pl.multiple_of(p * 128, 128), 128)

    nt = (((1,), (1,)), ((), ()))
    tn = (((0,), (0,)), ((), ()))

    def mm(a, b, dims):
        return lax.dot_general(a, b, dims, preferred_element_type=F32)

    o_, b1, b2, d_, e_ = gath_o, gath_1, gath_2, gath_d, gath_e
    comm = {
        0: ((e_.step_y, 0), (e_.step_y, 1)),
        1: ((e_.step_y, 2), (e_.step_y, 3)),
        2: ((o_.step_z, 1), (b1.step_z, 1), (d_.step_z, 1)),
        3: ((o_.step_z, 2), (b1.step_z, 2), (d_.step_z, 2)),
        4: ((o_.step_z, 3), (b1.step_z, 3), (d_.step_z, 3), (lambda j: b2.step_x(), 0)),
        5: ((o_.step_y, 0), (b1.step_y, 0), (d_.step_y, 1)),
        6: ((o_.step_y, 1), (b1.step_y, 1), (d_.step_y, 2)),
        7: ((o_.step_y, 2), (b1.step_y, 2), (d_.step_y, 3)),
        8: ((o_.step_y, 3), (b1.step_y, 3), (d_.step_x, 0), (b2.step_z, 1)),
        9: ((b2.step_z, 2), (d_.step_x, 1)),
        10: ((b2.step_z, 3), (b2.step_y, 0), (d_.step_x, 2)),
        11: ((b2.step_y, 1), (d_.step_x, 3)),
    }

    def attend(t, carry):
        p, i = t // mine, lax.rem(t, mine)
        pl.when(i == 0)(lambda: strips(p))
        rows = row_slice(i)
        q, k, v = QKV[rows, lanes(0, p)], QKV[rows, lanes(1, p)], QKV[rows, lanes(2, p)]
        outs = []
        for h in range(2):
            s = mm(jnp.where(own[h], q, ones[h]), masked_keys(h, k, lens[2 * x + i]), nt) + bias_of(h)
            top = jnp.max(s, axis=-1, keepdims=True)
            e = jnp.exp(s - top)
            total = jnp.sum(e, axis=-1, keepdims=True)
            LSE[rows, :] = jnp.where(lane == 2 * p + h, top + jnp.log(total), LSE[rows, :])
            outs.append(jnp.dot((e * (1.0 / total)).astype(BF), v, preferred_element_type=F32))
        O[i, :, :, wide_lanes(p)] = jnp.where(low, outs[0], outs[1]).astype(BF).reshape(2, span, 128)
        for at, steps in comm.items():
            @pl.when(t == at)
            def _():
                for step, j in steps:
                    step(j)
        return carry

    LSE[...] = jnp.zeros_like(LSE)
    lax.fori_loop(0, 2 * mine, attend, 0)
    gath_e.done()
    for i in range(mine):
        project(i, 1, 2)
    lax.fori_loop(2 * mine, mine * pairs, attend, 0)
    ea.wait_send()
    eb.wait_send()
    gath_o.done()
    gath_1.done()
    gath_d.done_near()
    g_l.wait()
    g_in.wait_recv()

    gain2 = gain_row(1)
    DG[...] = jnp.zeros_like(DG)
    c0, c1 = 0.7978845608028654, 0.044715

    def dn_set(v):
        for n in range(width // 128):
            ACC[length * n : length * n + length, :] = v[:, 128 * n : 128 * n + 128]

    def dn_get(lo, n):
        return jnp.concatenate([ACC[length * k + lo : length * k + lo + n, :] for k in range(width // 128)], axis=1)

    def dn_add(v):
        for n in range(width // 128):
            at = slice(length * n, length * n + length)
            ACC[at, :] = ACC[at, :] + v[:, 128 * n : 128 * n + 128]

    wo_all = lambda: WB[:, :, :, :, 0:width].reshape(width, width)
    for i in range(mine):
        h1 = X[i].reshape(length, width).astype(F32) + jnp.dot(
            O[i].reshape(length, width), wo_all(), preferred_element_type=F32
        )
        H1[i] = h1.reshape(2, span, width)
        r = lax.rsqrt(jnp.mean(h1 * h1, axis=-1, keepdims=True) + EPS)
        N2[i] = (h1 * r * gain2).astype(BF).reshape(2, span, width)

    def chunk(n, carry):
        @pl.when(n == 2)
        def _():
            gath_2.done()
            gath_d.done_far()

        f = lax.rem(2 * x + n, 4)

        def one_row(i, carry):
            pl.when((n == 0) & (i == 0))(lambda: gath_2.step_y(2))
            pl.when((n == 0) & (i == 1))(lambda: gath_2.step_y(3))
            n2, g = N2[i].reshape(length, width), G[i].reshape(length, width)
            for part in range(3):
                fcols = pl.ds(pl.multiple_of(f * width + 256 * part, 256), 256)
                wcols = pl.ds(pl.multiple_of(width + f * width + 256 * part, 256), 256)
                wi_part = WB[:, :, :, :, wcols].reshape(width, 256)
                wf_part = WD[f // 2, pl.ds(2 * lax.rem(f, 2), 2)].reshape(width, width)[256 * part : 256 * part + 256]
                u = jnp.dot(n2, wi_part, preferred_element_type=F32)
                da = mm(g, wf_part, nt)
                sq = u * u
                t = jnp.tanh(u * (c0 + (c0 * c1) * sq))
                cdf = 0.5 + 0.5 * t
                ACT[row_slice(i), fcols] = (u * cdf).astype(BF)
                slope = cdf + (0.5 * u) * (1.0 - t * t) * (c0 + (3.0 * c0 * c1) * sq)
                DU[row_slice(i), fcols] = (da * slope).astype(BF)
            return carry

        return lax.fori_loop(0, mine, one_row, carry)

    lax.fori_loop(0, ff // width, chunk, 0)
    def keep(p, value, core):
        if p.groups is None:
            gf_o[:, pl.ds(pl.multiple_of(256 * p.part + 128 * core, 128), 128)] = value
            return
        for g in range(p.groups):
            if p.kind == "i":
                dst, base = gi_o, 1024 * p.part + 256 * g
            elif p.kind == "o":
                dst, base = go_o, 256 * g
            else:
                dst, base = (gq_o, gk_o, gv_o)[g], 256 * p.part
            dst[:, pl.ds(pl.multiple_of(base + 128 * core, 128), 128)] = value[24 * g : 24 * g + 24]

    red = Reduce(
        me, ACC, A1, A2, A3, CS, CR, S1S, S1R, S2S, S2R, S3S, S3R, FIN, FINR, keep, (c_s, c_r, a_s, a_r, b_s, b_r, z_s, z_r, f_s, f_r)
    )
    pieces = []
    kinds_of = [("f", 0), ("f", 1), ("f", 2), ("i", 0), ("i", 1), ("i", 2), ("o", 0), ("qkv", 0), ("qkv", 1), ("qkv", 2)]
    made_at = [0, 2, 4, 5, 6, 7, 8, 13, 15, 17]
    last = len(kinds_of)
    for n in range(last):
        kind, part = kinds_of[n]
        piece = Piece(n, 144 if kind in ("o", "qkv") else 192, ("y", "y") if n < last - 1 else ("x", "x"))
        piece.kind, piece.part = kind, part
        piece.groups = None if kind == "f" else piece.rows // 48
        pieces.append(piece)

    def stages(n):
        def at(k):
            return pieces[made_at.index(n - k)] if n - k in made_at else None

        def old(p):
            return pieces[p.index - 1] if p.index else None

        if at(4):
            red.h4(at(4))
        if at(3):
            red.h3(at(3), old(at(3)))
        if at(2):
            red.h2(at(2), old(at(2)))
        if at(1):
            red.h1(at(1), old(at(1)))
        if at(0):
            if old(at(0)):
                red.core_copy(old(at(0))).wait_send()
            produce(at(0))

    def split(res):
        a, b = res[:, 0:128], res[:, 128:256]
        return jnp.where(c == 0, a, b), jnp.where(c == 0, b, a).astype(BF)

    def outer_piece(j):

        def body(q, carry):
            xq, zh = q // 2, lax.rem(q, 2)
            lhs = ACT[:, pl.ds(pl.multiple_of(q * 768, 768), 768)]
            rhs = G[:, :, :, 256 * j : 256 * j + 256].reshape(flat, 256)
            own, other = split(mm(lhs, rhs, tn))
            for b in range(4):
                at = (xq, b % 2, 2 * zh + b // 2)
                ACC[acc_rows(*at, 0, 192), :] = own[192 * b : 192 * b + 192]
                CS[at] = other[192 * b : 192 * b + 192]
            return carry

        lax.fori_loop(0, 4, body, 0)

    def rows_piece(groups, rhs):
        def body(g, carry):
            own, other = split(jnp.dot(T[...], rhs(g), preferred_element_type=F32))
            at = pl.ds(pl.multiple_of(48 * g, 48), 48)
            for k in range(NX * NZ * NY):
                ACC[acc_rows(k // 8, k % 2, (k // 2) % 4, 48 * g, 48), :] = own[48 * k : 48 * k + 48]
                CS[k // 8, k % 2, (k // 2) % 4, at] = other[48 * k : 48 * k + 48]
            return carry

        lax.fori_loop(0, groups, body, 0)

    def produce(p):
        if p.kind == "f":
            outer_piece(p.part)
        elif p.kind == "i":
            rows_piece(4, lambda g: DU[:, pl.ds(pl.multiple_of(1024 * p.part + 256 * g, 256), 256)])
        elif p.kind == "o":
            T[...] = jnp.transpose(O[...].reshape(flat, width))
            rows_piece(3, lambda g: H1[:, :, :, pl.ds(pl.multiple_of(256 * g, 256), 256)].reshape(flat, 256).astype(BF))
        else:
            base, wide = (0, 256) if p.part == 0 else (width + 256 * (p.part - 1), width - 256)
            rows_piece(3, lambda g: QKV[:, pl.ds(pl.multiple_of(base + g * wide, 256), 256)])
        red.send_core(p)

    stages(0)
    T[...] = jnp.transpose(N2[...].reshape(flat, width))
    stages(1)

    def result(t, carry):
        i, f = t // 4, lax.rem(t, 4)
        a = ACT[row_slice(i), pl.ds(pl.multiple_of(f * width, width), width)]
        wf = WD[f // 2, pl.ds(2 * lax.rem(f, 2), 2)].reshape(width, width)
        out = jnp.dot(a, wf, preferred_element_type=F32)

        @pl.when(f == 0)
        def _():
            dn_set(H1[i].reshape(length, width) + out)

        @pl.when(f > 0)
        def _():
            dn_add(out)

        @pl.when(f == 3)
        def _():
            YB[i] = dn_get(0, length).astype(BF).reshape(2, span, width)

        return carry

    lax.fori_loop(0, 4 * mine, result, 0)
    y_out = [
        rcopy(YB.at[i, 1 - x], act_o.at[2 * (1 - x) + i], ys.at[i], yr.at[i], me.xn) for i in range(mine)
    ]
    y_loc = [pltpu.make_async_copy(YB.at[i, x], act_o.at[2 * x + i], yl.at[i]) for i in range(mine)]
    for i in range(mine):
        rcopy(YB.at[i, 1 - x], act_o.at[2 * x + i], ys.at[i], yr.at[i], me.xn).start()
        y_loc[i].start()

    stages(2)
    stages(3)

    def back(t, carry):
        i, f = t // 4, lax.rem(t, 4)
        du = DU[row_slice(i), pl.ds(pl.multiple_of(f * width, width), width)]
        wi_part = WB[:, :, :, :, pl.ds(pl.multiple_of((f + 1) * width, width), width)].reshape(width, width)
        out = mm(du, wi_part, nt)

        @pl.when(f == 0)
        def _():
            dn_set(out)

        @pl.when(f > 0)
        def _():
            dn_add(out)

        @pl.when(f == 3)
        def _():
            for half in range(2):
                dh, dgain = norm_back(H1[i, half], gain2, dn_get(span * half, span))
                DG[1:2, :] = DG[1:2, :] + dgain
                H1[i, half] = G[i, half].astype(F32) + dh

        return carry

    lax.fori_loop(0, 4 * mine, back, 0)

    stages(4)
    for i in range(mine):
        dab = H1[i].reshape(length, width).astype(BF)
        G[i] = mm(dab, wo_all(), nt).astype(BF).reshape(2, span, width)
    landing = lambda i: DU.at[pl.ds(i * span, span), 0:width]
    dx_r = [rcopy(X.at[i, 1 - x], landing(i), xs_.at[i], xr.at[i], me.xn) for i in range(mine)]
    dx_l = [pltpu.make_async_copy(H1.at[i, x], dx_o.at[2 * x + i], xl.at[i]) for i in range(mine)]
    dx_f = [pltpu.make_async_copy(H1.at[i, 1 - x], dx_o.at[2 * (1 - x) + i], xl.at[mine + i]) for i in range(mine)]

    def input_grad(i):
        for n in range(3):
            out = mm(
                QKV[row_slice(i), n * width : (n + 1) * width],
                WA[:, :, :, :, 256 + n * width : 256 + (n + 1) * width].reshape(width, width),
                nt,
            )
            (dn_set if n == 0 else dn_add)(out)
        for half in range(2):
            dh, dgain = norm_back(X[i, half].astype(F32), gain1, dn_get(span * half, span))
            DG[0:1, :] = DG[0:1, :] + dgain
            H1[i, half] = H1[i, half] + dh
        X[i, 1 - x] = H1[i, 1 - x].astype(BF)
        dx_r[i].start()
        dx_l[i].start()

    def norm_again():
        for i in range(mine):
            y_out[i].wait_recv()
            y_out[i].wait_send()
            y_loc[i].wait()
        for i in range(mine):
            first_norm(i)
        T[...] = jnp.transpose(N2[...].reshape(flat, width))

    def attend_back(t, carry):
        i, p = t // pairs, lax.rem(t, pairs)
        strips(p)
        MACC[...] = jnp.zeros_like(MACC)
        rows = row_slice(i)
        q, k, v = QKV[rows, lanes(0, p)], QKV[rows, lanes(1, p)], QKV[rows, lanes(2, p)]
        do = G[i, :, :, wide_lanes(p)].reshape(length, 128)
        prod = do.astype(F32) * O[i, :, :, wide_lanes(p)].reshape(length, 128).astype(F32)
        dqs, dks, dvs = [], [], []
        for h in range(2):
            lse = jnp.sum(jnp.where(lane == 2 * p + h, LSE[rows, :], 0.0), axis=-1, keepdims=True)
            delta = jnp.sum(jnp.where(own[h], prod, 0.0), axis=-1, keepdims=True)
            s = mm(jnp.where(own[h], q, ones[h]), masked_keys(h, k, lens[2 * x + i]), nt) + bias_of(h)
            pr = jnp.exp(s - lse)
            ds = pr * (mm(jnp.where(own[h], do, none), v, nt) - delta)
            for a in range(blocks):
                at = 128 * (blocks - 1 - a)
                MACC[h, :, at : at + length] = MACC[h, :, at : at + length] + ds[128 * a : 128 * a + 128]
            low_p, low_ds = pr.astype(BF), ds.astype(BF)
            dqs.append(jnp.dot(low_ds, k, preferred_element_type=F32))
            dks.append(mm(low_ds, q, tn))
            dvs.append(mm(low_p, do, tn))
        for n, parts in enumerate((dqs, dks, dvs)):
            QKV[rows, lanes(n, p)] = jnp.where(low, parts[0], parts[1]).astype(BF)

        for h in range(2):
            part = jnp.zeros((8, cols), F32)
            for a in range(16):
                part = part + pltpu.roll(MACC[h, 8 * a : 8 * a + 8, :], (cols - 8 * a) % cols, 1)
            line = part[0:1]
            for a in range(1, 8):
                line = line + pltpu.roll(part[a : a + 1], cols - a, 1)
            at = pl.ds(2 * p + h, 1)
            RG[at, :] = RG[at, :] + pltpu.roll(line, 127, 1)

        for n in range(mine * pairs):
            @pl.when(t == n)
            def _():
                stages(5 + n)
                if n == pairs - 1:
                    norm_again()
                if n == pairs:
                    input_grad(0)

        return carry

    RG[...] = jnp.zeros_like(RG)
    MACC[...] = jnp.zeros_like(MACC)
    lax.fori_loop(0, mine * pairs, attend_back, 0)

    stages(17)
    stages(18)
    input_grad(1)
    stages(19)
    stages(20)
    for n in range(width // 128):
        SM[0, n : n + 1, :] = DG[0:1, 128 * n : 128 * n + 128]
        SM[0, 8 + n : 9 + n, :] = DG[1:2, 128 * n : 128 * n + 128]
    rest = jnp.concatenate([RG[...], jnp.zeros((112, cols), F32)], axis=0)
    spread = jnp.zeros((kinds, 128), F32)
    for _ in range(3):
        part = rest.astype(BF)
        rest = rest - part.astype(F32)
        spread = spread + mm(hot, part, nt)
    SM[0, 16 : 16 + kinds, :] = spread
    sm_copies = [
        rcopy(SM.at[k], SMR.at[k], ms.at[k], mr.at[k], to) for k, to in enumerate((me.core, me.xn, me.yn))
    ]
    sm_copies[0].start()
    stages(21)
    for k in range(3):
        sm_copies[k].wait_recv()
        SM[k + 1] = SM[k] + SMR[k]
        if k < 2:
            sm_copies[k + 1].start()
    ZB[z] = SM[3]
    sm_z = [None] + [rcopy(SM.at[3], ZB.at[z], ms.at[2 + j], mr.at[6 - j], me.zp[j]) for j in range(1, NZ)]
    for j in range(1, NZ):
        sm_z[j].start()
    for i in range(mine):
        dx_r[i].wait_recv()
        H1[i, 1 - x] = DU[pl.ds(i * span, span), 0:width].astype(F32)
        dx_f[i].start()
    for p in pieces:
        red.fin_copy(p).wait_recv()
        keep(p, FINR[p.index, 0 : p.rows // 2], 1 - c)
    for j in range(1, NZ):
        rcopy(SM.at[3], ZB.at[me.zz(j)], ms.at[2 + j], mr.at[2 + j], me.zp[j]).wait_recv()
    sm_o[...] = ZB[0] + ZB[1] + ZB[2] + ZB[3]
    g_r.wait_send()
    for k in range(3):
        sm_copies[k].wait_send()
    for j in range(1, NZ):
        sm_z[j].wait_send()
    for g in (gath_a, gath_e, gath_o, gath_1, gath_2, gath_d):
        g.sent()
    for i in range(mine):
        tok_r[i].wait_send()
        dx_r[i].wait_send()
        dx_l[i].wait()
        dx_f[i].wait()
    for p in pieces[-1:]:
        red.core_copy(p).wait_send()
        for k in range(2):
            red.one_copy(p, k).wait_send()
            red.two_copy(p, k).wait_send()
        for j in range(1, NZ):
            red.z_copy(p, j).wait_send()
    for p in pieces:
        red.fin_copy(p).wait_send()


def layer_call(tok, gin, gains, wq, wk, wv, wo, wi, pd, relb, table, lens, heads):
    rows_dev, span, width = tok.shape
    length = 2 * span
    mine = rows_dev // 2
    flat = mine * length
    dma = pltpu.SemaphoreType.DMA
    ff = wi.shape[1]
    na, nb = (gains.shape[1] + 3 * width) // 2, (width + ff) // 2
    count = width // 256 + ff // 1024 + 4
    wa = (NX, NZ, NY, 48, 2 * na)
    wb = (NX, NZ, NY, 48, 2 * nb)
    wd = (NX, NZ, NY, NC) + pd.shape
    xs = (mine, 2, span, width)
    block = (192, 128)
    bf = lambda *s: pltpu.VMEM(s, BF)
    f32 = lambda *s: pltpu.VMEM(s, F32)
    out = lambda *s: jax.ShapeDtypeStruct(s, F32)
    shard = wq.shape[0]
    return pl.pallas_call(
        layer_kernel,
        out_shape=[jax.ShapeDtypeStruct(tok.shape, BF), out(*tok.shape)]
        + [out(shard, width)] * 4 + [out(shard, ff), out(*pd.shape), out(48, 128)],
        in_specs=[HBM, HBM] + [VMEM] * 9 + [SMEM],
        out_specs=[HBM, HBM] + [VMEM] * 7,
        scratch_shapes=[
            bf(*wa), bf(*wb), bf(*wd), bf(*xs), bf(*xs), bf(*xs), bf(flat, 3 * width), bf(*xs), f32(*xs),
             bf(flat, ff), bf(flat, ff), bf(width, flat), f32(2, 128, 896), f32(2, 128, 1024),
            f32(flat, 128), f32(16, relb.shape[1]), f32(16, relb.shape[1]),
            f32(NX * NY * NZ * 192, 128), f32(2, 2, NZ, 96, 128), f32(2, NZ, 96, 128), f32(*block), bf(NX, NY, NZ, *block), bf(2, NX, NY, NZ, *block),
            bf(2, 2, NZ, 96, 128), bf(2, 2, 2, NZ, 96, 128), bf(2, NZ, 96, 128), bf(2, 2, NZ, 96, 128),
            bf(NZ, *block), bf(2, NZ, *block), f32(count, 96, 128), f32(count, 96, 128),
            f32(4, 48, 128), f32(3, 48, 128), f32(NZ, 48, 128), f32(8, width),
            dma((2,)), dma((2,)), dma((2,)), dma, dma, dma, dma((2,)), dma((2,)),
            *[dma((n,)) for _ in range(5) for n in (16, 8, 8)], dma((19,)), dma((11,)), dma((8,)),
            dma((2,)), dma((2,)), dma((2,)), dma((2,)), dma((2,)), dma((4,)),
            dma((2,)), dma((2,)), dma((2, 2)), dma((2, 2)), dma((2, 2)), dma((2, 2)), dma((2, NZ)), dma((2, NZ)),
            dma((count,)), dma((count,)), dma((6,)), dma((6,)),
        ],
        compiler_params=pltpu.CompilerParams(
            collective_id=0, has_side_effects=True, vmem_limit_bytes=VMEM_LIMIT, fuse_transposed_lhs_in_matmul=True
        ),
        name="layer",
    )(tok, gin, gains, wq, wk, wv, wo, wi, pd, relb, table, lens)


VMEM_LIMIT = 67_000_000


def close_kernel(n_dev, *refs):
    srcs, small, dsts = refs[:8], refs[8], refs[9:17]
    g1, g2, table = refs[17:20]
    held, came, left = refs[20:22], refs[22], refs[23]
    large = [(srcs[k].at[i], held[k].at[i], dsts[k].at[i]) for k in range(2) for i in range(srcs[k].shape[0])]
    loads = [pltpu.make_async_copy(a, b, came.at[n]) for n, (a, b, _) in enumerate(large)]
    stores = [pltpu.make_async_copy(b, c, left.at[n]) for n, (_, b, c) in enumerate(large)]
    for cp in loads:
        cp.start()
    for a, b in zip(srcs[2:], dsts[2:]):
        b[...] = a[...]
    for cp, out in zip(loads, stores):
        cp.wait()
        out.start()
    me = lax.axis_index("seq") * lax.axis_size("rows") + lax.axis_index("rows")
    cut = g1.shape[1]
    width = cut * n_dev
    for k, out in enumerate((g1, g2)):
        row = jnp.concatenate([small[8 * k + j : 8 * k + j + 1, :] for j in range(width // 128)], axis=1)
        out[...] = pltpu.roll(row, lax.rem(width - me * cut, width), 1)[:, 0:cut]
    table[...] = small[16 : 16 + table.shape[0], 0 : table.shape[1]]
    for cp in stores:
        cp.wait()


def close_call(arrays, small, cut, n_bins, heads):
    n_dev = NX * NZ * NY * NC
    like = [jax.ShapeDtypeStruct(a.shape, a.dtype) for a in arrays]
    out = lambda *s: jax.ShapeDtypeStruct(s, F32)
    count = sum(a.shape[0] for a in arrays[:2])
    res = pl.pallas_call(
        functools.partial(close_kernel, n_dev),
        out_shape=like + [out(1, cut), out(1, cut), out(n_bins, heads)],
        in_specs=[HBM] * 2 + [VMEM] * 7,
        out_specs=[HBM] * 2 + [VMEM] * 9,
        scratch_shapes=[pltpu.VMEM(a.shape, a.dtype) for a in arrays[:2]]
        + [pltpu.SemaphoreType.DMA((count,))] * 2,
        name="close",
    )(*arrays, small)
    return (*res[:8], res[8].reshape(-1), res[9].reshape(-1), res[10])


def fast(
    tokens, doc_lengths, rel_buckets, w_query, w_key, w_value, w_output, w_inner, w_outer,
    attn_gain, ffn_gain, bias_table, out_grad,
):
    n_bins, heads = bias_table.shape
    wide = lambda g: jnp.broadcast_to(g[:, None], (g.shape[0], 128))
    gains = jnp.concatenate([wide(attn_gain), wide(ffn_gain)], axis=1)
    relb = jnp.pad(rel_buckets, (0, 1))[None, :]
    table = jnp.pad(bias_table, ((0, 0), (0, 128 - heads)))
    act, dx, gq, gk, gv, go, gi, gf, small = layer_call(
        tokens, out_grad, gains, w_query, w_key, w_value, w_output, w_inner, w_outer, relb, table, doc_lengths, heads
    )
    return close_call((act, dx, gq, gk, gv, go, gi, gf), small, attn_gain.shape[0], n_bins, heads)


def solution(mesh):
    split = P(("seq", "rows"), None)
    rows = P("rows", "seq", None)
    in_specs = (rows, P("rows"), P()) + (split,) * 6 + (P(("seq", "rows")),) * 2 + (P(), rows)
    out_specs = (rows, rows) + (split,) * 6 + (P(("seq", "rows")),) * 2 + (P(),)
    shape = (mesh.shape["seq"], mesh.shape["rows"])
    program = fast if shape == (NX, NZ * NY * NC) else local
    return jax.shard_map(program, mesh=mesh, in_specs=in_specs, out_specs=out_specs, check_vma=False)
```

```python
import functools

import jax
import jax.numpy as jnp
from jax import lax
from jax.experimental import pallas as pl
from jax.experimental.pallas import tpu as pltpu
from jax.sharding import PartitionSpec as P

MB = 2


EPS = 1e-06
NEG = -1000000000.0
HIGH = lax.Precision.HIGHEST


def normed(h, gain):
    return h * lax.rsqrt(jnp.mean(h * h, axis=-1, keepdims=True) + EPS) * gain


def fetch(shards):
    return (
        lax.all_gather(shards[0], ("seq", "rows"), axis=0, tiled=True),
        lax.all_gather(shards[1], ("seq", "rows"), axis=0, tiled=True),
        lax.all_gather(shards[2], ("seq", "rows"), axis=0, tiled=True),
        lax.all_gather(shards[3], ("seq", "rows"), axis=0, tiled=True),
        lax.all_gather(shards[4], ("seq", "rows"), axis=0, tiled=True),
        lax.all_gather(shards[5], ("seq", "rows"), axis=0, tiled=True),
        lax.all_gather(shards[6], ("seq", "rows"), axis=0, tiled=True),
        lax.all_gather(shards[7], ("seq", "rows"), axis=0, tiled=True),
    )


def local(
    tokens,
    doc_lengths,
    rel_buckets,
    w_query,
    w_key,
    w_value,
    w_output,
    w_inner,
    w_outer,
    attn_gain,
    ffn_gain,
    bias_table,
    out_grad,
):
    f32 = jnp.float32
    bf16 = jnp.bfloat16
    rows_dev, span, width = tokens.shape
    n_bins, heads = bias_table.shape
    head_dim = width // heads
    seq_count = lax.axis_size("seq")
    seq_place = lax.axis_index("seq")
    total = span * seq_count
    q_start = seq_place * span
    per = rows_dev // MB
    flat_rows = per * span
    shards = (w_query, w_key, w_value, w_output, w_inner, w_outer, attn_gain, ffn_gain)
    table = bias_table.astype(f32)
    k_pos = jnp.arange(total, dtype=jnp.int32)
    onehot = (rel_buckets[:, None] == jnp.arange(n_bins, dtype=jnp.int32)[None, :]).astype(f32)
    rel_bias = jnp.dot(onehot, table, precision=HIGH)
    spread = jnp.concatenate([rel_bias.T, jnp.zeros((heads, 1), f32)], axis=1)
    tiled = jnp.tile(spread, (1, total))
    full_bias = tiled[:, : total * (2 * total - 1)].reshape(heads, total, 2 * total - 1)[
        :, :, total - 1 :
    ]
    bias = lax.dynamic_slice_in_dim(full_bias, q_start, span, 1)
    ff_width = w_inner.shape[1]
    grad_wq = jnp.zeros((width, width), f32)
    grad_wk = jnp.zeros((width, width), f32)
    grad_wv = jnp.zeros((width, width), f32)
    grad_wo = jnp.zeros((width, width), f32)
    grad_wi = jnp.zeros((width, ff_width), f32)
    grad_wf = jnp.zeros((ff_width, width), f32)
    grad_g1 = jnp.zeros((width,), f32)
    grad_g2 = jnp.zeros((width,), f32)
    grad_bias = jnp.zeros((heads, span, total), f32)
    outputs = []
    input_grads = []
    for batch in range(MB):
        whole = fetch(shards)
        wq, wk, wv, wo, wi, wf, gain_one, gain_two = whole
        g1 = gain_one.astype(f32)
        g2 = gain_two.astype(f32)
        first = batch * per
        xflat = tokens[first : first + per].astype(f32).reshape(flat_rows, width)
        lens = doc_lengths[first : first + per]
        upstream = out_grad[first : first + per].reshape(flat_rows, width)
        n1 = normed(xflat, g1).astype(bf16)
        query = jnp.dot(n1, wq, preferred_element_type=f32).astype(bf16)
        key_local = jnp.dot(n1, wk, preferred_element_type=f32).astype(bf16)
        value_local = jnp.dot(n1, wv, preferred_element_type=f32).astype(bf16)
        keys_all, values_all = (
            lax.all_gather(key_local.reshape(per, span, width), "seq", axis=1, tiled=True),
            lax.all_gather(value_local.reshape(per, span, width), "seq", axis=1, tiled=True),
        )
        q4 = query.reshape(per, span, heads, head_dim)
        k4 = keys_all.reshape(per, total, heads, head_dim)
        v4 = values_all.reshape(per, total, heads, head_dim)
        valid = k_pos[None, :] < lens[:, None]

        def scores():
            raw = jnp.einsum("bqhd,bkhd->bhqk", q4, k4, preferred_element_type=f32) + bias[None]
            return jnp.where(valid[:, None, None, :], raw, NEG)

        first_scores = scores()
        top = jnp.max(first_scores, axis=-1, keepdims=True)
        expo = jnp.exp(first_scores - top)
        denom = jnp.sum(expo, axis=-1, keepdims=True)
        probs_low = (expo / denom).astype(bf16)
        mixed = jnp.einsum("bhqk,bkhd->bqhd", probs_low, v4, preferred_element_type=f32)
        mixed = mixed.reshape(flat_rows, width).astype(bf16)
        h1 = xflat + jnp.dot(mixed, wo, preferred_element_type=f32)
        n2 = normed(h1, g2).astype(bf16)
        inner = jnp.dot(n2, wi, preferred_element_type=f32)
        act_full, gelu_pull = jax.vjp(jax.nn.gelu, inner)
        act = act_full.astype(bf16)
        result = h1 + jnp.dot(act, wf, preferred_element_type=f32)
        outputs.append(result.astype(bf16).reshape(per, span, width))
        grad_wf = grad_wf + jnp.einsum("tf,td->fd", act, upstream, preferred_element_type=f32)
        d_act = jnp.einsum("td,fd->tf", upstream, wf, preferred_element_type=f32)
        d_inner = gelu_pull(d_act)[0].astype(bf16)
        grad_wi = grad_wi + jnp.einsum("td,tf->df", n2, d_inner, preferred_element_type=f32)
        d_n2 = jnp.einsum("tf,df->td", d_inner, wi, preferred_element_type=f32)
        norm_pull = jax.vjp(normed, h1, g2)[1]
        dh_part, dg_two = norm_pull(d_n2)
        grad_g2 = grad_g2 + dg_two
        dh1 = upstream.astype(f32) + dh_part
        d_attn = dh1.astype(bf16)
        grad_wo = grad_wo + jnp.einsum("td,te->de", mixed, d_attn, preferred_element_type=f32)
        d_mixed = jnp.einsum("te,de->td", d_attn, wo, preferred_element_type=f32).astype(bf16)
        dm4 = d_mixed.reshape(per, span, heads, head_dim)
        probs = jnp.exp(scores() - top) / denom
        d_probs = jnp.einsum("bqhd,bkhd->bhqk", dm4, v4, preferred_element_type=f32)
        value_terms = jnp.einsum("bhqk,bqhd->bkhd", probs_low, dm4, preferred_element_type=f32)
        delta = jnp.sum(probs * d_probs, axis=-1, keepdims=True)
        d_scores = (probs * (d_probs - delta)).astype(bf16)
        grad_bias = grad_bias + jnp.sum(d_scores.astype(f32), axis=0)
        d_query = jnp.einsum("bhqk,bkhd->bqhd", d_scores, k4, preferred_element_type=f32)
        d_query = d_query.reshape(flat_rows, width).astype(bf16)
        key_terms = jnp.einsum("bhqk,bqhd->bkhd", d_scores, q4, preferred_element_type=f32)
        key_share, value_share = (
            lax.psum_scatter(
                key_terms.reshape(per, total, width), "seq", scatter_dimension=1, tiled=True
            ),
            lax.psum_scatter(
                value_terms.reshape(per, total, width), "seq", scatter_dimension=1, tiled=True
            ),
        )
        d_key = key_share.reshape(flat_rows, width).astype(bf16)
        d_value = value_share.reshape(flat_rows, width).astype(bf16)
        grad_wq = grad_wq + jnp.einsum("td,te->de", n1, d_query, preferred_element_type=f32)
        grad_wk = grad_wk + jnp.einsum("td,te->de", n1, d_key, preferred_element_type=f32)
        grad_wv = grad_wv + jnp.einsum("td,te->de", n1, d_value, preferred_element_type=f32)
        d_n1 = jnp.einsum("te,de->td", d_query, wq, preferred_element_type=f32)
        d_n1 = d_n1 + jnp.einsum("te,de->td", d_key, wk, preferred_element_type=f32)
        d_n1 = d_n1 + jnp.einsum("te,de->td", d_value, wv, preferred_element_type=f32)
        first_pull = jax.vjp(normed, xflat, g1)[1]
        dx_part, dg_one = first_pull(d_n1)
        grad_g1 = grad_g1 + dg_one
        input_grads.append((dh1 + dx_part).reshape(per, span, width))
    owned = (
        lax.psum_scatter(grad_wq, ("seq", "rows"), scatter_dimension=0, tiled=True),
        lax.psum_scatter(grad_wk, ("seq", "rows"), scatter_dimension=0, tiled=True),
        lax.psum_scatter(grad_wv, ("seq", "rows"), scatter_dimension=0, tiled=True),
        lax.psum_scatter(grad_wo, ("seq", "rows"), scatter_dimension=0, tiled=True),
        lax.psum_scatter(grad_wi, ("seq", "rows"), scatter_dimension=0, tiled=True),
        lax.psum_scatter(grad_wf, ("seq", "rows"), scatter_dimension=0, tiled=True),
        lax.psum_scatter(grad_g1, ("seq", "rows"), scatter_dimension=0, tiled=True),
        lax.psum_scatter(grad_g2, ("seq", "rows"), scatter_dimension=0, tiled=True),
    )
    grad_full = lax.dynamic_update_slice_in_dim(
        jnp.zeros((heads, total, total), f32), grad_bias, q_start, 1
    )
    widened = jnp.pad(grad_full, ((0, 0), (0, 0), (total - 1, 0)))
    folded = jnp.pad(widened.reshape(heads, total * (2 * total - 1)), ((0, 0), (0, total)))
    rel_grad = jnp.sum(folded.reshape(heads, total, 2 * total), axis=1)[:, : 2 * total - 1]
    table_local = jnp.dot(onehot.T, rel_grad.T, precision=HIGH)
    table_grad = lax.psum(table_local, ("seq", "rows"))
    result_rows = jnp.concatenate(outputs, axis=0)
    grad_rows = jnp.concatenate(input_grads, axis=0)
    return (
        result_rows,
        grad_rows,
        owned[0],
        owned[1],
        owned[2],
        owned[3],
        owned[4],
        owned[5],
        owned[6],
        owned[7],
        table_grad,
    )


MESH_ID = pl.DeviceIdType.MESH
HBM = pl.BlockSpec(memory_space=pl.ANY)
VMEM = pl.BlockSpec(memory_space=pltpu.VMEM)
SMEM = pl.BlockSpec(memory_space=pltpu.SMEM)
BF = jnp.bfloat16
F32 = jnp.float32
NX, NZ, NY, NC = 2, 4, 2, 2


def rcopy(src, dst, send, recv, to):
    return pltpu.make_async_remote_copy(
        src_ref=src, dst_ref=dst, send_sem=send, recv_sem=recv, device_id=to, device_id_type=MESH_ID
    )


class Place:
    def __init__(self):
        self.x = lax.axis_index("seq")
        r = lax.axis_index("rows")
        self.c = lax.rem(r, 2)
        self.y = lax.rem(r // 2, 2)
        self.z = r // 4
        self.core = self.at(self.x, self.y, self.z, 1 - self.c)
        self.xn = self.at(1 - self.x, self.y, self.z, self.c)
        self.yn = self.at(self.x, 1 - self.y, self.z, self.c)
        self.zp = [None] + [self.at(self.x, self.y, self.zz(j), self.c) for j in range(1, NZ)]

    def at(self, x, y, z, c):
        return (x, z * 4 + y * 2 + c)

    def zz(self, j):
        return lax.rem(self.z + j, NZ)

    def barrier(self):
        sem = pltpu.get_barrier_semaphore()
        peers = [self.core, self.xn, self.yn] + self.zp[1:]
        for p in peers:
            pl.semaphore_signal(sem, inc=1, device_id=p, device_id_type=MESH_ID)
        pl.semaphore_wait(sem, len(peers))


class GatherXZY:
    def __init__(self, me, w, base, nh, ss, rr, dd):
        self.me, self.w, self.ss, self.rr, self.dd = me, w, ss, rr, dd
        self.base, self.nh = base, nh

    def cols(self, plane, c):
        return pl.ds(pl.multiple_of(self.base(plane) + c * self.nh, 128), self.nh)

    def ref(self, x, z, y, c, plane):
        return self.w.at[x, z, y, :, self.cols(plane, c)]

    def pair(self, z, y, c):
        return self.w.at[:, z, y, :, self.cols(self.me.x, c)]

    def send(self, ref, s, recv, to):
        rcopy(ref, ref, self.ss.at[s], recv, to).start()

    def got(self, ref, recv):
        rcopy(ref, ref, self.ss.at[0], recv, self.me.core).wait_recv()

    def start(self):
        m = self.me
        self.send(self.ref(m.x, m.z, m.y, m.c, 1 - m.x), 0, self.rr.at[0], m.xn)

    def step_x(self):
        m = self.me
        self.got(self.ref(1 - m.x, m.z, m.y, m.c, m.x), self.rr.at[0])
        p = self.pair(m.z, m.y, m.c)
        for j in range(1, NZ):
            self.send(p, j, self.rr.at[NZ - j], m.zp[j])
        self.send(p, 4, self.rr.at[4], m.yn)
        self.send(p, 8, self.dd.at[0], m.core)

    def step_z(self, j):
        m = self.me
        p = self.pair(m.zz(j), m.y, m.c)
        self.got(p, self.rr.at[j])
        self.send(p, 4 + j, self.rr.at[4 + j], m.yn)
        self.send(p, 8 + j, self.dd.at[j], m.core)

    def step_y(self, j):
        m = self.me
        p = self.pair(m.zz(j), 1 - m.y, m.c)
        self.got(p, self.rr.at[4 + j])
        self.send(p, 12 + j, self.dd.at[4 + j], m.core)

    def done(self):
        m = self.me
        for j in range(NZ):
            self.got(self.pair(m.zz(j), m.y, 1 - m.c), self.dd.at[j])
        for j in range(NZ):
            self.got(self.pair(m.zz(j), 1 - m.y, 1 - m.c), self.dd.at[4 + j])

    def sent(self):
        m = self.me
        one = self.ref(m.x, m.z, m.y, m.c, m.x)
        rcopy(one, one, self.ss.at[0], self.rr.at[0], m.core).wait_send()
        p = self.pair(m.z, m.y, m.c)
        for s in range(1, 16):
            rcopy(p, p, self.ss.at[s], self.rr.at[0], m.core).wait_send()


class GatherZYX:
    def __init__(self, me, w, ss, rr, dd):
        self.me, self.w, self.ss, self.rr, self.dd = me, w, ss, rr, dd

    def send(self, ref, s, recv, to):
        rcopy(ref, ref, self.ss.at[s], recv, to).start()

    def got(self, ref, recv):
        rcopy(ref, ref, self.ss.at[0], recv, self.me.core).wait_recv()

    def start(self):
        m = self.me
        own = self.w.at[m.x, m.z, m.y, m.c]
        for j in range(1, NZ):
            self.send(own, j - 1, self.rr.at[NZ - j - 1], m.zp[j])
        self.send(own, 3, self.rr.at[3], m.yn)

    def step_z(self, j):
        m = self.me
        b = self.w.at[m.x, m.zz(j), m.y, m.c]
        self.got(b, self.rr.at[j - 1])
        self.send(b, 5 + j, self.rr.at[3 + j], m.yn)

    def step_y(self, j):
        m = self.me
        self.got(self.w.at[m.x, m.zz(j), 1 - m.y, m.c], self.rr.at[3 + j])
        p = self.w.at[m.x, m.zz(j), :, m.c]
        self.send(p, 4 if j == 0 else 8 + j, self.rr.at[7 + j], m.xn)
        self.send(p, 5 if j == 0 else 11 + j, self.dd.at[j], m.core)

    def step_x(self, j):
        m = self.me
        p = self.w.at[1 - m.x, m.zz(j), :, m.c]
        self.got(p, self.rr.at[7 + j])
        self.send(p, 15 + j, self.dd.at[4 + j], m.core)

    def done_near(self):
        m = self.me
        for j in range(NZ):
            self.got(self.w.at[m.x, m.zz(j), :, 1 - m.c], self.dd.at[j])

    def done_far(self):
        m = self.me
        for j in range(NZ):
            self.got(self.w.at[1 - m.x, m.zz(j), :, 1 - m.c], self.dd.at[4 + j])

    def sent(self):
        m = self.me
        one = self.w.at[m.x, m.z, m.y, m.c]
        p = self.w.at[m.x, m.z, :, m.c]
        for s in range(19):
            r = one if s in (0, 1, 2, 3, 6, 7, 8) else p
            rcopy(r, r, self.ss.at[s], self.rr.at[0], m.core).wait_send()


def own_block(me, mine, theirs, w, parts):
    a = mine[...].astype(F32)[:24]
    b = theirs[...].astype(F32)[:24]
    first = jnp.where(me.c == 0, a, b)
    second = jnp.where(me.c == 0, b, a)
    both = jnp.concatenate([first, second], axis=0).astype(BF)
    at = 0
    for n, base in parts:
        w[me.x, me.z, me.y, :, pl.ds(pl.multiple_of(base, 128), n)] = both[:, at : at + n]
        at += n


class Piece:
    def __init__(self, index, rows, first):
        self.index, self.slot, self.rows = index, index % 2, rows
        cut = rows // 2 if rows // 2 % 16 == 0 else rows // 2 + 8
        self.subs = ((0, cut, first[0]), (cut, rows - cut, first[1]))


def acc_rows(x, y, z, lo, n):
    return pl.ds(pl.multiple_of(((x * NY + y) * NZ + z) * 192 + lo, 8), n)


class Reduce:
    def __init__(self, me, acc, a1, a2, a3, cs, cr, s1s, s1r, s2s, s2r, s3s, s3r, fin, finr, keep, sems):
        self.me = me
        self.acc, self.a1, self.a2, self.a3, self.cs, self.cr = acc, a1, a2, a3, cs, cr
        self.s1s, self.s1r, self.s2s, self.s2r, self.s3s, self.s3r = s1s, s1r, s2s, s2r, s3s, s3r
        self.fin, self.finr = fin, finr
        self.keep = keep
        (self.c_s, self.c_r, self.a_s, self.a_r, self.b_s, self.b_r, self.z_s, self.z_r, self.f_s, self.f_r) = sems

    def near(self, axis):
        return self.me.xn if axis == "x" else self.me.yn

    def core_copy(self, p):
        s, n = p.slot, p.rows
        return rcopy(
            self.cs.at[:, :, :, 0:n], self.cr.at[s, :, :, :, 0:n], self.c_s.at[s], self.c_r.at[s], self.me.core
        )

    def one_copy(self, p, k):
        s, (_, n, axis) = p.slot, p.subs[k]
        return rcopy(
            self.s1s.at[k, :, :, 0:n], self.s1r.at[s, k, :, :, 0:n], self.a_s.at[s, k], self.a_r.at[s, k], self.near(axis)
        )

    def two_copy(self, p, k):
        s, (_, n, axis) = p.slot, p.subs[k]
        to = self.near("y" if axis == "x" else "x")
        return rcopy(self.s2s.at[k, :, 0:n], self.s2r.at[s, k, :, 0:n], self.b_s.at[s, k], self.b_r.at[s, k], to)

    def z_copy(self, p, j):
        s, n = p.slot, p.rows
        return rcopy(
            self.s3s.at[j, 0:n], self.s3r.at[s, NZ - j, 0:n], self.z_s.at[s, j], self.z_r.at[s, NZ - j], self.me.zp[j]
        )

    def fin_copy(self, p):
        i, n = p.index, p.rows // 2
        return rcopy(
            self.fin.at[i, 0:n], self.finr.at[i, 0:n], self.f_s.at[i], self.f_r.at[i], self.me.core
        )

    def send_core(self, p):
        self.core_copy(p).start()

    def h1(self, p, old):
        me, s, n = self.me, p.slot, p.rows
        self.core_copy(p).wait_recv()
        for k, (lo, n, axis) in enumerate(p.subs):
            if old is not None:
                self.one_copy(old, k).wait_send()
            rows = pl.ds(lo, n)

            def body(q, carry):
                a, zq = q // NZ, lax.rem(q, NZ)
                if axis == "x":
                    keep, away = (me.x, a, zq, rows), (1 - me.x, a, zq, rows)
                else:
                    keep, away = (a, me.y, zq, rows), (a, 1 - me.y, zq, rows)
                held = [self.acc[acc_rows(*at[:3], lo, n), :] for at in (keep, away)]
                self.a1[k, a, zq, 0:n] = held[0] + self.cr[(s,) + keep].astype(F32)
                self.s1s[k, a, zq, 0:n] = (held[1] + self.cr[(s,) + away].astype(F32)).astype(BF)
                return carry

            lax.fori_loop(0, 2 * NZ, body, 0)
            self.one_copy(p, k).start()

    def h2(self, p, old):
        me, s = self.me, p.slot
        for k, (lo, n, axis) in enumerate(p.subs):
            self.one_copy(p, k).wait_recv()
            if old is not None:
                self.two_copy(old, k).wait_send()
            b = me.y if axis == "x" else me.x

            def body(zq, carry):
                self.a2[k, zq, 0:n] = self.a1[k, b, zq, 0:n] + self.s1r[s, k, b, zq, 0:n].astype(F32)
                self.s2s[k, zq, 0:n] = (
                    self.a1[k, 1 - b, zq, 0:n] + self.s1r[s, k, 1 - b, zq, 0:n].astype(F32)
                ).astype(BF)
                return carry

            lax.fori_loop(0, NZ, body, 0)
            self.two_copy(p, k).start()

    def h3(self, p, old):
        me, s = self.me, p.slot
        for k in range(2):
            self.two_copy(p, k).wait_recv()
        for j in range(1, NZ):
            if old is not None:
                self.z_copy(old, j).wait_send()
        for k, (lo, n, _) in enumerate(p.subs):
            rows = pl.ds(lo, n)
            for j in range(NZ):
                zq = me.zz(j)
                v = self.a2[k, zq, 0:n] + self.s2r[s, k, zq, 0:n].astype(F32)
                if j == 0:
                    self.a3[rows] = v
                else:
                    self.s3s[j, rows] = v.astype(BF)
        for j in range(1, NZ):
            self.z_copy(p, j).start()

    def h4(self, p):
        me, s, n, i = self.me, p.slot, p.rows, p.index
        for j in range(1, NZ):
            self.z_copy(p, NZ - j).wait_recv()
        total = self.a3[0:n]
        for j in range(1, NZ):
            total = total + self.s3r[s, j, 0:n].astype(F32)
        if p.groups is None:
            a, b = total[0 : n // 2], total[n // 2 :]
        else:
            a, b = (
                jnp.concatenate([total[48 * g + 24 * k : 48 * g + 24 * k + 24] for g in range(p.groups)], axis=0)
                for k in range(NC)
            )
        self.fin[i, 0 : n // 2] = jnp.where(me.c == 0, b, a)
        self.keep(p, jnp.where(me.c == 0, a, b), me.c)
        self.fin_copy(p).start()


def norm_back(h, gain, up):
    r = lax.rsqrt(jnp.mean(h * h, axis=-1, keepdims=True) + EPS)
    hr = h * r
    w = up * gain
    dgain = jnp.sum(up * hr, axis=0, keepdims=True)
    return r * (w - hr * jnp.mean(w * hr, axis=-1, keepdims=True)), dgain


def layer_kernel(
    tok, gin, gains, wq, wk, wv, wo, wi, pd, relb, table, lens,
    act_o, dx_o, gq_o, gk_o, gv_o, go_o, gi_o, gf_o, sm_o,
    WA, WB, WD, X, G, N2, QKV, O, H1, ACT, DU, T, M, MACC, LSE, R, RG,
    ACC, A1, A2, A3, CS, CR, S1S, S1R, S2S, S2R, S3S, S3R, FIN, FINR, SM, SMR, ZB, DG,
    ts, tr, tl, gs, gr, gl, es, er, as_, ar, ad, a2s, a2r, a2d, os_, or_, od, bs, br, bd, b2s, b2r, b2d, ds_, dr, dd, ys, yr, yl, xs_, xr, xl,
    c_s, c_r, a_s, a_r, b_s, b_r, z_s, z_r, f_s, f_r, ms, mr,
):
    me = Place()
    x, y, z, c = me.x, me.y, me.z, me.c
    mine, span, width = X.shape[0], X.shape[2], X.shape[3]
    length = 2 * span
    flat = mine * length
    ff = DU.shape[1]
    na, nb = WA.shape[4] // 2, WB.shape[4] // 2
    PA, PB = DU.at[pl.ds(32 * c, 32), 0:na], DU.at[pl.ds(64 + 32 * c, 32), 0:nb]
    RA, RB = DU.at[128:160, 0:na], DU.at[160:192, 0:nb]
    hd = 64
    YB = N2
    pairs = width // hd // 2
    half_ff, half_w = ff // 2, width // 2
    n1, n2_ = (256 + 3 * 256) // 2, 3 * (width - 256) // 2
    gath_a = GatherXZY(me, WA, lambda plane: 0, n1, as_, ar, ad)
    gath_e = GatherXZY(me, WA, lambda plane: 2 * n1, n2_, a2s, a2r, a2d)
    gath_o = GatherXZY(me, WB, lambda plane: 0, half_w, os_, or_, od)
    gath_1 = GatherXZY(me, WB, lambda plane: width + half_ff * plane, half_ff // 2, bs, br, bd)
    gath_2 = GatherXZY(me, WB, lambda plane: width + half_ff * (1 - plane), half_ff // 2, b2s, b2r, b2d)
    gath_d = GatherZYX(me, WD, ds_, dr, dd)

    def pack(first, n, parts):
        filled = [
            jnp.concatenate([p.astype(F32), jnp.zeros((32 - p.shape[0], p.shape[1]), F32)], axis=0) for p in parts
        ]
        DU[first : first + 32, 0:n] = jnp.concatenate(filled, axis=1).astype(BF)

    quarter = half_ff // 2
    part = width - 256
    pack(0, na, (gains[...], wq[:, 0:256], wq[:, 256:], wk[:, 256 : 256 + part // 2]))
    pack(32, na, (wk[:, 0:256], wv[:, 0:256], wk[:, 256 + part // 2 :], wv[:, 256:]))
    me.barrier()
    ea = rcopy(DU.at[pl.ds(32 * (1 - c), 32), 0:na], RA, es.at[0], er.at[0], me.core)
    eb = rcopy(DU.at[pl.ds(64 + 32 * (1 - c), 32), 0:nb], RB, es.at[1], er.at[1], me.core)
    ea.start()
    for k in range(2):
        first = wi[:, quarter * k : quarter * k + quarter]
        second = wi[:, half_ff + quarter * k : half_ff + quarter * k + quarter]
        pack(64 + 32 * k, nb, (wo[:, half_w * k : half_w * k + half_w], first, second))
    eb.start()
    tok_r = [rcopy(tok.at[2 * (1 - x) + i], X.at[i, x], ts.at[i], tr.at[i], me.xn) for i in range(mine)]
    tok_in = [rcopy(X.at[i, 1 - x], X.at[i, 1 - x], ts.at[i], tr.at[i], me.xn) for i in range(mine)]
    tok_l = [pltpu.make_async_copy(tok.at[2 * x + i], X.at[i, x], tl.at[i]) for i in range(mine)]
    g_r = rcopy(gin.at[pl.ds(2 * (1 - x), 2)], G.at[:, x], gs, gr, me.xn)
    g_in = rcopy(G.at[:, 1 - x], G.at[:, 1 - x], gs, gr, me.xn)
    g_l = pltpu.make_async_copy(gin.at[pl.ds(2 * x, 2)], G.at[:, x], gl)
    ea.wait_recv()
    own_block(me, PA, RA, WA, ((n1, c * n1), (n2_, 2 * n1 + c * n2_)))
    gath_a.start()
    for i in range(mine):
        tok_r[i].start()
        tok_l[i].start()
    g_l.start()
    eb.wait_recv()
    own_block(
        me, PB, RB, WB,
        ((half_w, c * half_w), (quarter, width + c * quarter), (quarter, width + half_ff + c * quarter)),
    )
    WD[x, z, y, c] = pd[...]
    cols = relb.shape[1]
    kinds = table.shape[0]
    hot = (lax.broadcasted_iota(jnp.int32, (kinds, cols), 0) == relb[...]).astype(BF)
    R[...] = lax.dot_general(table[...], hot, (((0,), (0,)), ((), ())), preferred_element_type=F32)[0:16]
    gath_a.step_x()
    gath_e.start()
    gath_o.start()
    gath_1.start()
    gath_d.start()
    for j in range(1, NZ):
        gath_a.step_z(j)
    gath_e.step_x()
    for j in range(NZ):
        gath_a.step_y(j)
    gath_o.step_x()
    gath_1.step_x()
    gath_d.step_y(0)
    for j in range(1, NZ):
        gath_e.step_z(j)
    gath_a.done()

    def gain_row(k):
        return jnp.transpose(WA[:, :, :, :, 128 * k : 128 * k + 128].reshape(width, 128).astype(F32))[0:1, :]

    gain1 = gain_row(0)

    def row_slice(i):
        return pl.ds(pl.multiple_of(i * length, length), length)

    def first_norm(i):
        for half in range(2):
            xf = X[i, half].astype(F32)
            scale = lax.rsqrt(jnp.mean(xf * xf, axis=-1, keepdims=True) + EPS)
            N2[i, half] = (xf * scale * gain1).astype(BF)

    def project(i, first, count):
        for n in range(count):
            lo = (first + n) * width
            QKV[row_slice(i), lo : lo + width] = jnp.dot(
                N2[i].reshape(length, width),
                WA[:, :, :, :, 256 + lo : 256 + lo + width].reshape(width, width),
                preferred_element_type=F32,
            ).astype(BF)

    for i in range(mine):
        tok_l[i].wait()
        tok_in[i].wait_recv()
        first_norm(i)
        project(i, 0, 1)
    gath_2.start()
    g_r.start()
    low = lax.broadcasted_iota(jnp.int32, (1, 128), 1) < hd
    lane = lax.broadcasted_iota(jnp.int32, (1, 128), 1)
    kpos = lax.broadcasted_iota(jnp.int32, (length, 128), 0)
    blocks = length // 128

    def strips(p):
        for h in range(2):
            row = jnp.broadcast_to(R[pl.ds(2 * p + h, 1), :], (128, cols))
            M[h] = pltpu.roll(row, cols - 127, 1, stride=1, stride_axis=0)[:, : M.shape[2]]

    def bias_of(h):
        return jnp.concatenate(
            [M[h, :, 128 * (blocks - 1 - a) : 128 * (blocks - 1 - a) + length] for a in range(blocks)], axis=0
        )

    own = (low, jnp.logical_not(low))
    spare = (hd, 0)
    ones = [(lane == spare[h]).astype(F32).astype(BF) for h in range(2)]
    none = jnp.zeros((), BF)

    def masked_keys(h, k, count):
        pad = jnp.where((lane == spare[h]) & (kpos >= count), NEG, 0.0).astype(BF)
        return jnp.where(own[h], k, pad)

    def lanes(n, p):
        at = jnp.where(p < 2, n * 256 + p * 128, width + n * (width - 256) + (p - 2) * 128)
        return pl.ds(pl.multiple_of(at, 128), 128)

    def wide_lanes(p):
        return pl.ds(pl.multiple_of(p * 128, 128), 128)

    nt = (((1,), (1,)), ((), ()))
    tn = (((0,), (0,)), ((), ()))

    def mm(a, b, dims):
        return lax.dot_general(a, b, dims, preferred_element_type=F32)

    o_, b1, b2, d_, e_ = gath_o, gath_1, gath_2, gath_d, gath_e
    comm = {
        0: ((e_.step_y, 0), (e_.step_y, 1)),
        1: ((e_.step_y, 2), (e_.step_y, 3)),
        2: ((o_.step_z, 1), (b1.step_z, 1), (d_.step_z, 1)),
        3: ((o_.step_z, 2), (b1.step_z, 2), (d_.step_z, 2)),
        4: ((o_.step_z, 3), (b1.step_z, 3), (d_.step_z, 3), (lambda j: b2.step_x(), 0)),
        5: ((o_.step_y, 0), (b1.step_y, 0), (d_.step_y, 1)),
        6: ((o_.step_y, 1), (b1.step_y, 1), (d_.step_y, 2)),
        7: ((o_.step_y, 2), (b1.step_y, 2), (d_.step_y, 3)),
        8: ((o_.step_y, 3), (b1.step_y, 3), (d_.step_x, 0), (b2.step_z, 1)),
        9: ((b2.step_z, 2), (d_.step_x, 1)),
        10: ((b2.step_z, 3), (b2.step_y, 0), (d_.step_x, 2)),
        11: ((b2.step_y, 1), (d_.step_x, 3)),
    }

    def attend(t, carry):
        p, i = t // mine, lax.rem(t, mine)
        pl.when(i == 0)(lambda: strips(p))
        rows = row_slice(i)
        q, k, v = QKV[rows, lanes(0, p)], QKV[rows, lanes(1, p)], QKV[rows, lanes(2, p)]
        outs = []
        for h in range(2):
            s = mm(jnp.where(own[h], q, ones[h]), masked_keys(h, k, lens[2 * x + i]), nt) + bias_of(h)
            top = jnp.max(s, axis=-1, keepdims=True)
            e = jnp.exp(s - top)
            total = jnp.sum(e, axis=-1, keepdims=True)
            LSE[rows, :] = jnp.where(lane == 2 * p + h, top + jnp.log(total), LSE[rows, :])
            outs.append(jnp.dot((e * (1.0 / total)).astype(BF), v, preferred_element_type=F32))
        O[i, :, :, wide_lanes(p)] = jnp.where(low, outs[0], outs[1]).astype(BF).reshape(2, span, 128)
        for at, steps in comm.items():
            @pl.when(t == at)
            def _():
                for step, j in steps:
                    step(j)
        return carry

    LSE[...] = jnp.zeros_like(LSE)
    lax.fori_loop(0, 2 * mine, attend, 0)
    gath_e.done()
    for i in range(mine):
        project(i, 1, 2)
    lax.fori_loop(2 * mine, mine * pairs, attend, 0)
    ea.wait_send()
    eb.wait_send()
    gath_o.done()
    gath_1.done()
    gath_d.done_near()
    g_l.wait()
    g_in.wait_recv()

    gain2 = gain_row(1)
    DG[...] = jnp.zeros_like(DG)
    c0, c1 = 0.7978845608028654, 0.044715

    def dn_set(v):
        for n in range(width // 128):
            ACC[length * n : length * n + length, :] = v[:, 128 * n : 128 * n + 128]

    def dn_get(lo, n):
        return jnp.concatenate([ACC[length * k + lo : length * k + lo + n, :] for k in range(width // 128)], axis=1)

    def dn_add(v):
        for n in range(width // 128):
            at = slice(length * n, length * n + length)
            ACC[at, :] = ACC[at, :] + v[:, 128 * n : 128 * n + 128]

    wo_all = lambda: WB[:, :, :, :, 0:width].reshape(width, width)
    for i in range(mine):
        h1 = X[i].reshape(length, width).astype(F32) + jnp.dot(
            O[i].reshape(length, width), wo_all(), preferred_element_type=F32
        )
        H1[i] = h1.reshape(2, span, width)
        r = lax.rsqrt(jnp.mean(h1 * h1, axis=-1, keepdims=True) + EPS)
        N2[i] = (h1 * r * gain2).astype(BF).reshape(2, span, width)

    def chunk(n, carry):
        @pl.when(n == 2)
        def _():
            gath_2.done()
            gath_d.done_far()

        f = lax.rem(2 * x + n, 4)

        def one_row(i, carry):
            pl.when((n == 0) & (i == 0))(lambda: gath_2.step_y(2))
            pl.when((n == 0) & (i == 1))(lambda: gath_2.step_y(3))
            n2, g = N2[i].reshape(length, width), G[i].reshape(length, width)
            for part in range(3):
                fcols = pl.ds(pl.multiple_of(f * width + 256 * part, 256), 256)
                wcols = pl.ds(pl.multiple_of(width + f * width + 256 * part, 256), 256)
                wi_part = WB[:, :, :, :, wcols].reshape(width, 256)
                wf_part = WD[f // 2, pl.ds(2 * lax.rem(f, 2), 2)].reshape(width, width)[256 * part : 256 * part + 256]
                u = jnp.dot(n2, wi_part, preferred_element_type=F32)
                da = mm(g, wf_part, nt)
                sq = u * u
                t = jnp.tanh(u * (c0 + (c0 * c1) * sq))
                cdf = 0.5 + 0.5 * t
                ACT[row_slice(i), fcols] = (u * cdf).astype(BF)
                slope = cdf + (0.5 * u) * (1.0 - t * t) * (c0 + (3.0 * c0 * c1) * sq)
                DU[row_slice(i), fcols] = (da * slope).astype(BF)
            return carry

        return lax.fori_loop(0, mine, one_row, carry)

    lax.fori_loop(0, ff // width, chunk, 0)
    def keep(p, value, core):
        if p.groups is None:
            gf_o[:, pl.ds(pl.multiple_of(256 * p.part + 128 * core, 128), 128)] = value
            return
        for g in range(p.groups):
            if p.kind == "i":
                dst, base = gi_o, 1024 * p.part + 256 * g
            elif p.kind == "o":
                dst, base = go_o, 256 * g
            else:
                dst, base = (gq_o, gk_o, gv_o)[g], 256 * p.part
            dst[:, pl.ds(pl.multiple_of(base + 128 * core, 128), 128)] = value[24 * g : 24 * g + 24]

    red = Reduce(
        me, ACC, A1, A2, A3, CS, CR, S1S, S1R, S2S, S2R, S3S, S3R, FIN, FINR, keep, (c_s, c_r, a_s, a_r, b_s, b_r, z_s, z_r, f_s, f_r)
    )
    pieces = []
    kinds_of = [("f", 0), ("f", 1), ("f", 2), ("i", 0), ("i", 1), ("i", 2), ("o", 0), ("qkv", 0), ("qkv", 1), ("qkv", 2)]
    made_at = [0, 2, 4, 5, 6, 7, 8, 13, 15, 17]
    last = len(kinds_of)
    for n in range(last):
        kind, part = kinds_of[n]
        piece = Piece(n, 144 if kind in ("o", "qkv") else 192, ("y", "y") if n < last - 1 else ("x", "x"))
        piece.kind, piece.part = kind, part
        piece.groups = None if kind == "f" else piece.rows // 48
        pieces.append(piece)

    def stages(n):
        def at(k):
            return pieces[made_at.index(n - k)] if n - k in made_at else None

        def old(p):
            return pieces[p.index - 1] if p.index else None

        if at(4):
            red.h4(at(4))
        if at(3):
            red.h3(at(3), old(at(3)))
        if at(2):
            red.h2(at(2), old(at(2)))
        if at(1):
            red.h1(at(1), old(at(1)))
        if at(0):
            if old(at(0)):
                red.core_copy(old(at(0))).wait_send()
            produce(at(0))

    def split(res):
        a, b = res[:, 0:128], res[:, 128:256]
        return jnp.where(c == 0, a, b), jnp.where(c == 0, b, a).astype(BF)

    def outer_piece(j):

        def body(q, carry):
            xq, zh = q // 2, lax.rem(q, 2)
            lhs = ACT[:, pl.ds(pl.multiple_of(q * 768, 768), 768)]
            rhs = G[:, :, :, 256 * j : 256 * j + 256].reshape(flat, 256)
            own, other = split(mm(lhs, rhs, tn))
            for b in range(4):
                at = (xq, b % 2, 2 * zh + b // 2)
                ACC[acc_rows(*at, 0, 192), :] = own[192 * b : 192 * b + 192]
                CS[at] = other[192 * b : 192 * b + 192]
            return carry

        lax.fori_loop(0, 4, body, 0)

    def rows_piece(groups, rhs):
        def body(g, carry):
            own, other = split(jnp.dot(T[...], rhs(g), preferred_element_type=F32))
            at = pl.ds(pl.multiple_of(48 * g, 48), 48)
            for k in range(NX * NZ * NY):
                ACC[acc_rows(k // 8, k % 2, (k // 2) % 4, 48 * g, 48), :] = own[48 * k : 48 * k + 48]
                CS[k // 8, k % 2, (k // 2) % 4, at] = other[48 * k : 48 * k + 48]
            return carry

        lax.fori_loop(0, groups, body, 0)

    def produce(p):
        if p.kind == "f":
            outer_piece(p.part)
        elif p.kind == "i":
            rows_piece(4, lambda g: DU[:, pl.ds(pl.multiple_of(1024 * p.part + 256 * g, 256), 256)])
        elif p.kind == "o":
            T[...] = jnp.transpose(O[...].reshape(flat, width))
            rows_piece(3, lambda g: H1[:, :, :, pl.ds(pl.multiple_of(256 * g, 256), 256)].reshape(flat, 256).astype(BF))
        else:
            base, wide = (0, 256) if p.part == 0 else (width + 256 * (p.part - 1), width - 256)
            rows_piece(3, lambda g: QKV[:, pl.ds(pl.multiple_of(base + g * wide, 256), 256)])
        red.send_core(p)

    stages(0)
    T[...] = jnp.transpose(N2[...].reshape(flat, width))
    stages(1)

    def result(t, carry):
        i, f = t // 4, lax.rem(t, 4)
        a = ACT[row_slice(i), pl.ds(pl.multiple_of(f * width, width), width)]
        wf = WD[f // 2, pl.ds(2 * lax.rem(f, 2), 2)].reshape(width, width)
        out = jnp.dot(a, wf, preferred_element_type=F32)

        @pl.when(f == 0)
        def _():
            dn_set(H1[i].reshape(length, width) + out)

        @pl.when(f > 0)
        def _():
            dn_add(out)

        @pl.when(f == 3)
        def _():
            YB[i] = dn_get(0, length).astype(BF).reshape(2, span, width)

        return carry

    lax.fori_loop(0, 4 * mine, result, 0)
    y_out = [
        rcopy(YB.at[i, 1 - x], act_o.at[2 * (1 - x) + i], ys.at[i], yr.at[i], me.xn) for i in range(mine)
    ]
    y_loc = [pltpu.make_async_copy(YB.at[i, x], act_o.at[2 * x + i], yl.at[i]) for i in range(mine)]
    for i in range(mine):
        rcopy(YB.at[i, 1 - x], act_o.at[2 * x + i], ys.at[i], yr.at[i], me.xn).start()
        y_loc[i].start()

    stages(2)
    stages(3)

    def back(t, carry):
        i, f = t // 4, lax.rem(t, 4)
        du = DU[row_slice(i), pl.ds(pl.multiple_of(f * width, width), width)]
        wi_part = WB[:, :, :, :, pl.ds(pl.multiple_of((f + 1) * width, width), width)].reshape(width, width)
        out = mm(du, wi_part, nt)

        @pl.when(f == 0)
        def _():
            dn_set(out)

        @pl.when(f > 0)
        def _():
            dn_add(out)

        @pl.when(f == 3)
        def _():
            for half in range(2):
                dh, dgain = norm_back(H1[i, half], gain2, dn_get(span * half, span))
                DG[1:2, :] = DG[1:2, :] + dgain
                H1[i, half] = G[i, half].astype(F32) + dh

        return carry

    lax.fori_loop(0, 4 * mine, back, 0)

    stages(4)
    for i in range(mine):
        dab = H1[i].reshape(length, width).astype(BF)
        G[i] = mm(dab, wo_all(), nt).astype(BF).reshape(2, span, width)
    landing = lambda i: DU.at[pl.ds(i * span, span), 0:width]
    dx_r = [rcopy(X.at[i, 1 - x], landing(i), xs_.at[i], xr.at[i], me.xn) for i in range(mine)]
    dx_l = [pltpu.make_async_copy(H1.at[i, x], dx_o.at[2 * x + i], xl.at[i]) for i in range(mine)]
    dx_f = [pltpu.make_async_copy(H1.at[i, 1 - x], dx_o.at[2 * (1 - x) + i], xl.at[mine + i]) for i in range(mine)]

    def input_grad(i):
        for n in range(3):
            out = mm(
                QKV[row_slice(i), n * width : (n + 1) * width],
                WA[:, :, :, :, 256 + n * width : 256 + (n + 1) * width].reshape(width, width),
                nt,
            )
            (dn_set if n == 0 else dn_add)(out)
        for half in range(2):
            dh, dgain = norm_back(X[i, half].astype(F32), gain1, dn_get(span * half, span))
            DG[0:1, :] = DG[0:1, :] + dgain
            H1[i, half] = H1[i, half] + dh
        X[i, 1 - x] = H1[i, 1 - x].astype(BF)
        dx_r[i].start()
        dx_l[i].start()

    def norm_again():
        for i in range(mine):
            y_out[i].wait_recv()
            y_out[i].wait_send()
            y_loc[i].wait()
        for i in range(mine):
            first_norm(i)
        T[...] = jnp.transpose(N2[...].reshape(flat, width))

    def attend_back(t, carry):
        i, p = t // pairs, lax.rem(t, pairs)
        strips(p)
        MACC[...] = jnp.zeros_like(MACC)
        rows = row_slice(i)
        q, k, v = QKV[rows, lanes(0, p)], QKV[rows, lanes(1, p)], QKV[rows, lanes(2, p)]
        do = G[i, :, :, wide_lanes(p)].reshape(length, 128)
        prod = do.astype(F32) * O[i, :, :, wide_lanes(p)].reshape(length, 128).astype(F32)
        dqs, dks, dvs = [], [], []
        for h in range(2):
            lse = jnp.sum(jnp.where(lane == 2 * p + h, LSE[rows, :], 0.0), axis=-1, keepdims=True)
            delta = jnp.sum(jnp.where(own[h], prod, 0.0), axis=-1, keepdims=True)
            s = mm(jnp.where(own[h], q, ones[h]), masked_keys(h, k, lens[2 * x + i]), nt) + bias_of(h)
            pr = jnp.exp(s - lse)
            ds = pr * (mm(jnp.where(own[h], do, none), v, nt) - delta)
            for a in range(blocks):
                at = 128 * (blocks - 1 - a)
                MACC[h, :, at : at + length] = MACC[h, :, at : at + length] + ds[128 * a : 128 * a + 128]
            low_p, low_ds = pr.astype(BF), ds.astype(BF)
            dqs.append(jnp.dot(low_ds, k, preferred_element_type=F32))
            dks.append(mm(low_ds, q, tn))
            dvs.append(mm(low_p, do, tn))
        for n, parts in enumerate((dqs, dks, dvs)):
            QKV[rows, lanes(n, p)] = jnp.where(low, parts[0], parts[1]).astype(BF)

        for h in range(2):
            part = jnp.zeros((8, cols), F32)
            for a in range(16):
                part = part + pltpu.roll(MACC[h, 8 * a : 8 * a + 8, :], (cols - 8 * a) % cols, 1)
            line = part[0:1]
            for a in range(1, 8):
                line = line + pltpu.roll(part[a : a + 1], cols - a, 1)
            at = pl.ds(2 * p + h, 1)
            RG[at, :] = RG[at, :] + pltpu.roll(line, 127, 1)

        for n in range(mine * pairs):
            @pl.when(t == n)
            def _():
                stages(5 + n)
                if n == pairs - 1:
                    norm_again()
                if n == pairs:
                    input_grad(0)

        return carry

    RG[...] = jnp.zeros_like(RG)
    MACC[...] = jnp.zeros_like(MACC)
    lax.fori_loop(0, mine * pairs, attend_back, 0)

    stages(17)
    stages(18)
    input_grad(1)
    stages(19)
    stages(20)
    for n in range(width // 128):
        SM[0, n : n + 1, :] = DG[0:1, 128 * n : 128 * n + 128]
        SM[0, 8 + n : 9 + n, :] = DG[1:2, 128 * n : 128 * n + 128]
    rest = jnp.concatenate([RG[...], jnp.zeros((112, cols), F32)], axis=0)
    spread = jnp.zeros((kinds, 128), F32)
    for _ in range(3):
        part = rest.astype(BF)
        rest = rest - part.astype(F32)
        spread = spread + mm(hot, part, nt)
    SM[0, 16 : 16 + kinds, :] = spread
    sm_copies = [
        rcopy(SM.at[k], SMR.at[k], ms.at[k], mr.at[k], to) for k, to in enumerate((me.core, me.xn, me.yn))
    ]
    sm_copies[0].start()
    stages(21)
    for k in range(3):
        sm_copies[k].wait_recv()
        SM[k + 1] = SM[k] + SMR[k]
        if k < 2:
            sm_copies[k + 1].start()
    ZB[z] = SM[3]
    sm_z = [None] + [rcopy(SM.at[3], ZB.at[z], ms.at[2 + j], mr.at[6 - j], me.zp[j]) for j in range(1, NZ)]
    for j in range(1, NZ):
        sm_z[j].start()
    for i in range(mine):
        dx_r[i].wait_recv()
        H1[i, 1 - x] = DU[pl.ds(i * span, span), 0:width].astype(F32)
        dx_f[i].start()
    for p in pieces:
        red.fin_copy(p).wait_recv()
        keep(p, FINR[p.index, 0 : p.rows // 2], 1 - c)
    for j in range(1, NZ):
        rcopy(SM.at[3], ZB.at[me.zz(j)], ms.at[2 + j], mr.at[2 + j], me.zp[j]).wait_recv()
    sm_o[...] = ZB[0] + ZB[1] + ZB[2] + ZB[3]
    g_r.wait_send()
    for k in range(3):
        sm_copies[k].wait_send()
    for j in range(1, NZ):
        sm_z[j].wait_send()
    for g in (gath_a, gath_e, gath_o, gath_1, gath_2, gath_d):
        g.sent()
    for i in range(mine):
        tok_r[i].wait_send()
        dx_r[i].wait_send()
        dx_l[i].wait()
        dx_f[i].wait()
    for p in pieces[-1:]:
        red.core_copy(p).wait_send()
        for k in range(2):
            red.one_copy(p, k).wait_send()
            red.two_copy(p, k).wait_send()
        for j in range(1, NZ):
            red.z_copy(p, j).wait_send()
    for p in pieces:
        red.fin_copy(p).wait_send()


def layer_call(tok, gin, gains, wq, wk, wv, wo, wi, pd, relb, table, lens, heads):
    rows_dev, span, width = tok.shape
    length = 2 * span
    mine = rows_dev // 2
    flat = mine * length
    dma = pltpu.SemaphoreType.DMA
    ff = wi.shape[1]
    na, nb = (gains.shape[1] + 3 * width) // 2, (width + ff) // 2
    count = width // 256 + ff // 1024 + 4
    wa = (NX, NZ, NY, 48, 2 * na)
    wb = (NX, NZ, NY, 48, 2 * nb)
    wd = (NX, NZ, NY, NC) + pd.shape
    xs = (mine, 2, span, width)
    block = (192, 128)
    bf = lambda *s: pltpu.VMEM(s, BF)
    f32 = lambda *s: pltpu.VMEM(s, F32)
    out = lambda *s: jax.ShapeDtypeStruct(s, F32)
    shard = wq.shape[0]
    return pl.pallas_call(
        layer_kernel,
        out_shape=[jax.ShapeDtypeStruct(tok.shape, BF), out(*tok.shape)]
        + [out(shard, width)] * 4 + [out(shard, ff), out(*pd.shape), out(48, 128)],
        in_specs=[HBM, HBM] + [VMEM] * 9 + [SMEM],
        out_specs=[HBM, HBM] + [VMEM] * 7,
        scratch_shapes=[
            bf(*wa), bf(*wb), bf(*wd), bf(*xs), bf(*xs), bf(*xs), bf(flat, 3 * width), bf(*xs), f32(*xs),
             bf(flat, ff), bf(flat, ff), bf(width, flat), f32(2, 128, 896), f32(2, 128, 1024),
            f32(flat, 128), f32(16, relb.shape[1]), f32(16, relb.shape[1]),
            f32(NX * NY * NZ * 192, 128), f32(2, 2, NZ, 96, 128), f32(2, NZ, 96, 128), f32(*block), bf(NX, NY, NZ, *block), bf(2, NX, NY, NZ, *block),
            bf(2, 2, NZ, 96, 128), bf(2, 2, 2, NZ, 96, 128), bf(2, NZ, 96, 128), bf(2, 2, NZ, 96, 128),
            bf(NZ, *block), bf(2, NZ, *block), f32(count, 96, 128), f32(count, 96, 128),
            f32(4, 48, 128), f32(3, 48, 128), f32(NZ, 48, 128), f32(8, width),
            dma((2,)), dma((2,)), dma((2,)), dma, dma, dma, dma((2,)), dma((2,)),
            *[dma((n,)) for _ in range(5) for n in (16, 8, 8)], dma((19,)), dma((11,)), dma((8,)),
            dma((2,)), dma((2,)), dma((2,)), dma((2,)), dma((2,)), dma((4,)),
            dma((2,)), dma((2,)), dma((2, 2)), dma((2, 2)), dma((2, 2)), dma((2, 2)), dma((2, NZ)), dma((2, NZ)),
            dma((count,)), dma((count,)), dma((6,)), dma((6,)),
        ],
        compiler_params=pltpu.CompilerParams(
            collective_id=0, has_side_effects=True, vmem_limit_bytes=VMEM_LIMIT
        ),
        name="layer",
    )(tok, gin, gains, wq, wk, wv, wo, wi, pd, relb, table, lens)


VMEM_LIMIT = 67_000_000


def close_kernel(n_dev, *refs):
    srcs, small, dsts = refs[:8], refs[8], refs[9:17]
    g1, g2, table = refs[17:20]
    held, came, left = refs[20:22], refs[22], refs[23]
    large = [(srcs[k].at[i], held[k].at[i], dsts[k].at[i]) for k in range(2) for i in range(srcs[k].shape[0])]
    loads = [pltpu.make_async_copy(a, b, came.at[n]) for n, (a, b, _) in enumerate(large)]
    stores = [pltpu.make_async_copy(b, c, left.at[n]) for n, (_, b, c) in enumerate(large)]
    for cp in loads:
        cp.start()
    for a, b in zip(srcs[2:], dsts[2:]):
        b[...] = a[...]
    for cp, out in zip(loads, stores):
        cp.wait()
        out.start()
    me = lax.axis_index("seq") * lax.axis_size("rows") + lax.axis_index("rows")
    cut = g1.shape[1]
    width = cut * n_dev
    for k, out in enumerate((g1, g2)):
        row = jnp.concatenate([small[8 * k + j : 8 * k + j + 1, :] for j in range(width // 128)], axis=1)
        out[...] = pltpu.roll(row, lax.rem(width - me * cut, width), 1)[:, 0:cut]
    table[...] = small[16 : 16 + table.shape[0], 0 : table.shape[1]]
    for cp in stores:
        cp.wait()


def close_call(arrays, small, cut, n_bins, heads):
    n_dev = NX * NZ * NY * NC
    like = [jax.ShapeDtypeStruct(a.shape, a.dtype) for a in arrays]
    out = lambda *s: jax.ShapeDtypeStruct(s, F32)
    count = sum(a.shape[0] for a in arrays[:2])
    res = pl.pallas_call(
        functools.partial(close_kernel, n_dev),
        out_shape=like + [out(1, cut), out(1, cut), out(n_bins, heads)],
        in_specs=[HBM] * 2 + [VMEM] * 7,
        out_specs=[HBM] * 2 + [VMEM] * 9,
        scratch_shapes=[pltpu.VMEM(a.shape, a.dtype) for a in arrays[:2]]
        + [pltpu.SemaphoreType.DMA((count,))] * 2,
        name="close",
    )(*arrays, small)
    return (*res[:8], res[8].reshape(-1), res[9].reshape(-1), res[10])


def fast(
    tokens, doc_lengths, rel_buckets, w_query, w_key, w_value, w_output, w_inner, w_outer,
    attn_gain, ffn_gain, bias_table, out_grad,
):
    n_bins, heads = bias_table.shape
    wide = lambda g: jnp.broadcast_to(g[:, None], (g.shape[0], 128))
    gains = jnp.concatenate([wide(attn_gain), wide(ffn_gain)], axis=1)
    relb = jnp.pad(rel_buckets, (0, 1))[None, :]
    table = jnp.pad(bias_table, ((0, 0), (0, 128 - heads)))
    act, dx, gq, gk, gv, go, gi, gf, small = layer_call(
        tokens, out_grad, gains, w_query, w_key, w_value, w_output, w_inner, w_outer, relb, table, doc_lengths, heads
    )
    return close_call((act, dx, gq, gk, gv, go, gi, gf), small, attn_gain.shape[0], n_bins, heads)


def solution(mesh):
    split = P(("seq", "rows"), None)
    rows = P("rows", "seq", None)
    in_specs = (rows, P("rows"), P()) + (split,) * 6 + (P(("seq", "rows")),) * 2 + (P(), rows)
    out_specs = (rows, rows) + (split,) * 6 + (P(("seq", "rows")),) * 2 + (P(),)
    shape = (mesh.shape["seq"], mesh.shape["rows"])
    program = fast if shape == (NX, NZ * NY * NC) else local
    return jax.shard_map(program, mesh=mesh, in_specs=in_specs, out_specs=out_specs, check_vma=False)
```
